32 devices in a mesh: dp: 4 (over y, x), seq: 8 (over z, core).
Axes of the slice: x: 2, y: 2, z: 4, core: 2. Of those that a mesh axis runs over, the one named last changes fastest.
Arguments:
- tokens: bfloat16 [32768, 1024], P(('dp', 'seq')), may hold values from -6 to 6
- segments: int32 [4, 8192], P('dp', 'seq'), may hold values from 0 to 1, never falling along the last dimension, each value on 1 to 6144 neighbouring positions
- cotangent: bfloat16 [32768, 1024], P(('dp', 'seq')), may hold values from -6 to 6
- tile_of_slot: int32 [768], replicated, may hold values from 0 to 767, as said below
- tiles: float32 [768, 128, 128], P(('dp', 'seq'))
- left_bases: float32 [768, 128, 128], P(('dp', 'seq')), as said below
- right_bases: float32 [768, 128, 128], P(('dp', 'seq')), as said below
- first_moments: float32 [768, 128, 128], P(('dp', 'seq'))
- second_moments: float32 [768, 128, 128], P(('dp', 'seq')), as said below
- small_params: float32 [12288], P(('dp', 'seq'))
- small_first: float32 [12288], P(('dp', 'seq'))
- small_second: float32 [12288], P(('dp', 'seq')), as said below
- threshold: float32 [1], replicated, may hold values from 1.5 to 2.5
Outputs:
- block_output: bfloat16 [32768, 1024], P(('dp', 'seq'))
- input_grad: float32 [32768, 1024], P(('dp', 'seq'))
- tile_grads: float32 [768, 128, 128], P(('dp', 'seq'))
- small_grads: float32 [12288], P(('dp', 'seq'))
- new_tiles: float32 [768, 128, 128], P(('dp', 'seq'))
- new_tiles_low: bfloat16 [768, 128, 128], P(('dp', 'seq'))
- new_first_moments: float32 [768, 128, 128], P(('dp', 'seq'))
- new_second_moments: float32 [768, 128, 128], P(('dp', 'seq'))
- new_small: float32 [12288], P(('dp', 'seq'))
- new_small_low: bfloat16 [12288], P(('dp', 'seq'))
- new_small_first: float32 [12288], P(('dp', 'seq'))
- new_small_second: float32 [12288], P(('dp', 'seq'))
- clip_factors: float32 [16], replicated
The draws below stay inside these ranges and needn't reach their ends.
Inputs may be any that keep to these rules, and one draw needn't show every extreme that they name: `tile_of_slot`: a permutation of the numbers 0 to 767. `segments`: segment numbers never fall along a row; each row holds two documents, each of 2048 tokens or more. `left_bases`: every tile is an orthogonal matrix. `right_bases`: every tile is an orthogonal matrix. `second_moments`: all entries are positive. `small_second`: all entries are positive.
All inputs are finite; a program needn't handle non-finite values.
Results may differ from the reference program's by a relative error of at most 0.011.
Values may be sent and summed in bfloat16 or wider, within the bound.
A program may use at most 448 MiB of HBM per device.

```python
import math
import jax
import jax.numpy as jnp
import numpy as np
from jax import lax

D = 1024
FF = 4096
HEADS = 16
HEAD = 64
ROT = 16
BLK = 128
WINDOW = 1024
QBLK = 512
SEQ_LEN = 8192
TOKENS = 32768
GROUPS = 4
GROUP_LEN = 8192
TILES = 768
SMALL = 12288


def slot_numbers(base_key):
    return jax.random.permutation(jax.random.fold_in(base_key, 11), TILES).astype(jnp.int32)


def region_values(tile_ids, qkv_value, out_value, up_value, down_value):
    count_qkv = D // BLK * (3 * D // BLK)
    count_out = D // BLK * (D // BLK)
    count_up = D // BLK * (FF // BLK)
    return jnp.where(tile_ids < count_qkv, qkv_value, jnp.where(tile_ids < count_qkv + count_out, out_value, jnp.where(tile_ids < count_qkv + count_out + count_up, up_value, down_value))).astype(jnp.float32)


def gradient_scale(base_key):
    return region_values(slot_numbers(base_key), 0.5, 0.07, 0.3, 0.65) * float(TOKENS) ** 0.5


def permute_block(block_key):
    return jax.random.permutation(block_key, BLK).astype(jnp.int32)


def signed_hadamard(base_key):
    order_key = jax.random.fold_in(base_key, 1)
    left_key = jax.random.fold_in(base_key, 2)
    right_key = jax.random.fold_in(base_key, 3)
    orders = jax.vmap(permute_block)(jax.random.split(order_key, TILES))
    row_ids = jnp.arange(BLK, dtype=jnp.int32)
    joined = jnp.bitwise_and(row_ids[None, :, None], orders[:, None, :])
    parity = jnp.zeros((TILES, BLK, BLK), jnp.int32)
    for level in range(BLK.bit_length() - 1):
        parity = parity + jnp.bitwise_and(jnp.right_shift(joined, level), 1)
    entries = (1 - 2 * (parity % 2)).astype(jnp.float32)
    left_sign = jax.random.rademacher(left_key, (TILES, BLK, 1), dtype=jnp.float32)
    right_sign = jax.random.rademacher(right_key, (TILES, 1, BLK), dtype=jnp.float32)
    return entries * left_sign * right_sign * float(BLK) ** (-0.5)


def draw_tile_of_slot(key, part):
    return slot_numbers(key)


def draw_tiles(key, part):
    scales = region_values(slot_numbers(key), float(D) ** (-0.5), 0.3, float(D) ** (-0.5), float(FF) ** (-0.5))
    noise = jax.random.truncated_normal(jax.random.fold_in(key, 12), -4.0, 4.0, (TILES, BLK, BLK), jnp.float32)
    return noise * scales[:, None, None]


def draw_left_bases(key, part):
    return signed_hadamard(jax.random.fold_in(key, 13))


def draw_right_bases(key, part):
    return signed_hadamard(jax.random.fold_in(key, 14))


def draw_first_moments(key, part):
    noise = jax.random.truncated_normal(jax.random.fold_in(key, 15), -4.0, 4.0, (TILES, BLK, BLK), jnp.float32)
    return noise * gradient_scale(key)[:, None, None]


def draw_second_moments(key, part):
    spread = jax.random.uniform(jax.random.fold_in(key, 16), (TILES, BLK, BLK), jnp.float32, jnp.log(0.3), jnp.log(3.0))
    level = gradient_scale(key)
    return jnp.exp(spread) * (level * level)[:, None, None]


def draw_small_params(key, part):
    index_all = jnp.arange(SMALL, dtype=jnp.int32)
    noise = jax.random.truncated_normal(jax.random.fold_in(key, 17), -4.0, 4.0, (SMALL,), jnp.float32) * 0.15
    spread = jax.random.uniform(jax.random.fold_in(key, 18), (SMALL,), jnp.float32, -0.3, 0.3)
    place = index_all % 12
    gain_entry = (place == 8) | (place == 10)
    return jnp.where(gain_entry, 1.0 + spread, noise)


def draw_small_first(key, part):
    noise = jax.random.truncated_normal(jax.random.fold_in(key, 19), -4.0, 4.0, (SMALL,), jnp.float32)
    return noise * (0.5 * float(TOKENS) ** 0.5)


def draw_small_second(key, part):
    spread = jax.random.uniform(jax.random.fold_in(key, 20), (SMALL,), jnp.float32, jnp.log(0.3), jnp.log(3.0))
    return jnp.exp(spread) * (0.25 * float(TOKENS))


def block_scale(rng, shape, shards, least, top_value):
    def one(position, shards_of):
        steps = jax.random.uniform(jax.random.fold_in(jax.random.fold_in(rng, 6), position), (shards_of,), jnp.float32, least / len(shards), top_value / len(shards))
        return jnp.repeat(jnp.exp(steps), shape[position] // shards_of).reshape((-1,) + (1,) * (len(shape) - position - 1))

    level = one(*shards[0])
    for cut in shards[1:]:
        level = level * one(*cut)
    return level


def profile(amount, total, most, lean):
    portions = [(1 << 20) // math.isqrt(grade ** lean) + 1 for grade in range(2, amount + 1)]
    rest, holding = total - most - (amount - 1), [1] * (amount - 1)
    while rest > 0:
        movable = [i for i in range(amount - 1) if holding[i] < most]
        pool, budget = sum([portions[i] for i in movable]), rest
        for i in movable:
            extra = min(most - holding[i], max(1, budget * portions[i] // pool), rest)
            holding[i] = holding[i] + extra
            rest = rest - extra
    return np.array([most] + holding)


def ragged(key, count, total, most, lean):
    if count == 2:
        one = jax.random.randint(key, (), max(1, total - most), min(most, total - 1) + 1)
        return jnp.stack([one, total - one])
    sizes = jnp.asarray(profile(count, total, most, lean), jnp.int32)
    couples = (count - 1) // 2
    donor, taker = sizes[1:1 + 2 * couples:2], sizes[2:2 + 2 * couples:2]
    room = jnp.minimum(donor - 1, most - taker)
    moved = jax.random.randint(jax.random.fold_in(key, 1), (couples,), 0, 1 << 20) % (room + 1)
    sizes = sizes.at[1:1 + 2 * couples:2].set(donor - moved).at[2:2 + 2 * couples:2].set(taker + moved)
    return sizes[jax.random.permutation(jax.random.fold_in(key, 2), count)]


def scatter_about(own_key, shape, scale, most, cuts=(), held_as=jnp.bfloat16):
    factor_of = block_scale(own_key, shape, cuts, -0.22, 0.18) if cuts else 1.0
    values = jax.random.normal(own_key, shape, jnp.float32) * scale * factor_of
    return jnp.minimum(jnp.maximum(values, -most), most).astype(held_as)


def setup_inputs(seed: int = 0) -> dict:
    streams_of = jax.random.split(jax.random.key(seed), 14)
    tokens = scatter_about(streams_of[0], (TOKENS, D), 1.0, 6.0, ((0, 32),))
    segments = jax.vmap(lambda own: jnp.searchsorted(jnp.cumsum(ragged(own, 2, GROUP_LEN, 3 * SEQ_LEN // 4, 0)), jnp.arange(GROUP_LEN), side="right"))(jax.random.split(streams_of[1], GROUPS)).reshape((GROUPS, GROUP_LEN)).astype(jnp.int32)
    cotangent = scatter_about(streams_of[2], (TOKENS, D), 1.0, 6.0, ((0, 32),))
    tile_of_slot = draw_tile_of_slot(jax.random.fold_in(streams_of[13], 71), 0)
    tiles = draw_tiles(jax.random.fold_in(streams_of[13], 71), 0)
    left_bases = draw_left_bases(jax.random.fold_in(streams_of[13], 71), 0)
    right_bases = draw_right_bases(jax.random.fold_in(streams_of[13], 71), 0)
    first_moments = draw_first_moments(jax.random.fold_in(streams_of[13], 71), 0)
    second_moments = draw_second_moments(jax.random.fold_in(streams_of[13], 71), 0)
    small_params = draw_small_params(jax.random.fold_in(streams_of[13], 71), 0)
    small_first = draw_small_first(jax.random.fold_in(streams_of[13], 71), 0)
    small_second = draw_small_second(jax.random.fold_in(streams_of[13], 71), 0)
    threshold = jnp.clip(jax.random.uniform(streams_of[12], (1,), jnp.float32, 1.5, 2.5), 1.5, 2.5)
    return dict(tokens=tokens, segments=segments, cotangent=cotangent, tile_of_slot=tile_of_slot, tiles=tiles, left_bases=left_bases, right_bases=right_bases, first_moments=first_moments, second_moments=second_moments, small_params=small_params, small_first=small_first, small_second=small_second, threshold=threshold)


NORM_EPS = 1e-05
ADAM_EPS = 1e-08
BETA = 0.5
LEARN = 0.03
SMALL_LEARN = 0.2
ROPE_BASE = 10000.0
MASKED = -1e+30
HIGH = lax.Precision.HIGHEST

@jax.custom_vjp
def low(v):
    return lax.optimization_barrier(v.astype(jnp.bfloat16)).astype(jnp.float32)

@jax.custom_vjp
def low_back(v):
    return v

def low_keep(v):
    return (low(v), None)

def low_pass(kept, grad):
    return (grad,)

def back_keep(v):
    return (v, None)

def back_low(kept, grad):
    return (low(grad),)
low.defvjp(low_keep, low_pass)
low_back.defvjp(back_keep, back_low)

def untile(tile_block, height, breadth):
    tile_grid = tile_block.reshape(height // BLK, breadth // BLK, BLK, BLK)
    return tile_grid.transpose(0, 2, 1, 3).reshape(height, breadth)

def split_tiles(by_number):
    count_qkv = D // BLK * (3 * D // BLK)
    count_out = D // BLK * (D // BLK)
    count_up = D // BLK * (FF // BLK)
    first_end = count_qkv
    second_end = first_end + count_out
    third_end = second_end + count_up
    return (untile(by_number[:first_end], D, 3 * D), untile(by_number[first_end:second_end], D, D), untile(by_number[second_end:third_end], D, FF), untile(by_number[third_end:], FF, D))

def split_small(small_vector):
    small_table = small_vector.reshape(D, 12)
    return (small_table[:, 0], small_table[:, 1], small_table[:, 2], small_table[:, 3:7].reshape(FF), small_table[:, 7], small_table[:, 8], small_table[:, 9], small_table[:, 10], small_table[:, 11])

def rope_tables(positions):
    half_rot = ROT // 2
    exponent = jnp.arange(half_rot, dtype=jnp.float32) * (2.0 / ROT)
    frequency = jnp.power(ROPE_BASE, -exponent)
    angle = positions.astype(jnp.float32)[:, None] * frequency[None, :]
    return (jnp.cos(angle), jnp.sin(angle))

def rotate(heads_value, cosine_table, sine_table, direction):
    half_rot = ROT // 2
    first_half = heads_value[..., :half_rot]
    second_half = heads_value[..., half_rot:ROT]
    rest_part = heads_value[..., ROT:]
    cos_part = cosine_table[:, None, :]
    sin_part = sine_table[:, None, :] * direction
    return jnp.concatenate([first_half * cos_part - second_half * sin_part, second_half * cos_part + first_half * sin_part, rest_part], axis=-1)

def allowed_mask(query_place, key_place, query_seg, key_seg):
    distance = query_place[:, None] - key_place[None, :]
    same_sequence = query_place[:, None] // SEQ_LEN == key_place[None, :] // SEQ_LEN
    return (distance >= 0) & (distance < WINDOW) & same_sequence & (query_seg[:, None] == key_seg[None, :])

def sequence_attention(queries, key_heads, values, seg_ids):
    key_count = WINDOW + QBLK
    score_scale = HEAD ** (-0.5)
    padded_keys = jnp.concatenate([jnp.zeros((WINDOW, HEADS, HEAD), jnp.float32), key_heads], 0)
    padded_values = jnp.concatenate([jnp.zeros((WINDOW, HEADS, HEAD), jnp.float32), values], 0)
    padded_seg = jnp.concatenate([jnp.full((WINDOW,), -1, jnp.int32), seg_ids], 0)

    def one_block(start):
        query_block = lax.dynamic_slice_in_dim(queries, start, QBLK, 0)
        key_block = lax.dynamic_slice_in_dim(padded_keys, start, key_count, 0)
        value_block = lax.dynamic_slice_in_dim(padded_values, start, key_count, 0)
        key_seg = lax.dynamic_slice_in_dim(padded_seg, start, key_count, 0)
        query_seg = lax.dynamic_slice_in_dim(seg_ids, start, QBLK, 0)
        query_place = start + jnp.arange(QBLK, dtype=jnp.int32)
        key_place = start - WINDOW + jnp.arange(key_count, dtype=jnp.int32)
        allowed = allowed_mask(query_place, key_place, query_seg, key_seg)
        raw_scores = score_scale * jnp.einsum('qhd,khd->hqk', query_block, key_block, precision=HIGH)
        scores = low_back(raw_scores)
        masked = jnp.where(allowed[None], scores, MASKED)
        attn_prob = low(jax.nn.softmax(masked, axis=-1))
        block_out = jnp.einsum('hqk,khd->qhd', attn_prob, value_block, precision=HIGH)
        return (block_out, lax.optimization_barrier(jnp.max(masked, axis=(1, 2))))
    block_starts = jnp.arange(SEQ_LEN // QBLK, dtype=jnp.int32) * QBLK
    block_outs, block_peaks = lax.map(jax.checkpoint(one_block), block_starts)
    return (block_outs.reshape(SEQ_LEN, HEADS, HEAD), lax.optimization_barrier(jnp.max(block_peaks, axis=0)))

def gelu_exact(value):
    return jax.nn.gelu(value, approximate=False)

def forward(x_float, by_number, small_vector, seg_ids, positions):
    w_qkv, w_out, w_up, w_down = split_tiles(low(by_number))
    q_bias, v_bias, out_bias, up_bias, down_bias, gain_one, shift_one, gain_two, shift_two = split_small(low(small_vector))
    centered = x_float - lax.optimization_barrier(jnp.mean(x_float, axis=-1, keepdims=True))
    normed = centered * lax.rsqrt(lax.optimization_barrier(jnp.mean(centered * centered, axis=-1, keepdims=True)) + NORM_EPS)
    attn_in = low(normed * gain_one + shift_one)
    mlp_in = low(normed * gain_two + shift_two)
    bias_qkv = jnp.concatenate([q_bias, jnp.zeros((D,), jnp.float32), v_bias])
    projected = low_back(jnp.dot(attn_in, w_qkv, precision=HIGH) + bias_qkv)
    cosine_table, sine_table = rope_tables(positions)
    queries = low(rotate(projected[:, :D].reshape(-1, HEADS, HEAD), cosine_table, sine_table, 1.0))
    key_heads = low(rotate(projected[:, D:2 * D].reshape(-1, HEADS, HEAD), cosine_table, sine_table, 1.0))
    values = low(projected[:, 2 * D:].reshape(-1, HEADS, HEAD))
    seq_shape = (TOKENS // SEQ_LEN, SEQ_LEN, HEADS, HEAD)

    def one_sequence(seq_items):
        return sequence_attention(seq_items[0], seq_items[1], seq_items[2], seq_items[3])
    seq_outs, seq_peaks = lax.map(jax.checkpoint(one_sequence), (queries.reshape(seq_shape), key_heads.reshape(seq_shape), values.reshape(seq_shape), seg_ids.reshape(-1, SEQ_LEN)))
    attn_out = low(low_back(seq_outs.reshape(-1, D)))
    attn_result = jnp.dot(attn_out, w_out, precision=HIGH) + out_bias
    up_pre = low_back(jnp.dot(mlp_in, w_up, precision=HIGH) + up_bias)
    hidden = low(gelu_exact(up_pre))
    mlp_result = jnp.dot(hidden, w_down, precision=HIGH) + down_bias
    return (x_float + attn_result + mlp_result, lax.optimization_barrier(jnp.max(seq_peaks, axis=0)))

def column_scales(tile_ids, factors):
    count_qkv = D // BLK * (3 * D // BLK)
    columns = (tile_ids % (3 * D // BLK))[:, None] * BLK + jnp.arange(BLK, dtype=jnp.int32)[None, :]
    head_index = columns % D // HEAD
    root_factor = jnp.sqrt(factors)
    picked = lax.optimization_barrier(jnp.sum(jnp.where(head_index[..., None] == jnp.arange(HEADS, dtype=jnp.int32), root_factor, 0.0), axis=-1))
    clipped = (tile_ids[:, None] < count_qkv) & (columns < 2 * D)
    return jnp.where(clipped, picked, 1.0)

def rotate_update(grads, weights, left, right, first_moment, second_moment, column_scale):
    turned = jnp.einsum('sji,sjk->sik', left, grads, precision=HIGH)
    turned = jnp.einsum('sik,skl->sil', turned, right, precision=HIGH)
    first_new = BETA * first_moment + (1.0 - BETA) * turned
    second_new = BETA * second_moment + (1.0 - BETA) * turned * turned
    ratio = first_new / (jnp.sqrt(second_new) + ADAM_EPS)
    back_turned = jnp.einsum('sij,sjk->sik', left, ratio, precision=HIGH)
    back_turned = jnp.einsum('sik,slk->sil', back_turned, right, precision=HIGH)
    updated = (weights - LEARN * back_turned) * column_scale[:, None, :]
    return (updated, first_new, second_new)

def small_update(grads, params, first_moment, second_moment):
    first_new = BETA * first_moment + (1.0 - BETA) * grads
    second_new = BETA * second_moment + (1.0 - BETA) * grads * grads
    updated = params - SMALL_LEARN * first_new / (jnp.sqrt(second_new) + ADAM_EPS)
    return (updated, first_new, second_new)

def reference(tokens, segments, cotangent, tile_of_slot, tiles, left_bases, right_bases, first_moments, second_moments, small_params, small_first, small_second, threshold):
    inverse = jnp.argsort(tile_of_slot).astype(jnp.int32)
    by_number = tiles[inverse]
    positions = jnp.arange(TOKENS, dtype=jnp.int32) % SEQ_LEN
    seg_ids = segments.reshape(TOKENS)

    def run_layer(x_float, weight_tiles, small_vector):
        return forward(x_float, weight_tiles, small_vector, seg_ids, positions)
    result, pullback, peaks = jax.vjp(run_layer, tokens.astype(jnp.float32), by_number, small_params, has_aux=True)
    input_grad, grad_by_number, small_grads = pullback(cotangent.astype(jnp.float32))
    tile_grads = grad_by_number[tile_of_slot]
    limit = threshold[0]
    factors = limit / jnp.maximum(peaks, limit)
    column_scale = column_scales(tile_of_slot, factors)
    new_tiles, new_first, new_second = rotate_update(tile_grads, tiles, left_bases, right_bases, first_moments, second_moments, column_scale)
    new_small, new_small_first, new_small_second = small_update(small_grads, small_params, small_first, small_second)
    return (result.astype(jnp.bfloat16), input_grad, tile_grads, small_grads, new_tiles, new_tiles.astype(jnp.bfloat16), new_first, new_second, new_small, new_small.astype(jnp.bfloat16), new_small_first, new_small_second, factors)
```

```python
import functools

import jax
import jax.numpy as jnp
from jax import lax
from jax.experimental import pallas as pl
from jax.experimental.pallas import tpu as pltpu
from jax.sharding import PartitionSpec as P

D = 1024
FF = 4096
HEADS = 16
HEAD = 64
ROT = 16
BLK = 128
WINDOW = 1024
TILES = 768
SMALL = 12288
QKV_TILES = D // BLK * (3 * D // BLK)
OUT_TILES = D // BLK * (D // BLK)
UP_TILES = D // BLK * (FF // BLK)
OUT_BASE = QKV_TILES
UP_BASE = QKV_TILES + OUT_TILES
DOWN_BASE = UP_BASE + UP_TILES

NORM_EPS = 1e-05
ADAM_EPS = 1e-08
BETA = 0.5
LEARN = 0.03
SMALL_LEARN = 0.2
ROPE_BASE = 10000.0
MASKED = -1e30
HIGH = lax.Precision.HIGHEST

F32 = jnp.float32
BF16 = jnp.bfloat16
MESH = pl.DeviceIdType.MESH
ANY = pl.BlockSpec(memory_space=pl.ANY)
VMEM = pl.BlockSpec(memory_space=pltpu.VMEM)
VMEM_LIMIT = 58 << 20

NN = (((1,), (0,)), ((), ()))
NT = (((1,), (1,)), ((), ()))
TN = (((0,), (0,)), ((), ()))


def dot(a, b, dims=NN, precision=None):
    return lax.dot_general(a, b, dims, precision=precision, preferred_element_type=F32)


def params(**kw):
    return pltpu.CompilerParams(vmem_limit_bytes=VMEM_LIMIT, **kw)


def norm_rows(x):
    centered = x - jnp.mean(x, axis=-1, keepdims=True)
    inv = lax.rsqrt(jnp.mean(centered * centered, axis=-1, keepdims=True) + NORM_EPS)
    return centered * inv, inv


def tile_loop(first, count, body):
    def step(t, carry):
        body(t)
        return carry

    lax.fori_loop(first, first + count, step, 0)


ROWS_PER_TILE = BLK
HALF_ROWS = 1536


def gather_weights(payload, tokens, seg_rows):
    rows = payload.shape[0]
    top = pl.ds(0, HALF_ROWS)
    low = pl.ds(HALF_ROWS, rows - HALF_ROWS)

    def kernel(x_ref, tok_ref, seg_ref, out_ref, ptok_ref, pseg_ref, lsem, ss, rs, hss, hrs, hls):
        d = lax.axis_index("dp")
        s = lax.axis_index("seq")
        z = s // 2
        c = s % 2
        xn = d + 1 - 2 * (d % 2)
        yn = d + 2 - 4 * (d // 2)
        xyn = 3 - d
        sib = z * 2 + 1 - c
        halo = s - 1 + 2 * c
        halo_ok = ((c == 0) & (z > 0)) | ((c == 1) & (z < 3))

        barrier = pltpu.get_barrier_semaphore()

        def greet(dev):
            pl.semaphore_signal(barrier, inc=1, device_id=dev, device_id_type=MESH)

        greet((d, sib))
        greet((xn, s))
        greet((yn, s))

        @pl.when(z > 0)
        def _():
            greet((d, s - 2))

        @pl.when(z < 3)
        def _():
            greet((d, s + 2))

        @pl.when(halo_ok)
        def _():
            greet((d, halo))

        below, above = (z + 2) // 3, (5 - z) // 3
        pl.semaphore_wait(barrier, 3 + below + above + (1 - c) * below + c * above)

        def place(dd, zz):
            return out_ref.at[dd * 8 + zz * 2 + c]

        def remote(src, dst, kind, zz, dev):
            return pltpu.make_async_remote_copy(
                src_ref=src,
                dst_ref=dst,
                send_sem=ss.at[kind, zz],
                recv_sem=rs.at[kind, zz],
                device_id=dev,
                device_id_type=MESH,
            )

        def block_of(zz, own):
            return x_ref if own else place(d, zz)

        def up(zz, own):
            return remote(block_of(zz, own), place(d, zz), 0, zz, (d, s + 2))

        def down(zz, own):
            return remote(block_of(zz, own), place(d, zz), 1, zz, (d, s - 2))

        def to_x(zz, own):
            return remote(block_of(zz, own), place(d, zz), 2, zz, (xn, s))

        def to_y(zz, own):
            return remote(block_of(zz, own), place(d, zz), 3, zz, (yn, s))

        def on_y(zz):
            return remote(place(xn, zz).at[top], place(xn, zz).at[top], 4, zz, (yn, s))

        def on_x(zz):
            return remote(place(yn, zz).at[low], place(yn, zz).at[low], 5, zz, (xn, s))

        def to_sib(dd, zz, kind, own=False):
            src = x_ref if own else place(dd, zz)
            return remote(src, place(dd, zz), kind, zz, (d, sib))

        def from_x(zz):
            return remote(x_ref, place(xn, zz), 2, zz, (xn, s))

        def from_y(zz):
            return remote(x_ref, place(yn, zz), 3, zz, (yn, s))

        def diag_top(zz):
            return remote(x_ref.at[top], place(xyn, zz).at[top], 4, zz, (yn, s))

        def diag_low(zz):
            return remote(x_ref.at[low], place(xyn, zz).at[low], 5, zz, (xn, s))

        order = [z, 1 + z % 2, (2 + 3 * z) % 5, 3 * (1 - z // 2)]
        local = pltpu.make_async_copy(x_ref, place(d, z), lsem)
        local.start()

        def halo_copies(dev):
            tok = pltpu.make_async_remote_copy(
                src_ref=tok_ref,
                dst_ref=ptok_ref,
                send_sem=hss.at[0],
                recv_sem=hrs.at[0],
                device_id=dev,
                device_id_type=MESH,
            )
            seg = pltpu.make_async_remote_copy(
                src_ref=seg_ref,
                dst_ref=pseg_ref,
                send_sem=hss.at[1],
                recv_sem=hrs.at[1],
                device_id=dev,
                device_id_type=MESH,
            )
            return tok, seg

        def launch(k):
            zz = order[k]
            own = k == 0
            if own:

                @pl.when(z < 3)
                def _():
                    up(zz, True).start()

                @pl.when(z > 0)
                def _():
                    down(zz, True).start()
            else:

                @pl.when(zz < z)
                def _():
                    up(zz, False).wait_recv()

                @pl.when((zz < z) & (z < 3))
                def _():
                    up(zz, False).start()

                @pl.when(zz > z)
                def _():
                    down(zz, False).wait_recv()

                @pl.when((zz > z) & (z > 0))
                def _():
                    down(zz, False).start()

            to_x(zz, own).start()
            to_y(zz, own).start()
            to_sib(d, zz, 6, own).start()

        def second(k):
            zz = order[k]
            from_x(zz).wait_recv()
            on_y(zz).start()
            to_sib(xn, zz, 7).start()
            from_y(zz).wait_recv()
            on_x(zz).start()
            to_sib(yn, zz, 8).start()

        def third(k):
            zz = order[k]
            diag_top(zz).wait_recv()
            diag_low(zz).wait_recv()
            to_sib(xyn, zz, 9).start()

        launch(0)
        own_tok = pltpu.make_async_copy(tok_ref, ptok_ref, hls.at[0])
        own_seg = pltpu.make_async_copy(seg_ref, pseg_ref, hls.at[1])

        @pl.when(s < 7)
        def _():
            for cp in halo_copies((d, s + 1)):
                cp.start()

        @pl.when(s == 0)
        def _():
            own_tok.start()
            own_seg.start()

        launch(1)
        second(0)
        launch(2)
        second(1)
        third(0)
        launch(3)
        second(2)
        third(1)
        second(3)
        third(2)
        third(3)

        local.wait()
        other = 1 - c

        def sib_place(dd, zz):
            return out_ref.at[dd * 8 + zz * 2 + other]

        for k in range(4):
            zz = order[k]
            own = k == 0
            for kind, dd in ((6, d), (7, xn), (8, yn), (9, xyn)):
                remote(sib_place(dd, zz), sib_place(dd, zz), kind, zz, (d, sib)).wait_recv()
                to_sib(dd, zz, kind, own and kind == 6).wait_send()
            to_x(zz, own).wait_send()
            to_y(zz, own).wait_send()
            on_y(zz).wait_send()
            on_x(zz).wait_send()

            @pl.when((zz <= z) & (z < 3))
            def _():
                up(zz, own).wait_send()

            @pl.when((zz >= z) & (z > 0))
            def _():
                down(zz, own).wait_send()

        @pl.when(s < 7)
        def _():
            for cp in halo_copies((d, s + 1)):
                cp.wait_send()

        @pl.when(s > 0)
        def _():
            for cp in halo_copies((d, s - 1)):
                cp.wait_recv()

        @pl.when(s == 0)
        def _():
            own_tok.wait()
            own_seg.wait()

    return pl.pallas_call(
        kernel,
        out_shape=[
            jax.ShapeDtypeStruct((32, rows, BLK), BF16),
            jax.ShapeDtypeStruct(tokens.shape, BF16),
            jax.ShapeDtypeStruct(seg_rows.shape, jnp.int32),
        ],
        in_specs=[ANY, ANY, ANY],
        out_specs=[ANY, ANY, ANY],
        scratch_shapes=[
            pltpu.SemaphoreType.DMA,
            pltpu.SemaphoreType.DMA((10, 4)),
            pltpu.SemaphoreType.DMA((10, 4)),
            pltpu.SemaphoreType.DMA((2,)),
            pltpu.SemaphoreType.DMA((2,)),
            pltpu.SemaphoreType.DMA((2,)),
        ],
        compiler_params=params(collective_id=0, has_side_effects=True),
        name="gather_weights",
    )(payload, tokens, seg_rows)


OWNED = 24 * BLK
HALF = OWNED // 2
SMALL_ROWS = SMALL // BLK
EXTRA_ROWS = SMALL_ROWS + 8


def add_rows(dst, terms, rows, step=256):
    def body(i, carry):
        at = pl.ds(pl.multiple_of(i * step, step), step)
        total = terms[0][at].astype(F32)
        for term in terms[1:]:
            total = total + term[at].astype(F32)
        dst[at] = total.astype(dst.dtype)
        return carry

    lax.fori_loop(0, rows // step, body, 0)


def sum_gradients(grads, extra):
    def kernel(g_ref, e_ref, out_ref, eout_ref, own, crecv, s1a, s1b, s2, zup, zdn, epart, erecv, ls, ss, rs, zss, zrs, es, er):
        d = lax.axis_index("dp")
        s = lax.axis_index("seq")
        z = s // 2
        c = s % 2
        xn = d + 1 - 2 * (d % 2)
        yn = d + 2 - 4 * (d // 2)
        xyn = 3 - d
        sib = z * 2 + 1 - c
        zpair = s + 2 - 4 * (z % 2)
        zfar = s + 4 - 8 * (z // 2)
        top = pl.ds(0, HALF)
        low = pl.ds(HALF, HALF)

        barrier = pltpu.get_barrier_semaphore()

        def greet(dev):
            pl.semaphore_signal(barrier, inc=1, device_id=dev, device_id_type=MESH)

        greet((d, sib))
        greet((xn, s))
        greet((yn, s))
        greet((d, zfar))

        @pl.when(z > 0)
        def _():
            greet((d, s - 2))

        @pl.when(z < 3)
        def _():
            greet((d, s + 2))

        order = [3 * (1 - z // 2), (2 + 3 * z) % 5, 1 + z % 2, z]

        def owner_rows(dd, zz, cc):
            return g_ref.at[pl.ds(pl.multiple_of((dd * 8 + zz * 2 + cc) * OWNED, OWNED), OWNED)]

        def load(zz, dd):
            return pltpu.make_async_copy(owner_rows(dd, zz, c), own.at[zz, dd], ls.at[zz, dd])

        for k in range(4):
            for dd in range(4):
                load(order[k], dd).start()

        pl.semaphore_wait(barrier, 4 + (z + 2) // 3 + (5 - z) // 3)

        def remote(src, dst, ssem, rsem, dev):
            return pltpu.make_async_remote_copy(
                src_ref=src, dst_ref=dst, send_sem=ssem, recv_sem=rsem, device_id=dev, device_id_type=MESH
            )

        def core(zz, dd):
            return remote(owner_rows(dd, zz, 1 - c), crecv.at[zz, dd], ss.at[zz, dd], rs.at[zz, dd], (d, sib))

        def y_own(zz):
            return remote(own.at[zz, yn, top], s1a.at[zz, 0], ss.at[zz, 4], rs.at[zz, 4], (yn, s))

        def y_cross(zz):
            return remote(own.at[zz, xyn, top], s1a.at[zz, 1], ss.at[zz, 5], rs.at[zz, 5], (yn, s))

        def x_own(zz):
            return remote(own.at[zz, xn, low], s1b.at[zz, 0], ss.at[zz, 6], rs.at[zz, 6], (xn, s))

        def x_cross(zz):
            return remote(own.at[zz, xyn, low], s1b.at[zz, 1], ss.at[zz, 7], rs.at[zz, 7], (xn, s))

        def x_last(zz):
            return remote(own.at[zz, xn, top], s2.at[zz, top], ss.at[zz, 8], rs.at[zz, 8], (xn, s))

        def y_last(zz):
            return remote(own.at[zz, yn, low], s2.at[zz, low], ss.at[zz, 9], rs.at[zz, 9], (yn, s))

        def z_up(zz):
            return remote(own.at[zz, d], zup.at[zz], zss.at[0, zz], zrs.at[0, zz], (d, s + 2))

        def z_dn(zz):
            return remote(own.at[zz, d], zdn.at[zz], zss.at[1, zz], zrs.at[1, zz], (d, s - 2))

        def extra_step(i, dev):
            return remote(epart.at[i], erecv.at[i], es.at[i], er.at[i], dev)

        extra_devs = [(d, sib), (xn, s), (yn, s), (d, zpair), (d, zfar)]

        def extra_add(i):
            extra_step(i, extra_devs[i]).wait_recv()
            a = epart[i]
            b = erecv[i]
            row = lax.broadcasted_iota(jnp.int32, a.shape, 0)
            total = jnp.where(row < SMALL_ROWS, a + b, jnp.maximum(a, b))
            if i < 4:
                epart[i + 1] = total
                extra_step(i + 1, extra_devs[i + 1]).start()
            else:
                eout_ref[...] = total

        for k in range(4):
            for dd in range(4):
                core(order[k], dd).start()
            if k == 0:
                epart[0] = e_ref[...]
                extra_step(0, extra_devs[0]).start()

        def first(k):
            zz = order[k]

            def one(dd, start):
                load(zz, dd).wait()
                core(zz, dd).wait_recv()
                add_rows(own.at[zz, dd], [own.at[zz, dd], crecv.at[zz, dd]], OWNED)
                for cp in start:
                    cp.start()

            one(xyn, [y_cross(zz), x_cross(zz)])
            one(yn, [y_own(zz)])
            one(xn, [x_own(zz)])
            one(d, [])

        def second(k):
            zz = order[k]
            y_cross(zz).wait_recv()
            a = own.at[zz, xn, top]
            add_rows(a, [a, s1a.at[zz, 1]], HALF)
            x_last(zz).start()
            x_cross(zz).wait_recv()
            b = own.at[zz, yn, low]
            add_rows(b, [b, s1b.at[zz, 1]], HALF)
            y_last(zz).start()

        def third(k):
            zz = order[k]
            y_own(zz).wait_recv()
            x_own(zz).wait_recv()
            x_last(zz).wait_recv()
            y_last(zz).wait_recv()
            a = own.at[zz, d, top]
            b = own.at[zz, d, low]
            if k < 3:

                @pl.when((zz > z) & (z > 0))
                def _():
                    z_up(zz).wait_recv()
                    add_rows(a, [a, s1a.at[zz, 0], s2.at[zz, top], zup.at[zz, top]], HALF)
                    add_rows(b, [b, s1b.at[zz, 0], s2.at[zz, low], zup.at[zz, low]], HALF)

                @pl.when((zz < z) & (z < 3))
                def _():
                    z_dn(zz).wait_recv()
                    add_rows(a, [a, s1a.at[zz, 0], s2.at[zz, top], zdn.at[zz, top]], HALF)
                    add_rows(b, [b, s1b.at[zz, 0], s2.at[zz, low], zdn.at[zz, low]], HALF)

                @pl.when(((zz > z) & (z == 0)) | ((zz < z) & (z == 3)))
                def _():
                    add_rows(a, [a, s1a.at[zz, 0], s2.at[zz, top]], HALF)
                    add_rows(b, [b, s1b.at[zz, 0], s2.at[zz, low]], HALF)

                @pl.when(zz > z)
                def _():
                    z_up(zz).start()

                @pl.when(zz < z)
                def _():
                    z_dn(zz).start()
            else:

                @pl.when(z > 0)
                def _():
                    z_up(zz).wait_recv()

                @pl.when(z < 3)
                def _():
                    z_dn(zz).wait_recv()

                o_top = out_ref.at[top]
                o_low = out_ref.at[low]

                @pl.when((z > 0) & (z < 3))
                def _():
                    add_rows(o_top, [a, s1a.at[zz, 0], s2.at[zz, top], zup.at[zz, top], zdn.at[zz, top]], HALF)
                    add_rows(o_low, [b, s1b.at[zz, 0], s2.at[zz, low], zup.at[zz, low], zdn.at[zz, low]], HALF)

                @pl.when(z == 0)
                def _():
                    add_rows(o_top, [a, s1a.at[zz, 0], s2.at[zz, top], zdn.at[zz, top]], HALF)
                    add_rows(o_low, [b, s1b.at[zz, 0], s2.at[zz, low], zdn.at[zz, low]], HALF)

                @pl.when(z == 3)
                def _():
                    add_rows(o_top, [a, s1a.at[zz, 0], s2.at[zz, top], zup.at[zz, top]], HALF)
                    add_rows(o_low, [b, s1b.at[zz, 0], s2.at[zz, low], zup.at[zz, low]], HALF)

        first(0)
        first(1)
        extra_add(0)
        second(0)
        first(2)
        extra_add(1)
        third(0)
        second(1)
        first(3)
        extra_add(2)
        third(1)
        second(2)
        extra_add(3)
        third(2)
        second(3)
        extra_add(4)
        third(3)

        for i in range(5):
            extra_step(i, extra_devs[i]).wait_send()
        for k in range(4):
            zz = order[k]
            for dd in range(4):
                core(zz, dd).wait_send()
            for cp in (y_own(zz), y_cross(zz), x_own(zz), x_cross(zz), x_last(zz), y_last(zz)):
                cp.wait_send()
            if k < 3:

                @pl.when(zz > z)
                def _():
                    z_up(zz).wait_send()

                @pl.when(zz < z)
                def _():
                    z_dn(zz).wait_send()

    return pl.pallas_call(
        kernel,
        out_shape=[
            jax.ShapeDtypeStruct((OWNED, BLK), F32),
            jax.ShapeDtypeStruct((EXTRA_ROWS, BLK), F32),
        ],
        in_specs=[ANY, VMEM],
        out_specs=[VMEM, VMEM],
        scratch_shapes=[
            pltpu.VMEM((4, 4, OWNED, BLK), BF16),
            pltpu.VMEM((4, 4, OWNED, BLK), BF16),
            pltpu.VMEM((4, 2, HALF, BLK), BF16),
            pltpu.VMEM((4, 2, HALF, BLK), BF16),
            pltpu.VMEM((4, OWNED, BLK), BF16),
            pltpu.VMEM((4, OWNED, BLK), BF16),
            pltpu.VMEM((4, OWNED, BLK), BF16),
            pltpu.VMEM((5, EXTRA_ROWS, BLK), F32),
            pltpu.VMEM((5, EXTRA_ROWS, BLK), F32),
            pltpu.SemaphoreType.DMA((4, 4)),
            pltpu.SemaphoreType.DMA((4, 10)),
            pltpu.SemaphoreType.DMA((4, 10)),
            pltpu.SemaphoreType.DMA((2, 4)),
            pltpu.SemaphoreType.DMA((2, 4)),
            pltpu.SemaphoreType.DMA((5,)),
            pltpu.SemaphoreType.DMA((5,)),
        ],
        compiler_params=params(collective_id=1, has_side_effects=True),
        name="sum_gradients",
    )(grads, extra)


ROWB = 256


def rope_rows(value, cos_t, fwd_t, back_t):
    pieces = []
    for j in range(value.shape[1] // BLK):
        p = value[:, j * BLK : (j + 1) * BLK]
        pieces.append(
            p * cos_t + pltpu.roll(p, BLK - ROT // 2, 1) * fwd_t + pltpu.roll(p, ROT // 2, 1) * back_t
        )
    return jnp.concatenate(pieces, axis=1)


def project(w_rows, w_all, prev_tokens, tokens, cotangent, smalls, tables):
    rows = tokens.shape[0]
    steps = rows // ROWB
    cos_t, fwd_t, back_t = tables

    def kernel(
        w_rows_ref, w_ref, prev_ref, tok_ref, g_ref, small_ref, cos_ref, fwd_ref, back_ref,
        q_ref, k_ref, v_ref, do_ref, m_ref, wqkv, wo, sems,
    ):
        i = pl.program_id(0)

        def third_copy(third):
            def body(t):
                r, cc = t // 8, t % 8
                src = w_ref.at[pl.ds(pl.multiple_of(w_rows_ref[r * 24 + third * 8 + cc], 16), BLK)]
                dst = wqkv.at[pl.ds(pl.multiple_of(r * BLK, BLK), BLK), pl.ds(pl.multiple_of(third * D + cc * BLK, BLK), BLK)]
                pltpu.make_async_copy(src, dst, sems.at[third]).start()

            tile_loop(0, 64, body)

        def third_wait(third):
            part = wqkv.at[:, pl.ds(third * D, D)]
            pltpu.make_async_copy(part, part, sems.at[third]).wait()

        @pl.when(i == 0)
        def _():
            third_copy(1)
            third_copy(2)
            third_copy(0)

            def body(t):
                r, cc = t // 8, t % 8
                src = w_ref.at[pl.ds(pl.multiple_of(w_rows_ref[OUT_BASE + t], 16), BLK)]
                dst = wo.at[pl.ds(pl.multiple_of(r * BLK, BLK), BLK), pl.ds(pl.multiple_of(cc * BLK, BLK), BLK)]
                pltpu.make_async_copy(src, dst, sems.at[3]).start()

            tile_loop(0, 64, body)
            third_wait(1)
            third_wait(2)

        @pl.when(i == steps)
        def _():
            third_wait(0)
            pltpu.make_async_copy(wo, wo, sems.at[3]).wait()

        def keys(x):
            normed, _ = norm_rows(x)
            attn_in = (normed * small_ref[4:5, :] + small_ref[5:6, :]).astype(BF16)
            k = dot(attn_in, wqkv[:, D : 2 * D])
            v = dot(attn_in, wqkv[:, 2 * D :]) + small_ref[1:2, :]
            k_ref[...] = rope_rows(k, cos_ref[...], fwd_ref[...], back_ref[...]).astype(BF16)
            v_ref[...] = v.astype(BF16)
            return normed, attn_in

        @pl.when(i < steps)
        def _():
            keys(prev_ref[...].astype(F32))

        @pl.when(i >= steps)
        def _():
            normed, attn_in = keys(tok_ref[...].astype(F32))
            m_ref[...] = (normed * small_ref[6:7, :] + small_ref[7:8, :]).astype(BF16)
            q = dot(attn_in, wqkv[:, :D]) + small_ref[0:1, :]
            q = rope_rows(q, cos_ref[...], fwd_ref[...], back_ref[...])
            q_ref[...] = q.astype(BF16)
            do_ref[...] = dot(g_ref[...], wo[...], NT).astype(BF16)

    own = lambda i, *_: (jnp.maximum(i - steps, 0), 0)
    prev = lambda i, *_: (jnp.minimum(i, steps - 1), 0)
    here = lambda i, *_: (i, 0)
    block = lambda m: pl.BlockSpec((ROWB, D), m)
    table = pl.BlockSpec((ROWB, BLK), here)
    return pl.pallas_call(
        kernel,
        grid_spec=pltpu.PrefetchScalarGridSpec(
            num_scalar_prefetch=1,
            grid=(2 * steps,),
            in_specs=[
                ANY, block(prev), block(own), block(own),
                pl.BlockSpec((16, D), lambda i, *_: (0, 0)), table, table, table,
            ],
            out_specs=[block(own), block(here), block(here), block(own), block(own)],
            scratch_shapes=[
                pltpu.VMEM((D, 3 * D), BF16),
                pltpu.VMEM((D, D), BF16),
                pltpu.SemaphoreType.DMA((4,)),
            ],
        ),
        out_shape=[
            jax.ShapeDtypeStruct((rows, D), BF16),
            jax.ShapeDtypeStruct((2 * rows, D), BF16),
            jax.ShapeDtypeStruct((2 * rows, D), BF16),
            jax.ShapeDtypeStruct((rows, D), BF16),
            jax.ShapeDtypeStruct((rows, D), BF16),
        ],
        compiler_params=params(dimension_semantics=("arbitrary",)),
        name="project",
    )(w_rows, w_all, prev_tokens, tokens, cotangent, smalls, cos_t, fwd_t, back_t)


QB = 256
SPAN = WINDOW + QB


def attend(q, k, v, d_out, seg_q, seg_k, cos8, sin8):
    rows = q.shape[0]
    blocks = rows // QB
    pairs = HEADS // 2
    scale = HEAD ** (-0.5)
    half = ROT // 2

    def kernel(
        q_ref, k_ref, v_ref, do_ref, sq_ref, sk_ref, cos_ref, sin_ref,
        o_ref, dq_ref, dk_ref, dv_ref, peak_ref, bias, kt, vt,
    ):
        p = pl.program_id(0)
        i = pl.program_id(1)
        start = pl.multiple_of(i * QB, QB)
        span = pl.ds(start, SPAN)

        @pl.when(p == 0)
        def _():
            gap = (
                WINDOW
                + lax.broadcasted_iota(jnp.int32, (SPAN, QB), 1)
                - lax.broadcasted_iota(jnp.int32, (SPAN, QB), 0)
            )
            allowed = (gap >= 0) & (gap < WINDOW) & (sk_ref[span, :] == sq_ref[...])
            bias[i] = jnp.where(allowed, 0.0, MASKED)

        @pl.when(i == 0)
        def _():
            kt[...] = k_ref[...].T
            vt[...] = v_ref[...].T
            dk_ref[...] = jnp.zeros_like(dk_ref)
            dv_ref[...] = jnp.zeros_like(dv_ref)

        k_pair = k_ref[span, :]
        v_pair = v_ref[span, :]
        lane = lax.broadcasted_iota(jnp.int32, (QB, BLK), 1)
        q_all = (q_ref[...].astype(F32) * scale).astype(BF16)
        do_all = do_ref[...]
        outs, dqs = [], []
        dk_sum = None
        for h in range(2):
            mine = (lane >= h * HEAD) & (lane < (h + 1) * HEAD)
            q_h = jnp.where(mine, q_all, jnp.zeros_like(q_all))
            do_h = jnp.where(mine, do_all, jnp.zeros_like(do_all))
            st = dot(k_pair, q_h, NT) + bias[i]
            top = jnp.max(st, axis=0, keepdims=True)
            e = jnp.exp(st - top)
            prob = e * (1.0 / jnp.sum(e, axis=0, keepdims=True))
            prob_low = prob.astype(BF16)
            dpt = dot(v_pair, do_h, NT)
            mean = jnp.sum(prob * dpt, axis=0, keepdims=True)
            dst = (prob * (dpt - mean)).astype(BF16)
            at = pl.ds(h * HEAD, HEAD)
            outs.append(dot(vt[at, span], prob_low))
            dq = dot(kt[at, span], dst) * scale
            a, b = dq[:half], dq[half:ROT]
            cos_t, sin_t = cos_ref[...], sin_ref[...]
            dqs += [a * cos_t + b * sin_t, b * cos_t - a * sin_t, dq[ROT:]]
            dv_h = dot(prob_low, do_h)
            dk_h = dot(dst, q_h)
            dk_sum = dk_h if h == 0 else dk_sum + dk_h
            dv_sum = dv_h if h == 0 else dv_sum + dv_h
            row = pl.ds(h, 1)

            @pl.when(i == 0)
            def _():
                peak_ref[row, :] = top

            @pl.when(i > 0)
            def _():
                peak_ref[row, :] = jnp.maximum(peak_ref[row, :], top)

        dk_ref[span, :] += dk_sum
        dv_ref[span, :] += dv_sum
        o_ref[...] = jnp.concatenate(outs, axis=0).T.astype(BF16)
        dq_ref[...] = jnp.concatenate(dqs, axis=0).T.astype(BF16)

    qblock = pl.BlockSpec((QB, BLK), lambda p, i: (i, p))
    kblock = pl.BlockSpec((2 * rows, BLK), lambda p, i: (0, p))
    rot = pl.BlockSpec((half, QB), lambda p, i: (0, i))
    return pl.pallas_call(
        kernel,
        grid=(pairs, blocks),
        in_specs=[
            qblock, kblock, kblock, qblock,
            pl.BlockSpec((1, QB), lambda p, i: (0, i)),
            pl.BlockSpec((2 * rows, 1), lambda p, i: (0, 0)),
            rot, rot,
        ],
        out_specs=[qblock, qblock, kblock, kblock, pl.BlockSpec((8, QB), lambda p, i: (p, 0))],
        out_shape=[
            jax.ShapeDtypeStruct((rows, D), BF16),
            jax.ShapeDtypeStruct((rows, D), BF16),
            jax.ShapeDtypeStruct((2 * rows, D), F32),
            jax.ShapeDtypeStruct((2 * rows, D), F32),
            jax.ShapeDtypeStruct((8 * pairs, QB), F32),
        ],
        scratch_shapes=[
            pltpu.VMEM((blocks, SPAN, QB), F32),
            pltpu.VMEM((BLK, 2 * rows), BF16),
            pltpu.VMEM((BLK, 2 * rows), BF16),
        ],
        compiler_params=params(dimension_semantics=("arbitrary", "arbitrary")),
        cost_estimate=pl.CostEstimate(flops=40 << 30, bytes_accessed=32 << 20, transcendentals=20 << 20),
        name="attend",
    )(q, k, v, d_out, seg_q, seg_k, cos8, sin8)


FB = 512


def gelu_parts(v):
    a = jnp.abs(v)
    t = 1.0 / (1.0 + a * (0.3275911 * 0.7071067811865476))
    poly = t * (
        0.5 * 0.254829592
        + t * (0.5 * -0.284496736 + t * (0.5 * 1.421413741 + t * (0.5 * -1.453152027 + t * (0.5 * 1.061405429))))
    )
    e = jnp.exp(v * v * -0.5)
    tail = poly * e
    cdf = jnp.where(v >= 0, 1.0 - tail, tail)
    return v * cdf, cdf + v * e * 0.3989422804014327


def feed_forward(w_rows, g_rows, w_all, m, cotangent, b_up):
    rows = m.shape[0]
    steps = FF // FB

    def kernel(
        w_rows_ref, g_rows_ref, w_ref, m_ref, g_ref, b_ref, out_ref, dm_ref, db_ref, gr_ref,
        mt, wup, wdn, hs, dus, gup, gdn, wsem, gsem,
    ):
        f = pl.program_id(0)
        slot = f % 2
        per = FB // BLK

        def up_at(buf, t):
            return buf.at[pl.ds(pl.multiple_of((t // per) * BLK, BLK), BLK), pl.ds(pl.multiple_of((t % per) * BLK, BLK), BLK)]

        def up_tile(ff, t):
            return UP_BASE + (t // per) * (FF // BLK) + ff * per + t % per

        def down_at(buf, t):
            return buf.at[pl.ds(pl.multiple_of((t // 8) * BLK, BLK), BLK), pl.ds(pl.multiple_of((t % 8) * BLK, BLK), BLK)]

        def down_tile(ff, t):
            return DOWN_BASE + ff * per * 8 + t

        def fetch(ff, sl):
            def body(t):
                src = w_ref.at[pl.ds(pl.multiple_of(w_rows_ref[up_tile(ff, t)], 16), BLK)]
                pltpu.make_async_copy(src, up_at(wup.at[sl], t), wsem.at[0, sl]).start()
                src = w_ref.at[pl.ds(pl.multiple_of(w_rows_ref[down_tile(ff, t)], 16), BLK)]
                pltpu.make_async_copy(src, down_at(wdn.at[sl], t), wsem.at[1, sl]).start()

            tile_loop(0, 8 * per, body)

        def store(ff, sl):
            def body(t):
                dst = gr_ref.at[pl.ds(pl.multiple_of(g_rows_ref[up_tile(ff, t)], 16), BLK)]
                pltpu.make_async_copy(up_at(gup.at[sl], t), dst, gsem.at[0, sl]).start()
                dst = gr_ref.at[pl.ds(pl.multiple_of(g_rows_ref[down_tile(ff, t)], 16), BLK)]
                pltpu.make_async_copy(down_at(gdn.at[sl], t), dst, gsem.at[1, sl]).start()

            tile_loop(0, 8 * per, body)

        def whole_wait(buf, sem):
            pltpu.make_async_copy(buf, buf, sem).wait()

        @pl.when(f == 0)
        def _():
            fetch(0, 0)
            mt[...] = m_ref[...].T
            out_ref[...] = jnp.zeros_like(out_ref)
            dm_ref[...] = jnp.zeros_like(dm_ref)

        whole_wait(wup.at[slot], wsem.at[0, slot])
        whole_wait(wdn.at[slot], wsem.at[1, slot])

        @pl.when(f + 1 < steps)
        def _():
            fetch(f + 1, 1 - slot)

        @pl.when(f >= 2)
        def _():
            whole_wait(gup.at[slot], gsem.at[0, slot])
            whole_wait(gdn.at[slot], gsem.at[1, slot])

        w_u = wup[slot]
        w_d = wdn[slot]
        u = dot(m_ref[...], w_u) + b_ref[...]
        dh = dot(g_ref[...], w_d, NT)
        hidden, slope = gelu_parts(u)
        hs[...] = hidden.astype(BF16)
        du = (dh * slope).astype(BF16)
        dus[...] = du
        db_ref[...] = jnp.sum(du.astype(F32), axis=0, keepdims=True)
        out_ref[...] += dot(hs[...], w_d)
        dm_ref[...] += dot(dus[...], w_u, NT)
        gdn[slot] = dot(hs[...], g_ref[...], TN).astype(BF16)
        gup[slot] = dot(mt[...], dus[...]).astype(BF16)
        store(f, slot)

        @pl.when(f == steps - 1)
        def _():
            for sl in range(2):
                whole_wait(gup.at[sl], gsem.at[0, sl])
                whole_wait(gdn.at[sl], gsem.at[1, sl])

    full = pl.BlockSpec((rows, D), lambda f, *_: (0, 0))
    bias = pl.BlockSpec((1, FB), lambda f, *_: (0, f))
    return pl.pallas_call(
        kernel,
        grid_spec=pltpu.PrefetchScalarGridSpec(
            num_scalar_prefetch=2,
            grid=(steps,),
            in_specs=[ANY, full, full, bias],
            out_specs=[full, full, bias, ANY],
            scratch_shapes=[
                pltpu.VMEM((D, rows), BF16),
                pltpu.VMEM((2, D, FB), BF16),
                pltpu.VMEM((2, FB, D), BF16),
                pltpu.VMEM((rows, FB), BF16),
                pltpu.VMEM((rows, FB), BF16),
                pltpu.VMEM((2, D, FB), BF16),
                pltpu.VMEM((2, FB, D), BF16),
                pltpu.SemaphoreType.DMA((2, 2)),
                pltpu.SemaphoreType.DMA((2, 2)),
            ],
        ),
        out_shape=[
            jax.ShapeDtypeStruct((rows, D), F32),
            jax.ShapeDtypeStruct((rows, D), F32),
            jax.ShapeDtypeStruct((1, FF), F32),
            jax.ShapeDtypeStruct((TILES * BLK, BLK), BF16),
        ],
        compiler_params=params(dimension_semantics=("arbitrary",)),
        cost_estimate=pl.CostEstimate(flops=52 << 30, bytes_accessed=48 << 20, transcendentals=8 << 20),
        name="feed_forward",
    )(w_rows, g_rows, w_all, m, cotangent, b_up)


def finish(w_rows, w_all, tokens, cotangent, smalls, attn_out, mlp_out, dm, dq, dk, dv, dk_back, dv_back, tables):
    rows = tokens.shape[0]
    steps = rows // ROWB
    cos_t, fwd_t, back_t = tables

    def kernel(
        w_rows_ref, w_ref, tok_ref, g_ref, small_ref, o_ref, mlp_ref, dm_ref, dq_ref, dk_ref, dv_ref, dkb_ref, dvb_ref,
        cos_ref, fwd_ref, back_ref,
        out_ref, dx_ref, dp_ref, a_ref, sum_ref, wqkv, wo, sems,
    ):
        i = pl.program_id(0)

        @pl.when(i == 0)
        def _():
            def body(t):
                src = w_ref.at[pl.ds(pl.multiple_of(w_rows_ref[OUT_BASE + t], 16), BLK)]
                dst = wo.at[pl.ds(pl.multiple_of((t // 8) * BLK, BLK), BLK), pl.ds(pl.multiple_of((t % 8) * BLK, BLK), BLK)]
                pltpu.make_async_copy(src, dst, sems.at[0]).start()

            tile_loop(0, 64, body)

            def body(t):
                src = w_ref.at[pl.ds(pl.multiple_of(w_rows_ref[t], 16), BLK)]
                dst = wqkv.at[pl.ds(pl.multiple_of((t // 24) * BLK, BLK), BLK), pl.ds(pl.multiple_of((t % 24) * BLK, BLK), BLK)]
                pltpu.make_async_copy(src, dst, sems.at[1]).start()

            tile_loop(0, 192, body)
            pltpu.make_async_copy(wo, wo, sems.at[0]).wait()
            sum_ref[...] = jnp.zeros_like(sum_ref)

        x = tok_ref[...].astype(F32)
        grad = g_ref[...].astype(F32)
        normed, inv = norm_rows(x)
        g1, g2 = small_ref[4:5, :], small_ref[6:7, :]
        a_ref[...] = (normed * g1 + small_ref[5:6, :]).astype(BF16)
        attn = dot(o_ref[...], wo[...]) + small_ref[2:3, :]
        out_ref[...] = (x + attn + (mlp_ref[...] + small_ref[3:4, :])).astype(BF16)
        dk_all = dk_ref[...] + dkb_ref[...].astype(F32)
        dk_all = rope_rows(dk_all, cos_ref[...], -fwd_ref[...], -back_ref[...])
        dv_all = dv_ref[...] + dvb_ref[...].astype(F32)
        dq_low = dq_ref[...]
        dv_low = dv_all.astype(BF16)
        dp_ref[:, :D] = dq_low
        dp_ref[:, D : 2 * D] = dk_all.astype(BF16)
        dp_ref[:, 2 * D :] = dv_low

        @pl.when(i == 0)
        def _():
            pltpu.make_async_copy(wqkv, wqkv, sems.at[1]).wait()

        da = dot(dp_ref[...], wqkv[...], NT)
        dmv = dm_ref[...]
        dn = da * g1 + dmv * g2
        mean_dn = jnp.mean(dn, axis=-1, keepdims=True)
        mean_dnn = jnp.mean(dn * normed, axis=-1, keepdims=True)
        dx_ref[...] = grad + inv * (dn - mean_dn - normed * mean_dnn)

        def add(row, value):
            sum_ref[row : row + 1, :] += jnp.sum(value, axis=0, keepdims=True)

        add(0, dq_low.astype(F32))
        add(1, dv_low.astype(F32))
        add(2, grad)
        add(3, da * normed)
        add(4, da)
        add(5, dmv * normed)
        add(6, dmv)

    here = lambda i, *_: (i, 0)
    later = lambda i, *_: (i + steps, 0)
    block = pl.BlockSpec((ROWB, D), here)
    upper = pl.BlockSpec((ROWB, D), later)
    table = pl.BlockSpec((ROWB, BLK), later)
    return pl.pallas_call(
        kernel,
        grid_spec=pltpu.PrefetchScalarGridSpec(
            num_scalar_prefetch=1,
            grid=(steps,),
            in_specs=[
                ANY, block, block, pl.BlockSpec((16, D), lambda i, *_: (0, 0)),
                block, block, block, block, upper, upper, block, block, table, table, table,
            ],
            out_specs=[
                block, block, pl.BlockSpec((ROWB, 3 * D), here), block,
                pl.BlockSpec((8, D), lambda i, *_: (0, 0)),
            ],
            scratch_shapes=[
                pltpu.VMEM((D, 3 * D), BF16),
                pltpu.VMEM((D, D), BF16),
                pltpu.SemaphoreType.DMA((2,)),
            ],
        ),
        out_shape=[
            jax.ShapeDtypeStruct((rows, D), BF16),
            jax.ShapeDtypeStruct((rows, D), F32),
            jax.ShapeDtypeStruct((rows, 3 * D), BF16),
            jax.ShapeDtypeStruct((rows, D), BF16),
            jax.ShapeDtypeStruct((8, D), F32),
        ],
        compiler_params=params(dimension_semantics=("arbitrary",)),
        name="finish",
    )(w_rows, w_all, tokens, cotangent, smalls, attn_out, mlp_out, dm, dq, dk, dv, dk_back, dv_back, cos_t, fwd_t, back_t)


def attention_weight_grads(g_rows, grads, attn_in, d_proj, attn_out, cotangent):
    rows = attn_in.shape[0]
    steps = 4 * D // FB

    def kernel(g_rows_ref, a_ref, dp_ref, o_ref, g_ref, _, gr_ref, at, ot, stage, sem):
        i = pl.program_id(0)
        slot = i % 2
        per = FB // BLK

        @pl.when(i == 0)
        def _():
            at[...] = a_ref[...].T

        @pl.when(i == 3 * D // FB)
        def _():
            ot[...] = o_ref[...].T

        @pl.when(i >= 2)
        def _():
            pltpu.make_async_copy(stage.at[slot], stage.at[slot], sem.at[slot]).wait()

        def piece(buf, t):
            return buf.at[pl.ds(pl.multiple_of((t // per) * BLK, BLK), BLK), pl.ds(pl.multiple_of((t % per) * BLK, BLK), BLK)]

        @pl.when(i < 3 * D // FB)
        def _():
            stage[slot] = dot(at[...], dp_ref[...]).astype(BF16)

            def body(t):
                tile = (t // per) * 24 + i * per + t % per
                dst = gr_ref.at[pl.ds(pl.multiple_of(g_rows_ref[tile], 16), BLK)]
                pltpu.make_async_copy(piece(stage.at[slot], t), dst, sem.at[slot]).start()

            tile_loop(0, 8 * per, body)

        @pl.when(i >= 3 * D // FB)
        def _():
            stage[slot] = dot(ot[...], g_ref[...]).astype(BF16)

            def body(t):
                tile = OUT_BASE + (t // per) * 8 + (i - 3 * D // FB) * per + t % per
                dst = gr_ref.at[pl.ds(pl.multiple_of(g_rows_ref[tile], 16), BLK)]
                pltpu.make_async_copy(piece(stage.at[slot], t), dst, sem.at[slot]).start()

            tile_loop(0, 8 * per, body)

        @pl.when(i == steps - 1)
        def _():
            for sl in range(2):
                pltpu.make_async_copy(stage.at[sl], stage.at[sl], sem.at[sl]).wait()

    full = pl.BlockSpec((rows, D), lambda i, *_: (0, 0))
    last = 3 * D // FB - 1
    return pl.pallas_call(
        kernel,
        grid_spec=pltpu.PrefetchScalarGridSpec(
            num_scalar_prefetch=1,
            grid=(steps,),
            in_specs=[
                full,
                pl.BlockSpec((rows, FB), lambda i, *_: (0, jnp.minimum(i, last))),
                full,
                pl.BlockSpec((rows, FB), lambda i, *_: (0, jnp.maximum(i - last - 1, 0))),
                ANY,
            ],
            out_specs=ANY,
            scratch_shapes=[
                pltpu.VMEM((D, rows), BF16),
                pltpu.VMEM((D, rows), BF16),
                pltpu.VMEM((2, D, FB), BF16),
                pltpu.SemaphoreType.DMA((2,)),
            ],
        ),
        out_shape=jax.ShapeDtypeStruct(grads.shape, BF16),
        input_output_aliases={5: 0},
        compiler_params=params(dimension_semantics=("arbitrary",)),
        name="attention_weight_grads",
    )(g_rows, attn_in, d_proj, attn_out, cotangent, grads)


def update_tiles(grads, tiles, left, right, first, second, scale):
    count = tiles.shape[0]
    group = max(g for g in (1, 2, 3, 4) if count % g == 0)

    def kernel(g_ref, w_ref, l_ref, r_ref, m_ref, v_ref, s_ref, w_out, low_out, m_out, v_out):
        for t in range(group):
            l, r = l_ref[t], r_ref[t]
            turned = dot(dot(l, g_ref[t], TN, HIGH), r, NN, HIGH)
            m_new = BETA * m_ref[t] + (1.0 - BETA) * turned
            v_new = BETA * v_ref[t] + (1.0 - BETA) * turned * turned
            ratio = m_new / (jnp.sqrt(v_new) + ADAM_EPS)
            back = dot(dot(l, ratio, NN, HIGH), r, NT, HIGH)
            w_new = (w_ref[t] - LEARN * back) * s_ref[t]
            w_out[t] = w_new
            low_out[t] = w_new.astype(BF16)
            m_out[t] = m_new
            v_out[t] = v_new

    block = pl.BlockSpec((group, BLK, BLK), lambda i: (i, 0, 0))
    row = pl.BlockSpec((group, 1, BLK), lambda i: (i, 0, 0))
    like = lambda t: jax.ShapeDtypeStruct(tiles.shape, t)
    return pl.pallas_call(
        kernel,
        grid=(count // group,),
        in_specs=[block] * 6 + [row],
        out_specs=[block] * 4,
        out_shape=[like(F32), like(BF16), like(F32), like(F32)],
        compiler_params=params(dimension_semantics=("arbitrary",)),
        name="update_tiles",
    )(grads, tiles, left, right, first, second, scale)


def column_scales(tile_ids, factors):
    columns = (tile_ids % (3 * D // BLK))[:, None] * BLK + jnp.arange(BLK, dtype=jnp.int32)[None, :]
    head_index = columns % D // HEAD
    root_factor = jnp.sqrt(factors)
    picked = jnp.sum(
        jnp.where(head_index[..., None] == jnp.arange(HEADS, dtype=jnp.int32), root_factor, 0.0),
        axis=-1,
    )
    clipped = (tile_ids[:, None] < QKV_TILES) & (columns < 2 * D)
    return jnp.where(clipped, picked, 1.0)


def small_update(grads, params_, first_moment, second_moment):
    first_new = BETA * first_moment + (1.0 - BETA) * grads
    second_new = BETA * second_moment + (1.0 - BETA) * grads * grads
    updated = params_ - SMALL_LEARN * first_new / (jnp.sqrt(second_new) + ADAM_EPS)
    return (updated, first_new, second_new)


def passed_along(value, axis, steps):
    count = lax.axis_size(axis)
    leading, last = (max(0, -steps), min(count, count - steps))
    return lax.ppermute(value, axis, [(source, source + steps) for source in range(leading, last)])


def on_device(
    ring,
    tokens,
    segments,
    cotangent,
    tile_of_slot,
    tiles,
    left_bases,
    right_bases,
    first_moments,
    second_moments,
    small_params,
    small_first,
    small_second,
    threshold,
):
    rows = tokens.shape[0]
    slot_count = tiles.shape[0]
    small_count = small_params.shape[0]
    axes = ("dp", "seq")
    seq_index = lax.axis_index("seq")
    owner_index = lax.axis_index(axes)
    first_place = seq_index * rows
    seg_local = segments.reshape(1, rows)

    numbers = jnp.arange(TILES, dtype=jnp.int32)
    slot_of_tile = jnp.sum(
        jnp.where(tile_of_slot[None, :] == numbers[:, None], numbers[None, :], 0), axis=1
    ).astype(jnp.int32)
    g_rows = slot_of_tile * BLK

    if ring:
        small_block = jnp.zeros((16 * BLK,), BF16).at[:small_count].set(small_params.astype(BF16))
        payload = jnp.concatenate(
            [tiles.astype(BF16).reshape(slot_count * BLK, BLK), small_block.reshape(16, BLK)], axis=0
        )
        seg_rows = jnp.broadcast_to(seg_local, (8, rows))
        gathered, prev_tokens, prev_seg = gather_weights(payload, tokens, seg_rows)
        stride = payload.shape[0]
        w_all = gathered.reshape(-1, BLK)
        w_rows = slot_of_tile // slot_count * stride + slot_of_tile % slot_count * BLK
        tail = slot_count * BLK
        small_all = gathered[:, tail : tail + small_count // BLK, :].reshape(SMALL)
        prev_seg = prev_seg[:1]
    else:
        w_all = lax.all_gather(tiles.astype(BF16), axes, axis=0, tiled=True).reshape(-1, BLK)
        w_rows = g_rows
        small_all = lax.all_gather(small_params.astype(BF16), axes, axis=0, tiled=True)
        prev_tokens, prev_seg = passed_along((tokens, seg_local), "seq", 1)

    table = small_all.astype(F32).reshape(D, 12)
    smalls = jnp.concatenate(
        [
            jnp.stack([table[:, r] for r in (0, 1, 2, 7, 8, 9, 10, 11)], axis=0),
            jnp.zeros((8, D), F32),
        ],
        axis=0,
    )
    b_up = table[:, 3:7].reshape(1, FF)

    half = ROT // 2
    exponent = jnp.arange(half, dtype=F32) * (2.0 / ROT)
    frequency = jnp.power(ROPE_BASE, -exponent)
    places = first_place - rows + jnp.arange(2 * rows, dtype=jnp.int32)
    angle = places.astype(F32)[None, :] * frequency[:, None]
    cos8, sin8 = jnp.cos(angle), jnp.sin(angle)
    cos_c, sin_c = cos8.T, sin8.T
    ones = jnp.ones((2 * rows, HEAD - ROT), F32)
    none = jnp.zeros((2 * rows, half), F32)
    rest = jnp.zeros((2 * rows, HEAD - ROT), F32)
    cos_t = jnp.concatenate([cos_c, cos_c, ones] * 2, axis=1)
    fwd_t = jnp.concatenate([-sin_c, none, rest] * 2, axis=1)
    back_t = jnp.concatenate([none, sin_c, rest] * 2, axis=1)
    tables = (cos_t, fwd_t, back_t)

    prev_seg = jnp.where(seq_index == 0, -1, prev_seg)
    seg_k = jnp.concatenate([prev_seg, seg_local], axis=1).reshape(2 * rows, 1)

    q, k, v, d_out, m = project(w_rows, w_all, prev_tokens, tokens, cotangent, smalls, tables)
    attn_out, dq, dk, dv, peaks = attend(
        q, k, v, d_out, seg_local, seg_k, cos8[:, rows:], sin8[:, rows:]
    )
    dk_back = passed_along(dk[:rows].astype(BF16), "seq", -1)
    dv_back = passed_along(dv[:rows].astype(BF16), "seq", -1)
    mlp_out, dm, db_up, grads = feed_forward(w_rows, g_rows, w_all, m, cotangent, b_up)
    block_output, input_grad, d_proj, attn_in, sums = finish(
        w_rows, w_all, tokens, cotangent, smalls, attn_out, mlp_out, dm, dq, dk, dv, dk_back, dv_back, tables
    )
    grads = attention_weight_grads(g_rows, grads, attn_in, d_proj, attn_out, cotangent)

    small_terms = jnp.concatenate(
        [
            sums[:3].T,
            db_up.reshape(D, FF // D),
            sums[2:7].T,
        ],
        axis=1,
    ).reshape(SMALL)
    head_peak = jnp.max(peaks.reshape(HEADS // 2, 8, QB)[:, :2, :], axis=-1).reshape(HEADS)
    if ring:
        peak_rows = jnp.zeros((8, BLK), F32).at[:, :HEADS].set(head_peak[None, :])
        extra = jnp.concatenate([small_terms.reshape(SMALL_ROWS, BLK), peak_rows], axis=0)
        tile_grads, extra = sum_gradients(grads, extra)
        tile_grads = tile_grads.reshape(slot_count, BLK, BLK)
        small_grads = lax.dynamic_slice_in_dim(
            extra[:SMALL_ROWS].reshape(SMALL), owner_index * small_count, small_count, 0
        )
        head_peak = extra[SMALL_ROWS, :HEADS]
    else:
        tile_grads = lax.psum_scatter(
            grads.astype(F32).reshape(TILES, BLK, BLK), axes, scatter_dimension=0, tiled=True
        )
        small_grads = lax.psum_scatter(small_terms, axes, scatter_dimension=0, tiled=True)
        head_peak = lax.pmax(head_peak, axes)

    local_ids = lax.dynamic_slice_in_dim(tile_of_slot, owner_index * slot_count, slot_count, 0)
    limit = threshold[0]
    factors = limit / jnp.maximum(head_peak, limit)
    scale = column_scales(local_ids, factors).reshape(slot_count, 1, BLK)
    new_tiles, new_low, new_first, new_second = update_tiles(
        tile_grads, tiles, left_bases, right_bases, first_moments, second_moments, scale
    )
    new_small, new_small_first, new_small_second = small_update(
        small_grads, small_params, small_first, small_second
    )
    return (
        block_output,
        input_grad,
        tile_grads,
        small_grads,
        new_tiles,
        new_low,
        new_first,
        new_second,
        new_small,
        new_small.astype(BF16),
        new_small_first,
        new_small_second,
        factors,
    )


def solution(mesh):
    split = P(("dp", "seq"))
    in_specs = (split, P("dp", "seq"), split, P()) + (split,) * 8 + (P(),)
    out_specs = (split,) * 12 + (P(),)
    ring = (mesh.shape["dp"], mesh.shape["seq"]) == (4, 8)
    return jax.shard_map(
        functools.partial(on_device, ring), mesh=mesh, in_specs=in_specs, out_specs=out_specs, check_vma=False
    )
```

```python
import functools

import jax
import jax.numpy as jnp
from jax import lax
from jax.experimental import pallas as pl
from jax.experimental.pallas import tpu as pltpu
from jax.sharding import PartitionSpec as P

D = 1024
FF = 4096
HEADS = 16
HEAD = 64
ROT = 16
BLK = 128
WINDOW = 1024
TILES = 768
SMALL = 12288
QKV_TILES = D // BLK * (3 * D // BLK)
OUT_TILES = D // BLK * (D // BLK)
UP_TILES = D // BLK * (FF // BLK)
OUT_BASE = QKV_TILES
UP_BASE = QKV_TILES + OUT_TILES
DOWN_BASE = UP_BASE + UP_TILES

NORM_EPS = 1e-05
ADAM_EPS = 1e-08
BETA = 0.5
LEARN = 0.03
SMALL_LEARN = 0.2
ROPE_BASE = 10000.0
MASKED = -1e30
HIGH = lax.Precision.HIGHEST

F32 = jnp.float32
BF16 = jnp.bfloat16
MESH = pl.DeviceIdType.MESH
ANY = pl.BlockSpec(memory_space=pl.ANY)
VMEM = pl.BlockSpec(memory_space=pltpu.VMEM)
VMEM_LIMIT = 58 << 20

NN = (((1,), (0,)), ((), ()))
NT = (((1,), (1,)), ((), ()))
TN = (((0,), (0,)), ((), ()))


def dot(a, b, dims=NN, precision=None):
    return lax.dot_general(a, b, dims, precision=precision, preferred_element_type=F32)


def interleave(*parts):
    live = list(parts)
    while live:
        for part in list(live):
            try:
                next(part)
            except StopIteration:
                live.remove(part)


def params(**kw):
    return pltpu.CompilerParams(vmem_limit_bytes=VMEM_LIMIT, **kw)


def norm_rows(x):
    centered = x - jnp.mean(x, axis=-1, keepdims=True)
    inv = lax.rsqrt(jnp.mean(centered * centered, axis=-1, keepdims=True) + NORM_EPS)
    return centered * inv, inv


def tile_loop(first, count, body):
    def step(t, carry):
        body(t)
        return carry

    lax.fori_loop(first, first + count, step, 0)


ROWS_PER_TILE = BLK
HALF_ROWS = 1536


def gather_weights(payload, tokens, seg_rows):
    rows = payload.shape[0]
    top = pl.ds(0, HALF_ROWS)
    low = pl.ds(HALF_ROWS, rows - HALF_ROWS)

    def kernel(x_ref, tok_ref, seg_ref, out_ref, ptok_ref, pseg_ref, lsem, ss, rs, hss, hrs, hls):
        d = lax.axis_index("dp")
        s = lax.axis_index("seq")
        z = s // 2
        c = s % 2
        xn = d + 1 - 2 * (d % 2)
        yn = d + 2 - 4 * (d // 2)
        xyn = 3 - d
        sib = z * 2 + 1 - c
        halo = s - 1 + 2 * c
        halo_ok = ((c == 0) & (z > 0)) | ((c == 1) & (z < 3))

        barrier = pltpu.get_barrier_semaphore()

        def greet(dev):
            pl.semaphore_signal(barrier, inc=1, device_id=dev, device_id_type=MESH)

        greet((d, sib))
        greet((xn, s))
        greet((yn, s))

        @pl.when(z > 0)
        def _():
            greet((d, s - 2))

        @pl.when(z < 3)
        def _():
            greet((d, s + 2))

        @pl.when(halo_ok)
        def _():
            greet((d, halo))

        below, above = (z + 2) // 3, (5 - z) // 3
        pl.semaphore_wait(barrier, 3 + below + above + (1 - c) * below + c * above)

        def place(dd, zz):
            return out_ref.at[dd * 8 + zz * 2 + c]

        def remote(src, dst, kind, zz, dev):
            return pltpu.make_async_remote_copy(
                src_ref=src,
                dst_ref=dst,
                send_sem=ss.at[kind, zz],
                recv_sem=rs.at[kind, zz],
                device_id=dev,
                device_id_type=MESH,
            )

        def block_of(zz, own):
            return x_ref if own else place(d, zz)

        def up(zz, own):
            return remote(block_of(zz, own), place(d, zz), 0, zz, (d, s + 2))

        def down(zz, own):
            return remote(block_of(zz, own), place(d, zz), 1, zz, (d, s - 2))

        def to_x(zz, own):
            return remote(block_of(zz, own), place(d, zz), 2, zz, (xn, s))

        def to_y(zz, own):
            return remote(block_of(zz, own), place(d, zz), 3, zz, (yn, s))

        def on_y(zz):
            return remote(place(xn, zz).at[top], place(xn, zz).at[top], 4, zz, (yn, s))

        def on_x(zz):
            return remote(place(yn, zz).at[low], place(yn, zz).at[low], 5, zz, (xn, s))

        def to_sib(dd, zz, kind, own=False):
            src = x_ref if own else place(dd, zz)
            return remote(src, place(dd, zz), kind, zz, (d, sib))

        def from_x(zz):
            return remote(x_ref, place(xn, zz), 2, zz, (xn, s))

        def from_y(zz):
            return remote(x_ref, place(yn, zz), 3, zz, (yn, s))

        def diag_top(zz):
            return remote(x_ref.at[top], place(xyn, zz).at[top], 4, zz, (yn, s))

        def diag_low(zz):
            return remote(x_ref.at[low], place(xyn, zz).at[low], 5, zz, (xn, s))

        order = [z, 1 + z % 2, (2 + 3 * z) % 5, 3 * (1 - z // 2)]
        local = pltpu.make_async_copy(x_ref, place(d, z), lsem)
        local.start()

        def halo_copies(dev):
            tok = pltpu.make_async_remote_copy(
                src_ref=tok_ref,
                dst_ref=ptok_ref,
                send_sem=hss.at[0],
                recv_sem=hrs.at[0],
                device_id=dev,
                device_id_type=MESH,
            )
            seg = pltpu.make_async_remote_copy(
                src_ref=seg_ref,
                dst_ref=pseg_ref,
                send_sem=hss.at[1],
                recv_sem=hrs.at[1],
                device_id=dev,
                device_id_type=MESH,
            )
            return tok, seg

        def launch(k):
            zz = order[k]
            own = k == 0
            if own:

                @pl.when(z < 3)
                def _():
                    up(zz, True).start()

                @pl.when(z > 0)
                def _():
                    down(zz, True).start()
            else:

                @pl.when(zz < z)
                def _():
                    up(zz, False).wait_recv()

                @pl.when((zz < z) & (z < 3))
                def _():
                    up(zz, False).start()

                @pl.when(zz > z)
                def _():
                    down(zz, False).wait_recv()

                @pl.when((zz > z) & (z > 0))
                def _():
                    down(zz, False).start()

            to_x(zz, own).start()
            to_y(zz, own).start()
            to_sib(d, zz, 6, own).start()

        def second(k):
            zz = order[k]
            from_x(zz).wait_recv()
            on_y(zz).start()
            to_sib(xn, zz, 7).start()
            from_y(zz).wait_recv()
            on_x(zz).start()
            to_sib(yn, zz, 8).start()

        def third(k):
            zz = order[k]
            diag_top(zz).wait_recv()
            diag_low(zz).wait_recv()
            to_sib(xyn, zz, 9).start()

        launch(0)
        own_tok = pltpu.make_async_copy(tok_ref, ptok_ref, hls.at[0])
        own_seg = pltpu.make_async_copy(seg_ref, pseg_ref, hls.at[1])

        @pl.when(s < 7)
        def _():
            for cp in halo_copies((d, s + 1)):
                cp.start()

        @pl.when(s == 0)
        def _():
            own_tok.start()
            own_seg.start()

        launch(1)
        second(0)
        launch(2)
        second(1)
        third(0)
        launch(3)
        second(2)
        third(1)
        second(3)
        third(2)
        third(3)

        local.wait()
        other = 1 - c

        def sib_place(dd, zz):
            return out_ref.at[dd * 8 + zz * 2 + other]

        for k in range(4):
            zz = order[k]
            own = k == 0
            for kind, dd in ((6, d), (7, xn), (8, yn), (9, xyn)):
                remote(sib_place(dd, zz), sib_place(dd, zz), kind, zz, (d, sib)).wait_recv()
                to_sib(dd, zz, kind, own and kind == 6).wait_send()
            to_x(zz, own).wait_send()
            to_y(zz, own).wait_send()
            on_y(zz).wait_send()
            on_x(zz).wait_send()

            @pl.when((zz <= z) & (z < 3))
            def _():
                up(zz, own).wait_send()

            @pl.when((zz >= z) & (z > 0))
            def _():
                down(zz, own).wait_send()

        @pl.when(s < 7)
        def _():
            for cp in halo_copies((d, s + 1)):
                cp.wait_send()

        @pl.when(s > 0)
        def _():
            for cp in halo_copies((d, s - 1)):
                cp.wait_recv()

        @pl.when(s == 0)
        def _():
            own_tok.wait()
            own_seg.wait()

    return pl.pallas_call(
        kernel,
        out_shape=[
            jax.ShapeDtypeStruct((32, rows, BLK), BF16),
            jax.ShapeDtypeStruct(tokens.shape, BF16),
            jax.ShapeDtypeStruct(seg_rows.shape, jnp.int32),
        ],
        in_specs=[ANY, ANY, ANY],
        out_specs=[ANY, ANY, ANY],
        scratch_shapes=[
            pltpu.SemaphoreType.DMA,
            pltpu.SemaphoreType.DMA((10, 4)),
            pltpu.SemaphoreType.DMA((10, 4)),
            pltpu.SemaphoreType.DMA((2,)),
            pltpu.SemaphoreType.DMA((2,)),
            pltpu.SemaphoreType.DMA((2,)),
        ],
        compiler_params=params(collective_id=0, has_side_effects=True),
        name="gather_weights",
    )(payload, tokens, seg_rows)


OWNED = 24 * BLK
HALF = OWNED // 2
SMALL_ROWS = SMALL // BLK
EXTRA_ROWS = SMALL_ROWS + 8


def add_rows(dst, terms, rows, step=256):
    def body(i, carry):
        at = pl.ds(pl.multiple_of(i * step, step), step)
        total = terms[0][at].astype(F32)
        for term in terms[1:]:
            total = total + term[at].astype(F32)
        dst[at] = total.astype(dst.dtype)
        return carry

    lax.fori_loop(0, rows // step, body, 0)


def sum_gradients(grads, extra):
    def kernel(g_ref, e_ref, out_ref, eout_ref, own, crecv, s1a, s1b, s2, zup, zdn, epart, erecv, ls, ss, rs, zss, zrs, es, er):
        d = lax.axis_index("dp")
        s = lax.axis_index("seq")
        z = s // 2
        c = s % 2
        xn = d + 1 - 2 * (d % 2)
        yn = d + 2 - 4 * (d // 2)
        xyn = 3 - d
        sib = z * 2 + 1 - c
        zpair = s + 2 - 4 * (z % 2)
        zfar = s + 4 - 8 * (z // 2)
        top = pl.ds(0, HALF)
        low = pl.ds(HALF, HALF)

        barrier = pltpu.get_barrier_semaphore()

        def greet(dev):
            pl.semaphore_signal(barrier, inc=1, device_id=dev, device_id_type=MESH)

        greet((d, sib))
        greet((xn, s))
        greet((yn, s))
        greet((d, zfar))

        @pl.when(z > 0)
        def _():
            greet((d, s - 2))

        @pl.when(z < 3)
        def _():
            greet((d, s + 2))

        order = [3 * (1 - z // 2), (2 + 3 * z) % 5, 1 + z % 2, z]

        def owner_rows(dd, zz, cc):
            return g_ref.at[pl.ds(pl.multiple_of((dd * 8 + zz * 2 + cc) * OWNED, OWNED), OWNED)]

        def load(zz, dd):
            return pltpu.make_async_copy(owner_rows(dd, zz, c), own.at[zz, dd], ls.at[zz, dd])

        for k in range(4):
            for dd in range(4):
                load(order[k], dd).start()

        pl.semaphore_wait(barrier, 4 + (z + 2) // 3 + (5 - z) // 3)

        def remote(src, dst, ssem, rsem, dev):
            return pltpu.make_async_remote_copy(
                src_ref=src, dst_ref=dst, send_sem=ssem, recv_sem=rsem, device_id=dev, device_id_type=MESH
            )

        def core(zz, dd):
            return remote(owner_rows(dd, zz, 1 - c), crecv.at[zz, dd], ss.at[zz, dd], rs.at[zz, dd], (d, sib))

        def y_own(zz):
            return remote(own.at[zz, yn, top], s1a.at[zz, 0], ss.at[zz, 4], rs.at[zz, 4], (yn, s))

        def y_cross(zz):
            return remote(own.at[zz, xyn, top], s1a.at[zz, 1], ss.at[zz, 5], rs.at[zz, 5], (yn, s))

        def x_own(zz):
            return remote(own.at[zz, xn, low], s1b.at[zz, 0], ss.at[zz, 6], rs.at[zz, 6], (xn, s))

        def x_cross(zz):
            return remote(own.at[zz, xyn, low], s1b.at[zz, 1], ss.at[zz, 7], rs.at[zz, 7], (xn, s))

        def x_last(zz):
            return remote(own.at[zz, xn, top], s2.at[zz, top], ss.at[zz, 8], rs.at[zz, 8], (xn, s))

        def y_last(zz):
            return remote(own.at[zz, yn, low], s2.at[zz, low], ss.at[zz, 9], rs.at[zz, 9], (yn, s))

        def z_up(zz):
            return remote(own.at[zz, d], zup.at[zz], zss.at[0, zz], zrs.at[0, zz], (d, s + 2))

        def z_dn(zz):
            return remote(own.at[zz, d], zdn.at[zz], zss.at[1, zz], zrs.at[1, zz], (d, s - 2))

        def extra_step(i, dev):
            return remote(epart.at[i], erecv.at[i], es.at[i], er.at[i], dev)

        extra_devs = [(d, sib), (xn, s), (yn, s), (d, zpair), (d, zfar)]

        def extra_add(i):
            extra_step(i, extra_devs[i]).wait_recv()
            a = epart[i]
            b = erecv[i]
            row = lax.broadcasted_iota(jnp.int32, a.shape, 0)
            total = jnp.where(row < SMALL_ROWS, a + b, jnp.maximum(a, b))
            if i < 4:
                epart[i + 1] = total
                extra_step(i + 1, extra_devs[i + 1]).start()
            else:
                eout_ref[...] = total

        for k in range(4):
            for dd in range(4):
                core(order[k], dd).start()
            if k == 0:
                epart[0] = e_ref[...]
                extra_step(0, extra_devs[0]).start()

        def first(k):
            zz = order[k]

            def one(dd, start):
                load(zz, dd).wait()
                core(zz, dd).wait_recv()
                add_rows(own.at[zz, dd], [own.at[zz, dd], crecv.at[zz, dd]], OWNED)
                for cp in start:
                    cp.start()

            one(xyn, [y_cross(zz), x_cross(zz)])
            one(yn, [y_own(zz)])
            one(xn, [x_own(zz)])
            one(d, [])

        def second(k):
            zz = order[k]
            y_cross(zz).wait_recv()
            a = own.at[zz, xn, top]
            add_rows(a, [a, s1a.at[zz, 1]], HALF)
            x_last(zz).start()
            x_cross(zz).wait_recv()
            b = own.at[zz, yn, low]
            add_rows(b, [b, s1b.at[zz, 1]], HALF)
            y_last(zz).start()

        def third(k):
            zz = order[k]
            y_own(zz).wait_recv()
            x_own(zz).wait_recv()
            x_last(zz).wait_recv()
            y_last(zz).wait_recv()
            a = own.at[zz, d, top]
            b = own.at[zz, d, low]
            if k < 3:

                @pl.when((zz > z) & (z > 0))
                def _():
                    z_up(zz).wait_recv()
                    add_rows(a, [a, s1a.at[zz, 0], s2.at[zz, top], zup.at[zz, top]], HALF)
                    add_rows(b, [b, s1b.at[zz, 0], s2.at[zz, low], zup.at[zz, low]], HALF)

                @pl.when((zz < z) & (z < 3))
                def _():
                    z_dn(zz).wait_recv()
                    add_rows(a, [a, s1a.at[zz, 0], s2.at[zz, top], zdn.at[zz, top]], HALF)
                    add_rows(b, [b, s1b.at[zz, 0], s2.at[zz, low], zdn.at[zz, low]], HALF)

                @pl.when(((zz > z) & (z == 0)) | ((zz < z) & (z == 3)))
                def _():
                    add_rows(a, [a, s1a.at[zz, 0], s2.at[zz, top]], HALF)
                    add_rows(b, [b, s1b.at[zz, 0], s2.at[zz, low]], HALF)

                @pl.when(zz > z)
                def _():
                    z_up(zz).start()

                @pl.when(zz < z)
                def _():
                    z_dn(zz).start()
            else:

                @pl.when(z > 0)
                def _():
                    z_up(zz).wait_recv()

                @pl.when(z < 3)
                def _():
                    z_dn(zz).wait_recv()

                o_top = out_ref.at[top]
                o_low = out_ref.at[low]

                @pl.when((z > 0) & (z < 3))
                def _():
                    add_rows(o_top, [a, s1a.at[zz, 0], s2.at[zz, top], zup.at[zz, top], zdn.at[zz, top]], HALF)
                    add_rows(o_low, [b, s1b.at[zz, 0], s2.at[zz, low], zup.at[zz, low], zdn.at[zz, low]], HALF)

                @pl.when(z == 0)
                def _():
                    add_rows(o_top, [a, s1a.at[zz, 0], s2.at[zz, top], zdn.at[zz, top]], HALF)
                    add_rows(o_low, [b, s1b.at[zz, 0], s2.at[zz, low], zdn.at[zz, low]], HALF)

                @pl.when(z == 3)
                def _():
                    add_rows(o_top, [a, s1a.at[zz, 0], s2.at[zz, top], zup.at[zz, top]], HALF)
                    add_rows(o_low, [b, s1b.at[zz, 0], s2.at[zz, low], zup.at[zz, low]], HALF)

        first(0)
        first(1)
        extra_add(0)
        second(0)
        first(2)
        extra_add(1)
        third(0)
        second(1)
        first(3)
        extra_add(2)
        third(1)
        second(2)
        extra_add(3)
        third(2)
        second(3)
        extra_add(4)
        third(3)

        for i in range(5):
            extra_step(i, extra_devs[i]).wait_send()
        for k in range(4):
            zz = order[k]
            for dd in range(4):
                core(zz, dd).wait_send()
            for cp in (y_own(zz), y_cross(zz), x_own(zz), x_cross(zz), x_last(zz), y_last(zz)):
                cp.wait_send()
            if k < 3:

                @pl.when(zz > z)
                def _():
                    z_up(zz).wait_send()

                @pl.when(zz < z)
                def _():
                    z_dn(zz).wait_send()

    return pl.pallas_call(
        kernel,
        out_shape=[
            jax.ShapeDtypeStruct((OWNED, BLK), F32),
            jax.ShapeDtypeStruct((EXTRA_ROWS, BLK), F32),
        ],
        in_specs=[ANY, VMEM],
        out_specs=[VMEM, VMEM],
        scratch_shapes=[
            pltpu.VMEM((4, 4, OWNED, BLK), BF16),
            pltpu.VMEM((4, 4, OWNED, BLK), BF16),
            pltpu.VMEM((4, 2, HALF, BLK), BF16),
            pltpu.VMEM((4, 2, HALF, BLK), BF16),
            pltpu.VMEM((4, OWNED, BLK), BF16),
            pltpu.VMEM((4, OWNED, BLK), BF16),
            pltpu.VMEM((4, OWNED, BLK), BF16),
            pltpu.VMEM((5, EXTRA_ROWS, BLK), F32),
            pltpu.VMEM((5, EXTRA_ROWS, BLK), F32),
            pltpu.SemaphoreType.DMA((4, 4)),
            pltpu.SemaphoreType.DMA((4, 10)),
            pltpu.SemaphoreType.DMA((4, 10)),
            pltpu.SemaphoreType.DMA((2, 4)),
            pltpu.SemaphoreType.DMA((2, 4)),
            pltpu.SemaphoreType.DMA((5,)),
            pltpu.SemaphoreType.DMA((5,)),
        ],
        compiler_params=params(collective_id=1, has_side_effects=True),
        name="sum_gradients",
    )(grads, extra)


ROWB = 256


def rope_rows(value, cos_t, fwd_t, back_t):
    pieces = []
    for j in range(value.shape[1] // BLK):
        p = value[:, j * BLK : (j + 1) * BLK]
        pieces.append(
            p * cos_t + pltpu.roll(p, BLK - ROT // 2, 1) * fwd_t + pltpu.roll(p, ROT // 2, 1) * back_t
        )
    return jnp.concatenate(pieces, axis=1)


def project(w_rows, w_all, prev_tokens, tokens, cotangent, smalls, tables):
    rows = tokens.shape[0]
    steps = rows // ROWB
    cos_t, fwd_t, back_t = tables

    def kernel(
        w_rows_ref, w_ref, prev_ref, tok_ref, g_ref, small_ref, cos_ref, fwd_ref, back_ref,
        q_ref, k_ref, v_ref, do_ref, m_ref, wqkv, wo, sems,
    ):
        i = pl.program_id(0)

        def third_copy(third):
            def body(t):
                r, cc = t // 8, t % 8
                src = w_ref.at[pl.ds(pl.multiple_of(w_rows_ref[r * 24 + third * 8 + cc], 16), BLK)]
                dst = wqkv.at[pl.ds(pl.multiple_of(r * BLK, BLK), BLK), pl.ds(pl.multiple_of(third * D + cc * BLK, BLK), BLK)]
                pltpu.make_async_copy(src, dst, sems.at[third]).start()

            tile_loop(0, 64, body)

        def third_wait(third):
            part = wqkv.at[:, pl.ds(third * D, D)]
            pltpu.make_async_copy(part, part, sems.at[third]).wait()

        @pl.when(i == 0)
        def _():
            third_copy(1)
            third_copy(2)
            third_copy(0)

            def body(t):
                r, cc = t // 8, t % 8
                src = w_ref.at[pl.ds(pl.multiple_of(w_rows_ref[OUT_BASE + t], 16), BLK)]
                dst = wo.at[pl.ds(pl.multiple_of(r * BLK, BLK), BLK), pl.ds(pl.multiple_of(cc * BLK, BLK), BLK)]
                pltpu.make_async_copy(src, dst, sems.at[3]).start()

            tile_loop(0, 64, body)
            third_wait(1)
            third_wait(2)

        @pl.when(i == steps)
        def _():
            third_wait(0)
            pltpu.make_async_copy(wo, wo, sems.at[3]).wait()

        def keys(x):
            normed, _ = norm_rows(x)
            attn_in = (normed * small_ref[4:5, :] + small_ref[5:6, :]).astype(BF16)
            k = dot(attn_in, wqkv[:, D : 2 * D])
            v = dot(attn_in, wqkv[:, 2 * D :]) + small_ref[1:2, :]
            k_ref[...] = rope_rows(k, cos_ref[...], fwd_ref[...], back_ref[...]).astype(BF16)
            v_ref[...] = v.astype(BF16)
            return normed, attn_in

        @pl.when(i < steps)
        def _():
            keys(prev_ref[...].astype(F32))

        @pl.when(i >= steps)
        def _():
            normed, attn_in = keys(tok_ref[...].astype(F32))
            m_ref[...] = (normed * small_ref[6:7, :] + small_ref[7:8, :]).astype(BF16)
            q = dot(attn_in, wqkv[:, :D]) + small_ref[0:1, :]
            q = rope_rows(q, cos_ref[...], fwd_ref[...], back_ref[...])
            q_ref[...] = q.astype(BF16)
            do_ref[...] = dot(g_ref[...], wo[...], NT).astype(BF16)

    own = lambda i, *_: (jnp.maximum(i - steps, 0), 0)
    prev = lambda i, *_: (jnp.minimum(i, steps - 1), 0)
    here = lambda i, *_: (i, 0)
    block = lambda m: pl.BlockSpec((ROWB, D), m)
    table = pl.BlockSpec((ROWB, BLK), here)
    return pl.pallas_call(
        kernel,
        grid_spec=pltpu.PrefetchScalarGridSpec(
            num_scalar_prefetch=1,
            grid=(2 * steps,),
            in_specs=[
                ANY, block(prev), block(own), block(own),
                pl.BlockSpec((16, D), lambda i, *_: (0, 0)), table, table, table,
            ],
            out_specs=[block(own), block(here), block(here), block(own), block(own)],
            scratch_shapes=[
                pltpu.VMEM((D, 3 * D), BF16),
                pltpu.VMEM((D, D), BF16),
                pltpu.SemaphoreType.DMA((4,)),
            ],
        ),
        out_shape=[
            jax.ShapeDtypeStruct((rows, D), BF16),
            jax.ShapeDtypeStruct((2 * rows, D), BF16),
            jax.ShapeDtypeStruct((2 * rows, D), BF16),
            jax.ShapeDtypeStruct((rows, D), BF16),
            jax.ShapeDtypeStruct((rows, D), BF16),
        ],
        compiler_params=params(dimension_semantics=("arbitrary",)),
        name="project",
    )(w_rows, w_all, prev_tokens, tokens, cotangent, smalls, cos_t, fwd_t, back_t)


QB = 256
SPAN = WINDOW + QB


CHUNK = 256
SAFE_SCORE = 60.0


def attend(q, k, v, d_out, seg_q, seg_k, cos8, sin8):
    rows = q.shape[0]
    blocks = rows // QB
    pairs = HEADS // 2
    scale = HEAD ** (-0.5)
    half = ROT // 2
    n = SPAN // CHUNK

    def heads_apart(x):
        row = lax.broadcasted_iota(jnp.int32, x.shape, 0)
        zero = jnp.zeros_like(x)
        return jnp.concatenate([jnp.where(row < HEAD, x, zero), jnp.where(row < HEAD, zero, x)], axis=1)

    def stacked(x):
        lane = lax.broadcasted_iota(jnp.int32, x.shape, 1)
        zero = jnp.zeros_like(x)
        return jnp.concatenate([jnp.where(lane < HEAD, x, zero), jnp.where(lane < HEAD, zero, x)], axis=0)

    def fold(x, op):
        return op(x.reshape(x.shape[0] // 8, 8, x.shape[1]), axis=0)

    def two(x):
        return jnp.concatenate([x, x], axis=1)

    def kernel(
        q_ref, k_ref, v_ref, do_ref, sq_ref, sk_ref, cos_ref, sin_ref,
        o_ref, dq_ref, dk_ref, dv_ref, halo_ref, peak_ref, bias, kt, vt, el_ref, ds_ref, dks, dvs,
    ):
        p = pl.program_id(0)

        @pl.when(p == 0)
        def _():
            gap = (
                WINDOW
                + lax.broadcasted_iota(jnp.int32, (SPAN, QB), 1)
                - lax.broadcasted_iota(jnp.int32, (SPAN, QB), 0)
            )
            for i in range(blocks):
                same = sk_ref[i * QB : i * QB + SPAN, :] == sq_ref[:, i * QB : (i + 1) * QB]
                bias[i] = jnp.where((gap >= 0) & (gap < WINDOW) & same, 0.0, MASKED)

        kt[...] = k_ref[...].T
        vt[...] = v_ref[...].T
        k_float = kt[...].astype(F32)
        q_float = q_ref[...].astype(F32) * scale
        reach = jnp.max(jnp.sum(k_float * k_float, axis=0)) * jnp.max(jnp.sum(q_float * q_float, axis=1))
        safe = reach < SAFE_SCORE * SAFE_SCORE

        def keys_at(ref, i, c):
            return ref[i * QB + c * CHUNK : i * QB + (c + 1) * CHUNK, :]

        def prepare(i):
            q_all = (q_ref[i * QB : (i + 1) * QB, :].astype(F32) * scale).astype(BF16)
            return q_all, heads_apart(q_all.T)

        def scores(i, c, q_apart):
            return dot(keys_at(k_ref, i, c), q_apart) + two(bias[i, c * CHUNK : (c + 1) * CHUNK])

        def forward(i, q_apart, shifted, found):
            base = None
            if shifted:
                for c in range(n):
                    t = fold(scores(i, c, q_apart), jnp.max)
                    base = t if c == 0 else jnp.maximum(base, t)
                base = jnp.max(base, axis=0, keepdims=True)
            top8 = sum8 = None
            for c in range(n):
                st = scores(i, c, q_apart)
                e = jnp.exp(st - base if shifted else st)
                el_ref[i % 2, c * CHUNK : (c + 1) * CHUNK] = e.astype(BF16)
                t, u = fold(st, jnp.max), fold(e, jnp.sum)
                top8, sum8 = (t, u) if c == 0 else (jnp.maximum(top8, t), sum8 + u)
                yield
            found.append(jnp.max(top8, axis=0, keepdims=True))
            found.append(1.0 / jnp.sum(sum8, axis=0, keepdims=True))

        def per_head(x):
            return jnp.concatenate(
                [jnp.broadcast_to(x[:, :QB], (HEAD, QB)), jnp.broadcast_to(x[:, QB:], (HEAD, QB))], axis=0
            )

        def both(t, x_ref, i):
            span = slice(i * QB, i * QB + SPAN)
            return jnp.concatenate(
                [dot(t[:HEAD, span], x_ref[i % 2, :, :QB]), dot(t[HEAD:, span], x_ref[i % 2, :, QB:])], axis=0
            )

        def output(i, inv):
            raw = both(vt, el_ref, i)
            inv2 = per_head(inv)
            o_ref[i * QB : (i + 1) * QB, :] = (raw * inv2).T.astype(BF16)
            do_s = (do_ref[i * QB : (i + 1) * QB, :].astype(F32).T * inv2).astype(BF16)
            m = do_s.astype(F32) * raw
            mean = jnp.concatenate(
                [jnp.sum(m[:HEAD], axis=0, keepdims=True), jnp.sum(m[HEAD:], axis=0, keepdims=True)], axis=1
            )
            return do_s, mean * inv

        def score_grads(i, do_s, mean):
            do_apart = heads_apart(do_s)
            for c in range(n):
                w = slice(c * CHUNK, (c + 1) * CHUNK)
                dpt = dot(keys_at(v_ref, i, c), do_apart)
                ds_ref[i % 2, w] = (el_ref[i % 2, w].astype(F32) * (dpt - mean)).astype(BF16)

        def input_grads(i, q_all, do_s):
            do_rows = stacked(do_s.T)
            q_rows = stacked(q_all)
            for c in range(n):
                w = slice(c * CHUNK, (c + 1) * CHUNK)
                at = slice(i * QB + c * CHUNK, i * QB + (c + 1) * CHUNK)
                v_part = dot(el_ref[i % 2, w], do_rows)
                k_part = dot(ds_ref[i % 2, w], q_rows)
                if i == 0 or c == n - 1:
                    dvs[at, :] = v_part
                    dks[at, :] = k_part
                else:
                    dvs[at, :] += v_part
                    dks[at, :] += k_part
                yield
            dq = both(kt, ds_ref, i) * scale
            cos_t, sin_t = cos_ref[:, i * QB : (i + 1) * QB], sin_ref[:, i * QB : (i + 1) * QB]
            turned = []
            for h in range(2):
                f, g = dq[h * HEAD : h * HEAD + half], dq[h * HEAD + half : h * HEAD + ROT]
                turned += [f * cos_t + g * sin_t, g * cos_t - f * sin_t, dq[h * HEAD + ROT : (h + 1) * HEAD]]
            dq_ref[i * QB : (i + 1) * QB, :] = jnp.concatenate(turned, axis=0).T.astype(BF16)
            yield

        def run(shifted):
            top = held = None
            for i in range(blocks + 1):
                parts, found = [], []
                if held is not None:
                    parts.append(input_grads(i - 1, *held))
                if i < blocks:
                    q_all, q_apart = prepare(i)
                    parts.append(forward(i, q_apart, shifted, found))
                interleave(*parts)
                if i < blocks:
                    t, inv = found
                    top = t if top is None else jnp.maximum(top, t)
                    do_s, mean = output(i, inv)
                    score_grads(i, do_s, mean)
                    held = (q_all, do_s)
            peak_ref[...] = jnp.broadcast_to(top, peak_ref.shape)
            halo_ref[0] = dks[:rows, :].astype(BF16)
            halo_ref[1] = dvs[:rows, :].astype(BF16)
            dk_ref[...] = dks[rows:, :]
            dv_ref[...] = dvs[rows:, :]

        @pl.when(safe)
        def _():
            run(False)

        @pl.when(jnp.logical_not(safe))
        def _():
            run(True)

    block = pl.BlockSpec((rows, BLK), lambda p: (0, p))
    keys = pl.BlockSpec((2 * rows, BLK), lambda p: (0, p))
    whole = lambda *shape: pl.BlockSpec(shape, lambda p: (0, 0))
    return pl.pallas_call(
        kernel,
        grid=(pairs,),
        in_specs=[
            block, keys, keys, block, whole(1, rows), whole(2 * rows, 1), whole(half, rows), whole(half, rows),
        ],
        out_specs=[
            block, block, block, block,
            pl.BlockSpec((2, rows, BLK), lambda p: (0, 0, p)),
            pl.BlockSpec((8, 2 * QB), lambda p: (p, 0)),
        ],
        out_shape=[
            jax.ShapeDtypeStruct((rows, D), BF16),
            jax.ShapeDtypeStruct((rows, D), BF16),
            jax.ShapeDtypeStruct((rows, D), F32),
            jax.ShapeDtypeStruct((rows, D), F32),
            jax.ShapeDtypeStruct((2, rows, D), BF16),
            jax.ShapeDtypeStruct((8 * pairs, 2 * QB), F32),
        ],
        scratch_shapes=[
            pltpu.VMEM((blocks, SPAN, QB), F32),
            pltpu.VMEM((BLK, 2 * rows), BF16),
            pltpu.VMEM((BLK, 2 * rows), BF16),
            pltpu.VMEM((2, SPAN, 2 * QB), BF16),
            pltpu.VMEM((2, SPAN, 2 * QB), BF16),
            pltpu.VMEM((2 * rows, BLK), F32),
            pltpu.VMEM((2 * rows, BLK), F32),
        ],
        compiler_params=params(dimension_semantics=("arbitrary",)),
        cost_estimate=pl.CostEstimate(flops=40 << 30, bytes_accessed=32 << 20, transcendentals=20 << 20),
        name="attend",
    )(q, k, v, d_out, seg_q, seg_k, cos8, sin8)


FB = 512


def gelu_parts(v):
    a = jnp.abs(v)
    t = 1.0 / (1.0 + a * (0.3275911 * 0.7071067811865476))
    poly = t * (
        0.5 * 0.254829592
        + t * (0.5 * -0.284496736 + t * (0.5 * 1.421413741 + t * (0.5 * -1.453152027 + t * (0.5 * 1.061405429))))
    )
    e = jnp.exp(v * v * -0.5)
    tail = poly * e
    cdf = jnp.where(v >= 0, 1.0 - tail, tail)
    return v * cdf, cdf + v * e * 0.3989422804014327


def feed_forward(w_rows, g_rows, w_all, m, cotangent, b_up):
    rows = m.shape[0]
    steps = FF // FB

    def kernel(
        w_rows_ref, g_rows_ref, w_ref, m_ref, g_ref, b_ref, out_ref, dm_ref, db_ref, gr_ref,
        mt, wup, wdn, hs, dus, gup, gdn, u_ref, h_ref, wsem, gsem,
    ):
        f = pl.program_id(0)
        slot = f % 2
        per = FB // BLK

        def up_at(buf, t):
            return buf.at[pl.ds(pl.multiple_of((t // per) * BLK, BLK), BLK), pl.ds(pl.multiple_of((t % per) * BLK, BLK), BLK)]

        def up_tile(ff, t):
            return UP_BASE + (t // per) * (FF // BLK) + ff * per + t % per

        def down_at(buf, t):
            return buf.at[pl.ds(pl.multiple_of((t // 8) * BLK, BLK), BLK), pl.ds(pl.multiple_of((t % 8) * BLK, BLK), BLK)]

        def down_tile(ff, t):
            return DOWN_BASE + ff * per * 8 + t

        def fetch_one(ff, sl, t):
            src = w_ref.at[pl.ds(pl.multiple_of(w_rows_ref[up_tile(ff, t)], 16), BLK)]
            pltpu.make_async_copy(src, up_at(wup.at[sl], t), wsem.at[0, sl]).start()
            src = w_ref.at[pl.ds(pl.multiple_of(w_rows_ref[down_tile(ff, t)], 16), BLK)]
            pltpu.make_async_copy(src, down_at(wdn.at[sl], t), wsem.at[1, sl]).start()

        def store_one(ff, sl, t):
            dst = gr_ref.at[pl.ds(pl.multiple_of(g_rows_ref[up_tile(ff, t)], 16), BLK)]
            pltpu.make_async_copy(up_at(gup.at[sl], t), dst, gsem.at[0, sl]).start()
            dst = gr_ref.at[pl.ds(pl.multiple_of(g_rows_ref[down_tile(ff, t)], 16), BLK)]
            pltpu.make_async_copy(down_at(gdn.at[sl], t), dst, gsem.at[1, sl]).start()

        def whole_wait(buf, sem):
            pltpu.make_async_copy(buf, buf, sem).wait()

        count = 8 * per

        @pl.when(f == 0)
        def _():
            tile_loop(0, count, lambda t: fetch_one(0, 0, t))
            mt[...] = m_ref[...].T
            out_ref[...] = jnp.zeros_like(out_ref)
            dm_ref[...] = jnp.zeros_like(dm_ref)

        whole_wait(wup.at[slot], wsem.at[0, slot])
        whole_wait(wdn.at[slot], wsem.at[1, slot])

        @pl.when(f >= 2)
        def _():
            whole_wait(gup.at[slot], gsem.at[0, slot])
            whole_wait(gdn.at[slot], gsem.at[1, slot])

        n = rows // ROWB

        def stage1(c):
            at = slice(c * ROWB, (c + 1) * ROWB)
            for k in range(FB // 256):
                cols = slice(k * 256, (k + 1) * 256)
                u_ref[c % 2, :, cols] = dot(m_ref[at, :], wup[slot, :, cols]) + b_ref[:, cols]
                yield
                h_ref[c % 2, :, cols] = dot(g_ref[at, :], wdn[slot, cols, :], NT)
                yield

        db = [None]

        def stage2(c):
            step = ROWB // 8
            for k in range(8):
                at = slice(k * step, (k + 1) * step)
                to = slice(c * ROWB + k * step, c * ROWB + (k + 1) * step)
                hidden, slope = gelu_parts(u_ref[c % 2, at, :])
                hs[to, :] = hidden.astype(BF16)
                du = (h_ref[c % 2, at, :] * slope).astype(BF16)
                dus[to, :] = du
                t = jnp.sum(du.astype(F32).reshape(step // 8, 8, FB), axis=0)
                db[0] = t if db[0] is None else db[0] + t
                yield

        def stage3(c):
            at = slice(c * ROWB, (c + 1) * ROWB)
            for k in range(D // 256):
                cols = slice(k * 256, (k + 1) * 256)
                out_ref[at, cols] += dot(hs[at, :], wdn[slot, :, cols])
                yield
                dm_ref[at, cols] += dot(dus[at, :], wup[slot, cols, :], NT)
                yield

        nxt = jnp.minimum(f + 1, steps - 1)
        for t in range(count):
            fetch_one(nxt, 1 - slot, t)

        for c in range(n + 2):
            gens = []
            if c < n:
                gens.append(stage1(c))
            if 0 <= c - 1 < n:
                gens.append(stage2(c - 1))
            if 0 <= c - 2 < n:
                gens.append(stage3(c - 2))
            interleave(*gens)
        db_ref[...] = jnp.sum(db[0], axis=0, keepdims=True)
        gdn[slot] = dot(hs[...], g_ref[...], TN).astype(BF16)
        gup[slot] = dot(mt[...], dus[...]).astype(BF16)
        for t in range(count):
            store_one(f, slot, t)


        @pl.when(f == steps - 1)
        def _():
            whole_wait(wup.at[1 - slot], wsem.at[0, 1 - slot])
            whole_wait(wdn.at[1 - slot], wsem.at[1, 1 - slot])
            for sl in range(2):
                whole_wait(gup.at[sl], gsem.at[0, sl])
                whole_wait(gdn.at[sl], gsem.at[1, sl])

    full = pl.BlockSpec((rows, D), lambda f, *_: (0, 0))
    bias = pl.BlockSpec((1, FB), lambda f, *_: (0, f))
    return pl.pallas_call(
        kernel,
        grid_spec=pltpu.PrefetchScalarGridSpec(
            num_scalar_prefetch=2,
            grid=(steps,),
            in_specs=[ANY, full, full, bias],
            out_specs=[full, full, bias, ANY],
            scratch_shapes=[
                pltpu.VMEM((D, rows), BF16),
                pltpu.VMEM((2, D, FB), BF16),
                pltpu.VMEM((2, FB, D), BF16),
                pltpu.VMEM((rows, FB), BF16),
                pltpu.VMEM((rows, FB), BF16),
                pltpu.VMEM((2, D, FB), BF16),
                pltpu.VMEM((2, FB, D), BF16),
                pltpu.VMEM((2, ROWB, FB), F32),
                pltpu.VMEM((2, ROWB, FB), F32),
                pltpu.SemaphoreType.DMA((2, 2)),
                pltpu.SemaphoreType.DMA((2, 2)),
            ],
        ),
        out_shape=[
            jax.ShapeDtypeStruct((rows, D), F32),
            jax.ShapeDtypeStruct((rows, D), F32),
            jax.ShapeDtypeStruct((1, FF), F32),
            jax.ShapeDtypeStruct((TILES * BLK, BLK), BF16),
        ],
        compiler_params=params(dimension_semantics=("arbitrary",)),
        cost_estimate=pl.CostEstimate(flops=52 << 30, bytes_accessed=48 << 20, transcendentals=8 << 20),
        name="feed_forward",
    )(w_rows, g_rows, w_all, m, cotangent, b_up)


def finish(w_rows, w_all, tokens, cotangent, smalls, attn_out, mlp_out, dm, dq, dk, dv, halo, tables):
    rows = tokens.shape[0]
    steps = rows // ROWB
    cos_t, fwd_t, back_t = tables

    def kernel(
        w_rows_ref, w_ref, tok_ref, g_ref, small_ref, o_ref, mlp_ref, dm_ref, dq_ref, dk_ref, dv_ref, halo_ref,
        cos_ref, fwd_ref, back_ref,
        out_ref, dx_ref, dp_ref, a_ref, sum_ref, wqkv, wo, sems,
    ):
        i = pl.program_id(0)

        @pl.when(i == 0)
        def _():
            def body(t):
                src = w_ref.at[pl.ds(pl.multiple_of(w_rows_ref[OUT_BASE + t], 16), BLK)]
                dst = wo.at[pl.ds(pl.multiple_of((t // 8) * BLK, BLK), BLK), pl.ds(pl.multiple_of((t % 8) * BLK, BLK), BLK)]
                pltpu.make_async_copy(src, dst, sems.at[0]).start()

            tile_loop(0, 64, body)

            def body(t):
                src = w_ref.at[pl.ds(pl.multiple_of(w_rows_ref[t], 16), BLK)]
                dst = wqkv.at[pl.ds(pl.multiple_of((t // 24) * BLK, BLK), BLK), pl.ds(pl.multiple_of((t % 24) * BLK, BLK), BLK)]
                pltpu.make_async_copy(src, dst, sems.at[1]).start()

            tile_loop(0, 192, body)
            pltpu.make_async_copy(wo, wo, sems.at[0]).wait()
            sum_ref[...] = jnp.zeros_like(sum_ref)

        x = tok_ref[...].astype(F32)
        grad = g_ref[...].astype(F32)
        normed, inv = norm_rows(x)
        g1, g2 = small_ref[4:5, :], small_ref[6:7, :]
        a_ref[...] = (normed * g1 + small_ref[5:6, :]).astype(BF16)
        attn = dot(o_ref[...], wo[...]) + small_ref[2:3, :]
        out_ref[...] = (x + attn + (mlp_ref[...] + small_ref[3:4, :])).astype(BF16)
        dk_all = dk_ref[...] + halo_ref[0].astype(F32)
        dk_all = rope_rows(dk_all, cos_ref[...], -fwd_ref[...], -back_ref[...])
        dv_all = dv_ref[...] + halo_ref[1].astype(F32)
        dq_low = dq_ref[...]
        dv_low = dv_all.astype(BF16)
        dp_ref[:, :D] = dq_low
        dp_ref[:, D : 2 * D] = dk_all.astype(BF16)
        dp_ref[:, 2 * D :] = dv_low

        @pl.when(i == 0)
        def _():
            pltpu.make_async_copy(wqkv, wqkv, sems.at[1]).wait()

        da = dot(dp_ref[...], wqkv[...], NT)
        dmv = dm_ref[...]
        dn = da * g1 + dmv * g2
        mean_dn = jnp.mean(dn, axis=-1, keepdims=True)
        mean_dnn = jnp.mean(dn * normed, axis=-1, keepdims=True)
        dx_ref[...] = grad + inv * (dn - mean_dn - normed * mean_dnn)

        def add(row, value):
            sum_ref[row : row + 1, :] += jnp.sum(value, axis=0, keepdims=True)

        add(0, dq_low.astype(F32))
        add(1, dv_low.astype(F32))
        add(2, grad)
        add(3, da * normed)
        add(4, da)
        add(5, dmv * normed)
        add(6, dmv)

    here = lambda i, *_: (i, 0)
    later = lambda i, *_: (i + steps, 0)
    block = pl.BlockSpec((ROWB, D), here)
    table = pl.BlockSpec((ROWB, BLK), later)
    return pl.pallas_call(
        kernel,
        grid_spec=pltpu.PrefetchScalarGridSpec(
            num_scalar_prefetch=1,
            grid=(steps,),
            in_specs=[
                ANY, block, block, pl.BlockSpec((16, D), lambda i, *_: (0, 0)),
                block, block, block, block, block, block,
                pl.BlockSpec((2, ROWB, D), lambda i, *_: (0, i, 0)), table, table, table,
            ],
            out_specs=[
                block, block, pl.BlockSpec((ROWB, 3 * D), here), block,
                pl.BlockSpec((8, D), lambda i, *_: (0, 0)),
            ],
            scratch_shapes=[
                pltpu.VMEM((D, 3 * D), BF16),
                pltpu.VMEM((D, D), BF16),
                pltpu.SemaphoreType.DMA((2,)),
            ],
        ),
        out_shape=[
            jax.ShapeDtypeStruct((rows, D), BF16),
            jax.ShapeDtypeStruct((rows, D), F32),
            jax.ShapeDtypeStruct((rows, 3 * D), BF16),
            jax.ShapeDtypeStruct((rows, D), BF16),
            jax.ShapeDtypeStruct((8, D), F32),
        ],
        compiler_params=params(dimension_semantics=("arbitrary",)),
        name="finish",
    )(w_rows, w_all, tokens, cotangent, smalls, attn_out, mlp_out, dm, dq, dk, dv, halo, cos_t, fwd_t, back_t)


def attention_weight_grads(g_rows, grads, attn_in, d_proj, attn_out, cotangent):
    rows = attn_in.shape[0]
    steps = 4 * D // FB

    def kernel(g_rows_ref, a_ref, dp_ref, o_ref, g_ref, _, gr_ref, at, ot, stage, sem):
        i = pl.program_id(0)
        slot = i % 2
        per = FB // BLK

        @pl.when(i == 0)
        def _():
            at[...] = a_ref[...].T

        @pl.when(i == 3 * D // FB)
        def _():
            ot[...] = o_ref[...].T

        @pl.when(i >= 2)
        def _():
            pltpu.make_async_copy(stage.at[slot], stage.at[slot], sem.at[slot]).wait()

        def piece(buf, t):
            return buf.at[pl.ds(pl.multiple_of((t // per) * BLK, BLK), BLK), pl.ds(pl.multiple_of((t % per) * BLK, BLK), BLK)]

        @pl.when(i < 3 * D // FB)
        def _():
            stage[slot] = dot(at[...], dp_ref[...]).astype(BF16)

            def body(t):
                tile = (t // per) * 24 + i * per + t % per
                dst = gr_ref.at[pl.ds(pl.multiple_of(g_rows_ref[tile], 16), BLK)]
                pltpu.make_async_copy(piece(stage.at[slot], t), dst, sem.at[slot]).start()

            tile_loop(0, 8 * per, body)

        @pl.when(i >= 3 * D // FB)
        def _():
            stage[slot] = dot(ot[...], g_ref[...]).astype(BF16)

            def body(t):
                tile = OUT_BASE + (t // per) * 8 + (i - 3 * D // FB) * per + t % per
                dst = gr_ref.at[pl.ds(pl.multiple_of(g_rows_ref[tile], 16), BLK)]
                pltpu.make_async_copy(piece(stage.at[slot], t), dst, sem.at[slot]).start()

            tile_loop(0, 8 * per, body)

        @pl.when(i == steps - 1)
        def _():
            for sl in range(2):
                pltpu.make_async_copy(stage.at[sl], stage.at[sl], sem.at[sl]).wait()

    full = pl.BlockSpec((rows, D), lambda i, *_: (0, 0))
    last = 3 * D // FB - 1
    return pl.pallas_call(
        kernel,
        grid_spec=pltpu.PrefetchScalarGridSpec(
            num_scalar_prefetch=1,
            grid=(steps,),
            in_specs=[
                full,
                pl.BlockSpec((rows, FB), lambda i, *_: (0, jnp.minimum(i, last))),
                full,
                pl.BlockSpec((rows, FB), lambda i, *_: (0, jnp.maximum(i - last - 1, 0))),
                ANY,
            ],
            out_specs=ANY,
            scratch_shapes=[
                pltpu.VMEM((D, rows), BF16),
                pltpu.VMEM((D, rows), BF16),
                pltpu.VMEM((2, D, FB), BF16),
                pltpu.SemaphoreType.DMA((2,)),
            ],
        ),
        out_shape=jax.ShapeDtypeStruct(grads.shape, BF16),
        input_output_aliases={5: 0},
        compiler_params=params(dimension_semantics=("arbitrary",)),
        name="attention_weight_grads",
    )(g_rows, attn_in, d_proj, attn_out, cotangent, grads)


def update_tiles(grads, tiles, left, right, first, second, scale):
    count = tiles.shape[0]
    group = max(g for g in (1, 2, 3, 4) if count % g == 0)

    def kernel(g_ref, w_ref, l_ref, r_ref, m_ref, v_ref, s_ref, w_out, low_out, m_out, v_out):
        for t in range(group):
            l, r = l_ref[t], r_ref[t]
            turned = dot(dot(l, g_ref[t], TN, HIGH), r, NN, HIGH)
            m_new = BETA * m_ref[t] + (1.0 - BETA) * turned
            v_new = BETA * v_ref[t] + (1.0 - BETA) * turned * turned
            ratio = m_new / (jnp.sqrt(v_new) + ADAM_EPS)
            back = dot(dot(l, ratio, NN, HIGH), r, NT, HIGH)
            w_new = (w_ref[t] - LEARN * back) * s_ref[t]
            w_out[t] = w_new
            low_out[t] = w_new.astype(BF16)
            m_out[t] = m_new
            v_out[t] = v_new

    block = pl.BlockSpec((group, BLK, BLK), lambda i: (i, 0, 0))
    row = pl.BlockSpec((group, 1, BLK), lambda i: (i, 0, 0))
    like = lambda t: jax.ShapeDtypeStruct(tiles.shape, t)
    return pl.pallas_call(
        kernel,
        grid=(count // group,),
        in_specs=[block] * 6 + [row],
        out_specs=[block] * 4,
        out_shape=[like(F32), like(BF16), like(F32), like(F32)],
        compiler_params=params(dimension_semantics=("arbitrary",)),
        name="update_tiles",
    )(grads, tiles, left, right, first, second, scale)


def column_scales(tile_ids, factors):
    columns = (tile_ids % (3 * D // BLK))[:, None] * BLK + jnp.arange(BLK, dtype=jnp.int32)[None, :]
    head_index = columns % D // HEAD
    root_factor = jnp.sqrt(factors)
    picked = jnp.sum(
        jnp.where(head_index[..., None] == jnp.arange(HEADS, dtype=jnp.int32), root_factor, 0.0),
        axis=-1,
    )
    clipped = (tile_ids[:, None] < QKV_TILES) & (columns < 2 * D)
    return jnp.where(clipped, picked, 1.0)


def small_update(grads, params_, first_moment, second_moment):
    first_new = BETA * first_moment + (1.0 - BETA) * grads
    second_new = BETA * second_moment + (1.0 - BETA) * grads * grads
    updated = params_ - SMALL_LEARN * first_new / (jnp.sqrt(second_new) + ADAM_EPS)
    return (updated, first_new, second_new)


def passed_along(value, axis, steps):
    count = lax.axis_size(axis)
    leading, last = (max(0, -steps), min(count, count - steps))
    return lax.ppermute(value, axis, [(source, source + steps) for source in range(leading, last)])


def on_device(
    ring,
    tokens,
    segments,
    cotangent,
    tile_of_slot,
    tiles,
    left_bases,
    right_bases,
    first_moments,
    second_moments,
    small_params,
    small_first,
    small_second,
    threshold,
):
    rows = tokens.shape[0]
    slot_count = tiles.shape[0]
    small_count = small_params.shape[0]
    axes = ("dp", "seq")
    seq_index = lax.axis_index("seq")
    owner_index = lax.axis_index(axes)
    first_place = seq_index * rows
    seg_local = segments.reshape(1, rows)

    numbers = jnp.arange(TILES, dtype=jnp.int32)
    slot_of_tile = jnp.sum(
        jnp.where(tile_of_slot[None, :] == numbers[:, None], numbers[None, :], 0), axis=1
    ).astype(jnp.int32)
    g_rows = slot_of_tile * BLK

    if ring:
        small_block = jnp.zeros((16 * BLK,), BF16).at[:small_count].set(small_params.astype(BF16))
        payload = jnp.concatenate(
            [tiles.astype(BF16).reshape(slot_count * BLK, BLK), small_block.reshape(16, BLK)], axis=0
        )
        seg_rows = jnp.broadcast_to(seg_local, (8, rows))
        gathered, prev_tokens, prev_seg = gather_weights(payload, tokens, seg_rows)
        stride = payload.shape[0]
        w_all = gathered.reshape(-1, BLK)
        w_rows = slot_of_tile // slot_count * stride + slot_of_tile % slot_count * BLK
        tail = slot_count * BLK
        small_all = gathered[:, tail : tail + small_count // BLK, :].reshape(SMALL)
        prev_seg = prev_seg[:1]
    else:
        w_all = lax.all_gather(tiles.astype(BF16), axes, axis=0, tiled=True).reshape(-1, BLK)
        w_rows = g_rows
        small_all = lax.all_gather(small_params.astype(BF16), axes, axis=0, tiled=True)
        prev_tokens, prev_seg = passed_along((tokens, seg_local), "seq", 1)

    table = small_all.astype(F32).reshape(D, 12)
    smalls = jnp.concatenate(
        [
            jnp.stack([table[:, r] for r in (0, 1, 2, 7, 8, 9, 10, 11)], axis=0),
            jnp.zeros((8, D), F32),
        ],
        axis=0,
    )
    b_up = table[:, 3:7].reshape(1, FF)

    half = ROT // 2
    exponent = jnp.arange(half, dtype=F32) * (2.0 / ROT)
    frequency = jnp.power(ROPE_BASE, -exponent)
    places = first_place - rows + jnp.arange(2 * rows, dtype=jnp.int32)
    angle = places.astype(F32)[None, :] * frequency[:, None]
    cos8, sin8 = jnp.cos(angle), jnp.sin(angle)
    cos_c, sin_c = cos8.T, sin8.T
    ones = jnp.ones((2 * rows, HEAD - ROT), F32)
    none = jnp.zeros((2 * rows, half), F32)
    rest = jnp.zeros((2 * rows, HEAD - ROT), F32)
    cos_t = jnp.concatenate([cos_c, cos_c, ones] * 2, axis=1)
    fwd_t = jnp.concatenate([-sin_c, none, rest] * 2, axis=1)
    back_t = jnp.concatenate([none, sin_c, rest] * 2, axis=1)
    tables = (cos_t, fwd_t, back_t)

    prev_seg = jnp.where(seq_index == 0, -1, prev_seg)
    seg_k = jnp.concatenate([prev_seg, seg_local], axis=1).reshape(2 * rows, 1)

    q, k, v, d_out, m = project(w_rows, w_all, prev_tokens, tokens, cotangent, smalls, tables)
    attn_out, dq, dk, dv, halo, peaks = attend(
        q, k, v, d_out, seg_local, seg_k, cos8[:, rows:], sin8[:, rows:]
    )
    halo = passed_along(halo, "seq", -1)
    mlp_out, dm, db_up, grads = feed_forward(w_rows, g_rows, w_all, m, cotangent, b_up)
    block_output, input_grad, d_proj, attn_in, sums = finish(
        w_rows, w_all, tokens, cotangent, smalls, attn_out, mlp_out, dm, dq, dk, dv, halo, tables
    )
    grads = attention_weight_grads(g_rows, grads, attn_in, d_proj, attn_out, cotangent)

    small_terms = jnp.concatenate(
        [
            sums[:3].T,
            db_up.reshape(D, FF // D),
            sums[2:7].T,
        ],
        axis=1,
    ).reshape(SMALL)
    head_peak = jnp.max(peaks.reshape(HEADS // 2, 8, 2, QB)[:, 0], axis=-1).reshape(HEADS)
    if ring:
        peak_rows = jnp.zeros((8, BLK), F32).at[:, :HEADS].set(head_peak[None, :])
        extra = jnp.concatenate([small_terms.reshape(SMALL_ROWS, BLK), peak_rows], axis=0)
        tile_grads, extra = sum_gradients(grads, extra)
        tile_grads = tile_grads.reshape(slot_count, BLK, BLK)
        small_grads = lax.dynamic_slice_in_dim(
            extra[:SMALL_ROWS].reshape(SMALL), owner_index * small_count, small_count, 0
        )
        head_peak = extra[SMALL_ROWS, :HEADS]
    else:
        tile_grads = lax.psum_scatter(
            grads.astype(F32).reshape(TILES, BLK, BLK), axes, scatter_dimension=0, tiled=True
        )
        small_grads = lax.psum_scatter(small_terms, axes, scatter_dimension=0, tiled=True)
        head_peak = lax.pmax(head_peak, axes)

    local_ids = lax.dynamic_slice_in_dim(tile_of_slot, owner_index * slot_count, slot_count, 0)
    limit = threshold[0]
    factors = limit / jnp.maximum(head_peak, limit)
    scale = column_scales(local_ids, factors).reshape(slot_count, 1, BLK)
    new_tiles, new_low, new_first, new_second = update_tiles(
        tile_grads, tiles, left_bases, right_bases, first_moments, second_moments, scale
    )
    new_small, new_small_first, new_small_second = small_update(
        small_grads, small_params, small_first, small_second
    )
    return (
        block_output,
        input_grad,
        tile_grads,
        small_grads,
        new_tiles,
        new_low,
        new_first,
        new_second,
        new_small,
        new_small.astype(BF16),
        new_small_first,
        new_small_second,
        factors,
    )


def solution(mesh):
    split = P(("dp", "seq"))
    in_specs = (split, P("dp", "seq"), split, P()) + (split,) * 8 + (P(),)
    out_specs = (split,) * 12 + (P(),)
    ring = (mesh.shape["dp"], mesh.shape["seq"]) == (4, 8)
    return jax.shard_map(
        functools.partial(on_device, ring), mesh=mesh, in_specs=in_specs, out_specs=out_specs, check_vma=False
    )
```

```python
import functools

import jax
import jax.numpy as jnp
from jax import lax
from jax.experimental import pallas as pl
from jax.experimental.pallas import tpu as pltpu
from jax.sharding import PartitionSpec as P

D = 1024
FF = 4096
HEADS = 16
HEAD = 64
ROT = 16
BLK = 128
WINDOW = 1024
TILES = 768
SMALL = 12288
QKV_TILES = D // BLK * (3 * D // BLK)
OUT_TILES = D // BLK * (D // BLK)
UP_TILES = D // BLK * (FF // BLK)
OUT_BASE = QKV_TILES
UP_BASE = QKV_TILES + OUT_TILES
DOWN_BASE = UP_BASE + UP_TILES

NORM_EPS = 1e-05
ADAM_EPS = 1e-08
BETA = 0.5
LEARN = 0.03
SMALL_LEARN = 0.2
ROPE_BASE = 10000.0
MASKED = -1e30
HIGH = lax.Precision.HIGHEST

F32 = jnp.float32
BF16 = jnp.bfloat16
MESH = pl.DeviceIdType.MESH
ANY = pl.BlockSpec(memory_space=pl.ANY)
VMEM = pl.BlockSpec(memory_space=pltpu.VMEM)
VMEM_LIMIT = 58 << 20

NN = (((1,), (0,)), ((), ()))
NT = (((1,), (1,)), ((), ()))
TN = (((0,), (0,)), ((), ()))


def dot(a, b, dims=NN, precision=None):
    return lax.dot_general(a, b, dims, precision=precision, preferred_element_type=F32)


def interleave(*parts):
    live = list(parts)
    while live:
        for part in list(live):
            try:
                next(part)
            except StopIteration:
                live.remove(part)


def params(**kw):
    return pltpu.CompilerParams(vmem_limit_bytes=VMEM_LIMIT, **kw)


def norm_rows(x):
    centered = x - jnp.mean(x, axis=-1, keepdims=True)
    inv = lax.rsqrt(jnp.mean(centered * centered, axis=-1, keepdims=True) + NORM_EPS)
    return centered * inv, inv


def tile_loop(first, count, body):
    def step(t, carry):
        body(t)
        return carry

    lax.fori_loop(first, first + count, step, 0)


ROWS_PER_TILE = BLK
HALF_ROWS = 1536


def gather_weights(payload, tokens, seg_rows):
    rows = payload.shape[0]
    top = pl.ds(0, HALF_ROWS)
    low = pl.ds(HALF_ROWS, rows - HALF_ROWS)

    def kernel(x_ref, tok_ref, seg_ref, out_ref, ptok_ref, pseg_ref, lsem, ss, rs, hss, hrs, hls):
        d = lax.axis_index("dp")
        s = lax.axis_index("seq")
        z = s // 2
        c = s % 2
        xn = d + 1 - 2 * (d % 2)
        yn = d + 2 - 4 * (d // 2)
        xyn = 3 - d
        sib = z * 2 + 1 - c
        halo = s - 1 + 2 * c
        halo_ok = ((c == 0) & (z > 0)) | ((c == 1) & (z < 3))

        barrier = pltpu.get_barrier_semaphore()

        def greet(dev):
            pl.semaphore_signal(barrier, inc=1, device_id=dev, device_id_type=MESH)

        greet((d, sib))
        greet((xn, s))
        greet((yn, s))

        @pl.when(z > 0)
        def _():
            greet((d, s - 2))

        @pl.when(z < 3)
        def _():
            greet((d, s + 2))

        @pl.when(halo_ok)
        def _():
            greet((d, halo))

        below, above = (z + 2) // 3, (5 - z) // 3
        pl.semaphore_wait(barrier, 3 + below + above + (1 - c) * below + c * above)

        def place(dd, zz):
            return out_ref.at[dd * 8 + zz * 2 + c]

        def remote(src, dst, kind, zz, dev):
            return pltpu.make_async_remote_copy(
                src_ref=src,
                dst_ref=dst,
                send_sem=ss.at[kind, zz],
                recv_sem=rs.at[kind, zz],
                device_id=dev,
                device_id_type=MESH,
            )

        def block_of(zz, own):
            return x_ref if own else place(d, zz)

        def up(zz, own):
            return remote(block_of(zz, own), place(d, zz), 0, zz, (d, s + 2))

        def down(zz, own):
            return remote(block_of(zz, own), place(d, zz), 1, zz, (d, s - 2))

        def to_x(zz, own):
            return remote(block_of(zz, own), place(d, zz), 2, zz, (xn, s))

        def to_y(zz, own):
            return remote(block_of(zz, own), place(d, zz), 3, zz, (yn, s))

        def on_y(zz):
            return remote(place(xn, zz).at[top], place(xn, zz).at[top], 4, zz, (yn, s))

        def on_x(zz):
            return remote(place(yn, zz).at[low], place(yn, zz).at[low], 5, zz, (xn, s))

        def to_sib(dd, zz, kind, own=False):
            src = x_ref if own else place(dd, zz)
            return remote(src, place(dd, zz), kind, zz, (d, sib))

        def from_x(zz):
            return remote(x_ref, place(xn, zz), 2, zz, (xn, s))

        def from_y(zz):
            return remote(x_ref, place(yn, zz), 3, zz, (yn, s))

        def diag_up(zz):
            return remote(place(xyn, zz), place(xyn, zz), 10, zz, (d, s + 2))

        def diag_down(zz):
            return remote(place(xyn, zz), place(xyn, zz), 11, zz, (d, s - 2))

        def diag_top(zz):
            return remote(x_ref.at[top], place(xyn, zz).at[top], 4, zz, (yn, s))

        def diag_low(zz):
            return remote(x_ref.at[low], place(xyn, zz).at[low], 5, zz, (xn, s))

        order = [z, 1 + z % 2, (2 + 3 * z) % 5, 3 * (1 - z // 2)]
        local = pltpu.make_async_copy(x_ref, place(d, z), lsem)
        local.start()

        def halo_copies(dev):
            tok = pltpu.make_async_remote_copy(
                src_ref=tok_ref,
                dst_ref=ptok_ref,
                send_sem=hss.at[0],
                recv_sem=hrs.at[0],
                device_id=dev,
                device_id_type=MESH,
            )
            seg = pltpu.make_async_remote_copy(
                src_ref=seg_ref,
                dst_ref=pseg_ref,
                send_sem=hss.at[1],
                recv_sem=hrs.at[1],
                device_id=dev,
                device_id_type=MESH,
            )
            return tok, seg

        def in_plane(k, body):
            if k == 0:
                body()
            elif k == 3:
                pl.when((z == 0) | (z == 3))(body)

        def launch(k):
            zz = order[k]
            own = k == 0
            if own:

                @pl.when(z < 3)
                def _():
                    up(zz, True).start()

                @pl.when(z > 0)
                def _():
                    down(zz, True).start()
            else:

                @pl.when(zz < z)
                def _():
                    up(zz, False).wait_recv()

                @pl.when((zz < z) & (z < 3))
                def _():
                    up(zz, False).start()

                @pl.when(zz > z)
                def _():
                    down(zz, False).wait_recv()

                @pl.when((zz > z) & (z > 0))
                def _():
                    down(zz, False).start()

            to_x(zz, own).start()
            to_y(zz, own).start()
            to_sib(d, zz, 6, own).start()

        def second(k):
            zz = order[k]
            from_x(zz).wait_recv()
            in_plane(k, lambda: on_y(zz).start())
            to_sib(xn, zz, 7).start()
            from_y(zz).wait_recv()
            in_plane(k, lambda: on_x(zz).start())
            to_sib(yn, zz, 8).start()

        def third(k):
            zz = order[k]

            def arrive():
                diag_top(zz).wait_recv()
                diag_low(zz).wait_recv()

            in_plane(k, arrive)
            if k > 0:

                @pl.when((zz < z) & (z - zz <= 2))
                def _():
                    diag_up(zz).wait_recv()

                @pl.when((zz > z) & (zz - z <= 2))
                def _():
                    diag_down(zz).wait_recv()

            if k < 3:

                @pl.when((zz <= z) & (z - zz <= 1) & (z < 3))
                def _():
                    diag_up(zz).start()

                @pl.when((zz >= z) & (zz - z <= 1) & (z > 0))
                def _():
                    diag_down(zz).start()

            to_sib(xyn, zz, 9).start()

        launch(0)
        own_tok = pltpu.make_async_copy(tok_ref, ptok_ref, hls.at[0])
        own_seg = pltpu.make_async_copy(seg_ref, pseg_ref, hls.at[1])

        @pl.when(s < 7)
        def _():
            for cp in halo_copies((d, s + 1)):
                cp.start()

        @pl.when(s == 0)
        def _():
            own_tok.start()
            own_seg.start()

        launch(1)
        second(0)
        launch(2)
        second(1)
        third(0)
        launch(3)
        second(2)
        third(1)
        second(3)
        third(2)
        third(3)

        local.wait()
        other = 1 - c

        def sib_place(dd, zz):
            return out_ref.at[dd * 8 + zz * 2 + other]

        for k in range(4):
            zz = order[k]
            own = k == 0
            for kind, dd in ((6, d), (7, xn), (8, yn), (9, xyn)):
                remote(sib_place(dd, zz), sib_place(dd, zz), kind, zz, (d, sib)).wait_recv()
                to_sib(dd, zz, kind, own and kind == 6).wait_send()
            to_x(zz, own).wait_send()
            to_y(zz, own).wait_send()

            def halves_sent():
                on_y(zz).wait_send()
                on_x(zz).wait_send()

            in_plane(k, halves_sent)
            if k < 3:

                @pl.when((zz <= z) & (z - zz <= 1) & (z < 3))
                def _():
                    diag_up(zz).wait_send()

                @pl.when((zz >= z) & (zz - z <= 1) & (z > 0))
                def _():
                    diag_down(zz).wait_send()

            @pl.when((zz <= z) & (z < 3))
            def _():
                up(zz, own).wait_send()

            @pl.when((zz >= z) & (z > 0))
            def _():
                down(zz, own).wait_send()

        @pl.when(s < 7)
        def _():
            for cp in halo_copies((d, s + 1)):
                cp.wait_send()

        @pl.when(s > 0)
        def _():
            for cp in halo_copies((d, s - 1)):
                cp.wait_recv()

        @pl.when(s == 0)
        def _():
            own_tok.wait()
            own_seg.wait()

    return pl.pallas_call(
        kernel,
        out_shape=[
            jax.ShapeDtypeStruct((32, rows, BLK), BF16),
            jax.ShapeDtypeStruct(tokens.shape, BF16),
            jax.ShapeDtypeStruct(seg_rows.shape, jnp.int32),
        ],
        in_specs=[ANY, ANY, ANY],
        out_specs=[ANY, ANY, ANY],
        scratch_shapes=[
            pltpu.SemaphoreType.DMA,
            pltpu.SemaphoreType.DMA((12, 4)),
            pltpu.SemaphoreType.DMA((12, 4)),
            pltpu.SemaphoreType.DMA((2,)),
            pltpu.SemaphoreType.DMA((2,)),
            pltpu.SemaphoreType.DMA((2,)),
        ],
        compiler_params=params(collective_id=0, has_side_effects=True),
        name="gather_weights",
    )(payload, tokens, seg_rows)


OWNED = 24 * BLK
HALF = OWNED // 2
SMALL_ROWS = SMALL // BLK
EXTRA_ROWS = SMALL_ROWS + 8


def add_rows(dst, terms, rows, step=512):
    def body(i, carry):
        at = pl.ds(pl.multiple_of(i * step, step), step)
        if len(terms) == 2 and dst.dtype == BF16:
            dst[at] = terms[0][at] + terms[1][at]
        else:
            total = terms[0][at].astype(F32)
            for term in terms[1:]:
                total = total + term[at].astype(F32)
            dst[at] = total.astype(dst.dtype)
        return carry

    lax.fori_loop(0, rows // step, body, 0)


def sum_gradients(grads, extra):
    def kernel(g_ref, e_ref, out_ref, eout_ref, own, crecv, s1a, s1b, s2, zup, zdn, gup, gdn, epart, erecv, ls, ss, rs, zss, zrs, es, er):
        d = lax.axis_index("dp")
        s = lax.axis_index("seq")
        z = s // 2
        c = s % 2
        xn = d + 1 - 2 * (d % 2)
        yn = d + 2 - 4 * (d // 2)
        xyn = 3 - d
        sib = z * 2 + 1 - c
        zpair = s + 2 - 4 * (z % 2)
        zfar = s + 4 - 8 * (z // 2)
        top = pl.ds(0, HALF)
        low = pl.ds(HALF, HALF)

        barrier = pltpu.get_barrier_semaphore()

        def greet(dev):
            pl.semaphore_signal(barrier, inc=1, device_id=dev, device_id_type=MESH)

        greet((d, sib))
        greet((xn, s))
        greet((yn, s))
        greet((d, zfar))

        @pl.when(z > 0)
        def _():
            greet((d, s - 2))

        @pl.when(z < 3)
        def _():
            greet((d, s + 2))

        order = [3 * (1 - z // 2), (2 + 3 * z) % 5, 1 + z % 2, z]

        def owner_rows(dd, zz, cc):
            return g_ref.at[pl.ds(pl.multiple_of((dd * 8 + zz * 2 + cc) * OWNED, OWNED), OWNED)]

        def load(zz, dd):
            return pltpu.make_async_copy(owner_rows(dd, zz, c), own.at[zz, dd], ls.at[zz, dd])

        for k in range(4):
            for dd in range(4):
                load(order[k], dd).start()

        pl.semaphore_wait(barrier, 4 + (z + 2) // 3 + (5 - z) // 3)

        def remote(src, dst, ssem, rsem, dev):
            return pltpu.make_async_remote_copy(
                src_ref=src, dst_ref=dst, send_sem=ssem, recv_sem=rsem, device_id=dev, device_id_type=MESH
            )

        def core(zz, dd):
            return remote(owner_rows(dd, zz, 1 - c), crecv.at[zz, dd], ss.at[zz, dd], rs.at[zz, dd], (d, sib))

        def y_own(zz):
            return remote(own.at[zz, yn, top], s1a.at[zz, 0], ss.at[zz, 4], rs.at[zz, 4], (yn, s))

        def y_cross(zz):
            return remote(own.at[zz, xyn, top], s1a.at[zz, 1], ss.at[zz, 5], rs.at[zz, 5], (yn, s))

        def x_own(zz):
            return remote(own.at[zz, xn, low], s1b.at[zz, 0], ss.at[zz, 6], rs.at[zz, 6], (xn, s))

        def x_cross(zz):
            return remote(own.at[zz, xyn, low], s1b.at[zz, 1], ss.at[zz, 7], rs.at[zz, 7], (xn, s))

        def x_last(zz):
            return remote(own.at[zz, xn, top], s2.at[zz, top], ss.at[zz, 8], rs.at[zz, 8], (xn, s))

        def y_last(zz):
            return remote(own.at[zz, yn, low], s2.at[zz, low], ss.at[zz, 9], rs.at[zz, 9], (yn, s))

        def z_up(zz):
            return remote(own.at[zz, d], zup.at[zz], zss.at[0, zz], zrs.at[0, zz], (d, s + 2))

        def z_dn(zz):
            return remote(own.at[zz, d], zdn.at[zz], zss.at[1, zz], zrs.at[1, zz], (d, s - 2))

        def g_up(zz):
            return remote(own.at[zz, xyn], gup.at[zz], zss.at[2, zz], zrs.at[2, zz], (d, s + 2))

        def g_dn(zz):
            return remote(own.at[zz, xyn], gdn.at[zz], zss.at[3, zz], zrs.at[3, zz], (d, s - 2))

        ends = (z == 0) | (z == 3)
        inner = (z == 1) | (z == 2)

        def in_plane(k, body):
            if k == 3:
                body()
            elif k == 0:
                pl.when(ends)(body)

        def cross(zz):
            y_cross(zz).start()
            x_cross(zz).start()

        def along(zz, act):
            @pl.when(zz > z)
            def _():
                act(g_up(zz))

            @pl.when(zz < z)
            def _():
                act(g_dn(zz))

        def outward(k, act):
            zz = order[k]
            if k == 0:
                pl.when(inner)(lambda: along(zz, act))
            elif k < 3:
                along(zz, act)

        def diagonal(k):
            zz = order[k]
            mine = own.at[zz, xyn]
            if k < 3:

                @pl.when(inner)
                def _():
                    @pl.when(zz > z)
                    def _():
                        g_up(zz).wait_recv()
                        add_rows(mine, [mine, gup.at[zz]], OWNED)

                    @pl.when(zz < z)
                    def _():
                        g_dn(zz).wait_recv()
                        add_rows(mine, [mine, gdn.at[zz]], OWNED)

                    along(zz, lambda cp: cp.start())
            else:

                @pl.when(z > 0)
                def _():
                    g_up(zz).wait_recv()
                    add_rows(mine, [mine, gup.at[zz]], OWNED)

                @pl.when(z < 3)
                def _():
                    g_dn(zz).wait_recv()
                    add_rows(mine, [mine, gdn.at[zz]], OWNED)

                cross(zz)

        def extra_step(i, dev):
            return remote(epart.at[i], erecv.at[i], es.at[i], er.at[i], dev)

        extra_devs = [(d, sib), (xn, s), (yn, s), (d, zpair), (d, zfar)]

        def extra_add(i):
            extra_step(i, extra_devs[i]).wait_recv()
            a = epart[i]
            b = erecv[i]
            row = lax.broadcasted_iota(jnp.int32, a.shape, 0)
            total = jnp.where(row < SMALL_ROWS, a + b, jnp.maximum(a, b))
            if i < 4:
                epart[i + 1] = total
                extra_step(i + 1, extra_devs[i + 1]).start()
            else:
                eout_ref[...] = total

        def issue(k):
            for dd in (xyn, yn, xn, d):
                core(order[k], dd).start()

        issue(0)
        epart[0] = e_ref[...]
        extra_step(0, extra_devs[0]).start()

        def first(k):
            zz = order[k]
            if k < 3:
                issue(k + 1)

            def one(dd, start):
                load(zz, dd).wait()
                core(zz, dd).wait_recv()
                add_rows(own.at[zz, dd], [own.at[zz, dd], crecv.at[zz, dd]], OWNED)
                for cp in start:
                    cp.start()

            one(xyn, [])
            if k == 0:
                pl.when(ends)(lambda: cross(zz))
                outward(0, lambda cp: cp.start())
            elif k < 3:
                pl.when(ends)(lambda: along(zz, lambda cp: cp.start()))
            one(yn, [y_own(zz)])
            one(xn, [x_own(zz)])
            one(d, [])

        def second(k):
            zz = order[k]
            a = own.at[zz, xn, top]
            b = own.at[zz, yn, low]

            def crossed():
                y_cross(zz).wait_recv()
                add_rows(a, [a, s1a.at[zz, 1]], HALF)

            def crossed_low():
                x_cross(zz).wait_recv()
                add_rows(b, [b, s1b.at[zz, 1]], HALF)

            in_plane(k, crossed)
            x_last(zz).start()
            in_plane(k, crossed_low)
            y_last(zz).start()

        def third(k):
            zz = order[k]
            y_own(zz).wait_recv()
            x_own(zz).wait_recv()
            x_last(zz).wait_recv()
            y_last(zz).wait_recv()
            a = own.at[zz, d, top]
            b = own.at[zz, d, low]
            if k < 3:

                @pl.when((zz > z) & (z > 0))
                def _():
                    z_up(zz).wait_recv()
                    add_rows(a, [a, s1a.at[zz, 0], s2.at[zz, top], zup.at[zz, top]], HALF)
                    add_rows(b, [b, s1b.at[zz, 0], s2.at[zz, low], zup.at[zz, low]], HALF)

                @pl.when((zz < z) & (z < 3))
                def _():
                    z_dn(zz).wait_recv()
                    add_rows(a, [a, s1a.at[zz, 0], s2.at[zz, top], zdn.at[zz, top]], HALF)
                    add_rows(b, [b, s1b.at[zz, 0], s2.at[zz, low], zdn.at[zz, low]], HALF)

                @pl.when(((zz > z) & (z == 0)) | ((zz < z) & (z == 3)))
                def _():
                    add_rows(a, [a, s1a.at[zz, 0], s2.at[zz, top]], HALF)
                    add_rows(b, [b, s1b.at[zz, 0], s2.at[zz, low]], HALF)

                @pl.when(zz > z)
                def _():
                    z_up(zz).start()

                @pl.when(zz < z)
                def _():
                    z_dn(zz).start()
            else:

                @pl.when(z > 0)
                def _():
                    z_up(zz).wait_recv()

                @pl.when(z < 3)
                def _():
                    z_dn(zz).wait_recv()

                o_top = out_ref.at[top]
                o_low = out_ref.at[low]

                @pl.when((z > 0) & (z < 3))
                def _():
                    add_rows(o_top, [a, s1a.at[zz, 0], s2.at[zz, top], zup.at[zz, top], zdn.at[zz, top]], HALF)
                    add_rows(o_low, [b, s1b.at[zz, 0], s2.at[zz, low], zup.at[zz, low], zdn.at[zz, low]], HALF)

                @pl.when(z == 0)
                def _():
                    add_rows(o_top, [a, s1a.at[zz, 0], s2.at[zz, top], zdn.at[zz, top]], HALF)
                    add_rows(o_low, [b, s1b.at[zz, 0], s2.at[zz, low], zdn.at[zz, low]], HALF)

                @pl.when(z == 3)
                def _():
                    add_rows(o_top, [a, s1a.at[zz, 0], s2.at[zz, top], zup.at[zz, top]], HALF)
                    add_rows(o_low, [b, s1b.at[zz, 0], s2.at[zz, low], zup.at[zz, low]], HALF)

        first(0)
        first(1)
        extra_add(0)
        second(0)
        diagonal(1)
        first(2)
        second(1)
        extra_add(1)
        first(3)
        diagonal(2)
        second(2)
        third(0)
        extra_add(2)
        diagonal(3)
        extra_add(3)
        third(1)
        extra_add(4)
        third(2)
        second(3)
        third(3)

        for i in range(5):
            extra_step(i, extra_devs[i]).wait_send()
        for k in range(4):
            zz = order[k]
            for dd in range(4):
                core(zz, dd).wait_send()
            for cp in (y_own(zz), x_own(zz), x_last(zz), y_last(zz)):
                cp.wait_send()

            def crosses_sent():
                y_cross(zz).wait_send()
                x_cross(zz).wait_send()

            in_plane(k, crosses_sent)
            outward(k, lambda cp: cp.wait_send())
            if k < 3:

                @pl.when(zz > z)
                def _():
                    z_up(zz).wait_send()

                @pl.when(zz < z)
                def _():
                    z_dn(zz).wait_send()

    return pl.pallas_call(
        kernel,
        out_shape=[
            jax.ShapeDtypeStruct((OWNED, BLK), F32),
            jax.ShapeDtypeStruct((EXTRA_ROWS, BLK), F32),
        ],
        in_specs=[ANY, VMEM],
        out_specs=[VMEM, VMEM],
        scratch_shapes=[
            pltpu.VMEM((4, 4, OWNED, BLK), BF16),
            pltpu.VMEM((4, 4, OWNED, BLK), BF16),
            pltpu.VMEM((4, 2, HALF, BLK), BF16),
            pltpu.VMEM((4, 2, HALF, BLK), BF16),
            pltpu.VMEM((4, OWNED, BLK), BF16),
            pltpu.VMEM((4, OWNED, BLK), BF16),
            pltpu.VMEM((4, OWNED, BLK), BF16),
            pltpu.VMEM((4, OWNED, BLK), BF16),
            pltpu.VMEM((4, OWNED, BLK), BF16),
            pltpu.VMEM((5, EXTRA_ROWS, BLK), F32),
            pltpu.VMEM((5, EXTRA_ROWS, BLK), F32),
            pltpu.SemaphoreType.DMA((4, 4)),
            pltpu.SemaphoreType.DMA((4, 10)),
            pltpu.SemaphoreType.DMA((4, 10)),
            pltpu.SemaphoreType.DMA((4, 4)),
            pltpu.SemaphoreType.DMA((4, 4)),
            pltpu.SemaphoreType.DMA((5,)),
            pltpu.SemaphoreType.DMA((5,)),
        ],
        compiler_params=params(collective_id=1, has_side_effects=True),
        name="sum_gradients",
    )(grads, extra)


ROWB = 256


def rope_rows(value, cos_t, fwd_t, back_t):
    pieces = []
    for j in range(value.shape[1] // BLK):
        p = value[:, j * BLK : (j + 1) * BLK]
        pieces.append(
            p * cos_t + pltpu.roll(p, BLK - ROT // 2, 1) * fwd_t + pltpu.roll(p, ROT // 2, 1) * back_t
        )
    return jnp.concatenate(pieces, axis=1)


def spread_tables(cos8, sin8):
    none = jnp.zeros_like(cos8)
    rest = (HEAD - ROT) // none.shape[0]
    cos_t = [cos8, cos8] + [none + 1.0] * rest
    fwd_t = [-sin8, none] + [none] * rest
    back_t = [none, sin8] + [none] * rest
    return [jnp.concatenate(t * 2, axis=0).T for t in (cos_t, fwd_t, back_t)]


def project(w_rows, w_all, prev_tokens, tokens, cotangent, smalls, tables):
    rows = tokens.shape[0]
    steps = rows // ROWB
    cos8, sin8 = tables

    def kernel(
        w_rows_ref, w_ref, prev_ref, tok_ref, g_ref, small_ref, cos_ref, sin_ref,
        q_ref, k_ref, v_ref, do_ref, m_ref, wqkv, wo, sems,
    ):
        i = pl.program_id(0)

        def third_copy(third):
            def body(t):
                r, cc = t // 8, t % 8
                src = w_ref.at[pl.ds(pl.multiple_of(w_rows_ref[r * 24 + third * 8 + cc], 16), BLK)]
                dst = wqkv.at[pl.ds(pl.multiple_of(r * BLK, BLK), BLK), pl.ds(pl.multiple_of(third * D + cc * BLK, BLK), BLK)]
                pltpu.make_async_copy(src, dst, sems.at[third]).start()

            tile_loop(0, 64, body)

        def third_wait(third):
            part = wqkv.at[:, pl.ds(third * D, D)]
            pltpu.make_async_copy(part, part, sems.at[third]).wait()

        @pl.when(i == 0)
        def _():
            third_copy(1)
            third_copy(2)
            third_copy(0)

            def body(t):
                r, cc = t // 8, t % 8
                src = w_ref.at[pl.ds(pl.multiple_of(w_rows_ref[OUT_BASE + t], 16), BLK)]
                dst = wo.at[pl.ds(pl.multiple_of(r * BLK, BLK), BLK), pl.ds(pl.multiple_of(cc * BLK, BLK), BLK)]
                pltpu.make_async_copy(src, dst, sems.at[3]).start()

            tile_loop(0, 64, body)
            third_wait(1)
            third_wait(2)

        @pl.when(i == steps)
        def _():
            third_wait(0)
            pltpu.make_async_copy(wo, wo, sems.at[3]).wait()

        spread = spread_tables(cos_ref[...], sin_ref[...])

        def keys(x):
            normed, _ = norm_rows(x)
            attn_in = (normed * small_ref[4:5, :] + small_ref[5:6, :]).astype(BF16)
            k = dot(attn_in, wqkv[:, D : 2 * D])
            v = dot(attn_in, wqkv[:, 2 * D :]) + small_ref[1:2, :]
            k_ref[...] = rope_rows(k, *spread).astype(BF16)
            v_ref[...] = v.astype(BF16)
            return normed, attn_in

        @pl.when(i < steps)
        def _():
            keys(prev_ref[...].astype(F32))

        @pl.when(i >= steps)
        def _():
            normed, attn_in = keys(tok_ref[...].astype(F32))
            m_ref[...] = (normed * small_ref[6:7, :] + small_ref[7:8, :]).astype(BF16)
            q = dot(attn_in, wqkv[:, :D]) + small_ref[0:1, :]
            q = rope_rows(q, *spread)
            q_ref[...] = q.astype(BF16)
            do_ref[...] = dot(g_ref[...], wo[...], NT).astype(BF16)

    own = lambda i, *_: (jnp.maximum(i - steps, 0), 0)
    prev = lambda i, *_: (jnp.minimum(i, steps - 1), 0)
    here = lambda i, *_: (i, 0)
    block = lambda m: pl.BlockSpec((ROWB, D), m)
    table = pl.BlockSpec((ROT // 2, ROWB), lambda i, *_: (0, i))
    return pl.pallas_call(
        kernel,
        grid_spec=pltpu.PrefetchScalarGridSpec(
            num_scalar_prefetch=1,
            grid=(2 * steps,),
            in_specs=[
                ANY, block(prev), block(own), block(own),
                pl.BlockSpec((16, D), lambda i, *_: (0, 0)), table, table,
            ],
            out_specs=[block(own), block(here), block(here), block(own), block(own)],
            scratch_shapes=[
                pltpu.VMEM((D, 3 * D), BF16),
                pltpu.VMEM((D, D), BF16),
                pltpu.SemaphoreType.DMA((4,)),
            ],
        ),
        out_shape=[
            jax.ShapeDtypeStruct((rows, D), BF16),
            jax.ShapeDtypeStruct((2 * rows, D), BF16),
            jax.ShapeDtypeStruct((2 * rows, D), BF16),
            jax.ShapeDtypeStruct((rows, D), BF16),
            jax.ShapeDtypeStruct((rows, D), BF16),
        ],
        compiler_params=params(dimension_semantics=("arbitrary",)),
        name="project",
    )(w_rows, w_all, prev_tokens, tokens, cotangent, smalls, cos8, sin8)


QB = 256
SPAN = WINDOW + QB


CHUNK = 256
SAFE_SCORE = 60.0


def attend(q, k, v, d_out, seg_q, seg_k, cos8, sin8):
    rows = q.shape[0]
    blocks = rows // QB
    pairs = HEADS // 2
    scale = HEAD ** (-0.5)
    half = ROT // 2
    n = SPAN // CHUNK

    def heads_apart(x):
        row = lax.broadcasted_iota(jnp.int32, x.shape, 0)
        zero = jnp.zeros_like(x)
        return jnp.concatenate([jnp.where(row < HEAD, x, zero), jnp.where(row < HEAD, zero, x)], axis=1)

    def stacked(x):
        lane = lax.broadcasted_iota(jnp.int32, x.shape, 1)
        zero = jnp.zeros_like(x)
        return jnp.concatenate([jnp.where(lane < HEAD, x, zero), jnp.where(lane < HEAD, zero, x)], axis=0)

    def fold(x, op):
        return op(x.reshape(x.shape[0] // 8, 8, x.shape[1]), axis=0)

    def two(x):
        return jnp.concatenate([x, x], axis=1)

    def kernel(
        q_ref, k_ref, v_ref, do_ref, sq_ref, sk_ref, cos_ref, sin_ref,
        o_ref, dq_ref, dk_ref, dv_ref, halo_ref, peak_ref, bias, kt, vt, el_ref, ds_ref, dks, dvs,
    ):
        p = pl.program_id(0)

        @pl.when(p == 0)
        def _():
            gap = (
                WINDOW
                + lax.broadcasted_iota(jnp.int32, (SPAN, QB), 1)
                - lax.broadcasted_iota(jnp.int32, (SPAN, QB), 0)
            )
            for i in range(blocks):
                same = sk_ref[i * QB : i * QB + SPAN, :] == sq_ref[:, i * QB : (i + 1) * QB]
                bias[i] = jnp.where((gap >= 0) & (gap < WINDOW) & same, 0.0, MASKED)

        kt[...] = k_ref[...].T
        vt[...] = v_ref[...].T
        k_float = kt[...].astype(F32)
        q_float = q_ref[...].astype(F32) * scale
        reach = jnp.max(jnp.sum(k_float * k_float, axis=0)) * jnp.max(jnp.sum(q_float * q_float, axis=1))
        safe = reach < SAFE_SCORE * SAFE_SCORE

        def keys_at(ref, i, c):
            return ref[i * QB + c * CHUNK : i * QB + (c + 1) * CHUNK, :]

        def prepare(i):
            q_all = (q_ref[i * QB : (i + 1) * QB, :].astype(F32) * scale).astype(BF16)
            return q_all, heads_apart(q_all.T)

        def scores(i, c, q_apart):
            return dot(keys_at(k_ref, i, c), q_apart) + two(bias[i, c * CHUNK : (c + 1) * CHUNK])

        def forward(i, q_apart, shifted, found):
            base = None
            if shifted:
                for c in range(n):
                    t = fold(scores(i, c, q_apart), jnp.max)
                    base = t if c == 0 else jnp.maximum(base, t)
                base = jnp.max(base, axis=0, keepdims=True)
            top8 = sum8 = None
            for c in range(n):
                st = scores(i, c, q_apart)
                e = jnp.exp(st - base if shifted else st)
                el_ref[i % 2, c * CHUNK : (c + 1) * CHUNK] = e.astype(BF16)
                t, u = fold(st, jnp.max), fold(e, jnp.sum)
                top8, sum8 = (t, u) if c == 0 else (jnp.maximum(top8, t), sum8 + u)
                yield
            found.append(jnp.max(top8, axis=0, keepdims=True))
            found.append(1.0 / jnp.sum(sum8, axis=0, keepdims=True))

        def per_head(x):
            return jnp.concatenate(
                [jnp.broadcast_to(x[:, :QB], (HEAD, QB)), jnp.broadcast_to(x[:, QB:], (HEAD, QB))], axis=0
            )

        def both(t, x_ref, i):
            span = slice(i * QB, i * QB + SPAN)
            return jnp.concatenate(
                [dot(t[:HEAD, span], x_ref[i % 2, :, :QB]), dot(t[HEAD:, span], x_ref[i % 2, :, QB:])], axis=0
            )

        def output(i, inv):
            raw = both(vt, el_ref, i)
            inv2 = per_head(inv)
            o_ref[i * QB : (i + 1) * QB, :] = (raw * inv2).T.astype(BF16)
            do_s = (do_ref[i * QB : (i + 1) * QB, :].astype(F32).T * inv2).astype(BF16)
            m = do_s.astype(F32) * raw
            mean = jnp.concatenate(
                [jnp.sum(m[:HEAD], axis=0, keepdims=True), jnp.sum(m[HEAD:], axis=0, keepdims=True)], axis=1
            )
            return do_s, mean * inv

        def score_grads(i, do_s, mean):
            do_apart = heads_apart(do_s)
            for c in range(n):
                w = slice(c * CHUNK, (c + 1) * CHUNK)
                dpt = dot(keys_at(v_ref, i, c), do_apart)
                ds_ref[i % 2, w] = (el_ref[i % 2, w].astype(F32) * (dpt - mean)).astype(BF16)

        def input_grads(i, q_all, do_s):
            do_rows = stacked(do_s.T)
            q_rows = stacked(q_all)
            for c in range(n):
                w = slice(c * CHUNK, (c + 1) * CHUNK)
                at = slice(i * QB + c * CHUNK, i * QB + (c + 1) * CHUNK)
                v_part = dot(el_ref[i % 2, w], do_rows)
                k_part = dot(ds_ref[i % 2, w], q_rows)
                if i == 0 or c == n - 1:
                    dvs[at, :] = v_part
                    dks[at, :] = k_part
                else:
                    dvs[at, :] += v_part
                    dks[at, :] += k_part
                yield
            dq = both(kt, ds_ref, i) * scale
            cos_t, sin_t = cos_ref[:, i * QB : (i + 1) * QB], sin_ref[:, i * QB : (i + 1) * QB]
            turned = []
            for h in range(2):
                f, g = dq[h * HEAD : h * HEAD + half], dq[h * HEAD + half : h * HEAD + ROT]
                turned += [f * cos_t + g * sin_t, g * cos_t - f * sin_t, dq[h * HEAD + ROT : (h + 1) * HEAD]]
            dq_ref[i * QB : (i + 1) * QB, :] = jnp.concatenate(turned, axis=0).T.astype(BF16)
            yield

        def run(shifted):
            top = held = None
            for i in range(blocks + 1):
                parts, found = [], []
                if held is not None:
                    parts.append(input_grads(i - 1, *held))
                if i < blocks:
                    q_all, q_apart = prepare(i)
                    parts.append(forward(i, q_apart, shifted, found))
                interleave(*parts)
                if i < blocks:
                    t, inv = found
                    top = t if top is None else jnp.maximum(top, t)
                    do_s, mean = output(i, inv)
                    score_grads(i, do_s, mean)
                    held = (q_all, do_s)
            peak_ref[...] = jnp.broadcast_to(top, peak_ref.shape)
            halo_ref[0] = dks[:rows, :].astype(BF16)
            halo_ref[1] = dvs[:rows, :].astype(BF16)
            dk_ref[...] = dks[rows:, :]
            dv_ref[...] = dvs[rows:, :]

        @pl.when(safe)
        def _():
            run(False)

        @pl.when(jnp.logical_not(safe))
        def _():
            run(True)

    block = pl.BlockSpec((rows, BLK), lambda p: (0, p))
    keys = pl.BlockSpec((2 * rows, BLK), lambda p: (0, p))
    whole = lambda *shape: pl.BlockSpec(shape, lambda p: (0, 0))
    return pl.pallas_call(
        kernel,
        grid=(pairs,),
        in_specs=[
            block, keys, keys, block, whole(1, rows), whole(2 * rows, 1), whole(half, rows), whole(half, rows),
        ],
        out_specs=[
            block, block, block, block,
            pl.BlockSpec((2, rows, BLK), lambda p: (0, 0, p)),
            pl.BlockSpec((8, 2 * QB), lambda p: (p, 0)),
        ],
        out_shape=[
            jax.ShapeDtypeStruct((rows, D), BF16),
            jax.ShapeDtypeStruct((rows, D), BF16),
            jax.ShapeDtypeStruct((rows, D), F32),
            jax.ShapeDtypeStruct((rows, D), F32),
            jax.ShapeDtypeStruct((2, rows, D), BF16),
            jax.ShapeDtypeStruct((8 * pairs, 2 * QB), F32),
        ],
        scratch_shapes=[
            pltpu.VMEM((blocks, SPAN, QB), F32),
            pltpu.VMEM((BLK, 2 * rows), BF16),
            pltpu.VMEM((BLK, 2 * rows), BF16),
            pltpu.VMEM((2, SPAN, 2 * QB), BF16),
            pltpu.VMEM((2, SPAN, 2 * QB), BF16),
            pltpu.VMEM((2 * rows, BLK), F32),
            pltpu.VMEM((2 * rows, BLK), F32),
        ],
        compiler_params=params(dimension_semantics=("arbitrary",)),
        cost_estimate=pl.CostEstimate(flops=40 << 30, bytes_accessed=32 << 20, transcendentals=20 << 20),
        name="attend",
    )(q, k, v, d_out, seg_q, seg_k, cos8, sin8)


FB = 512


def gelu_parts(v):
    a = jnp.abs(v)
    t = 1.0 / (1.0 + a * (0.3275911 * 0.7071067811865476))
    poly = t * (
        0.5 * 0.254829592
        + t * (0.5 * -0.284496736 + t * (0.5 * 1.421413741 + t * (0.5 * -1.453152027 + t * (0.5 * 1.061405429))))
    )
    e = jnp.exp(v * v * -0.5)
    tail = poly * e
    cdf = jnp.where(v >= 0, 1.0 - tail, tail)
    return v * cdf, cdf + v * e * 0.3989422804014327


def feed_forward(w_rows, g_rows, w_all, m, cotangent, b_up):
    rows = m.shape[0]
    steps = FF // FB

    def kernel(
        w_rows_ref, g_rows_ref, w_ref, m_ref, g_ref, b_ref, out_ref, dm_ref, db_ref, gr_ref,
        mt, wup, wdn, hs, dus, gup, gdn, u_ref, h_ref, wsem, gsem,
    ):
        f = pl.program_id(0)
        slot = f % 2
        per = FB // BLK

        def up_at(buf, t):
            return buf.at[pl.ds(pl.multiple_of((t // per) * BLK, BLK), BLK), pl.ds(pl.multiple_of((t % per) * BLK, BLK), BLK)]

        def up_tile(ff, t):
            return UP_BASE + (t // per) * (FF // BLK) + ff * per + t % per

        def down_at(buf, t):
            return buf.at[pl.ds(pl.multiple_of((t // 8) * BLK, BLK), BLK), pl.ds(pl.multiple_of((t % 8) * BLK, BLK), BLK)]

        def down_tile(ff, t):
            return DOWN_BASE + ff * per * 8 + t

        def fetch_one(ff, sl, t):
            src = w_ref.at[pl.ds(pl.multiple_of(w_rows_ref[up_tile(ff, t)], 16), BLK)]
            pltpu.make_async_copy(src, up_at(wup.at[sl], t), wsem.at[0, sl]).start()
            src = w_ref.at[pl.ds(pl.multiple_of(w_rows_ref[down_tile(ff, t)], 16), BLK)]
            pltpu.make_async_copy(src, down_at(wdn.at[sl], t), wsem.at[1, sl]).start()

        def store_one(ff, sl, t):
            dst = gr_ref.at[pl.ds(pl.multiple_of(g_rows_ref[up_tile(ff, t)], 16), BLK)]
            pltpu.make_async_copy(up_at(gup.at[sl], t), dst, gsem.at[0, sl]).start()
            dst = gr_ref.at[pl.ds(pl.multiple_of(g_rows_ref[down_tile(ff, t)], 16), BLK)]
            pltpu.make_async_copy(down_at(gdn.at[sl], t), dst, gsem.at[1, sl]).start()

        def whole_wait(buf, sem):
            pltpu.make_async_copy(buf, buf, sem).wait()

        count = 8 * per

        @pl.when(f == 0)
        def _():
            tile_loop(0, count, lambda t: fetch_one(0, 0, t))
            mt[...] = m_ref[...].T
            out_ref[...] = jnp.zeros_like(out_ref)
            dm_ref[...] = jnp.zeros_like(dm_ref)

        whole_wait(wup.at[slot], wsem.at[0, slot])
        whole_wait(wdn.at[slot], wsem.at[1, slot])

        @pl.when(f >= 2)
        def _():
            whole_wait(gup.at[slot], gsem.at[0, slot])
            whole_wait(gdn.at[slot], gsem.at[1, slot])

        n = rows // ROWB

        def stage1(c):
            at = slice(c * ROWB, (c + 1) * ROWB)
            for k in range(FB // 256):
                cols = slice(k * 256, (k + 1) * 256)
                u_ref[c % 2, :, cols] = dot(m_ref[at, :], wup[slot, :, cols]) + b_ref[:, cols]
                yield
                h_ref[c % 2, :, cols] = dot(g_ref[at, :], wdn[slot, cols, :], NT)
                yield

        db = [None]

        def stage2(c):
            step = ROWB // 8
            for k in range(8):
                at = slice(k * step, (k + 1) * step)
                to = slice(c * ROWB + k * step, c * ROWB + (k + 1) * step)
                hidden, slope = gelu_parts(u_ref[c % 2, at, :])
                hs[to, :] = hidden.astype(BF16)
                du = (h_ref[c % 2, at, :] * slope).astype(BF16)
                dus[to, :] = du
                t = jnp.sum(du.astype(F32).reshape(step // 8, 8, FB), axis=0)
                db[0] = t if db[0] is None else db[0] + t
                yield

        def stage3(c):
            at = slice(c * ROWB, (c + 1) * ROWB)
            for k in range(D // 256):
                cols = slice(k * 256, (k + 1) * 256)
                out_ref[at, cols] += dot(hs[at, :], wdn[slot, :, cols])
                yield
                dm_ref[at, cols] += dot(dus[at, :], wup[slot, cols, :], NT)
                yield

        nxt = jnp.minimum(f + 1, steps - 1)
        for t in range(count):
            fetch_one(nxt, 1 - slot, t)

        for c in range(n + 2):
            gens = []
            if c < n:
                gens.append(stage1(c))
            if 0 <= c - 1 < n:
                gens.append(stage2(c - 1))
            if 0 <= c - 2 < n:
                gens.append(stage3(c - 2))
            interleave(*gens)
        db_ref[...] = jnp.sum(db[0], axis=0, keepdims=True)
        gdn[slot] = dot(hs[...], g_ref[...], TN).astype(BF16)
        gup[slot] = dot(mt[...], dus[...]).astype(BF16)
        for t in range(count):
            store_one(f, slot, t)


        @pl.when(f == steps - 1)
        def _():
            whole_wait(wup.at[1 - slot], wsem.at[0, 1 - slot])
            whole_wait(wdn.at[1 - slot], wsem.at[1, 1 - slot])
            for sl in range(2):
                whole_wait(gup.at[sl], gsem.at[0, sl])
                whole_wait(gdn.at[sl], gsem.at[1, sl])

    full = pl.BlockSpec((rows, D), lambda f, *_: (0, 0))
    bias = pl.BlockSpec((1, FB), lambda f, *_: (0, f))
    return pl.pallas_call(
        kernel,
        grid_spec=pltpu.PrefetchScalarGridSpec(
            num_scalar_prefetch=2,
            grid=(steps,),
            in_specs=[ANY, full, full, bias],
            out_specs=[full, full, bias, ANY],
            scratch_shapes=[
                pltpu.VMEM((D, rows), BF16),
                pltpu.VMEM((2, D, FB), BF16),
                pltpu.VMEM((2, FB, D), BF16),
                pltpu.VMEM((rows, FB), BF16),
                pltpu.VMEM((rows, FB), BF16),
                pltpu.VMEM((2, D, FB), BF16),
                pltpu.VMEM((2, FB, D), BF16),
                pltpu.VMEM((2, ROWB, FB), F32),
                pltpu.VMEM((2, ROWB, FB), F32),
                pltpu.SemaphoreType.DMA((2, 2)),
                pltpu.SemaphoreType.DMA((2, 2)),
            ],
        ),
        out_shape=[
            jax.ShapeDtypeStruct((rows, D), F32),
            jax.ShapeDtypeStruct((rows, D), F32),
            jax.ShapeDtypeStruct((1, FF), F32),
            jax.ShapeDtypeStruct((TILES * BLK, BLK), BF16),
        ],
        compiler_params=params(dimension_semantics=("arbitrary",)),
        cost_estimate=pl.CostEstimate(flops=52 << 30, bytes_accessed=48 << 20, transcendentals=8 << 20),
        name="feed_forward",
    )(w_rows, g_rows, w_all, m, cotangent, b_up)


def finish(w_rows, w_all, tokens, cotangent, smalls, attn_out, mlp_out, dm, dq, dk, dv, halo, tables):
    rows = tokens.shape[0]
    steps = rows // ROWB
    cos8, sin8 = tables

    def kernel(
        w_rows_ref, w_ref, tok_ref, g_ref, small_ref, o_ref, mlp_ref, dm_ref, dq_ref, dk_ref, dv_ref, halo_ref,
        cos_ref, sin_ref,
        out_ref, dx_ref, dp_ref, a_ref, sum_ref, wqkv, wo, sems,
    ):
        i = pl.program_id(0)

        @pl.when(i == 0)
        def _():
            def body(t):
                src = w_ref.at[pl.ds(pl.multiple_of(w_rows_ref[OUT_BASE + t], 16), BLK)]
                dst = wo.at[pl.ds(pl.multiple_of((t // 8) * BLK, BLK), BLK), pl.ds(pl.multiple_of((t % 8) * BLK, BLK), BLK)]
                pltpu.make_async_copy(src, dst, sems.at[0]).start()

            tile_loop(0, 64, body)

            def body(t):
                src = w_ref.at[pl.ds(pl.multiple_of(w_rows_ref[t], 16), BLK)]
                dst = wqkv.at[pl.ds(pl.multiple_of((t // 24) * BLK, BLK), BLK), pl.ds(pl.multiple_of((t % 24) * BLK, BLK), BLK)]
                pltpu.make_async_copy(src, dst, sems.at[1]).start()

            tile_loop(0, 192, body)
            pltpu.make_async_copy(wo, wo, sems.at[0]).wait()
            sum_ref[...] = jnp.zeros_like(sum_ref)

        x = tok_ref[...].astype(F32)
        grad = g_ref[...].astype(F32)
        normed, inv = norm_rows(x)
        g1, g2 = small_ref[4:5, :], small_ref[6:7, :]
        a_ref[...] = (normed * g1 + small_ref[5:6, :]).astype(BF16)
        attn = dot(o_ref[...], wo[...]) + small_ref[2:3, :]
        out_ref[...] = (x + attn + (mlp_ref[...] + small_ref[3:4, :])).astype(BF16)
        dk_all = dk_ref[...] + halo_ref[0].astype(F32)
        dk_all = rope_rows(dk_all, *spread_tables(cos_ref[...], -sin_ref[...]))
        dv_all = dv_ref[...] + halo_ref[1].astype(F32)
        dq_low = dq_ref[...]
        dv_low = dv_all.astype(BF16)
        dp_ref[:, :D] = dq_low
        dp_ref[:, D : 2 * D] = dk_all.astype(BF16)
        dp_ref[:, 2 * D :] = dv_low

        @pl.when(i == 0)
        def _():
            pltpu.make_async_copy(wqkv, wqkv, sems.at[1]).wait()

        da = dot(dp_ref[...], wqkv[...], NT)
        dmv = dm_ref[...]
        dn = da * g1 + dmv * g2
        mean_dn = jnp.mean(dn, axis=-1, keepdims=True)
        mean_dnn = jnp.mean(dn * normed, axis=-1, keepdims=True)
        dx_ref[...] = grad + inv * (dn - mean_dn - normed * mean_dnn)

        def add(row, value):
            sum_ref[row : row + 1, :] += jnp.sum(value, axis=0, keepdims=True)

        add(0, dq_low.astype(F32))
        add(1, dv_low.astype(F32))
        add(2, grad)
        add(3, da * normed)
        add(4, da)
        add(5, dmv * normed)
        add(6, dmv)

    here = lambda i, *_: (i, 0)
    block = pl.BlockSpec((ROWB, D), here)
    table = pl.BlockSpec((ROT // 2, ROWB), lambda i, *_: (0, i + steps))
    return pl.pallas_call(
        kernel,
        grid_spec=pltpu.PrefetchScalarGridSpec(
            num_scalar_prefetch=1,
            grid=(steps,),
            in_specs=[
                ANY, block, block, pl.BlockSpec((16, D), lambda i, *_: (0, 0)),
                block, block, block, block, block, block,
                pl.BlockSpec((2, ROWB, D), lambda i, *_: (0, i, 0)), table, table,
            ],
            out_specs=[
                block, block, pl.BlockSpec((ROWB, 3 * D), here), block,
                pl.BlockSpec((8, D), lambda i, *_: (0, 0)),
            ],
            scratch_shapes=[
                pltpu.VMEM((D, 3 * D), BF16),
                pltpu.VMEM((D, D), BF16),
                pltpu.SemaphoreType.DMA((2,)),
            ],
        ),
        out_shape=[
            jax.ShapeDtypeStruct((rows, D), BF16),
            jax.ShapeDtypeStruct((rows, D), F32),
            jax.ShapeDtypeStruct((rows, 3 * D), BF16),
            jax.ShapeDtypeStruct((rows, D), BF16),
            jax.ShapeDtypeStruct((8, D), F32),
        ],
        compiler_params=params(dimension_semantics=("arbitrary",)),
        name="finish",
    )(w_rows, w_all, tokens, cotangent, smalls, attn_out, mlp_out, dm, dq, dk, dv, halo, cos8, sin8)


def attention_weight_grads(g_rows, grads, attn_in, d_proj, attn_out, cotangent):
    rows = attn_in.shape[0]
    steps = 4 * D // FB

    def kernel(g_rows_ref, a_ref, dp_ref, o_ref, g_ref, _, gr_ref, at, ot, stage, sem):
        i = pl.program_id(0)
        slot = i % 2
        per = FB // BLK

        @pl.when(i == 0)
        def _():
            at[...] = a_ref[...].T

        @pl.when(i == 3 * D // FB)
        def _():
            ot[...] = o_ref[...].T

        @pl.when(i >= 2)
        def _():
            pltpu.make_async_copy(stage.at[slot], stage.at[slot], sem.at[slot]).wait()

        def piece(buf, t):
            return buf.at[pl.ds(pl.multiple_of((t // per) * BLK, BLK), BLK), pl.ds(pl.multiple_of((t % per) * BLK, BLK), BLK)]

        @pl.when(i < 3 * D // FB)
        def _():
            stage[slot] = dot(at[...], dp_ref[...]).astype(BF16)

            def body(t):
                tile = (t // per) * 24 + i * per + t % per
                dst = gr_ref.at[pl.ds(pl.multiple_of(g_rows_ref[tile], 16), BLK)]
                pltpu.make_async_copy(piece(stage.at[slot], t), dst, sem.at[slot]).start()

            tile_loop(0, 8 * per, body)

        @pl.when(i >= 3 * D // FB)
        def _():
            stage[slot] = dot(ot[...], g_ref[...]).astype(BF16)

            def body(t):
                tile = OUT_BASE + (t // per) * 8 + (i - 3 * D // FB) * per + t % per
                dst = gr_ref.at[pl.ds(pl.multiple_of(g_rows_ref[tile], 16), BLK)]
                pltpu.make_async_copy(piece(stage.at[slot], t), dst, sem.at[slot]).start()

            tile_loop(0, 8 * per, body)

        @pl.when(i == steps - 1)
        def _():
            for sl in range(2):
                pltpu.make_async_copy(stage.at[sl], stage.at[sl], sem.at[sl]).wait()

    full = pl.BlockSpec((rows, D), lambda i, *_: (0, 0))
    last = 3 * D // FB - 1
    return pl.pallas_call(
        kernel,
        grid_spec=pltpu.PrefetchScalarGridSpec(
            num_scalar_prefetch=1,
            grid=(steps,),
            in_specs=[
                full,
                pl.BlockSpec((rows, FB), lambda i, *_: (0, jnp.minimum(i, last))),
                full,
                pl.BlockSpec((rows, FB), lambda i, *_: (0, jnp.maximum(i - last - 1, 0))),
                ANY,
            ],
            out_specs=ANY,
            scratch_shapes=[
                pltpu.VMEM((D, rows), BF16),
                pltpu.VMEM((D, rows), BF16),
                pltpu.VMEM((2, D, FB), BF16),
                pltpu.SemaphoreType.DMA((2,)),
            ],
        ),
        out_shape=jax.ShapeDtypeStruct(grads.shape, BF16),
        input_output_aliases={5: 0},
        compiler_params=params(dimension_semantics=("arbitrary",)),
        name="attention_weight_grads",
    )(g_rows, attn_in, d_proj, attn_out, cotangent, grads)


def halves(x):
    high = x.astype(BF16)
    return high, (x - high.astype(F32)).astype(BF16)


def dot3(a, b, dims=NN):
    return dot(a[0], b[0], dims) + (dot(a[0], b[1], dims) + dot(a[1], b[0], dims))


def update_tiles(grads, tiles, left, right, first, second, scale):
    count = tiles.shape[0]
    group = max(g for g in (1, 2, 3, 4, 6, 8) if count % g == 0)

    def kernel(g_ref, w_ref, l_ref, r_ref, m_ref, v_ref, s_ref, w_out, low_out, m_out, v_out):
        turned = []
        for t in range(group):
            l, r = halves(l_ref[t]), halves(r_ref[t])
            turned.append(dot3(halves(dot3(l, halves(g_ref[t]), TN)), r))
        for t in range(group):
            l, r = halves(l_ref[t]), halves(r_ref[t])
            m_new = BETA * m_ref[t] + (1.0 - BETA) * turned[t]
            v_new = BETA * v_ref[t] + (1.0 - BETA) * turned[t] * turned[t]
            ratio = m_new / (jnp.sqrt(v_new) + ADAM_EPS)
            back = dot3(halves(dot3(l, halves(ratio))), r, NT)
            w_new = (w_ref[t] - LEARN * back) * s_ref[t]
            w_out[t] = w_new
            low_out[t] = w_new.astype(BF16)
            m_out[t] = m_new
            v_out[t] = v_new

    block = pl.BlockSpec((group, BLK, BLK), lambda i: (i, 0, 0))
    row = pl.BlockSpec((group, 1, BLK), lambda i: (i, 0, 0))
    like = lambda t: jax.ShapeDtypeStruct(tiles.shape, t)
    return pl.pallas_call(
        kernel,
        grid=(count // group,),
        in_specs=[block] * 6 + [row],
        out_specs=[block] * 4,
        out_shape=[like(F32), like(BF16), like(F32), like(F32)],
        compiler_params=params(dimension_semantics=("arbitrary",)),
        name="update_tiles",
    )(grads, tiles, left, right, first, second, scale)


def column_scales(tile_ids, factors):
    columns = (tile_ids % (3 * D // BLK))[:, None] * BLK + jnp.arange(BLK, dtype=jnp.int32)[None, :]
    head_index = columns % D // HEAD
    root_factor = jnp.sqrt(factors)
    picked = jnp.sum(
        jnp.where(head_index[..., None] == jnp.arange(HEADS, dtype=jnp.int32), root_factor, 0.0),
        axis=-1,
    )
    clipped = (tile_ids[:, None] < QKV_TILES) & (columns < 2 * D)
    return jnp.where(clipped, picked, 1.0)


def small_update(grads, params_, first_moment, second_moment):
    first_new = BETA * first_moment + (1.0 - BETA) * grads
    second_new = BETA * second_moment + (1.0 - BETA) * grads * grads
    updated = params_ - SMALL_LEARN * first_new / (jnp.sqrt(second_new) + ADAM_EPS)
    return (updated, first_new, second_new)


def passed_along(value, axis, steps):
    count = lax.axis_size(axis)
    leading, last = (max(0, -steps), min(count, count - steps))
    return lax.ppermute(value, axis, [(source, source + steps) for source in range(leading, last)])


def on_device(
    ring,
    tokens,
    segments,
    cotangent,
    tile_of_slot,
    tiles,
    left_bases,
    right_bases,
    first_moments,
    second_moments,
    small_params,
    small_first,
    small_second,
    threshold,
):
    rows = tokens.shape[0]
    slot_count = tiles.shape[0]
    small_count = small_params.shape[0]
    axes = ("dp", "seq")
    seq_index = lax.axis_index("seq")
    owner_index = lax.axis_index(axes)
    first_place = seq_index * rows
    seg_local = segments.reshape(1, rows)

    numbers = jnp.arange(TILES, dtype=jnp.int32)
    slot_of_tile = jnp.sum(
        jnp.where(tile_of_slot[None, :] == numbers[:, None], numbers[None, :], 0), axis=1
    ).astype(jnp.int32)
    g_rows = slot_of_tile * BLK

    if ring:
        small_block = jnp.zeros((16 * BLK,), BF16).at[:small_count].set(small_params.astype(BF16))
        payload = jnp.concatenate(
            [tiles.astype(BF16).reshape(slot_count * BLK, BLK), small_block.reshape(16, BLK)], axis=0
        )
        seg_rows = jnp.broadcast_to(seg_local, (8, rows))
        gathered, prev_tokens, prev_seg = gather_weights(payload, tokens, seg_rows)
        stride = payload.shape[0]
        w_all = gathered.reshape(-1, BLK)
        w_rows = slot_of_tile // slot_count * stride + slot_of_tile % slot_count * BLK
        tail = slot_count * BLK
        small_all = gathered[:, tail : tail + small_count // BLK, :].reshape(SMALL)
        prev_seg = prev_seg[:1]
    else:
        w_all = lax.all_gather(tiles.astype(BF16), axes, axis=0, tiled=True).reshape(-1, BLK)
        w_rows = g_rows
        small_all = lax.all_gather(small_params.astype(BF16), axes, axis=0, tiled=True)
        prev_tokens, prev_seg = passed_along((tokens, seg_local), "seq", 1)

    table = small_all.astype(F32).reshape(D, 12)
    smalls = jnp.concatenate(
        [
            jnp.stack([table[:, r] for r in (0, 1, 2, 7, 8, 9, 10, 11)], axis=0),
            jnp.zeros((8, D), F32),
        ],
        axis=0,
    )
    b_up = table[:, 3:7].reshape(1, FF)

    half = ROT // 2
    exponent = jnp.arange(half, dtype=F32) * (2.0 / ROT)
    frequency = jnp.power(ROPE_BASE, -exponent)
    places = first_place - rows + jnp.arange(2 * rows, dtype=jnp.int32)
    angle = places.astype(F32)[None, :] * frequency[:, None]
    cos8, sin8 = jnp.cos(angle), jnp.sin(angle)
    tables = (cos8, sin8)

    prev_seg = jnp.where(seq_index == 0, -1, prev_seg)
    seg_k = jnp.concatenate([prev_seg, seg_local], axis=1).reshape(2 * rows, 1)

    q, k, v, d_out, m = project(w_rows, w_all, prev_tokens, tokens, cotangent, smalls, tables)
    attn_out, dq, dk, dv, halo, peaks = attend(
        q, k, v, d_out, seg_local, seg_k, cos8[:, rows:], sin8[:, rows:]
    )
    halo = passed_along(halo, "seq", -1)
    mlp_out, dm, db_up, grads = feed_forward(w_rows, g_rows, w_all, m, cotangent, b_up)
    block_output, input_grad, d_proj, attn_in, sums = finish(
        w_rows, w_all, tokens, cotangent, smalls, attn_out, mlp_out, dm, dq, dk, dv, halo, tables
    )
    grads = attention_weight_grads(g_rows, grads, attn_in, d_proj, attn_out, cotangent)

    small_terms = jnp.concatenate(
        [
            sums[:3].T,
            db_up.reshape(D, FF // D),
            sums[2:7].T,
        ],
        axis=1,
    ).reshape(SMALL)
    head_peak = jnp.max(peaks.reshape(HEADS // 2, 8, 2, QB)[:, 0], axis=-1).reshape(HEADS)
    if ring:
        peak_rows = jnp.zeros((8, BLK), F32).at[:, :HEADS].set(head_peak[None, :])
        extra = jnp.concatenate([small_terms.reshape(SMALL_ROWS, BLK), peak_rows], axis=0)
        tile_grads, extra = sum_gradients(grads, extra)
        tile_grads = tile_grads.reshape(slot_count, BLK, BLK)
        small_grads = lax.dynamic_slice_in_dim(
            extra[:SMALL_ROWS].reshape(SMALL), owner_index * small_count, small_count, 0
        )
        head_peak = extra[SMALL_ROWS, :HEADS]
    else:
        tile_grads = lax.psum_scatter(
            grads.astype(F32).reshape(TILES, BLK, BLK), axes, scatter_dimension=0, tiled=True
        )
        small_grads = lax.psum_scatter(small_terms, axes, scatter_dimension=0, tiled=True)
        head_peak = lax.pmax(head_peak, axes)

    local_ids = lax.dynamic_slice_in_dim(tile_of_slot, owner_index * slot_count, slot_count, 0)
    limit = threshold[0]
    factors = limit / jnp.maximum(head_peak, limit)
    scale = column_scales(local_ids, factors).reshape(slot_count, 1, BLK)
    new_tiles, new_low, new_first, new_second = update_tiles(
        tile_grads, tiles, left_bases, right_bases, first_moments, second_moments, scale
    )
    new_small, new_small_first, new_small_second = small_update(
        small_grads, small_params, small_first, small_second
    )
    return (
        block_output,
        input_grad,
        tile_grads,
        small_grads,
        new_tiles,
        new_low,
        new_first,
        new_second,
        new_small,
        new_small.astype(BF16),
        new_small_first,
        new_small_second,
        factors,
    )


def solution(mesh):
    split = P(("dp", "seq"))
    in_specs = (split, P("dp", "seq"), split, P()) + (split,) * 8 + (P(),)
    out_specs = (split,) * 12 + (P(),)
    ring = (mesh.shape["dp"], mesh.shape["seq"]) == (4, 8)
    return jax.shard_map(
        functools.partial(on_device, ring), mesh=mesh, in_specs=in_specs, out_specs=out_specs, check_vma=False
    )
```

```python
import functools

import jax
import jax.numpy as jnp
from jax import lax
from jax.experimental import pallas as pl
from jax.experimental.pallas import tpu as pltpu
from jax.sharding import PartitionSpec as P

D = 1024
FF = 4096
HEADS = 16
HEAD = 64
ROT = 16
BLK = 128
WINDOW = 1024
TILES = 768
SMALL = 12288
QKV_TILES = D // BLK * (3 * D // BLK)
OUT_TILES = D // BLK * (D // BLK)
UP_TILES = D // BLK * (FF // BLK)
OUT_BASE = QKV_TILES
UP_BASE = QKV_TILES + OUT_TILES
DOWN_BASE = UP_BASE + UP_TILES

NORM_EPS = 1e-05
ADAM_EPS = 1e-08
BETA = 0.5
LEARN = 0.03
SMALL_LEARN = 0.2
ROPE_BASE = 10000.0
MASKED = -1e30
HIGH = lax.Precision.HIGHEST

F32 = jnp.float32
BF16 = jnp.bfloat16
MESH = pl.DeviceIdType.MESH
ANY = pl.BlockSpec(memory_space=pl.ANY)
VMEM = pl.BlockSpec(memory_space=pltpu.VMEM)
VMEM_LIMIT = 58 << 20

NN = (((1,), (0,)), ((), ()))
NT = (((1,), (1,)), ((), ()))
TN = (((0,), (0,)), ((), ()))


def dot(a, b, dims=NN, precision=None):
    return lax.dot_general(a, b, dims, precision=precision, preferred_element_type=F32)


def interleave(*parts):
    live = list(parts)
    while live:
        for part in list(live):
            try:
                next(part)
            except StopIteration:
                live.remove(part)


def params(**kw):
    return pltpu.CompilerParams(vmem_limit_bytes=VMEM_LIMIT, **kw)


def norm_rows(x):
    centered = x - jnp.mean(x, axis=-1, keepdims=True)
    inv = lax.rsqrt(jnp.mean(centered * centered, axis=-1, keepdims=True) + NORM_EPS)
    return centered * inv, inv


def tile_loop(first, count, body):
    def step(t, carry):
        body(t)
        return carry

    lax.fori_loop(first, first + count, step, 0)


ROWS_PER_TILE = BLK
HALF_ROWS = 1536


def gather_weights(payload, tokens, seg_rows):
    rows = payload.shape[0]
    top = pl.ds(0, HALF_ROWS)
    low = pl.ds(HALF_ROWS, rows - HALF_ROWS)

    def kernel(x_ref, tok_ref, seg_ref, out_ref, ptok_ref, pseg_ref, lsem, ss, rs, hss, hrs, hls):
        d = lax.axis_index("dp")
        s = lax.axis_index("seq")
        z = s // 2
        c = s % 2
        xn = d + 1 - 2 * (d % 2)
        yn = d + 2 - 4 * (d // 2)
        xyn = 3 - d
        sib = z * 2 + 1 - c
        halo = s - 1 + 2 * c
        halo_ok = ((c == 0) & (z > 0)) | ((c == 1) & (z < 3))

        barrier = pltpu.get_barrier_semaphore()

        def greet(dev):
            pl.semaphore_signal(barrier, inc=1, device_id=dev, device_id_type=MESH)

        greet((d, sib))
        greet((xn, s))
        greet((yn, s))

        @pl.when(z > 0)
        def _():
            greet((d, s - 2))

        @pl.when(z < 3)
        def _():
            greet((d, s + 2))

        @pl.when(halo_ok)
        def _():
            greet((d, halo))

        below, above = (z + 2) // 3, (5 - z) // 3
        pl.semaphore_wait(barrier, 3 + below + above + (1 - c) * below + c * above)

        def place(dd, zz):
            return out_ref.at[dd * 8 + zz * 2 + c]

        def remote(src, dst, kind, zz, dev):
            return pltpu.make_async_remote_copy(
                src_ref=src,
                dst_ref=dst,
                send_sem=ss.at[kind, zz],
                recv_sem=rs.at[kind, zz],
                device_id=dev,
                device_id_type=MESH,
            )

        def block_of(zz, own):
            return x_ref if own else place(d, zz)

        def up(zz, own):
            return remote(block_of(zz, own), place(d, zz), 0, zz, (d, s + 2))

        def down(zz, own):
            return remote(block_of(zz, own), place(d, zz), 1, zz, (d, s - 2))

        def to_x(zz, own):
            return remote(block_of(zz, own), place(d, zz), 2, zz, (xn, s))

        def to_y(zz, own):
            return remote(block_of(zz, own), place(d, zz), 3, zz, (yn, s))

        def on_y(zz):
            return remote(place(xn, zz).at[top], place(xn, zz).at[top], 4, zz, (yn, s))

        def on_x(zz):
            return remote(place(yn, zz).at[low], place(yn, zz).at[low], 5, zz, (xn, s))

        def to_sib(dd, zz, kind, own=False):
            src = x_ref if own else place(dd, zz)
            return remote(src, place(dd, zz), kind, zz, (d, sib))

        def from_x(zz):
            return remote(x_ref, place(xn, zz), 2, zz, (xn, s))

        def from_y(zz):
            return remote(x_ref, place(yn, zz), 3, zz, (yn, s))

        def diag_up(zz):
            return remote(place(xyn, zz), place(xyn, zz), 10, zz, (d, s + 2))

        def diag_down(zz):
            return remote(place(xyn, zz), place(xyn, zz), 11, zz, (d, s - 2))

        def diag_top(zz):
            return remote(x_ref.at[top], place(xyn, zz).at[top], 4, zz, (yn, s))

        def diag_low(zz):
            return remote(x_ref.at[low], place(xyn, zz).at[low], 5, zz, (xn, s))

        order = [z, 1 + z % 2, (2 + 3 * z) % 5, 3 * (1 - z // 2)]
        local = pltpu.make_async_copy(x_ref, place(d, z), lsem)
        local.start()

        def halo_copies(dev):
            tok = pltpu.make_async_remote_copy(
                src_ref=tok_ref,
                dst_ref=ptok_ref,
                send_sem=hss.at[0],
                recv_sem=hrs.at[0],
                device_id=dev,
                device_id_type=MESH,
            )
            seg = pltpu.make_async_remote_copy(
                src_ref=seg_ref,
                dst_ref=pseg_ref,
                send_sem=hss.at[1],
                recv_sem=hrs.at[1],
                device_id=dev,
                device_id_type=MESH,
            )
            return tok, seg

        def in_plane(k, body):
            if k == 0:
                body()
            else:
                pl.when((z - order[k] >= 2) | (order[k] - z >= 3))(body)

        def on_line(k, body):
            pl.when((z - order[k] < 2) & (order[k] - z < 3))(body)

        def launch(k):
            zz = order[k]
            own = k == 0
            if own:

                @pl.when(z < 3)
                def _():
                    up(zz, True).start()

                @pl.when(z > 0)
                def _():
                    down(zz, True).start()
            else:

                @pl.when(zz < z)
                def _():
                    up(zz, False).wait_recv()

                @pl.when((zz < z) & (z < 3))
                def _():
                    up(zz, False).start()

                @pl.when(zz > z)
                def _():
                    down(zz, False).wait_recv()

                @pl.when((zz > z) & (z > 0))
                def _():
                    down(zz, False).start()

            to_x(zz, own).start()
            to_y(zz, own).start()
            to_sib(d, zz, 6, own).start()

        def second(k):
            zz = order[k]

            def pass_on():
                from_x(zz).wait_recv()
                on_y(zz).start()
                to_sib(xn, zz, 7).start()
                from_y(zz).wait_recv()
                on_x(zz).start()
                to_sib(yn, zz, 8).start()

            in_plane(k, pass_on)

        def rest(k):
            zz = order[k]

            def share():
                from_x(zz).wait_recv()
                to_sib(xn, zz, 7).start()
                from_y(zz).wait_recv()
                to_sib(yn, zz, 8).start()

            on_line(k, share)

        def third(k):
            zz = order[k]

            def arrive():
                diag_top(zz).wait_recv()
                diag_low(zz).wait_recv()

            in_plane(k, arrive)
            if k > 0:

                @pl.when((zz < z) & (z - zz <= 1))
                def _():
                    diag_up(zz).wait_recv()

                @pl.when((zz > z) & (zz - z <= 2))
                def _():
                    diag_down(zz).wait_recv()

            if k < 3:

                @pl.when((zz == z) & (z < 3))
                def _():
                    diag_up(zz).start()

                @pl.when((zz >= z) & (zz - z <= 1) & (z > 0))
                def _():
                    diag_down(zz).start()

            to_sib(xyn, zz, 9).start()

        own_tok = pltpu.make_async_copy(tok_ref, ptok_ref, hls.at[0])
        own_seg = pltpu.make_async_copy(seg_ref, pseg_ref, hls.at[1])


        @pl.when(s == 0)
        def _():
            own_tok.start()
            own_seg.start()

        launch(0)
        launch(1)
        second(0)
        launch(2)
        launch(3)
        third(0)
        second(1)
        third(1)
        second(2)

        @pl.when(s < 7)
        def _():
            for cp in halo_copies((d, s + 1)):
                cp.start()

        second(3)
        rest(1)
        rest(2)
        rest(3)
        third(2)
        third(3)

        local.wait()
        other = 1 - c

        def sib_place(dd, zz):
            return out_ref.at[dd * 8 + zz * 2 + other]

        for k in range(4):
            zz = order[k]
            own = k == 0
            for kind, dd in ((6, d), (7, xn), (8, yn), (9, xyn)):
                remote(sib_place(dd, zz), sib_place(dd, zz), kind, zz, (d, sib)).wait_recv()
                to_sib(dd, zz, kind, own and kind == 6).wait_send()
            to_x(zz, own).wait_send()
            to_y(zz, own).wait_send()

            def halves_sent():
                on_y(zz).wait_send()
                on_x(zz).wait_send()

            in_plane(k, halves_sent)
            if k < 3:

                @pl.when((zz == z) & (z < 3))
                def _():
                    diag_up(zz).wait_send()

                @pl.when((zz >= z) & (zz - z <= 1) & (z > 0))
                def _():
                    diag_down(zz).wait_send()

            @pl.when((zz <= z) & (z < 3))
            def _():
                up(zz, own).wait_send()

            @pl.when((zz >= z) & (z > 0))
            def _():
                down(zz, own).wait_send()

        @pl.when(s < 7)
        def _():
            for cp in halo_copies((d, s + 1)):
                cp.wait_send()

        @pl.when(s > 0)
        def _():
            for cp in halo_copies((d, s - 1)):
                cp.wait_recv()

        @pl.when(s == 0)
        def _():
            own_tok.wait()
            own_seg.wait()

    return pl.pallas_call(
        kernel,
        out_shape=[
            jax.ShapeDtypeStruct((32, rows, BLK), BF16),
            jax.ShapeDtypeStruct(tokens.shape, BF16),
            jax.ShapeDtypeStruct(seg_rows.shape, jnp.int32),
        ],
        in_specs=[ANY, ANY, ANY],
        out_specs=[ANY, ANY, ANY],
        scratch_shapes=[
            pltpu.SemaphoreType.DMA,
            pltpu.SemaphoreType.DMA((12, 4)),
            pltpu.SemaphoreType.DMA((12, 4)),
            pltpu.SemaphoreType.DMA((2,)),
            pltpu.SemaphoreType.DMA((2,)),
            pltpu.SemaphoreType.DMA((2,)),
        ],
        compiler_params=params(collective_id=0, has_side_effects=True),
        name="gather_weights",
    )(payload, tokens, seg_rows)


OWNED = 24 * BLK
HALF = OWNED // 2
SMALL_ROWS = SMALL // BLK
EXTRA_ROWS = SMALL_ROWS + 8


def add_rows(dst, terms, rows, step=512):
    def body(i, carry):
        at = pl.ds(pl.multiple_of(i * step, step), step)
        if len(terms) == 2 and dst.dtype == BF16:
            dst[at] = terms[0][at] + terms[1][at]
        else:
            total = terms[0][at].astype(F32)
            for term in terms[1:]:
                total = total + term[at].astype(F32)
            dst[at] = total.astype(dst.dtype)
        return carry

    lax.fori_loop(0, rows // step, body, 0)


def sum_gradients(grads, extra):
    def kernel(g_ref, e_ref, out_ref, eout_ref, own, crecv, s1a, s1b, s2, zup, zdn, gup, gdn, epart, erecv, ls, ss, rs, zss, zrs, es, er):
        d = lax.axis_index("dp")
        s = lax.axis_index("seq")
        z = s // 2
        c = s % 2
        xn = d + 1 - 2 * (d % 2)
        yn = d + 2 - 4 * (d // 2)
        xyn = 3 - d
        sib = z * 2 + 1 - c
        zpair = s + 2 - 4 * (z % 2)
        zfar = s + 4 - 8 * (z // 2)
        top = pl.ds(0, HALF)
        low = pl.ds(HALF, HALF)

        barrier = pltpu.get_barrier_semaphore()

        def greet(dev):
            pl.semaphore_signal(barrier, inc=1, device_id=dev, device_id_type=MESH)

        greet((d, sib))
        greet((xn, s))
        greet((yn, s))
        greet((d, zfar))

        @pl.when(z > 0)
        def _():
            greet((d, s - 2))

        @pl.when(z < 3)
        def _():
            greet((d, s + 2))

        order = [3 * (1 - z // 2), (2 + 3 * z) % 5, 1 + z % 2, z]

        def owner_rows(dd, zz, cc):
            return g_ref.at[pl.ds(pl.multiple_of((dd * 8 + zz * 2 + cc) * OWNED, OWNED), OWNED)]

        def load(zz, dd):
            return pltpu.make_async_copy(owner_rows(dd, zz, c), own.at[zz, dd], ls.at[zz, dd])

        for k in range(4):
            for dd in range(4):
                load(order[k], dd).start()

        pl.semaphore_wait(barrier, 4 + (z + 2) // 3 + (5 - z) // 3)

        def remote(src, dst, ssem, rsem, dev):
            return pltpu.make_async_remote_copy(
                src_ref=src, dst_ref=dst, send_sem=ssem, recv_sem=rsem, device_id=dev, device_id_type=MESH
            )

        def core(zz, dd):
            return remote(owner_rows(dd, zz, 1 - c), crecv.at[zz, dd], ss.at[zz, dd], rs.at[zz, dd], (d, sib))

        def y_own(zz):
            return remote(own.at[zz, yn, top], s1a.at[zz, 0], ss.at[zz, 4], rs.at[zz, 4], (yn, s))

        def y_cross(zz):
            return remote(own.at[zz, xyn, top], s1a.at[zz, 1], ss.at[zz, 5], rs.at[zz, 5], (yn, s))

        def x_own(zz):
            return remote(own.at[zz, xn, low], s1b.at[zz, 0], ss.at[zz, 6], rs.at[zz, 6], (xn, s))

        def x_cross(zz):
            return remote(own.at[zz, xyn, low], s1b.at[zz, 1], ss.at[zz, 7], rs.at[zz, 7], (xn, s))

        def x_last(zz):
            return remote(own.at[zz, xn, top], s2.at[zz, top], ss.at[zz, 8], rs.at[zz, 8], (xn, s))

        def y_last(zz):
            return remote(own.at[zz, yn, low], s2.at[zz, low], ss.at[zz, 9], rs.at[zz, 9], (yn, s))

        def z_up(zz):
            return remote(own.at[zz, d], zup.at[zz], zss.at[0, zz], zrs.at[0, zz], (d, s + 2))

        def z_dn(zz):
            return remote(own.at[zz, d], zdn.at[zz], zss.at[1, zz], zrs.at[1, zz], (d, s - 2))

        def g_up(zz):
            return remote(own.at[zz, xyn], gup.at[zz], zss.at[2, zz], zrs.at[2, zz], (d, s + 2))

        def g_dn(zz):
            return remote(own.at[zz, xyn], gdn.at[zz], zss.at[3, zz], zrs.at[3, zz], (d, s - 2))

        ends = (z == 0) | (z == 3)
        inner = (z == 1) | (z == 2)

        def in_plane(k, body):
            if k == 3:
                body()
            elif k == 0:
                pl.when(ends)(body)

        def cross(zz):
            y_cross(zz).start()
            x_cross(zz).start()

        def along(zz, act):
            @pl.when(zz > z)
            def _():
                act(g_up(zz))

            @pl.when(zz < z)
            def _():
                act(g_dn(zz))

        def outward(k, act):
            zz = order[k]
            if k == 0:
                pl.when(inner)(lambda: along(zz, act))
            elif k < 3:
                along(zz, act)

        def diagonal(k):
            zz = order[k]
            mine = own.at[zz, xyn]
            if k < 3:

                @pl.when(inner)
                def _():
                    @pl.when(zz > z)
                    def _():
                        g_up(zz).wait_recv()
                        add_rows(mine, [mine, gup.at[zz]], OWNED)

                    @pl.when(zz < z)
                    def _():
                        g_dn(zz).wait_recv()
                        add_rows(mine, [mine, gdn.at[zz]], OWNED)

                    along(zz, lambda cp: cp.start())
            else:

                @pl.when(z > 0)
                def _():
                    g_up(zz).wait_recv()
                    add_rows(mine, [mine, gup.at[zz]], OWNED)

                @pl.when(z < 3)
                def _():
                    g_dn(zz).wait_recv()
                    add_rows(mine, [mine, gdn.at[zz]], OWNED)

                cross(zz)

        def extra_step(i, dev):
            return remote(epart.at[i], erecv.at[i], es.at[i], er.at[i], dev)

        extra_devs = [(d, sib), (xn, s), (yn, s), (d, zpair), (d, zfar)]

        def extra_add(i):
            extra_step(i, extra_devs[i]).wait_recv()
            a = epart[i]
            b = erecv[i]
            row = lax.broadcasted_iota(jnp.int32, a.shape, 0)
            total = jnp.where(row < SMALL_ROWS, a + b, jnp.maximum(a, b))
            if i < 4:
                epart[i + 1] = total
                extra_step(i + 1, extra_devs[i + 1]).start()
            else:
                eout_ref[...] = total

        def issue(k):
            for dd in (xyn, yn, xn, d):
                core(order[k], dd).start()

        issue(0)
        epart[0] = e_ref[...]
        extra_step(0, extra_devs[0]).start()

        def first(k):
            zz = order[k]
            if k < 3:
                issue(k + 1)

            def one(dd, start):
                load(zz, dd).wait()
                core(zz, dd).wait_recv()
                add_rows(own.at[zz, dd], [own.at[zz, dd], crecv.at[zz, dd]], OWNED)
                for cp in start:
                    cp.start()

            one(xyn, [])
            if k == 0:
                pl.when(ends)(lambda: cross(zz))
                outward(0, lambda cp: cp.start())
            elif k < 3:
                pl.when(ends)(lambda: along(zz, lambda cp: cp.start()))
            one(yn, [y_own(zz)])
            one(xn, [x_own(zz)])
            one(d, [])

        def second(k):
            zz = order[k]
            a = own.at[zz, xn, top]
            b = own.at[zz, yn, low]

            def crossed():
                y_cross(zz).wait_recv()
                add_rows(a, [a, s1a.at[zz, 1]], HALF)

            def crossed_low():
                x_cross(zz).wait_recv()
                add_rows(b, [b, s1b.at[zz, 1]], HALF)

            in_plane(k, crossed)
            x_last(zz).start()
            in_plane(k, crossed_low)
            y_last(zz).start()

        def third(k):
            zz = order[k]
            y_own(zz).wait_recv()
            x_own(zz).wait_recv()
            x_last(zz).wait_recv()
            y_last(zz).wait_recv()
            a = own.at[zz, d, top]
            b = own.at[zz, d, low]
            if k < 3:

                @pl.when((zz > z) & (z > 0))
                def _():
                    z_up(zz).wait_recv()
                    add_rows(a, [a, s1a.at[zz, 0], s2.at[zz, top], zup.at[zz, top]], HALF)
                    add_rows(b, [b, s1b.at[zz, 0], s2.at[zz, low], zup.at[zz, low]], HALF)

                @pl.when((zz < z) & (z < 3))
                def _():
                    z_dn(zz).wait_recv()
                    add_rows(a, [a, s1a.at[zz, 0], s2.at[zz, top], zdn.at[zz, top]], HALF)
                    add_rows(b, [b, s1b.at[zz, 0], s2.at[zz, low], zdn.at[zz, low]], HALF)

                @pl.when(((zz > z) & (z == 0)) | ((zz < z) & (z == 3)))
                def _():
                    add_rows(a, [a, s1a.at[zz, 0], s2.at[zz, top]], HALF)
                    add_rows(b, [b, s1b.at[zz, 0], s2.at[zz, low]], HALF)

                @pl.when(zz > z)
                def _():
                    z_up(zz).start()

                @pl.when(zz < z)
                def _():
                    z_dn(zz).start()
            else:

                @pl.when(z > 0)
                def _():
                    z_up(zz).wait_recv()

                @pl.when(z < 3)
                def _():
                    z_dn(zz).wait_recv()

                o_top = out_ref.at[top]
                o_low = out_ref.at[low]

                @pl.when((z > 0) & (z < 3))
                def _():
                    add_rows(o_top, [a, s1a.at[zz, 0], s2.at[zz, top], zup.at[zz, top], zdn.at[zz, top]], HALF)
                    add_rows(o_low, [b, s1b.at[zz, 0], s2.at[zz, low], zup.at[zz, low], zdn.at[zz, low]], HALF)

                @pl.when(z == 0)
                def _():
                    add_rows(o_top, [a, s1a.at[zz, 0], s2.at[zz, top], zdn.at[zz, top]], HALF)
                    add_rows(o_low, [b, s1b.at[zz, 0], s2.at[zz, low], zdn.at[zz, low]], HALF)

                @pl.when(z == 3)
                def _():
                    add_rows(o_top, [a, s1a.at[zz, 0], s2.at[zz, top], zup.at[zz, top]], HALF)
                    add_rows(o_low, [b, s1b.at[zz, 0], s2.at[zz, low], zup.at[zz, low]], HALF)

        first(0)
        first(1)
        extra_add(0)
        second(0)
        diagonal(1)
        first(2)
        second(1)
        extra_add(1)
        first(3)
        diagonal(2)
        second(2)
        third(0)
        extra_add(2)
        diagonal(3)
        extra_add(3)
        third(1)
        extra_add(4)
        third(2)
        second(3)
        third(3)

        for i in range(5):
            extra_step(i, extra_devs[i]).wait_send()
        for k in range(4):
            zz = order[k]
            for dd in range(4):
                core(zz, dd).wait_send()
            for cp in (y_own(zz), x_own(zz), x_last(zz), y_last(zz)):
                cp.wait_send()

            def crosses_sent():
                y_cross(zz).wait_send()
                x_cross(zz).wait_send()

            in_plane(k, crosses_sent)
            outward(k, lambda cp: cp.wait_send())
            if k < 3:

                @pl.when(zz > z)
                def _():
                    z_up(zz).wait_send()

                @pl.when(zz < z)
                def _():
                    z_dn(zz).wait_send()

    return pl.pallas_call(
        kernel,
        out_shape=[
            jax.ShapeDtypeStruct((OWNED, BLK), F32),
            jax.ShapeDtypeStruct((EXTRA_ROWS, BLK), F32),
        ],
        in_specs=[ANY, VMEM],
        out_specs=[VMEM, VMEM],
        scratch_shapes=[
            pltpu.VMEM((4, 4, OWNED, BLK), BF16),
            pltpu.VMEM((4, 4, OWNED, BLK), BF16),
            pltpu.VMEM((4, 2, HALF, BLK), BF16),
            pltpu.VMEM((4, 2, HALF, BLK), BF16),
            pltpu.VMEM((4, OWNED, BLK), BF16),
            pltpu.VMEM((4, OWNED, BLK), BF16),
            pltpu.VMEM((4, OWNED, BLK), BF16),
            pltpu.VMEM((4, OWNED, BLK), BF16),
            pltpu.VMEM((4, OWNED, BLK), BF16),
            pltpu.VMEM((5, EXTRA_ROWS, BLK), F32),
            pltpu.VMEM((5, EXTRA_ROWS, BLK), F32),
            pltpu.SemaphoreType.DMA((4, 4)),
            pltpu.SemaphoreType.DMA((4, 10)),
            pltpu.SemaphoreType.DMA((4, 10)),
            pltpu.SemaphoreType.DMA((4, 4)),
            pltpu.SemaphoreType.DMA((4, 4)),
            pltpu.SemaphoreType.DMA((5,)),
            pltpu.SemaphoreType.DMA((5,)),
        ],
        compiler_params=params(collective_id=1, has_side_effects=True),
        name="sum_gradients",
    )(grads, extra)


ROWB = 256


def rope_rows(value, cos_t, fwd_t, back_t):
    pieces = []
    for j in range(value.shape[1] // BLK):
        p = value[:, j * BLK : (j + 1) * BLK]
        pieces.append(
            p * cos_t + pltpu.roll(p, BLK - ROT // 2, 1) * fwd_t + pltpu.roll(p, ROT // 2, 1) * back_t
        )
    return jnp.concatenate(pieces, axis=1)


def spread_tables(cos8, sin8):
    none = jnp.zeros_like(cos8)
    rest = (HEAD - ROT) // none.shape[0]
    cos_t = [cos8, cos8] + [none + 1.0] * rest
    fwd_t = [-sin8, none] + [none] * rest
    back_t = [none, sin8] + [none] * rest
    return [jnp.concatenate(t * 2, axis=0).T for t in (cos_t, fwd_t, back_t)]


def project(w_rows, w_all, prev_tokens, tokens, cotangent, smalls, tables):
    rows = tokens.shape[0]
    cos8, sin8 = tables

    def kernel(
        w_rows_ref, w_ref, prev_ref, tok_ref, g_ref, small_ref, cos_ref, sin_ref,
        q_ref, k_ref, v_ref, do_ref, m_ref, wqkv, wo, sems,
    ):
        i = pl.program_id(0)

        def third_copy(third):
            def body(t):
                r, cc = t // 8, t % 8
                src = w_ref.at[pl.ds(pl.multiple_of(w_rows_ref[r * 24 + third * 8 + cc], 16), BLK)]
                dst = wqkv.at[pl.ds(pl.multiple_of(r * BLK, BLK), BLK), pl.ds(pl.multiple_of(third * D + cc * BLK, BLK), BLK)]
                pltpu.make_async_copy(src, dst, sems.at[third]).start()

            tile_loop(0, 64, body)

        def third_wait(third):
            part = wqkv.at[:, pl.ds(third * D, D)]
            pltpu.make_async_copy(part, part, sems.at[third]).wait()

        @pl.when(i == 0)
        def _():
            third_copy(1)
            third_copy(2)
            third_copy(0)

            def body(t):
                r, cc = t // 8, t % 8
                src = w_ref.at[pl.ds(pl.multiple_of(w_rows_ref[OUT_BASE + t], 16), BLK)]
                dst = wo.at[pl.ds(pl.multiple_of(r * BLK, BLK), BLK), pl.ds(pl.multiple_of(cc * BLK, BLK), BLK)]
                pltpu.make_async_copy(src, dst, sems.at[3]).start()

            tile_loop(0, 64, body)
            third_wait(1)
            third_wait(2)

        @pl.when(i == 1)
        def _():
            third_wait(0)
            pltpu.make_async_copy(wo, wo, sems.at[3]).wait()

        n = rows // ROWB

        def run(own):
            x_ref = tok_ref if own else prev_ref
            ins, tabs, raw = {}, {}, {}

            def prepare(c):
                at = slice(c * ROWB, (c + 1) * ROWB)
                normed, _ = norm_rows(x_ref[at, :].astype(F32))
                ins[c] = (normed * small_ref[4:5, :] + small_ref[5:6, :]).astype(BF16)
                if own:
                    m_ref[at, :] = (normed * small_ref[6:7, :] + small_ref[7:8, :]).astype(BF16)
                yield
                tabs[c] = spread_tables(cos_ref[:, at], sin_ref[:, at])
                yield

            def multiply(c):
                at = slice(c * ROWB, (c + 1) * ROWB)
                raw[c] = [dot(ins[c], wqkv[:, D : 2 * D])]
                yield
                v_ref[at, :] = (dot(ins[c], wqkv[:, 2 * D :]) + small_ref[1:2, :]).astype(BF16)
                yield
                if own:
                    raw[c].append(dot(ins[c], wqkv[:, :D]) + small_ref[0:1, :])
                    yield
                    do_ref[at, :] = dot(g_ref[at, :], wo[...], NT).astype(BF16)
                    yield

            def turn(c):
                at = slice(c * ROWB, (c + 1) * ROWB)
                k_ref[at, :] = rope_rows(raw[c][0], *tabs[c]).astype(BF16)
                yield
                if own:
                    q_ref[at, :] = rope_rows(raw[c][1], *tabs[c]).astype(BF16)
                    yield

            for c in range(n + 2):
                parts = []
                if 0 <= c - 1 < n:
                    parts.append(multiply(c - 1))
                if c < n:
                    parts.append(prepare(c))
                if 0 <= c - 2 < n:
                    parts.append(turn(c - 2))
                interleave(*parts)

        @pl.when(i == 0)
        def _():
            run(False)

        @pl.when(i == 1)
        def _():
            run(True)

    block = pl.BlockSpec((rows, D), lambda i, *_: (0, 0))
    here = pl.BlockSpec((rows, D), lambda i, *_: (i, 0))
    table = pl.BlockSpec((ROT // 2, rows), lambda i, *_: (0, i))
    return pl.pallas_call(
        kernel,
        grid_spec=pltpu.PrefetchScalarGridSpec(
            num_scalar_prefetch=1,
            grid=(2,),
            in_specs=[
                ANY, block, block, block,
                pl.BlockSpec((16, D), lambda i, *_: (0, 0)), table, table,
            ],
            out_specs=[block, here, here, block, block],
            scratch_shapes=[
                pltpu.VMEM((D, 3 * D), BF16),
                pltpu.VMEM((D, D), BF16),
                pltpu.SemaphoreType.DMA((4,)),
            ],
        ),
        out_shape=[
            jax.ShapeDtypeStruct((rows, D), BF16),
            jax.ShapeDtypeStruct((2 * rows, D), BF16),
            jax.ShapeDtypeStruct((2 * rows, D), BF16),
            jax.ShapeDtypeStruct((rows, D), BF16),
            jax.ShapeDtypeStruct((rows, D), BF16),
        ],
        compiler_params=params(dimension_semantics=("arbitrary",)),
        name="project",
    )(w_rows, w_all, prev_tokens, tokens, cotangent, smalls, cos8, sin8)


QB = 256
SPAN = WINDOW + QB


CHUNK = 256
SAFE_SCORE = 60.0


def attend(q, k, v, d_out, seg_q, seg_k, cos8, sin8):
    rows = q.shape[0]
    blocks = rows // QB
    pairs = HEADS // 2
    scale = HEAD ** (-0.5)
    half = ROT // 2
    n = SPAN // CHUNK

    def heads_apart(x):
        row = lax.broadcasted_iota(jnp.int32, x.shape, 0)
        zero = jnp.zeros_like(x)
        return jnp.concatenate([jnp.where(row < HEAD, x, zero), jnp.where(row < HEAD, zero, x)], axis=1)

    def stacked(x):
        lane = lax.broadcasted_iota(jnp.int32, x.shape, 1)
        zero = jnp.zeros_like(x)
        return jnp.concatenate([jnp.where(lane < HEAD, x, zero), jnp.where(lane < HEAD, zero, x)], axis=0)

    def fold(x, op):
        return op(x.reshape(x.shape[0] // 8, 8, x.shape[1]), axis=0)

    def two(x):
        return jnp.concatenate([x, x], axis=1)

    def kernel(
        q_ref, k_ref, v_ref, do_ref, sq_ref, sk_ref, cos_ref, sin_ref,
        o_ref, dq_ref, dk_ref, dv_ref, halo_ref, peak_ref, bias, kt, vt, el_ref, ds_ref, dks, dvs,
    ):
        p = pl.program_id(0)

        @pl.when(p == 0)
        def _():
            gap = (
                WINDOW
                + lax.broadcasted_iota(jnp.int32, (SPAN, QB), 1)
                - lax.broadcasted_iota(jnp.int32, (SPAN, QB), 0)
            )
            for i in range(blocks):
                same = sk_ref[i * QB : i * QB + SPAN, :] == sq_ref[:, i * QB : (i + 1) * QB]
                bias[i] = jnp.where((gap >= 0) & (gap < WINDOW) & same, 0.0, MASKED)

        kt[...] = k_ref[...].T
        vt[...] = v_ref[...].T
        k_float = kt[...].astype(F32)
        q_float = q_ref[...].astype(F32) * scale
        reach = jnp.max(jnp.sum(k_float * k_float, axis=0)) * jnp.max(jnp.sum(q_float * q_float, axis=1))
        safe = reach < SAFE_SCORE * SAFE_SCORE

        def keys_at(ref, i, c):
            return ref[i * QB + c * CHUNK : i * QB + (c + 1) * CHUNK, :]

        def prepare(i):
            q_all = (q_ref[i * QB : (i + 1) * QB, :].astype(F32) * scale).astype(BF16)
            return q_all, heads_apart(q_all.T)

        def scores(i, c, q_apart):
            return dot(keys_at(k_ref, i, c), q_apart) + two(bias[i, c * CHUNK : (c + 1) * CHUNK])

        def forward(i, q_apart, shifted, found):
            base = None
            if shifted:
                for c in range(n):
                    t = fold(scores(i, c, q_apart), jnp.max)
                    base = t if c == 0 else jnp.maximum(base, t)
                base = jnp.max(base, axis=0, keepdims=True)
            top8 = sum8 = None
            for c in range(n):
                st = scores(i, c, q_apart)
                e = jnp.exp(st - base if shifted else st)
                el_ref[i % 2, c * CHUNK : (c + 1) * CHUNK] = e.astype(BF16)
                t, u = fold(st, jnp.max), fold(e, jnp.sum)
                top8, sum8 = (t, u) if c == 0 else (jnp.maximum(top8, t), sum8 + u)
                yield
            found.append(jnp.max(top8, axis=0, keepdims=True))
            found.append(1.0 / jnp.sum(sum8, axis=0, keepdims=True))

        def per_head(x):
            return jnp.concatenate(
                [jnp.broadcast_to(x[:, :QB], (HEAD, QB)), jnp.broadcast_to(x[:, QB:], (HEAD, QB))], axis=0
            )

        def both(t, x_ref, i):
            span = slice(i * QB, i * QB + SPAN)
            return jnp.concatenate(
                [dot(t[:HEAD, span], x_ref[i % 2, :, :QB]), dot(t[HEAD:, span], x_ref[i % 2, :, QB:])], axis=0
            )

        def output(i, inv):
            raw = both(vt, el_ref, i)
            inv2 = per_head(inv)
            o_ref[i * QB : (i + 1) * QB, :] = (raw * inv2).T.astype(BF16)
            do_s = (do_ref[i * QB : (i + 1) * QB, :].astype(F32).T * inv2).astype(BF16)
            m = do_s.astype(F32) * raw
            mean = jnp.concatenate(
                [jnp.sum(m[:HEAD], axis=0, keepdims=True), jnp.sum(m[HEAD:], axis=0, keepdims=True)], axis=1
            )
            return do_s, mean * inv

        def score_grads(i, do_s, mean):
            do_apart = heads_apart(do_s)
            for c in range(n):
                w = slice(c * CHUNK, (c + 1) * CHUNK)
                dpt = dot(keys_at(v_ref, i, c), do_apart)
                ds_ref[i % 2, w] = (el_ref[i % 2, w].astype(F32) * (dpt - mean)).astype(BF16)

        def input_grads(i, q_all, do_s):
            do_rows = stacked(do_s.T)
            q_rows = stacked(q_all)
            for c in range(n):
                w = slice(c * CHUNK, (c + 1) * CHUNK)
                at = slice(i * QB + c * CHUNK, i * QB + (c + 1) * CHUNK)
                v_part = dot(el_ref[i % 2, w], do_rows)
                k_part = dot(ds_ref[i % 2, w], q_rows)
                if i == 0 or c == n - 1:
                    dvs[at, :] = v_part
                    dks[at, :] = k_part
                else:
                    dvs[at, :] += v_part
                    dks[at, :] += k_part
                yield
            dq = both(kt, ds_ref, i) * scale
            cos_t, sin_t = cos_ref[:, i * QB : (i + 1) * QB], sin_ref[:, i * QB : (i + 1) * QB]
            turned = []
            for h in range(2):
                f, g = dq[h * HEAD : h * HEAD + half], dq[h * HEAD + half : h * HEAD + ROT]
                turned += [f * cos_t + g * sin_t, g * cos_t - f * sin_t, dq[h * HEAD + ROT : (h + 1) * HEAD]]
            dq_ref[i * QB : (i + 1) * QB, :] = jnp.concatenate(turned, axis=0).T.astype(BF16)
            yield

        def run(shifted):
            top = held = None
            for i in range(blocks + 1):
                parts, found = [], []
                if held is not None:
                    parts.append(input_grads(i - 1, *held))
                if i < blocks:
                    q_all, q_apart = prepare(i)
                    parts.append(forward(i, q_apart, shifted, found))
                interleave(*parts)
                if i < blocks:
                    t, inv = found
                    top = t if top is None else jnp.maximum(top, t)
                    do_s, mean = output(i, inv)
                    score_grads(i, do_s, mean)
                    held = (q_all, do_s)
            peak_ref[...] = jnp.broadcast_to(top, peak_ref.shape)
            halo_ref[0] = dks[:rows, :].astype(BF16)
            halo_ref[1] = dvs[:rows, :].astype(BF16)
            dk_ref[...] = dks[rows:, :]
            dv_ref[...] = dvs[rows:, :]

        @pl.when(safe)
        def _():
            run(False)

        @pl.when(jnp.logical_not(safe))
        def _():
            run(True)

    block = pl.BlockSpec((rows, BLK), lambda p: (0, p))
    keys = pl.BlockSpec((2 * rows, BLK), lambda p: (0, p))
    whole = lambda *shape: pl.BlockSpec(shape, lambda p: (0, 0))
    return pl.pallas_call(
        kernel,
        grid=(pairs,),
        in_specs=[
            block, keys, keys, block, whole(1, rows), whole(2 * rows, 1), whole(half, rows), whole(half, rows),
        ],
        out_specs=[
            block, block, block, block,
            pl.BlockSpec((2, rows, BLK), lambda p: (0, 0, p)),
            pl.BlockSpec((8, 2 * QB), lambda p: (p, 0)),
        ],
        out_shape=[
            jax.ShapeDtypeStruct((rows, D), BF16),
            jax.ShapeDtypeStruct((rows, D), BF16),
            jax.ShapeDtypeStruct((rows, D), F32),
            jax.ShapeDtypeStruct((rows, D), F32),
            jax.ShapeDtypeStruct((2, rows, D), BF16),
            jax.ShapeDtypeStruct((8 * pairs, 2 * QB), F32),
        ],
        scratch_shapes=[
            pltpu.VMEM((blocks, SPAN, QB), F32),
            pltpu.VMEM((BLK, 2 * rows), BF16),
            pltpu.VMEM((BLK, 2 * rows), BF16),
            pltpu.VMEM((2, SPAN, 2 * QB), BF16),
            pltpu.VMEM((2, SPAN, 2 * QB), BF16),
            pltpu.VMEM((2 * rows, BLK), F32),
            pltpu.VMEM((2 * rows, BLK), F32),
        ],
        compiler_params=params(dimension_semantics=("arbitrary",)),
        cost_estimate=pl.CostEstimate(flops=40 << 30, bytes_accessed=32 << 20, transcendentals=20 << 20),
        name="attend",
    )(q, k, v, d_out, seg_q, seg_k, cos8, sin8)


FB = 512


def gelu_parts(v):
    a = jnp.abs(v)
    t = 1.0 / (1.0 + a * (0.3275911 * 0.7071067811865476))
    poly = t * (
        0.5 * 0.254829592
        + t * (0.5 * -0.284496736 + t * (0.5 * 1.421413741 + t * (0.5 * -1.453152027 + t * (0.5 * 1.061405429))))
    )
    e = jnp.exp(v * v * -0.5)
    tail = poly * e
    cdf = jnp.where(v >= 0, 1.0 - tail, tail)
    return v * cdf, cdf + v * e * 0.3989422804014327


def feed_forward(w_rows, g_rows, w_all, m, cotangent, b_up):
    rows = m.shape[0]
    steps = FF // FB

    def kernel(
        w_rows_ref, g_rows_ref, w_ref, m_ref, g_ref, b_ref, out_ref, dm_ref, db_ref, gr_ref,
        mt, wup, wdn, hs, dus, gup, gdn, u_ref, h_ref, wsem, gsem,
    ):
        f = pl.program_id(0)
        slot = f % 2
        per = FB // BLK

        def up_at(buf, t):
            return buf.at[pl.ds(pl.multiple_of((t // per) * BLK, BLK), BLK), pl.ds(pl.multiple_of((t % per) * BLK, BLK), BLK)]

        def up_tile(ff, t):
            return UP_BASE + (t // per) * (FF // BLK) + ff * per + t % per

        def down_at(buf, t):
            return buf.at[pl.ds(pl.multiple_of((t // 8) * BLK, BLK), BLK), pl.ds(pl.multiple_of((t % 8) * BLK, BLK), BLK)]

        def down_tile(ff, t):
            return DOWN_BASE + ff * per * 8 + t

        def fetch_one(ff, sl, t):
            src = w_ref.at[pl.ds(pl.multiple_of(w_rows_ref[up_tile(ff, t)], 16), BLK)]
            pltpu.make_async_copy(src, up_at(wup.at[sl], t), wsem.at[0, sl]).start()
            src = w_ref.at[pl.ds(pl.multiple_of(w_rows_ref[down_tile(ff, t)], 16), BLK)]
            pltpu.make_async_copy(src, down_at(wdn.at[sl], t), wsem.at[1, sl]).start()

        def store_one(ff, sl, t):
            dst = gr_ref.at[pl.ds(pl.multiple_of(g_rows_ref[up_tile(ff, t)], 16), BLK)]
            pltpu.make_async_copy(up_at(gup.at[sl], t), dst, gsem.at[0, sl]).start()
            dst = gr_ref.at[pl.ds(pl.multiple_of(g_rows_ref[down_tile(ff, t)], 16), BLK)]
            pltpu.make_async_copy(down_at(gdn.at[sl], t), dst, gsem.at[1, sl]).start()

        def whole_wait(buf, sem):
            pltpu.make_async_copy(buf, buf, sem).wait()

        count = 8 * per

        @pl.when(f == 0)
        def _():
            tile_loop(0, count, lambda t: fetch_one(0, 0, t))
            mt[...] = m_ref[...].T
            out_ref[...] = jnp.zeros_like(out_ref)
            dm_ref[...] = jnp.zeros_like(dm_ref)

        whole_wait(wup.at[slot], wsem.at[0, slot])
        whole_wait(wdn.at[slot], wsem.at[1, slot])

        @pl.when(f >= 2)
        def _():
            whole_wait(gup.at[slot], gsem.at[0, slot])
            whole_wait(gdn.at[slot], gsem.at[1, slot])

        n = rows // ROWB

        def stage1(c):
            at = slice(c * ROWB, (c + 1) * ROWB)
            for k in range(FB // 256):
                cols = slice(k * 256, (k + 1) * 256)
                u_ref[c % 2, :, cols] = dot(m_ref[at, :], wup[slot, :, cols]) + b_ref[:, cols]
                yield
                h_ref[c % 2, :, cols] = dot(g_ref[at, :], wdn[slot, cols, :], NT)
                yield

        db = [None]

        def stage2(c):
            step = ROWB // 8
            for k in range(8):
                at = slice(k * step, (k + 1) * step)
                to = slice(c * ROWB + k * step, c * ROWB + (k + 1) * step)
                hidden, slope = gelu_parts(u_ref[c % 2, at, :])
                hs[to, :] = hidden.astype(BF16)
                du = (h_ref[c % 2, at, :] * slope).astype(BF16)
                dus[to, :] = du
                t = jnp.sum(du.astype(F32).reshape(step // 8, 8, FB), axis=0)
                db[0] = t if db[0] is None else db[0] + t
                yield

        def stage3(c):
            at = slice(c * ROWB, (c + 1) * ROWB)
            for k in range(D // 256):
                cols = slice(k * 256, (k + 1) * 256)
                out_ref[at, cols] += dot(hs[at, :], wdn[slot, :, cols])
                yield
                dm_ref[at, cols] += dot(dus[at, :], wup[slot, cols, :], NT)
                yield

        nxt = jnp.minimum(f + 1, steps - 1)
        for t in range(count):
            fetch_one(nxt, 1 - slot, t)

        for c in range(n + 2):
            gens = []
            if c < n:
                gens.append(stage1(c))
            if 0 <= c - 1 < n:
                gens.append(stage2(c - 1))
            if 0 <= c - 2 < n:
                gens.append(stage3(c - 2))
            interleave(*gens)
        db_ref[...] = jnp.sum(db[0], axis=0, keepdims=True)
        gdn[slot] = dot(hs[...], g_ref[...], TN).astype(BF16)
        gup[slot] = dot(mt[...], dus[...]).astype(BF16)
        for t in range(count):
            store_one(f, slot, t)


        @pl.when(f == steps - 1)
        def _():
            whole_wait(wup.at[1 - slot], wsem.at[0, 1 - slot])
            whole_wait(wdn.at[1 - slot], wsem.at[1, 1 - slot])
            for sl in range(2):
                whole_wait(gup.at[sl], gsem.at[0, sl])
                whole_wait(gdn.at[sl], gsem.at[1, sl])

    full = pl.BlockSpec((rows, D), lambda f, *_: (0, 0))
    bias = pl.BlockSpec((1, FB), lambda f, *_: (0, f))
    return pl.pallas_call(
        kernel,
        grid_spec=pltpu.PrefetchScalarGridSpec(
            num_scalar_prefetch=2,
            grid=(steps,),
            in_specs=[ANY, full, full, bias],
            out_specs=[full, full, bias, ANY],
            scratch_shapes=[
                pltpu.VMEM((D, rows), BF16),
                pltpu.VMEM((2, D, FB), BF16),
                pltpu.VMEM((2, FB, D), BF16),
                pltpu.VMEM((rows, FB), BF16),
                pltpu.VMEM((rows, FB), BF16),
                pltpu.VMEM((2, D, FB), BF16),
                pltpu.VMEM((2, FB, D), BF16),
                pltpu.VMEM((2, ROWB, FB), F32),
                pltpu.VMEM((2, ROWB, FB), F32),
                pltpu.SemaphoreType.DMA((2, 2)),
                pltpu.SemaphoreType.DMA((2, 2)),
            ],
        ),
        out_shape=[
            jax.ShapeDtypeStruct((rows, D), F32),
            jax.ShapeDtypeStruct((rows, D), F32),
            jax.ShapeDtypeStruct((1, FF), F32),
            jax.ShapeDtypeStruct((TILES * BLK, BLK), BF16),
        ],
        compiler_params=params(dimension_semantics=("arbitrary",)),
        cost_estimate=pl.CostEstimate(flops=52 << 30, bytes_accessed=48 << 20, transcendentals=8 << 20),
        name="feed_forward",
    )(w_rows, g_rows, w_all, m, cotangent, b_up)


def finish(
    w_rows, g_rows, w_all, tokens, cotangent, smalls, attn_out, mlp_out, dm, dq, dk, dv, halo, tables, grads
):
    rows = tokens.shape[0]
    steps = rows // ROWB
    q_cols = 3 * D // FB
    o_cols = D // FB
    per = FB // BLK
    last = steps + q_cols + o_cols
    cos8, sin8 = tables

    def kernel(
        w_rows_ref, g_rows_ref, w_ref, tok_ref, g_ref, small_ref, o_ref, mlp_ref, dm_ref, dq_ref, dk_ref, dv_ref,
        halo_ref, cos_ref, sin_ref, _,
        out_ref, dx_ref, sum_ref, gr_ref, wqkv, wo, at, dp, stage, sems, gsem,
    ):
        i = pl.program_id(0)

        def fetch(first, count, width, dst, sem):
            def body(t):
                src = w_ref.at[pl.ds(pl.multiple_of(w_rows_ref[first + t], 16), BLK)]
                r, c = t // width, t % width
                to = dst.at[pl.ds(pl.multiple_of(r * BLK, BLK), BLK), pl.ds(pl.multiple_of(c * BLK, BLK), BLK)]
                pltpu.make_async_copy(src, to, sem).start()

            tile_loop(0, count, body)

        @pl.when(i == 0)
        def _():
            fetch(OUT_BASE, OUT_TILES, D // BLK, wo, sems.at[0])
            fetch(0, QKV_TILES, 3 * D // BLK, wqkv, sems.at[1])
            sum_ref[...] = jnp.zeros_like(sum_ref)
            pltpu.make_async_copy(wo, wo, sems.at[0]).wait()

        @pl.when(i < steps)
        def _():
            here = pl.ds(pl.multiple_of(i * ROWB, ROWB), ROWB)
            x = tok_ref[...].astype(F32)
            grad = g_ref[here, :].astype(F32)
            normed, inv = norm_rows(x)
            g1, g2 = small_ref[4:5, :], small_ref[6:7, :]
            attn = dot(o_ref[here, :], wo[...]) + small_ref[2:3, :]
            out_ref[...] = (x + attn + (mlp_ref[...] + small_ref[3:4, :])).astype(BF16)
            dk_all = dk_ref[...].astype(F32) + halo_ref[0].astype(F32)
            dk_all = rope_rows(dk_all, *spread_tables(cos_ref[...], -sin_ref[...]))
            dv_low = (dv_ref[...].astype(F32) + halo_ref[1].astype(F32)).astype(BF16)
            dq_low = dq_ref[...]
            dp[here, :D] = dq_low
            dp[here, D : 2 * D] = dk_all.astype(BF16)
            dp[here, 2 * D :] = dv_low

            @pl.when(i == 0)
            def _():
                pltpu.make_async_copy(wqkv, wqkv, sems.at[1]).wait()

            da = dot(dp[here, :], wqkv[...], NT)
            at[:, here] = (normed * g1 + small_ref[5:6, :]).astype(BF16).T
            dmv = dm_ref[...]
            dn = da * g1 + dmv * g2
            mean_dn = jnp.mean(dn, axis=-1, keepdims=True)
            mean_dnn = jnp.mean(dn * normed, axis=-1, keepdims=True)
            dx_ref[...] = grad + inv * (dn - mean_dn - normed * mean_dnn)

            def add(row, value):
                sum_ref[row : row + 1, :] += jnp.sum(value, axis=0, keepdims=True)

            add(0, dq_low.astype(F32))
            add(1, dv_low.astype(F32))
            add(2, grad)
            add(3, da * normed)
            add(4, da)
            add(5, dmv * normed)
            add(6, dmv)

        slot = i % 2

        def drain(sl):
            pltpu.make_async_copy(stage.at[sl], stage.at[sl], gsem.at[sl]).wait()

        def send(first, width, c):
            for t in range(8 * per):
                tile = first + (t // per) * width + c * per + t % per
                dst = gr_ref.at[pl.ds(pl.multiple_of(g_rows_ref[tile], 16), BLK)]
                r, k = t // per * BLK, t % per * BLK
                pltpu.make_async_copy(stage.at[slot, r : r + BLK, k : k + BLK], dst, gsem.at[slot]).start()

        @pl.when(i >= steps + 2)
        def _():
            drain(slot)

        @pl.when((i >= steps) & (i < steps + q_cols))
        def _():
            c = i - steps
            stage[slot] = dot(at[...], dp[:, pl.ds(pl.multiple_of(c * FB, FB), FB)]).astype(BF16)
            send(0, 3 * D // BLK, c)

        @pl.when(i >= steps + q_cols)
        def _():
            c = i - steps - q_cols
            stage[slot] = dot(o_ref[...], g_ref[:, pl.ds(pl.multiple_of(c * FB, FB), FB)], TN).astype(BF16)
            send(OUT_BASE, D // BLK, c)

        @pl.when(i == last - 1)
        def _():
            drain(0)
            drain(1)

    here = lambda i, *_: (jnp.minimum(i, steps - 1), 0)
    whole = lambda *shape: pl.BlockSpec(shape, lambda i, *_: (0, 0))
    block = pl.BlockSpec((ROWB, D), here)
    table = pl.BlockSpec((ROT // 2, ROWB), lambda i, *_: (0, steps + jnp.minimum(i, steps - 1)))
    return pl.pallas_call(
        kernel,
        grid_spec=pltpu.PrefetchScalarGridSpec(
            num_scalar_prefetch=2,
            grid=(last,),
            in_specs=[
                ANY, block, whole(rows, D), whole(16, D), whole(rows, D), block, block, block, block, block,
                pl.BlockSpec((2, ROWB, D), lambda i, *_: (0, jnp.minimum(i, steps - 1), 0)), table, table, ANY,
            ],
            out_specs=[block, block, whole(8, D), ANY],
            scratch_shapes=[
                pltpu.VMEM((D, 3 * D), BF16),
                pltpu.VMEM((D, D), BF16),
                pltpu.VMEM((D, rows), BF16),
                pltpu.VMEM((rows, 3 * D), BF16),
                pltpu.VMEM((2, D, FB), BF16),
                pltpu.SemaphoreType.DMA((2,)),
                pltpu.SemaphoreType.DMA((2,)),
            ],
        ),
        out_shape=[
            jax.ShapeDtypeStruct((rows, D), BF16),
            jax.ShapeDtypeStruct((rows, D), F32),
            jax.ShapeDtypeStruct((8, D), F32),
            jax.ShapeDtypeStruct(grads.shape, BF16),
        ],
        input_output_aliases={15: 3},
        compiler_params=params(dimension_semantics=("arbitrary",)),
        name="finish",
    )(w_rows, g_rows, w_all, tokens, cotangent, smalls, attn_out, mlp_out, dm, dq, dk, dv, halo, cos8, sin8, grads)


def halves(x):
    high = x.astype(BF16)
    return high, (x - high.astype(F32)).astype(BF16)


def dot3(a, b, dims=NN):
    return dot(a[0], b[0], dims) + (dot(a[0], b[1], dims) + dot(a[1], b[0], dims))


def update_tiles(grads, tiles, left, right, first, second, scale):
    count = tiles.shape[0]
    group = max(g for g in (1, 2, 3, 4, 6, 8) if count % g == 0)

    def kernel(g_ref, w_ref, l_ref, r_ref, m_ref, v_ref, s_ref, w_out, low_out, m_out, v_out):
        turned = []
        for t in range(group):
            l, r = halves(l_ref[t]), halves(r_ref[t])
            turned.append(dot3(halves(dot3(l, halves(g_ref[t]), TN)), r))
        for t in range(group):
            l, r = halves(l_ref[t]), halves(r_ref[t])
            m_new = BETA * m_ref[t] + (1.0 - BETA) * turned[t]
            v_new = BETA * v_ref[t] + (1.0 - BETA) * turned[t] * turned[t]
            ratio = m_new / (jnp.sqrt(v_new) + ADAM_EPS)
            back = dot3(halves(dot3(l, halves(ratio))), r, NT)
            w_new = (w_ref[t] - LEARN * back) * s_ref[t]
            w_out[t] = w_new
            low_out[t] = w_new.astype(BF16)
            m_out[t] = m_new
            v_out[t] = v_new

    block = pl.BlockSpec((group, BLK, BLK), lambda i: (i, 0, 0))
    row = pl.BlockSpec((group, 1, BLK), lambda i: (i, 0, 0))
    like = lambda t: jax.ShapeDtypeStruct(tiles.shape, t)
    return pl.pallas_call(
        kernel,
        grid=(count // group,),
        in_specs=[block] * 6 + [row],
        out_specs=[block] * 4,
        out_shape=[like(F32), like(BF16), like(F32), like(F32)],
        compiler_params=params(dimension_semantics=("arbitrary",)),
        name="update_tiles",
    )(grads, tiles, left, right, first, second, scale)


def column_scales(tile_ids, factors):
    columns = (tile_ids % (3 * D // BLK))[:, None] * BLK + jnp.arange(BLK, dtype=jnp.int32)[None, :]
    head_index = columns % D // HEAD
    root_factor = jnp.sqrt(factors)
    picked = jnp.sum(
        jnp.where(head_index[..., None] == jnp.arange(HEADS, dtype=jnp.int32), root_factor, 0.0),
        axis=-1,
    )
    clipped = (tile_ids[:, None] < QKV_TILES) & (columns < 2 * D)
    return jnp.where(clipped, picked, 1.0)


def small_update(grads, params_, first_moment, second_moment):
    first_new = BETA * first_moment + (1.0 - BETA) * grads
    second_new = BETA * second_moment + (1.0 - BETA) * grads * grads
    updated = params_ - SMALL_LEARN * first_new / (jnp.sqrt(second_new) + ADAM_EPS)
    return (updated, first_new, second_new)


def passed_along(value, axis, steps):
    count = lax.axis_size(axis)
    leading, last = (max(0, -steps), min(count, count - steps))
    return lax.ppermute(value, axis, [(source, source + steps) for source in range(leading, last)])


def on_device(
    ring,
    tokens,
    segments,
    cotangent,
    tile_of_slot,
    tiles,
    left_bases,
    right_bases,
    first_moments,
    second_moments,
    small_params,
    small_first,
    small_second,
    threshold,
):
    rows = tokens.shape[0]
    slot_count = tiles.shape[0]
    small_count = small_params.shape[0]
    axes = ("dp", "seq")
    seq_index = lax.axis_index("seq")
    owner_index = lax.axis_index(axes)
    first_place = seq_index * rows
    seg_local = segments.reshape(1, rows)

    numbers = jnp.arange(TILES, dtype=jnp.int32)
    slot_of_tile = jnp.sum(
        jnp.where(tile_of_slot[None, :] == numbers[:, None], numbers[None, :], 0), axis=1
    ).astype(jnp.int32)
    g_rows = slot_of_tile * BLK

    if ring:
        small_block = jnp.zeros((16 * BLK,), BF16).at[:small_count].set(small_params.astype(BF16))
        payload = jnp.concatenate(
            [tiles.astype(BF16).reshape(slot_count * BLK, BLK), small_block.reshape(16, BLK)], axis=0
        )
        seg_rows = jnp.broadcast_to(seg_local, (8, rows))
        gathered, prev_tokens, prev_seg = gather_weights(payload, tokens, seg_rows)
        stride = payload.shape[0]
        w_all = gathered.reshape(-1, BLK)
        w_rows = slot_of_tile // slot_count * stride + slot_of_tile % slot_count * BLK
        tail = slot_count * BLK
        small_all = gathered[:, tail : tail + small_count // BLK, :].reshape(SMALL)
        prev_seg = prev_seg[:1]
    else:
        w_all = lax.all_gather(tiles.astype(BF16), axes, axis=0, tiled=True).reshape(-1, BLK)
        w_rows = g_rows
        small_all = lax.all_gather(small_params.astype(BF16), axes, axis=0, tiled=True)
        prev_tokens, prev_seg = passed_along((tokens, seg_local), "seq", 1)

    table = small_all.astype(F32).reshape(D, 12)
    smalls = jnp.concatenate(
        [
            jnp.stack([table[:, r] for r in (0, 1, 2, 7, 8, 9, 10, 11)], axis=0),
            jnp.zeros((8, D), F32),
        ],
        axis=0,
    )
    b_up = table[:, 3:7].reshape(1, FF)

    half = ROT // 2
    exponent = jnp.arange(half, dtype=F32) * (2.0 / ROT)
    frequency = jnp.power(ROPE_BASE, -exponent)
    places = first_place - rows + jnp.arange(2 * rows, dtype=jnp.int32)
    angle = places.astype(F32)[None, :] * frequency[:, None]
    cos8, sin8 = jnp.cos(angle), jnp.sin(angle)
    tables = (cos8, sin8)

    prev_seg = jnp.where(seq_index == 0, -1, prev_seg)
    seg_k = jnp.concatenate([prev_seg, seg_local], axis=1).reshape(2 * rows, 1)

    q, k, v, d_out, m = project(w_rows, w_all, prev_tokens, tokens, cotangent, smalls, tables)
    attn_out, dq, dk, dv, halo, peaks = attend(
        q, k, v, d_out, seg_local, seg_k, cos8[:, rows:], sin8[:, rows:]
    )
    halo = passed_along(halo, "seq", -1)
    mlp_out, dm, db_up, grads = feed_forward(w_rows, g_rows, w_all, m, cotangent, b_up)
    block_output, input_grad, sums, grads = finish(
        w_rows, g_rows, w_all, tokens, cotangent, smalls, attn_out, mlp_out, dm, dq, dk, dv, halo, tables, grads
    )

    small_terms = jnp.concatenate(
        [
            sums[:3].T,
            db_up.reshape(D, FF // D),
            sums[2:7].T,
        ],
        axis=1,
    ).reshape(SMALL)
    head_peak = jnp.max(peaks.reshape(HEADS // 2, 8, 2, QB)[:, 0], axis=-1).reshape(HEADS)
    if ring:
        peak_rows = jnp.zeros((8, BLK), F32).at[:, :HEADS].set(head_peak[None, :])
        extra = jnp.concatenate([small_terms.reshape(SMALL_ROWS, BLK), peak_rows], axis=0)
        tile_grads, extra = sum_gradients(grads, extra)
        tile_grads = tile_grads.reshape(slot_count, BLK, BLK)
        small_grads = lax.dynamic_slice_in_dim(
            extra[:SMALL_ROWS].reshape(SMALL), owner_index * small_count, small_count, 0
        )
        head_peak = extra[SMALL_ROWS, :HEADS]
    else:
        tile_grads = lax.psum_scatter(
            grads.astype(F32).reshape(TILES, BLK, BLK), axes, scatter_dimension=0, tiled=True
        )
        small_grads = lax.psum_scatter(small_terms, axes, scatter_dimension=0, tiled=True)
        head_peak = lax.pmax(head_peak, axes)

    local_ids = lax.dynamic_slice_in_dim(tile_of_slot, owner_index * slot_count, slot_count, 0)
    limit = threshold[0]
    factors = limit / jnp.maximum(head_peak, limit)
    scale = column_scales(local_ids, factors).reshape(slot_count, 1, BLK)
    new_tiles, new_low, new_first, new_second = update_tiles(
        tile_grads, tiles, left_bases, right_bases, first_moments, second_moments, scale
    )
    new_small, new_small_first, new_small_second = small_update(
        small_grads, small_params, small_first, small_second
    )
    return (
        block_output,
        input_grad,
        tile_grads,
        small_grads,
        new_tiles,
        new_low,
        new_first,
        new_second,
        new_small,
        new_small.astype(BF16),
        new_small_first,
        new_small_second,
        factors,
    )


def solution(mesh):
    split = P(("dp", "seq"))
    in_specs = (split, P("dp", "seq"), split, P()) + (split,) * 8 + (P(),)
    out_specs = (split,) * 12 + (P(),)
    ring = (mesh.shape["dp"], mesh.shape["seq"]) == (4, 8)
    return jax.shard_map(
        functools.partial(on_device, ring), mesh=mesh, in_specs=in_specs, out_specs=out_specs, check_vma=False
    )
```

```python
import functools

import jax
import jax.numpy as jnp
from jax import lax
from jax.experimental import pallas as pl
from jax.experimental.pallas import tpu as pltpu
from jax.sharding import PartitionSpec as P

D = 1024
FF = 4096
HEADS = 16
HEAD = 64
ROT = 16
BLK = 128
WINDOW = 1024
TILES = 768
SMALL = 12288
QKV_TILES = D // BLK * (3 * D // BLK)
OUT_TILES = D // BLK * (D // BLK)
UP_TILES = D // BLK * (FF // BLK)
OUT_BASE = QKV_TILES
UP_BASE = QKV_TILES + OUT_TILES
DOWN_BASE = UP_BASE + UP_TILES

NORM_EPS = 1e-05
ADAM_EPS = 1e-08
BETA = 0.5
LEARN = 0.03
SMALL_LEARN = 0.2
ROPE_BASE = 10000.0
MASKED = -1e30
HIGH = lax.Precision.HIGHEST

F32 = jnp.float32
BF16 = jnp.bfloat16
MESH = pl.DeviceIdType.MESH
ANY = pl.BlockSpec(memory_space=pl.ANY)
VMEM = pl.BlockSpec(memory_space=pltpu.VMEM)
VMEM_LIMIT = 58 << 20

NN = (((1,), (0,)), ((), ()))
NT = (((1,), (1,)), ((), ()))
TN = (((0,), (0,)), ((), ()))


def dot(a, b, dims=NN, precision=None):
    return lax.dot_general(a, b, dims, precision=precision, preferred_element_type=F32)


def interleave(*parts):
    live = list(parts)
    while live:
        for part in list(live):
            try:
                next(part)
            except StopIteration:
                live.remove(part)


def params(**kw):
    return pltpu.CompilerParams(vmem_limit_bytes=VMEM_LIMIT, **kw)


def norm_rows(x):
    centered = x - jnp.mean(x, axis=-1, keepdims=True)
    inv = lax.rsqrt(jnp.mean(centered * centered, axis=-1, keepdims=True) + NORM_EPS)
    return centered * inv, inv


def tile_loop(first, count, body):
    def step(t, carry):
        body(t)
        return carry

    lax.fori_loop(first, first + count, step, 0)


ROWS_PER_TILE = BLK
HALF_ROWS = 1536


def gather_weights(payload, tokens, seg_rows):
    rows = payload.shape[0]
    top = pl.ds(0, HALF_ROWS)
    low = pl.ds(HALF_ROWS, rows - HALF_ROWS)

    def kernel(x_ref, tok_ref, seg_ref, out_ref, ptok_ref, pseg_ref, lsem, ss, rs, hss, hrs, hls):
        d = lax.axis_index("dp")
        s = lax.axis_index("seq")
        z = s // 2
        c = s % 2
        xn = d + 1 - 2 * (d % 2)
        yn = d + 2 - 4 * (d // 2)
        xyn = 3 - d
        sib = z * 2 + 1 - c
        halo = s - 1 + 2 * c
        halo_ok = ((c == 0) & (z > 0)) | ((c == 1) & (z < 3))

        barrier = pltpu.get_barrier_semaphore()

        def greet(dev):
            pl.semaphore_signal(barrier, inc=1, device_id=dev, device_id_type=MESH)

        greet((d, sib))
        greet((xn, s))
        greet((yn, s))

        @pl.when(z > 0)
        def _():
            greet((d, s - 2))

        @pl.when(z < 3)
        def _():
            greet((d, s + 2))

        @pl.when(halo_ok)
        def _():
            greet((d, halo))

        below, above = (z + 2) // 3, (5 - z) // 3
        pl.semaphore_wait(barrier, 3 + below + above + (1 - c) * below + c * above)

        def place(dd, zz):
            return out_ref.at[dd * 8 + zz * 2 + c]

        def remote(src, dst, kind, zz, dev):
            return pltpu.make_async_remote_copy(
                src_ref=src,
                dst_ref=dst,
                send_sem=ss.at[kind, zz],
                recv_sem=rs.at[kind, zz],
                device_id=dev,
                device_id_type=MESH,
            )

        def block_of(zz, own):
            return x_ref if own else place(d, zz)

        def up(zz, own):
            return remote(block_of(zz, own), place(d, zz), 0, zz, (d, s + 2))

        def down(zz, own):
            return remote(block_of(zz, own), place(d, zz), 1, zz, (d, s - 2))

        def to_x(zz, own):
            return remote(block_of(zz, own), place(d, zz), 2, zz, (xn, s))

        def to_y(zz, own):
            return remote(block_of(zz, own), place(d, zz), 3, zz, (yn, s))

        def on_y(zz):
            return remote(place(xn, zz).at[top], place(xn, zz).at[top], 4, zz, (yn, s))

        def on_x(zz):
            return remote(place(yn, zz).at[low], place(yn, zz).at[low], 5, zz, (xn, s))

        def to_sib(dd, zz, kind, own=False):
            src = x_ref if own else place(dd, zz)
            return remote(src, place(dd, zz), kind, zz, (d, sib))

        def from_x(zz):
            return remote(x_ref, place(xn, zz), 2, zz, (xn, s))

        def from_y(zz):
            return remote(x_ref, place(yn, zz), 3, zz, (yn, s))

        def diag_up(zz):
            return remote(place(xyn, zz), place(xyn, zz), 10, zz, (d, s + 2))

        def diag_down(zz):
            return remote(place(xyn, zz), place(xyn, zz), 11, zz, (d, s - 2))

        def diag_top(zz):
            return remote(x_ref.at[top], place(xyn, zz).at[top], 4, zz, (yn, s))

        def diag_low(zz):
            return remote(x_ref.at[low], place(xyn, zz).at[low], 5, zz, (xn, s))

        order = [z, 1 + z % 2, (2 + 3 * z) % 5, 3 * (1 - z // 2)]
        local = pltpu.make_async_copy(x_ref, place(d, z), lsem)
        local.start()

        def halo_copies(dev):
            tok = pltpu.make_async_remote_copy(
                src_ref=tok_ref,
                dst_ref=ptok_ref,
                send_sem=hss.at[0],
                recv_sem=hrs.at[0],
                device_id=dev,
                device_id_type=MESH,
            )
            seg = pltpu.make_async_remote_copy(
                src_ref=seg_ref,
                dst_ref=pseg_ref,
                send_sem=hss.at[1],
                recv_sem=hrs.at[1],
                device_id=dev,
                device_id_type=MESH,
            )
            return tok, seg

        def in_plane(k, body):
            if k == 0:
                body()
            else:
                pl.when((z - order[k] >= 2) | (order[k] - z >= 3))(body)

        def on_line(k, body):
            pl.when((z - order[k] < 2) & (order[k] - z < 3))(body)

        def launch(k):
            zz = order[k]
            own = k == 0
            if own:

                @pl.when(z < 3)
                def _():
                    up(zz, True).start()

                @pl.when(z > 0)
                def _():
                    down(zz, True).start()
            else:

                @pl.when(zz < z)
                def _():
                    up(zz, False).wait_recv()

                @pl.when((zz < z) & (z < 3))
                def _():
                    up(zz, False).start()

                @pl.when(zz > z)
                def _():
                    down(zz, False).wait_recv()

                @pl.when((zz > z) & (z > 0))
                def _():
                    down(zz, False).start()

            to_x(zz, own).start()
            to_y(zz, own).start()
            to_sib(d, zz, 6, own).start()

        def second(k):
            zz = order[k]

            def pass_on():
                from_x(zz).wait_recv()
                on_y(zz).start()
                to_sib(xn, zz, 7).start()
                from_y(zz).wait_recv()
                on_x(zz).start()
                to_sib(yn, zz, 8).start()

            in_plane(k, pass_on)

        def rest(k):
            zz = order[k]

            def share():
                from_x(zz).wait_recv()
                to_sib(xn, zz, 7).start()
                from_y(zz).wait_recv()
                to_sib(yn, zz, 8).start()

            on_line(k, share)

        def third(k):
            zz = order[k]

            def arrive():
                diag_top(zz).wait_recv()
                diag_low(zz).wait_recv()

            in_plane(k, arrive)
            if k > 0:

                @pl.when((zz < z) & (z - zz <= 1))
                def _():
                    diag_up(zz).wait_recv()

                @pl.when((zz > z) & (zz - z <= 2))
                def _():
                    diag_down(zz).wait_recv()

            if k < 3:

                @pl.when((zz == z) & (z < 3))
                def _():
                    diag_up(zz).start()

                @pl.when((zz >= z) & (zz - z <= 1) & (z > 0))
                def _():
                    diag_down(zz).start()

            to_sib(xyn, zz, 9).start()

        own_tok = pltpu.make_async_copy(tok_ref, ptok_ref, hls.at[0])
        own_seg = pltpu.make_async_copy(seg_ref, pseg_ref, hls.at[1])


        @pl.when(s == 0)
        def _():
            own_tok.start()
            own_seg.start()

        launch(0)
        launch(1)
        second(0)
        launch(2)
        launch(3)
        third(0)
        second(1)
        third(1)
        second(2)

        @pl.when(s < 7)
        def _():
            for cp in halo_copies((d, s + 1)):
                cp.start()

        second(3)
        rest(1)
        rest(2)
        rest(3)
        third(2)
        third(3)

        local.wait()
        other = 1 - c

        def sib_place(dd, zz):
            return out_ref.at[dd * 8 + zz * 2 + other]

        for k in range(4):
            zz = order[k]
            own = k == 0
            for kind, dd in ((6, d), (7, xn), (8, yn), (9, xyn)):
                remote(sib_place(dd, zz), sib_place(dd, zz), kind, zz, (d, sib)).wait_recv()
                to_sib(dd, zz, kind, own and kind == 6).wait_send()
            to_x(zz, own).wait_send()
            to_y(zz, own).wait_send()

            def halves_sent():
                on_y(zz).wait_send()
                on_x(zz).wait_send()

            in_plane(k, halves_sent)
            if k < 3:

                @pl.when((zz == z) & (z < 3))
                def _():
                    diag_up(zz).wait_send()

                @pl.when((zz >= z) & (zz - z <= 1) & (z > 0))
                def _():
                    diag_down(zz).wait_send()

            @pl.when((zz <= z) & (z < 3))
            def _():
                up(zz, own).wait_send()

            @pl.when((zz >= z) & (z > 0))
            def _():
                down(zz, own).wait_send()

        @pl.when(s < 7)
        def _():
            for cp in halo_copies((d, s + 1)):
                cp.wait_send()

        @pl.when(s > 0)
        def _():
            for cp in halo_copies((d, s - 1)):
                cp.wait_recv()

        @pl.when(s == 0)
        def _():
            own_tok.wait()
            own_seg.wait()

    return pl.pallas_call(
        kernel,
        out_shape=[
            jax.ShapeDtypeStruct((32, rows, BLK), BF16),
            jax.ShapeDtypeStruct(tokens.shape, BF16),
            jax.ShapeDtypeStruct(seg_rows.shape, jnp.int32),
        ],
        in_specs=[ANY, ANY, ANY],
        out_specs=[ANY, ANY, ANY],
        scratch_shapes=[
            pltpu.SemaphoreType.DMA,
            pltpu.SemaphoreType.DMA((12, 4)),
            pltpu.SemaphoreType.DMA((12, 4)),
            pltpu.SemaphoreType.DMA((2,)),
            pltpu.SemaphoreType.DMA((2,)),
            pltpu.SemaphoreType.DMA((2,)),
        ],
        compiler_params=params(collective_id=0, has_side_effects=True),
        name="gather_weights",
    )(payload, tokens, seg_rows)


OWNED = 24 * BLK
HALF = OWNED // 2
SMALL_ROWS = SMALL // BLK
EXTRA_ROWS = SMALL_ROWS + 8


def add_rows(dst, terms, rows, step=512):
    def body(i, carry):
        at = pl.ds(pl.multiple_of(i * step, step), step)
        if len(terms) == 2 and dst.dtype == BF16:
            dst[at] = terms[0][at] + terms[1][at]
        else:
            total = terms[0][at].astype(F32)
            for term in terms[1:]:
                total = total + term[at].astype(F32)
            dst[at] = total.astype(dst.dtype)
        return carry

    lax.fori_loop(0, rows // step, body, 0)


def sum_gradients(grads, extra):
    def kernel(g_ref, e_ref, out_ref, eout_ref, own, crecv, s1a, s1b, s2, zup, zdn, gup, gdn, epart, erecv, ls, ss, rs, zss, zrs, es, er):
        d = lax.axis_index("dp")
        s = lax.axis_index("seq")
        z = s // 2
        c = s % 2
        xn = d + 1 - 2 * (d % 2)
        yn = d + 2 - 4 * (d // 2)
        xyn = 3 - d
        sib = z * 2 + 1 - c
        zpair = s + 2 - 4 * (z % 2)
        zfar = s + 4 - 8 * (z // 2)
        top = pl.ds(0, HALF)
        low = pl.ds(HALF, HALF)

        barrier = pltpu.get_barrier_semaphore()

        def greet(dev):
            pl.semaphore_signal(barrier, inc=1, device_id=dev, device_id_type=MESH)

        greet((d, sib))
        greet((xn, s))
        greet((yn, s))
        greet((d, zfar))

        @pl.when(z > 0)
        def _():
            greet((d, s - 2))

        @pl.when(z < 3)
        def _():
            greet((d, s + 2))

        order = [3 * (1 - z // 2), (2 + 3 * z) % 5, 1 + z % 2, z]

        def owner_rows(dd, zz, cc):
            return g_ref.at[pl.ds(pl.multiple_of((dd * 8 + zz * 2 + cc) * OWNED, OWNED), OWNED)]

        def load(zz, dd):
            return pltpu.make_async_copy(owner_rows(dd, zz, c), own.at[zz, dd], ls.at[zz, dd])

        for k in range(4):
            for dd in range(4):
                load(order[k], dd).start()

        pl.semaphore_wait(barrier, 4 + (z + 2) // 3 + (5 - z) // 3)

        def remote(src, dst, ssem, rsem, dev):
            return pltpu.make_async_remote_copy(
                src_ref=src, dst_ref=dst, send_sem=ssem, recv_sem=rsem, device_id=dev, device_id_type=MESH
            )

        def core(zz, dd):
            return remote(owner_rows(dd, zz, 1 - c), crecv.at[zz, dd], ss.at[zz, dd], rs.at[zz, dd], (d, sib))

        def y_own(zz):
            return remote(own.at[zz, yn, top], s1a.at[zz, 0], ss.at[zz, 4], rs.at[zz, 4], (yn, s))

        def y_cross(zz):
            return remote(own.at[zz, xyn, top], s1a.at[zz, 1], ss.at[zz, 5], rs.at[zz, 5], (yn, s))

        def x_own(zz):
            return remote(own.at[zz, xn, low], s1b.at[zz, 0], ss.at[zz, 6], rs.at[zz, 6], (xn, s))

        def x_cross(zz):
            return remote(own.at[zz, xyn, low], s1b.at[zz, 1], ss.at[zz, 7], rs.at[zz, 7], (xn, s))

        def x_last(zz):
            return remote(own.at[zz, xn, top], s2.at[zz, top], ss.at[zz, 8], rs.at[zz, 8], (xn, s))

        def y_last(zz):
            return remote(own.at[zz, yn, low], s2.at[zz, low], ss.at[zz, 9], rs.at[zz, 9], (yn, s))

        def z_up(zz):
            return remote(own.at[zz, d], zup.at[zz], zss.at[0, zz], zrs.at[0, zz], (d, s + 2))

        def z_dn(zz):
            return remote(own.at[zz, d], zdn.at[zz], zss.at[1, zz], zrs.at[1, zz], (d, s - 2))

        def g_up(zz):
            return remote(own.at[zz, xyn], gup.at[zz], zss.at[2, zz], zrs.at[2, zz], (d, s + 2))

        def g_dn(zz):
            return remote(own.at[zz, xyn], gdn.at[zz], zss.at[3, zz], zrs.at[3, zz], (d, s - 2))

        ends = (z == 0) | (z == 3)
        inner = (z == 1) | (z == 2)

        def in_plane(k, body):
            if k == 3:
                body()
            elif k == 0:
                pl.when(ends)(body)

        def cross(zz):
            y_cross(zz).start()
            x_cross(zz).start()

        def along(zz, act):
            @pl.when(zz > z)
            def _():
                act(g_up(zz))

            @pl.when(zz < z)
            def _():
                act(g_dn(zz))

        def outward(k, act):
            zz = order[k]
            if k == 0:
                pl.when(inner)(lambda: along(zz, act))
            elif k < 3:
                along(zz, act)

        def diagonal(k):
            zz = order[k]
            mine = own.at[zz, xyn]
            if k < 3:

                @pl.when(inner)
                def _():
                    @pl.when(zz > z)
                    def _():
                        g_up(zz).wait_recv()
                        add_rows(mine, [mine, gup.at[zz]], OWNED)

                    @pl.when(zz < z)
                    def _():
                        g_dn(zz).wait_recv()
                        add_rows(mine, [mine, gdn.at[zz]], OWNED)

                    along(zz, lambda cp: cp.start())
            else:

                @pl.when(z > 0)
                def _():
                    g_up(zz).wait_recv()
                    add_rows(mine, [mine, gup.at[zz]], OWNED)

                @pl.when(z < 3)
                def _():
                    g_dn(zz).wait_recv()
                    add_rows(mine, [mine, gdn.at[zz]], OWNED)

                cross(zz)

        def extra_step(i, dev):
            return remote(epart.at[i], erecv.at[i], es.at[i], er.at[i], dev)

        extra_devs = [(d, sib), (xn, s), (yn, s), (d, zpair), (d, zfar)]

        def extra_add(i):
            extra_step(i, extra_devs[i]).wait_recv()
            a = epart[i]
            b = erecv[i]
            row = lax.broadcasted_iota(jnp.int32, a.shape, 0)
            total = jnp.where(row < SMALL_ROWS, a + b, jnp.maximum(a, b))
            if i < 4:
                epart[i + 1] = total
                extra_step(i + 1, extra_devs[i + 1]).start()
            else:
                eout_ref[...] = total

        def issue(k):
            for dd in (xyn, yn, xn, d):
                core(order[k], dd).start()

        issue(0)
        epart[0] = e_ref[...]
        extra_step(0, extra_devs[0]).start()

        def first(k):
            zz = order[k]
            if k < 3:
                issue(k + 1)

            def one(dd, start):
                load(zz, dd).wait()
                core(zz, dd).wait_recv()
                add_rows(own.at[zz, dd], [own.at[zz, dd], crecv.at[zz, dd]], OWNED)
                for cp in start:
                    cp.start()

            one(xyn, [])
            if k == 0:
                pl.when(ends)(lambda: cross(zz))
                outward(0, lambda cp: cp.start())
            elif k < 3:
                pl.when(ends)(lambda: along(zz, lambda cp: cp.start()))
            one(yn, [y_own(zz)])
            one(xn, [x_own(zz)])
            one(d, [])

        def second(k):
            zz = order[k]
            a = own.at[zz, xn, top]
            b = own.at[zz, yn, low]

            def crossed():
                y_cross(zz).wait_recv()
                add_rows(a, [a, s1a.at[zz, 1]], HALF)

            def crossed_low():
                x_cross(zz).wait_recv()
                add_rows(b, [b, s1b.at[zz, 1]], HALF)

            in_plane(k, crossed)
            x_last(zz).start()
            in_plane(k, crossed_low)
            y_last(zz).start()

        def third(k):
            zz = order[k]
            y_own(zz).wait_recv()
            x_own(zz).wait_recv()
            x_last(zz).wait_recv()
            y_last(zz).wait_recv()
            a = own.at[zz, d, top]
            b = own.at[zz, d, low]
            if k < 3:

                @pl.when((zz > z) & (z > 0))
                def _():
                    z_up(zz).wait_recv()
                    add_rows(a, [a, s1a.at[zz, 0], s2.at[zz, top], zup.at[zz, top]], HALF)
                    add_rows(b, [b, s1b.at[zz, 0], s2.at[zz, low], zup.at[zz, low]], HALF)

                @pl.when((zz < z) & (z < 3))
                def _():
                    z_dn(zz).wait_recv()
                    add_rows(a, [a, s1a.at[zz, 0], s2.at[zz, top], zdn.at[zz, top]], HALF)
                    add_rows(b, [b, s1b.at[zz, 0], s2.at[zz, low], zdn.at[zz, low]], HALF)

                @pl.when(((zz > z) & (z == 0)) | ((zz < z) & (z == 3)))
                def _():
                    add_rows(a, [a, s1a.at[zz, 0], s2.at[zz, top]], HALF)
                    add_rows(b, [b, s1b.at[zz, 0], s2.at[zz, low]], HALF)

                @pl.when(zz > z)
                def _():
                    z_up(zz).start()

                @pl.when(zz < z)
                def _():
                    z_dn(zz).start()
            else:

                @pl.when(z > 0)
                def _():
                    z_up(zz).wait_recv()

                @pl.when(z < 3)
                def _():
                    z_dn(zz).wait_recv()

                o_top = out_ref.at[top]
                o_low = out_ref.at[low]

                @pl.when((z > 0) & (z < 3))
                def _():
                    add_rows(o_top, [a, s1a.at[zz, 0], s2.at[zz, top], zup.at[zz, top], zdn.at[zz, top]], HALF)
                    add_rows(o_low, [b, s1b.at[zz, 0], s2.at[zz, low], zup.at[zz, low], zdn.at[zz, low]], HALF)

                @pl.when(z == 0)
                def _():
                    add_rows(o_top, [a, s1a.at[zz, 0], s2.at[zz, top], zdn.at[zz, top]], HALF)
                    add_rows(o_low, [b, s1b.at[zz, 0], s2.at[zz, low], zdn.at[zz, low]], HALF)

                @pl.when(z == 3)
                def _():
                    add_rows(o_top, [a, s1a.at[zz, 0], s2.at[zz, top], zup.at[zz, top]], HALF)
                    add_rows(o_low, [b, s1b.at[zz, 0], s2.at[zz, low], zup.at[zz, low]], HALF)

        first(0)
        first(1)
        extra_add(0)
        second(0)
        diagonal(1)
        first(2)
        second(1)
        extra_add(1)
        first(3)
        diagonal(2)
        second(2)
        third(0)
        extra_add(2)
        diagonal(3)
        extra_add(3)
        third(1)
        extra_add(4)
        third(2)
        second(3)
        third(3)

        for i in range(5):
            extra_step(i, extra_devs[i]).wait_send()
        for k in range(4):
            zz = order[k]
            for dd in range(4):
                core(zz, dd).wait_send()
            for cp in (y_own(zz), x_own(zz), x_last(zz), y_last(zz)):
                cp.wait_send()

            def crosses_sent():
                y_cross(zz).wait_send()
                x_cross(zz).wait_send()

            in_plane(k, crosses_sent)
            outward(k, lambda cp: cp.wait_send())
            if k < 3:

                @pl.when(zz > z)
                def _():
                    z_up(zz).wait_send()

                @pl.when(zz < z)
                def _():
                    z_dn(zz).wait_send()

    return pl.pallas_call(
        kernel,
        out_shape=[
            jax.ShapeDtypeStruct((OWNED, BLK), F32),
            jax.ShapeDtypeStruct((EXTRA_ROWS, BLK), F32),
        ],
        in_specs=[ANY, VMEM],
        out_specs=[VMEM, VMEM],
        scratch_shapes=[
            pltpu.VMEM((4, 4, OWNED, BLK), BF16),
            pltpu.VMEM((4, 4, OWNED, BLK), BF16),
            pltpu.VMEM((4, 2, HALF, BLK), BF16),
            pltpu.VMEM((4, 2, HALF, BLK), BF16),
            pltpu.VMEM((4, OWNED, BLK), BF16),
            pltpu.VMEM((4, OWNED, BLK), BF16),
            pltpu.VMEM((4, OWNED, BLK), BF16),
            pltpu.VMEM((4, OWNED, BLK), BF16),
            pltpu.VMEM((4, OWNED, BLK), BF16),
            pltpu.VMEM((5, EXTRA_ROWS, BLK), F32),
            pltpu.VMEM((5, EXTRA_ROWS, BLK), F32),
            pltpu.SemaphoreType.DMA((4, 4)),
            pltpu.SemaphoreType.DMA((4, 10)),
            pltpu.SemaphoreType.DMA((4, 10)),
            pltpu.SemaphoreType.DMA((4, 4)),
            pltpu.SemaphoreType.DMA((4, 4)),
            pltpu.SemaphoreType.DMA((5,)),
            pltpu.SemaphoreType.DMA((5,)),
        ],
        compiler_params=params(collective_id=1, has_side_effects=True),
        name="sum_gradients",
    )(grads, extra)


ROWB = 256


PAIRS = HEADS // 2


def rope(p, cos_t, fwd_t, back_t):
    return p * cos_t + pltpu.roll(p, BLK - ROT // 2, 1) * fwd_t + pltpu.roll(p, ROT // 2, 1) * back_t


def by_pair(value):
    return [value[:, j * BLK : (j + 1) * BLK] for j in range(PAIRS)]


def side_by_side(ref, at=slice(None)):
    return jnp.concatenate([ref[j, at, :] for j in range(PAIRS)], axis=1)


def spread_tables(cos8, sin8):
    none = jnp.zeros_like(cos8)
    rest = (HEAD - ROT) // none.shape[0]
    cos_t = [cos8, cos8] + [none + 1.0] * rest
    fwd_t = [-sin8, none] + [none] * rest
    back_t = [none, sin8] + [none] * rest
    return [jnp.concatenate(t * 2, axis=0).T for t in (cos_t, fwd_t, back_t)]


def project(w_rows, w_all, prev_tokens, tokens, cotangent, smalls, tables):
    rows = tokens.shape[0]
    cos8, sin8 = tables

    def kernel(
        w_rows_ref, w_ref, prev_ref, tok_ref, g_ref, small_ref, cos_ref, sin_ref,
        q_ref, k_ref, v_ref, do_ref, m_ref, wqkv, wo, sems,
    ):
        i = pl.program_id(0)

        def third_copy(third):
            def body(t):
                r, cc = t // 8, t % 8
                src = w_ref.at[pl.ds(pl.multiple_of(w_rows_ref[r * 24 + third * 8 + cc], 16), BLK)]
                dst = wqkv.at[pl.ds(pl.multiple_of(r * BLK, BLK), BLK), pl.ds(pl.multiple_of(third * D + cc * BLK, BLK), BLK)]
                pltpu.make_async_copy(src, dst, sems.at[third]).start()

            tile_loop(0, 64, body)

        def third_wait(third):
            part = wqkv.at[:, pl.ds(third * D, D)]
            pltpu.make_async_copy(part, part, sems.at[third]).wait()

        @pl.when(i == 0)
        def _():
            third_copy(1)
            third_copy(2)
            third_copy(0)

            def body(t):
                r, cc = t // 8, t % 8
                src = w_ref.at[pl.ds(pl.multiple_of(w_rows_ref[OUT_BASE + t], 16), BLK)]
                dst = wo.at[pl.ds(pl.multiple_of(r * BLK, BLK), BLK), pl.ds(pl.multiple_of(cc * BLK, BLK), BLK)]
                pltpu.make_async_copy(src, dst, sems.at[3]).start()

            tile_loop(0, 64, body)
            third_wait(1)
            third_wait(2)

        @pl.when(i == 1)
        def _():
            third_wait(0)
            pltpu.make_async_copy(wo, wo, sems.at[3]).wait()

        n = rows // ROWB

        def put(ref, at, pieces):
            for j in range(PAIRS):
                ref[j, at, :] = pieces[j].astype(BF16)

        def run(own):
            x_ref = tok_ref if own else prev_ref
            ins, tabs, raw = {}, {}, {}

            def prepare(c):
                at = slice(c * ROWB, (c + 1) * ROWB)
                normed, _ = norm_rows(x_ref[at, :].astype(F32))
                ins[c] = (normed * small_ref[4:5, :] + small_ref[5:6, :]).astype(BF16)
                if own:
                    m_ref[at, :] = (normed * small_ref[6:7, :] + small_ref[7:8, :]).astype(BF16)
                yield
                tabs[c] = spread_tables(cos_ref[:, at], sin_ref[:, at])
                yield

            def multiply(c):
                at = slice(c * ROWB, (c + 1) * ROWB)
                raw[c] = [dot(ins[c], wqkv[:, D : 2 * D])]
                yield
                put(v_ref, at, by_pair(dot(ins[c], wqkv[:, 2 * D :]) + small_ref[1:2, :]))
                yield
                if own:
                    raw[c].append(dot(ins[c], wqkv[:, :D]) + small_ref[0:1, :])
                    yield
                    put(do_ref, at, by_pair(dot(g_ref[at, :], wo[...], NT)))
                    yield

            def turn(c):
                at = slice(c * ROWB, (c + 1) * ROWB)
                put(k_ref, at, [rope(p, *tabs[c]) for p in by_pair(raw[c][0])])
                yield
                if own:
                    put(q_ref, at, [rope(p, *tabs[c]) for p in by_pair(raw[c][1])])
                    yield

            for c in range(n + 2):
                parts = []
                if 0 <= c - 1 < n:
                    parts.append(multiply(c - 1))
                if c < n:
                    parts.append(prepare(c))
                if 0 <= c - 2 < n:
                    parts.append(turn(c - 2))
                interleave(*parts)

        @pl.when(i == 0)
        def _():
            run(False)

        @pl.when(i == 1)
        def _():
            run(True)

    block = pl.BlockSpec((rows, D), lambda i, *_: (0, 0))
    here = pl.BlockSpec((PAIRS, rows, BLK), lambda i, *_: (0, i, 0))
    own = pl.BlockSpec((PAIRS, rows, BLK), lambda i, *_: (0, 0, 0))
    table = pl.BlockSpec((ROT // 2, rows), lambda i, *_: (0, i))
    return pl.pallas_call(
        kernel,
        grid_spec=pltpu.PrefetchScalarGridSpec(
            num_scalar_prefetch=1,
            grid=(2,),
            in_specs=[
                ANY, block, block, block,
                pl.BlockSpec((16, D), lambda i, *_: (0, 0)), table, table,
            ],
            out_specs=[own, here, here, own, block],
            scratch_shapes=[
                pltpu.VMEM((D, 3 * D), BF16),
                pltpu.VMEM((D, D), BF16),
                pltpu.SemaphoreType.DMA((4,)),
            ],
        ),
        out_shape=[
            jax.ShapeDtypeStruct((PAIRS, rows, BLK), BF16),
            jax.ShapeDtypeStruct((PAIRS, 2 * rows, BLK), BF16),
            jax.ShapeDtypeStruct((PAIRS, 2 * rows, BLK), BF16),
            jax.ShapeDtypeStruct((PAIRS, rows, BLK), BF16),
            jax.ShapeDtypeStruct((rows, D), BF16),
        ],
        compiler_params=params(dimension_semantics=("arbitrary",)),
        name="project",
    )(w_rows, w_all, prev_tokens, tokens, cotangent, smalls, cos8, sin8)


QB = 256
SPAN = WINDOW + QB


CHUNK = 256
SAFE_SCORE = 60.0


def attend(q, k, v, d_out, seg_q, seg_k, cos8, sin8):
    rows = q.shape[1]
    blocks = rows // QB
    scale = HEAD ** (-0.5)
    half = ROT // 2
    n = SPAN // CHUNK

    def heads_apart(x):
        row = lax.broadcasted_iota(jnp.int32, x.shape, 0)
        zero = jnp.zeros_like(x)
        return jnp.concatenate([jnp.where(row < HEAD, x, zero), jnp.where(row < HEAD, zero, x)], axis=1)

    def stacked(x):
        lane = lax.broadcasted_iota(jnp.int32, x.shape, 1)
        zero = jnp.zeros_like(x)
        return jnp.concatenate([jnp.where(lane < HEAD, x, zero), jnp.where(lane < HEAD, zero, x)], axis=0)

    def fold(x, op):
        return op(x.reshape(x.shape[0] // 8, 8, x.shape[1]), axis=0)

    def two(x):
        return jnp.concatenate([x, x], axis=1)

    def kernel(
        q_ref, k_ref, v_ref, do_ref, sq_ref, sk_ref, cos_ref, sin_ref,
        o_ref, dq_ref, dk_ref, dv_ref, halo_ref, peak_ref, bias, kt, vt, el_ref, ds_ref, dks, dvs, base,
    ):
        p = pl.program_id(0)

        @pl.when(p == 0)
        def _():
            gap = (
                WINDOW
                + lax.broadcasted_iota(jnp.int32, (SPAN, QB), 1)
                - lax.broadcasted_iota(jnp.int32, (SPAN, QB), 0)
            )
            for i in range(blocks):
                same = sk_ref[i * QB : i * QB + SPAN, :] == sq_ref[:, i * QB : (i + 1) * QB]
                bias[i] = jnp.where((gap >= 0) & (gap < WINDOW) & same, 0.0, MASKED)

        kt[...] = k_ref[...].T
        vt[...] = v_ref[...].T
        k_float = kt[...].astype(F32)
        q_float = q_ref[...].astype(F32) * scale
        reach = jnp.max(jnp.sum(k_float * k_float, axis=0)) * jnp.max(jnp.sum(q_float * q_float, axis=1))
        safe = reach < SAFE_SCORE * SAFE_SCORE

        def keys_at(ref, i, c):
            return ref[i * QB + c * CHUNK : i * QB + (c + 1) * CHUNK, :]

        def prepare(i):
            q_all = (q_ref[i * QB : (i + 1) * QB, :].astype(F32) * scale).astype(BF16)
            return q_all, heads_apart(q_all.T)

        def scores(i, c, q_apart):
            return dot(keys_at(k_ref, i, c), q_apart) + two(bias[i, c * CHUNK : (c + 1) * CHUNK])

        def row_tops(i):
            q_apart = prepare(i)[1]
            for c in range(n):
                t = fold(scores(i, c, q_apart), jnp.max)
                most = t if c == 0 else jnp.maximum(most, t)
            base[i] = jnp.max(most, axis=0, keepdims=True)

        def forward(i, q_apart, found):
            low = base[i]
            top8 = sum8 = None
            for c in range(n):
                st = scores(i, c, q_apart)
                e = jnp.exp(st - low)
                el_ref[i % 2, c * CHUNK : (c + 1) * CHUNK] = e.astype(BF16)
                t, u = fold(st, jnp.max), fold(e, jnp.sum)
                top8, sum8 = (t, u) if c == 0 else (jnp.maximum(top8, t), sum8 + u)
                yield
            found.append(jnp.max(top8, axis=0, keepdims=True))
            found.append(1.0 / jnp.sum(sum8, axis=0, keepdims=True))

        def per_head(x):
            return jnp.concatenate(
                [jnp.broadcast_to(x[:, :QB], (HEAD, QB)), jnp.broadcast_to(x[:, QB:], (HEAD, QB))], axis=0
            )

        def both(t, x_ref, i):
            span = slice(i * QB, i * QB + SPAN)
            return jnp.concatenate(
                [dot(t[:HEAD, span], x_ref[i % 2, :, :QB]), dot(t[HEAD:, span], x_ref[i % 2, :, QB:])], axis=0
            )

        def output(i, inv):
            raw = both(vt, el_ref, i)
            inv2 = per_head(inv)
            o_ref[i * QB : (i + 1) * QB, :] = (raw * inv2).T.astype(BF16)
            do_s = (do_ref[i * QB : (i + 1) * QB, :].astype(F32).T * inv2).astype(BF16)
            m = do_s.astype(F32) * raw
            mean = jnp.concatenate(
                [jnp.sum(m[:HEAD], axis=0, keepdims=True), jnp.sum(m[HEAD:], axis=0, keepdims=True)], axis=1
            )
            return do_s, mean * inv

        def score_grads(i, do_s, mean):
            do_apart = heads_apart(do_s)
            for c in range(n):
                w = slice(c * CHUNK, (c + 1) * CHUNK)
                dpt = dot(keys_at(v_ref, i, c), do_apart)
                ds_ref[i % 2, w] = (el_ref[i % 2, w].astype(F32) * (dpt - mean)).astype(BF16)

        def input_grads(i, q_all, do_s):
            do_rows = stacked(do_s.T)
            q_rows = stacked(q_all)
            for c in range(n):
                w = slice(c * CHUNK, (c + 1) * CHUNK)
                at = slice(i * QB + c * CHUNK, i * QB + (c + 1) * CHUNK)
                v_part = dot(el_ref[i % 2, w], do_rows)
                k_part = dot(ds_ref[i % 2, w], q_rows)
                if i == 0 or c == n - 1:
                    dvs[at, :] = v_part
                    dks[at, :] = k_part
                else:
                    dvs[at, :] += v_part
                    dks[at, :] += k_part
                yield
            dq = both(kt, ds_ref, i) * scale
            cos_t, sin_t = cos_ref[:, i * QB : (i + 1) * QB], sin_ref[:, i * QB : (i + 1) * QB]
            turned = []
            for h in range(2):
                f, g = dq[h * HEAD : h * HEAD + half], dq[h * HEAD + half : h * HEAD + ROT]
                turned += [f * cos_t + g * sin_t, g * cos_t - f * sin_t, dq[h * HEAD + ROT : (h + 1) * HEAD]]
            dq_ref[i * QB : (i + 1) * QB, :] = jnp.concatenate(turned, axis=0).T.astype(BF16)
            yield

        def run():
            top = held = None
            for i in range(blocks + 1):
                parts, found = [], []
                if held is not None:
                    parts.append(input_grads(i - 1, *held))
                if i < blocks:
                    q_all, q_apart = prepare(i)
                    parts.append(forward(i, q_apart, found))
                interleave(*parts)
                if i < blocks:
                    t, inv = found
                    top = t if top is None else jnp.maximum(top, t)
                    do_s, mean = output(i, inv)
                    score_grads(i, do_s, mean)
                    held = (q_all, do_s)
            peak_ref[...] = jnp.broadcast_to(top, peak_ref.shape)
            halo_ref[0] = dks[:rows, :].astype(BF16)
            halo_ref[1] = dvs[:rows, :].astype(BF16)
            dk_ref[...] = dks[rows:, :]
            dv_ref[...] = dvs[rows:, :]

        base[...] = jnp.zeros_like(base)

        @pl.when(jnp.logical_not(safe))
        def _():
            for i in range(blocks):
                row_tops(i)

        run()

    block = pl.BlockSpec((None, rows, BLK), lambda p: (p, 0, 0))
    keys = pl.BlockSpec((None, 2 * rows, BLK), lambda p: (p, 0, 0))
    whole = lambda *shape: pl.BlockSpec(shape, lambda p: (0, 0))
    return pl.pallas_call(
        kernel,
        grid=(PAIRS,),
        in_specs=[
            block, keys, keys, block, whole(1, rows), whole(2 * rows, 1), whole(half, rows), whole(half, rows),
        ],
        out_specs=[
            block, block, block, block,
            pl.BlockSpec((2, None, rows, BLK), lambda p: (0, p, 0, 0)),
            pl.BlockSpec((8, 2 * QB), lambda p: (p, 0)),
        ],
        out_shape=[
            jax.ShapeDtypeStruct((PAIRS, rows, BLK), BF16),
            jax.ShapeDtypeStruct((PAIRS, rows, BLK), BF16),
            jax.ShapeDtypeStruct((PAIRS, rows, BLK), F32),
            jax.ShapeDtypeStruct((PAIRS, rows, BLK), F32),
            jax.ShapeDtypeStruct((2, PAIRS, rows, BLK), BF16),
            jax.ShapeDtypeStruct((8 * PAIRS, 2 * QB), F32),
        ],
        scratch_shapes=[
            pltpu.VMEM((blocks, SPAN, QB), F32),
            pltpu.VMEM((BLK, 2 * rows), BF16),
            pltpu.VMEM((BLK, 2 * rows), BF16),
            pltpu.VMEM((2, SPAN, 2 * QB), BF16),
            pltpu.VMEM((2, SPAN, 2 * QB), BF16),
            pltpu.VMEM((2 * rows, BLK), F32),
            pltpu.VMEM((2 * rows, BLK), F32),
            pltpu.VMEM((blocks, 1, 2 * QB), F32),
        ],
        compiler_params=params(dimension_semantics=("arbitrary",)),
        cost_estimate=pl.CostEstimate(flops=40 << 30, bytes_accessed=32 << 20, transcendentals=20 << 20),
        name="attend",
    )(q, k, v, d_out, seg_q, seg_k, cos8, sin8)


FB = 512


def gelu_parts(v):
    a = jnp.abs(v)
    t = 1.0 / (1.0 + a * (0.3275911 * 0.7071067811865476))
    poly = t * (
        0.5 * 0.254829592
        + t * (0.5 * -0.284496736 + t * (0.5 * 1.421413741 + t * (0.5 * -1.453152027 + t * (0.5 * 1.061405429))))
    )
    e = jnp.exp(v * v * -0.5)
    tail = poly * e
    cdf = jnp.where(v >= 0, 1.0 - tail, tail)
    return v * cdf, cdf + v * e * 0.3989422804014327


def feed_forward(w_rows, g_rows, w_all, m, cotangent, b_up):
    rows = m.shape[0]
    steps = FF // FB

    def kernel(
        w_rows_ref, g_rows_ref, w_ref, m_ref, g_ref, b_ref, out_ref, dm_ref, db_ref, gr_ref,
        mt, wup, wdn, hs, dus, gup, gdn, u_ref, h_ref, wsem, gsem,
    ):
        f = pl.program_id(0)
        slot = f % 2
        per = FB // BLK

        def up_at(buf, t):
            return buf.at[pl.ds(pl.multiple_of((t // per) * BLK, BLK), BLK), pl.ds(pl.multiple_of((t % per) * BLK, BLK), BLK)]

        def up_tile(ff, t):
            return UP_BASE + (t // per) * (FF // BLK) + ff * per + t % per

        def down_at(buf, t):
            return buf.at[pl.ds(pl.multiple_of((t // 8) * BLK, BLK), BLK), pl.ds(pl.multiple_of((t % 8) * BLK, BLK), BLK)]

        def down_tile(ff, t):
            return DOWN_BASE + ff * per * 8 + t

        def fetch_one(ff, sl, t):
            src = w_ref.at[pl.ds(pl.multiple_of(w_rows_ref[up_tile(ff, t)], 16), BLK)]
            pltpu.make_async_copy(src, up_at(wup.at[sl], t), wsem.at[0, sl]).start()
            src = w_ref.at[pl.ds(pl.multiple_of(w_rows_ref[down_tile(ff, t)], 16), BLK)]
            pltpu.make_async_copy(src, down_at(wdn.at[sl], t), wsem.at[1, sl]).start()

        def store_one(ff, sl, t):
            dst = gr_ref.at[pl.ds(pl.multiple_of(g_rows_ref[up_tile(ff, t)], 16), BLK)]
            pltpu.make_async_copy(up_at(gup.at[sl], t), dst, gsem.at[0, sl]).start()
            dst = gr_ref.at[pl.ds(pl.multiple_of(g_rows_ref[down_tile(ff, t)], 16), BLK)]
            pltpu.make_async_copy(down_at(gdn.at[sl], t), dst, gsem.at[1, sl]).start()

        def whole_wait(buf, sem):
            pltpu.make_async_copy(buf, buf, sem).wait()

        count = 8 * per

        @pl.when(f == 0)
        def _():
            tile_loop(0, count, lambda t: fetch_one(0, 0, t))
            mt[...] = m_ref[...].T
            out_ref[...] = jnp.zeros_like(out_ref)
            dm_ref[...] = jnp.zeros_like(dm_ref)

        whole_wait(wup.at[slot], wsem.at[0, slot])
        whole_wait(wdn.at[slot], wsem.at[1, slot])

        @pl.when(f >= 2)
        def _():
            whole_wait(gup.at[slot], gsem.at[0, slot])
            whole_wait(gdn.at[slot], gsem.at[1, slot])

        n = rows // ROWB

        def stage1(c):
            at = slice(c * ROWB, (c + 1) * ROWB)
            for k in range(FB // 256):
                cols = slice(k * 256, (k + 1) * 256)
                u_ref[c % 2, :, cols] = dot(m_ref[at, :], wup[slot, :, cols]) + b_ref[:, cols]
                yield
                h_ref[c % 2, :, cols] = dot(g_ref[at, :], wdn[slot, cols, :], NT)
                yield

        db = [None]

        def stage2(c):
            step = ROWB // 8
            for k in range(8):
                at = slice(k * step, (k + 1) * step)
                to = slice(c * ROWB + k * step, c * ROWB + (k + 1) * step)
                hidden, slope = gelu_parts(u_ref[c % 2, at, :])
                hs[to, :] = hidden.astype(BF16)
                du = (h_ref[c % 2, at, :] * slope).astype(BF16)
                dus[to, :] = du
                t = jnp.sum(du.astype(F32).reshape(step // 8, 8, FB), axis=0)
                db[0] = t if db[0] is None else db[0] + t
                yield

        def stage3(c):
            at = slice(c * ROWB, (c + 1) * ROWB)
            for k in range(D // 256):
                cols = slice(k * 256, (k + 1) * 256)
                out_ref[at, cols] += dot(hs[at, :], wdn[slot, :, cols])
                yield
                dm_ref[at, cols] += dot(dus[at, :], wup[slot, cols, :], NT)
                yield

        nxt = jnp.minimum(f + 1, steps - 1)
        for t in range(count):
            fetch_one(nxt, 1 - slot, t)

        for c in range(n + 2):
            gens = []
            if c < n:
                gens.append(stage1(c))
            if 0 <= c - 1 < n:
                gens.append(stage2(c - 1))
            if 0 <= c - 2 < n:
                gens.append(stage3(c - 2))
            interleave(*gens)
        db_ref[...] = jnp.sum(db[0], axis=0, keepdims=True)
        gdn[slot] = dot(hs[...], g_ref[...], TN).astype(BF16)
        gup[slot] = dot(mt[...], dus[...]).astype(BF16)
        for t in range(count):
            store_one(f, slot, t)


        @pl.when(f == steps - 1)
        def _():
            whole_wait(wup.at[1 - slot], wsem.at[0, 1 - slot])
            whole_wait(wdn.at[1 - slot], wsem.at[1, 1 - slot])
            for sl in range(2):
                whole_wait(gup.at[sl], gsem.at[0, sl])
                whole_wait(gdn.at[sl], gsem.at[1, sl])

    full = pl.BlockSpec((rows, D), lambda f, *_: (0, 0))
    bias = pl.BlockSpec((1, FB), lambda f, *_: (0, f))
    return pl.pallas_call(
        kernel,
        grid_spec=pltpu.PrefetchScalarGridSpec(
            num_scalar_prefetch=2,
            grid=(steps,),
            in_specs=[ANY, full, full, bias],
            out_specs=[full, full, bias, ANY],
            scratch_shapes=[
                pltpu.VMEM((D, rows), BF16),
                pltpu.VMEM((2, D, FB), BF16),
                pltpu.VMEM((2, FB, D), BF16),
                pltpu.VMEM((rows, FB), BF16),
                pltpu.VMEM((rows, FB), BF16),
                pltpu.VMEM((2, D, FB), BF16),
                pltpu.VMEM((2, FB, D), BF16),
                pltpu.VMEM((2, ROWB, FB), F32),
                pltpu.VMEM((2, ROWB, FB), F32),
                pltpu.SemaphoreType.DMA((2, 2)),
                pltpu.SemaphoreType.DMA((2, 2)),
            ],
        ),
        out_shape=[
            jax.ShapeDtypeStruct((rows, D), F32),
            jax.ShapeDtypeStruct((rows, D), F32),
            jax.ShapeDtypeStruct((1, FF), F32),
            jax.ShapeDtypeStruct((TILES * BLK, BLK), BF16),
        ],
        compiler_params=params(dimension_semantics=("arbitrary",)),
        cost_estimate=pl.CostEstimate(flops=52 << 30, bytes_accessed=48 << 20, transcendentals=8 << 20),
        name="feed_forward",
    )(w_rows, g_rows, w_all, m, cotangent, b_up)


def finish(
    w_rows, g_rows, w_all, tokens, cotangent, smalls, attn_out, mlp_out, dm, dq, dk, dv, halo, tables, grads
):
    rows = tokens.shape[0]
    steps = rows // ROWB
    q_cols = 3 * D // FB
    o_cols = D // FB
    per = FB // BLK
    last = steps + q_cols + o_cols
    cos8, sin8 = tables

    def kernel(
        w_rows_ref, g_rows_ref, w_ref, tok_ref, g_ref, small_ref, o_ref, mlp_ref, dm_ref, dq_ref, dk_ref, dv_ref,
        halo_ref, cos_ref, sin_ref, _,
        out_ref, dx_ref, sum_ref, gr_ref, wqkv, wo, at, dp, stage, sems, gsem,
    ):
        i = pl.program_id(0)

        def fetch(first, count, width, dst, sem):
            def body(t):
                src = w_ref.at[pl.ds(pl.multiple_of(w_rows_ref[first + t], 16), BLK)]
                r, c = t // width, t % width
                to = dst.at[pl.ds(pl.multiple_of(r * BLK, BLK), BLK), pl.ds(pl.multiple_of(c * BLK, BLK), BLK)]
                pltpu.make_async_copy(src, to, sem).start()

            tile_loop(0, count, body)

        @pl.when(i == 0)
        def _():
            fetch(OUT_BASE, OUT_TILES, D // BLK, wo, sems.at[0])
            fetch(0, QKV_TILES, 3 * D // BLK, wqkv, sems.at[1])
            sum_ref[...] = jnp.zeros_like(sum_ref)
            pltpu.make_async_copy(wo, wo, sems.at[0]).wait()

        @pl.when(i < steps)
        def _():
            here = pl.ds(pl.multiple_of(i * ROWB, ROWB), ROWB)
            x = tok_ref[...].astype(F32)
            grad = g_ref[here, :].astype(F32)
            normed, inv = norm_rows(x)
            g1, g2 = small_ref[4:5, :], small_ref[6:7, :]
            attn = dot(side_by_side(o_ref, here), wo[...]) + small_ref[2:3, :]
            out_ref[...] = (x + attn + (mlp_ref[...] + small_ref[3:4, :])).astype(BF16)
            back = spread_tables(cos_ref[...], -sin_ref[...])
            for j in range(PAIRS):
                cols = j * BLK
                dk_all = dk_ref[j].astype(F32) + halo_ref[0, j].astype(F32)
                dv_all = dv_ref[j].astype(F32) + halo_ref[1, j].astype(F32)
                dp[here, cols : cols + BLK] = dq_ref[j]
                dp[here, D + cols : D + cols + BLK] = rope(dk_all, *back).astype(BF16)
                dp[here, 2 * D + cols : 2 * D + cols + BLK] = dv_all.astype(BF16)

            @pl.when(i == 0)
            def _():
                pltpu.make_async_copy(wqkv, wqkv, sems.at[1]).wait()

            da = dot(dp[here, :], wqkv[...], NT)
            at[:, here] = (normed * g1 + small_ref[5:6, :]).astype(BF16).T
            dmv = dm_ref[...]
            dn = da * g1 + dmv * g2
            mean_dn = jnp.mean(dn, axis=-1, keepdims=True)
            mean_dnn = jnp.mean(dn * normed, axis=-1, keepdims=True)
            dx_ref[...] = grad + inv * (dn - mean_dn - normed * mean_dnn)

            def add(row, value):
                sum_ref[row : row + 1, :] += jnp.sum(value, axis=0, keepdims=True)

            add(0, dp[here, :D].astype(F32))
            add(1, dp[here, 2 * D :].astype(F32))
            add(2, grad)
            add(3, da * normed)
            add(4, da)
            add(5, dmv * normed)
            add(6, dmv)

        slot = i % 2

        def drain(sl):
            pltpu.make_async_copy(stage.at[sl], stage.at[sl], gsem.at[sl]).wait()

        def send(first, width, c):
            for t in range(8 * per):
                tile = first + (t // per) * width + c * per + t % per
                dst = gr_ref.at[pl.ds(pl.multiple_of(g_rows_ref[tile], 16), BLK)]
                r, k = t // per * BLK, t % per * BLK
                pltpu.make_async_copy(stage.at[slot, r : r + BLK, k : k + BLK], dst, gsem.at[slot]).start()

        @pl.when(i >= steps + 2)
        def _():
            drain(slot)

        @pl.when((i >= steps) & (i < steps + q_cols))
        def _():
            c = i - steps
            stage[slot] = dot(at[...], dp[:, pl.ds(pl.multiple_of(c * FB, FB), FB)]).astype(BF16)
            send(0, 3 * D // BLK, c)

        @pl.when(i >= steps + q_cols)
        def _():
            c = i - steps - q_cols
            stage[slot] = dot(side_by_side(o_ref), g_ref[:, pl.ds(pl.multiple_of(c * FB, FB), FB)], TN).astype(BF16)
            send(OUT_BASE, D // BLK, c)

        @pl.when(i == last - 1)
        def _():
            drain(0)
            drain(1)

    here = lambda i, *_: (jnp.minimum(i, steps - 1), 0)
    whole = lambda *shape: pl.BlockSpec(shape, lambda i, *_: (0, 0))
    block = pl.BlockSpec((ROWB, D), here)
    pairs = pl.BlockSpec((PAIRS, ROWB, BLK), lambda i, *_: (0, jnp.minimum(i, steps - 1), 0))
    table = pl.BlockSpec((ROT // 2, ROWB), lambda i, *_: (0, steps + jnp.minimum(i, steps - 1)))
    return pl.pallas_call(
        kernel,
        grid_spec=pltpu.PrefetchScalarGridSpec(
            num_scalar_prefetch=2,
            grid=(last,),
            in_specs=[
                ANY, block, whole(rows, D), whole(16, D), pl.BlockSpec((PAIRS, rows, BLK), lambda i, *_: (0, 0, 0)),
                block, block, pairs, pairs, pairs,
                pl.BlockSpec((2, PAIRS, ROWB, BLK), lambda i, *_: (0, 0, jnp.minimum(i, steps - 1), 0)),
                table, table, ANY,
            ],
            out_specs=[block, block, whole(8, D), ANY],
            scratch_shapes=[
                pltpu.VMEM((D, 3 * D), BF16),
                pltpu.VMEM((D, D), BF16),
                pltpu.VMEM((D, rows), BF16),
                pltpu.VMEM((rows, 3 * D), BF16),
                pltpu.VMEM((2, D, FB), BF16),
                pltpu.SemaphoreType.DMA((2,)),
                pltpu.SemaphoreType.DMA((2,)),
            ],
        ),
        out_shape=[
            jax.ShapeDtypeStruct((rows, D), BF16),
            jax.ShapeDtypeStruct((rows, D), F32),
            jax.ShapeDtypeStruct((8, D), F32),
            jax.ShapeDtypeStruct(grads.shape, BF16),
        ],
        input_output_aliases={15: 3},
        compiler_params=params(dimension_semantics=("arbitrary",)),
        name="finish",
    )(w_rows, g_rows, w_all, tokens, cotangent, smalls, attn_out, mlp_out, dm, dq, dk, dv, halo, cos8, sin8, grads)


def halves(x):
    high = x.astype(BF16)
    return high, (x - high.astype(F32)).astype(BF16)


def dot3(a, b, dims=NN):
    return dot(a[0], b[0], dims) + (dot(a[0], b[1], dims) + dot(a[1], b[0], dims))


def update_tiles(grads, tiles, left, right, first, second, scale):
    count = tiles.shape[0]
    group = max(g for g in (1, 2, 3, 4, 6, 8) if count % g == 0)

    def kernel(g_ref, w_ref, l_ref, r_ref, m_ref, v_ref, s_ref, w_out, low_out, m_out, v_out):
        turned = []
        for t in range(group):
            l, r = halves(l_ref[t]), halves(r_ref[t])
            turned.append(dot3(halves(dot3(l, halves(g_ref[t]), TN)), r))
        for t in range(group):
            l, r = halves(l_ref[t]), halves(r_ref[t])
            m_new = BETA * m_ref[t] + (1.0 - BETA) * turned[t]
            v_new = BETA * v_ref[t] + (1.0 - BETA) * turned[t] * turned[t]
            ratio = m_new / (jnp.sqrt(v_new) + ADAM_EPS)
            back = dot3(halves(dot3(l, halves(ratio))), r, NT)
            w_new = (w_ref[t] - LEARN * back) * s_ref[t]
            w_out[t] = w_new
            low_out[t] = w_new.astype(BF16)
            m_out[t] = m_new
            v_out[t] = v_new

    block = pl.BlockSpec((group, BLK, BLK), lambda i: (i, 0, 0))
    row = pl.BlockSpec((group, 1, BLK), lambda i: (i, 0, 0))
    like = lambda t: jax.ShapeDtypeStruct(tiles.shape, t)
    return pl.pallas_call(
        kernel,
        grid=(count // group,),
        in_specs=[block] * 6 + [row],
        out_specs=[block] * 4,
        out_shape=[like(F32), like(BF16), like(F32), like(F32)],
        compiler_params=params(dimension_semantics=("arbitrary",)),
        name="update_tiles",
    )(grads, tiles, left, right, first, second, scale)


def column_scales(tile_ids, factors):
    columns = (tile_ids % (3 * D // BLK))[:, None] * BLK + jnp.arange(BLK, dtype=jnp.int32)[None, :]
    head_index = columns % D // HEAD
    root_factor = jnp.sqrt(factors)
    picked = jnp.sum(
        jnp.where(head_index[..., None] == jnp.arange(HEADS, dtype=jnp.int32), root_factor, 0.0),
        axis=-1,
    )
    clipped = (tile_ids[:, None] < QKV_TILES) & (columns < 2 * D)
    return jnp.where(clipped, picked, 1.0)


def small_update(grads, params_, first_moment, second_moment):
    first_new = BETA * first_moment + (1.0 - BETA) * grads
    second_new = BETA * second_moment + (1.0 - BETA) * grads * grads
    updated = params_ - SMALL_LEARN * first_new / (jnp.sqrt(second_new) + ADAM_EPS)
    return (updated, first_new, second_new)


def passed_along(value, axis, steps):
    count = lax.axis_size(axis)
    leading, last = (max(0, -steps), min(count, count - steps))
    return lax.ppermute(value, axis, [(source, source + steps) for source in range(leading, last)])


def on_device(
    ring,
    tokens,
    segments,
    cotangent,
    tile_of_slot,
    tiles,
    left_bases,
    right_bases,
    first_moments,
    second_moments,
    small_params,
    small_first,
    small_second,
    threshold,
):
    rows = tokens.shape[0]
    slot_count = tiles.shape[0]
    small_count = small_params.shape[0]
    axes = ("dp", "seq")
    seq_index = lax.axis_index("seq")
    owner_index = lax.axis_index(axes)
    first_place = seq_index * rows
    seg_local = segments.reshape(1, rows)

    numbers = jnp.arange(TILES, dtype=jnp.int32)
    slot_of_tile = jnp.sum(
        jnp.where(tile_of_slot[None, :] == numbers[:, None], numbers[None, :], 0), axis=1
    ).astype(jnp.int32)
    g_rows = slot_of_tile * BLK

    if ring:
        small_block = jnp.zeros((16 * BLK,), BF16).at[:small_count].set(small_params.astype(BF16))
        payload = jnp.concatenate(
            [tiles.astype(BF16).reshape(slot_count * BLK, BLK), small_block.reshape(16, BLK)], axis=0
        )
        seg_rows = jnp.broadcast_to(seg_local, (8, rows))
        gathered, prev_tokens, prev_seg = gather_weights(payload, tokens, seg_rows)
        stride = payload.shape[0]
        w_all = gathered.reshape(-1, BLK)
        w_rows = slot_of_tile // slot_count * stride + slot_of_tile % slot_count * BLK
        tail = slot_count * BLK
        small_all = gathered[:, tail : tail + small_count // BLK, :].reshape(SMALL)
        prev_seg = prev_seg[:1]
    else:
        w_all = lax.all_gather(tiles.astype(BF16), axes, axis=0, tiled=True).reshape(-1, BLK)
        w_rows = g_rows
        small_all = lax.all_gather(small_params.astype(BF16), axes, axis=0, tiled=True)
        prev_tokens, prev_seg = passed_along((tokens, seg_local), "seq", 1)

    table = small_all.astype(F32).reshape(D, 12)
    smalls = jnp.concatenate(
        [
            jnp.stack([table[:, r] for r in (0, 1, 2, 7, 8, 9, 10, 11)], axis=0),
            jnp.zeros((8, D), F32),
        ],
        axis=0,
    )
    b_up = table[:, 3:7].reshape(1, FF)

    half = ROT // 2
    exponent = jnp.arange(half, dtype=F32) * (2.0 / ROT)
    frequency = jnp.power(ROPE_BASE, -exponent)
    places = first_place - rows + jnp.arange(2 * rows, dtype=jnp.int32)
    angle = places.astype(F32)[None, :] * frequency[:, None]
    cos8, sin8 = jnp.cos(angle), jnp.sin(angle)
    tables = (cos8, sin8)

    prev_seg = jnp.where(seq_index == 0, -1, prev_seg)
    seg_k = jnp.concatenate([prev_seg, seg_local], axis=1).reshape(2 * rows, 1)

    q, k, v, d_out, m = project(w_rows, w_all, prev_tokens, tokens, cotangent, smalls, tables)
    attn_out, dq, dk, dv, halo, peaks = attend(
        q, k, v, d_out, seg_local, seg_k, cos8[:, rows:], sin8[:, rows:]
    )
    halo = passed_along(halo, "seq", -1)
    mlp_out, dm, db_up, grads = feed_forward(w_rows, g_rows, w_all, m, cotangent, b_up)
    block_output, input_grad, sums, grads = finish(
        w_rows, g_rows, w_all, tokens, cotangent, smalls, attn_out, mlp_out, dm, dq, dk, dv, halo, tables, grads
    )

    small_terms = jnp.concatenate(
        [
            sums[:3].T,
            db_up.reshape(D, FF // D),
            sums[2:7].T,
        ],
        axis=1,
    ).reshape(SMALL)
    head_peak = jnp.max(peaks.reshape(PAIRS, 8, 2, QB)[:, 0], axis=-1).reshape(HEADS)
    if ring:
        peak_rows = jnp.zeros((8, BLK), F32).at[:, :HEADS].set(head_peak[None, :])
        extra = jnp.concatenate([small_terms.reshape(SMALL_ROWS, BLK), peak_rows], axis=0)
        tile_grads, extra = sum_gradients(grads, extra)
        tile_grads = tile_grads.reshape(slot_count, BLK, BLK)
        small_grads = lax.dynamic_slice_in_dim(
            extra[:SMALL_ROWS].reshape(SMALL), owner_index * small_count, small_count, 0
        )
        head_peak = extra[SMALL_ROWS, :HEADS]
    else:
        tile_grads = lax.psum_scatter(
            grads.astype(F32).reshape(TILES, BLK, BLK), axes, scatter_dimension=0, tiled=True
        )
        small_grads = lax.psum_scatter(small_terms, axes, scatter_dimension=0, tiled=True)
        head_peak = lax.pmax(head_peak, axes)

    local_ids = lax.dynamic_slice_in_dim(tile_of_slot, owner_index * slot_count, slot_count, 0)
    limit = threshold[0]
    factors = limit / jnp.maximum(head_peak, limit)
    scale = column_scales(local_ids, factors).reshape(slot_count, 1, BLK)
    new_tiles, new_low, new_first, new_second = update_tiles(
        tile_grads, tiles, left_bases, right_bases, first_moments, second_moments, scale
    )
    new_small, new_small_first, new_small_second = small_update(
        small_grads, small_params, small_first, small_second
    )
    return (
        block_output,
        input_grad,
        tile_grads,
        small_grads,
        new_tiles,
        new_low,
        new_first,
        new_second,
        new_small,
        new_small.astype(BF16),
        new_small_first,
        new_small_second,
        factors,
    )


def solution(mesh):
    split = P(("dp", "seq"))
    in_specs = (split, P("dp", "seq"), split, P()) + (split,) * 8 + (P(),)
    out_specs = (split,) * 12 + (P(),)
    ring = (mesh.shape["dp"], mesh.shape["seq"]) == (4, 8)
    return jax.shard_map(
        functools.partial(on_device, ring), mesh=mesh, in_specs=in_specs, out_specs=out_specs, check_vma=False
    )
```

```python
import functools

import jax
import jax.numpy as jnp
from jax import lax
from jax.experimental import pallas as pl
from jax.experimental.pallas import tpu as pltpu
from jax.sharding import PartitionSpec as P

D = 1024
FF = 4096
HEADS = 16
HEAD = 64
ROT = 16
BLK = 128
WINDOW = 1024
TILES = 768
SMALL = 12288
QKV_TILES = D // BLK * (3 * D // BLK)
OUT_TILES = D // BLK * (D // BLK)
UP_TILES = D // BLK * (FF // BLK)
OUT_BASE = QKV_TILES
UP_BASE = QKV_TILES + OUT_TILES
DOWN_BASE = UP_BASE + UP_TILES

B_Q, B_V, B_O = slice(0, 1), slice(1, 2), slice(2, 3)
B_DOWN, G1, C1, G2, C2 = slice(7, 8), slice(8, 9), slice(9, 10), slice(10, 11), slice(11, 12)

NORM_EPS = 1e-05
ADAM_EPS = 1e-08
BETA = 0.5
LEARN = 0.03
SMALL_LEARN = 0.2
ROPE_BASE = 10000.0
MASKED = -1e30
HIGH = lax.Precision.HIGHEST

F32 = jnp.float32
BF16 = jnp.bfloat16
MESH = pl.DeviceIdType.MESH
ANY = pl.BlockSpec(memory_space=pl.ANY)
VMEM = pl.BlockSpec(memory_space=pltpu.VMEM)
VMEM_LIMIT = 58 << 20

NN = (((1,), (0,)), ((), ()))
NT = (((1,), (1,)), ((), ()))
TN = (((0,), (0,)), ((), ()))


def dot(a, b, dims=NN, precision=None):
    return lax.dot_general(a, b, dims, precision=precision, preferred_element_type=F32)


def interleave(*parts):
    live = list(parts)
    while live:
        for part in list(live):
            try:
                next(part)
            except StopIteration:
                live.remove(part)


def params(**kw):
    return pltpu.CompilerParams(vmem_limit_bytes=VMEM_LIMIT, **kw)


def norm_rows(x):
    centered = x - jnp.mean(x, axis=-1, keepdims=True)
    inv = lax.rsqrt(jnp.mean(centered * centered, axis=-1, keepdims=True) + NORM_EPS)
    return centered * inv, inv


def tile_loop(first, count, body):
    def step(t, carry):
        body(t)
        return carry

    lax.fori_loop(first, first + count, step, 0)


ROWS_PER_TILE = BLK
HALF_ROWS = 1536


def gather_weights(payload, tokens, seg_rows):
    rows = payload.shape[0]
    top = pl.ds(0, HALF_ROWS)
    low = pl.ds(HALF_ROWS, rows - HALF_ROWS)

    def kernel(x_ref, tok_ref, seg_ref, out_ref, ptok_ref, pseg_ref, lsem, ss, rs, hss, hrs, hls):
        d = lax.axis_index("dp")
        s = lax.axis_index("seq")
        z = s // 2
        c = s % 2
        xn = d + 1 - 2 * (d % 2)
        yn = d + 2 - 4 * (d // 2)
        xyn = 3 - d
        sib = z * 2 + 1 - c
        halo = s - 1 + 2 * c
        halo_ok = ((c == 0) & (z > 0)) | ((c == 1) & (z < 3))

        barrier = pltpu.get_barrier_semaphore()

        def greet(dev):
            pl.semaphore_signal(barrier, inc=1, device_id=dev, device_id_type=MESH)

        greet((d, sib))
        greet((xn, s))
        greet((yn, s))

        @pl.when(z > 0)
        def _():
            greet((d, s - 2))

        @pl.when(z < 3)
        def _():
            greet((d, s + 2))

        @pl.when(halo_ok)
        def _():
            greet((d, halo))

        below, above = (z + 2) // 3, (5 - z) // 3
        pl.semaphore_wait(barrier, 3 + below + above + (1 - c) * below + c * above)

        def place(dd, zz):
            return out_ref.at[dd * 8 + zz * 2 + c]

        def remote(src, dst, kind, zz, dev):
            return pltpu.make_async_remote_copy(
                src_ref=src,
                dst_ref=dst,
                send_sem=ss.at[kind, zz],
                recv_sem=rs.at[kind, zz],
                device_id=dev,
                device_id_type=MESH,
            )

        def block_of(zz, own):
            return x_ref if own else place(d, zz)

        def up(zz, own):
            return remote(block_of(zz, own), place(d, zz), 0, zz, (d, s + 2))

        def down(zz, own):
            return remote(block_of(zz, own), place(d, zz), 1, zz, (d, s - 2))

        def to_x(zz, own):
            return remote(block_of(zz, own), place(d, zz), 2, zz, (xn, s))

        def to_y(zz, own):
            return remote(block_of(zz, own), place(d, zz), 3, zz, (yn, s))

        def on_y(zz):
            return remote(place(xn, zz).at[top], place(xn, zz).at[top], 4, zz, (yn, s))

        def on_x(zz):
            return remote(place(yn, zz).at[low], place(yn, zz).at[low], 5, zz, (xn, s))

        def to_sib(dd, zz, kind, own=False):
            src = x_ref if own else place(dd, zz)
            return remote(src, place(dd, zz), kind, zz, (d, sib))

        def from_x(zz):
            return remote(x_ref, place(xn, zz), 2, zz, (xn, s))

        def from_y(zz):
            return remote(x_ref, place(yn, zz), 3, zz, (yn, s))

        def diag_up(zz):
            return remote(place(xyn, zz), place(xyn, zz), 10, zz, (d, s + 2))

        def diag_down(zz):
            return remote(place(xyn, zz), place(xyn, zz), 11, zz, (d, s - 2))

        def diag_top(zz):
            return remote(x_ref.at[top], place(xyn, zz).at[top], 4, zz, (yn, s))

        def diag_low(zz):
            return remote(x_ref.at[low], place(xyn, zz).at[low], 5, zz, (xn, s))

        order = [z, 1 + z % 2, (2 + 3 * z) % 5, 3 * (1 - z // 2)]
        local = pltpu.make_async_copy(x_ref, place(d, z), lsem)
        local.start()

        def halo_copies(dev):
            tok = pltpu.make_async_remote_copy(
                src_ref=tok_ref,
                dst_ref=ptok_ref,
                send_sem=hss.at[0],
                recv_sem=hrs.at[0],
                device_id=dev,
                device_id_type=MESH,
            )
            seg = pltpu.make_async_remote_copy(
                src_ref=seg_ref,
                dst_ref=pseg_ref,
                send_sem=hss.at[1],
                recv_sem=hrs.at[1],
                device_id=dev,
                device_id_type=MESH,
            )
            return tok, seg

        def in_plane(k, body):
            if k == 0:
                body()
            else:
                pl.when((z - order[k] >= 2) | (order[k] - z >= 3))(body)

        def on_line(k, body):
            pl.when((z - order[k] < 2) & (order[k] - z < 3))(body)

        def launch(k):
            zz = order[k]
            own = k == 0
            if own:

                @pl.when(z < 3)
                def _():
                    up(zz, True).start()

                @pl.when(z > 0)
                def _():
                    down(zz, True).start()
            else:

                @pl.when(zz < z)
                def _():
                    up(zz, False).wait_recv()

                @pl.when((zz < z) & (z < 3))
                def _():
                    up(zz, False).start()

                @pl.when(zz > z)
                def _():
                    down(zz, False).wait_recv()

                @pl.when((zz > z) & (z > 0))
                def _():
                    down(zz, False).start()

            to_x(zz, own).start()
            to_y(zz, own).start()
            to_sib(d, zz, 6, own).start()

        def second(k):
            zz = order[k]

            def pass_on():
                from_x(zz).wait_recv()
                on_y(zz).start()
                to_sib(xn, zz, 7).start()
                from_y(zz).wait_recv()
                on_x(zz).start()
                to_sib(yn, zz, 8).start()

            in_plane(k, pass_on)

        def rest(k):
            zz = order[k]

            def share():
                from_x(zz).wait_recv()
                to_sib(xn, zz, 7).start()
                from_y(zz).wait_recv()
                to_sib(yn, zz, 8).start()

            on_line(k, share)

        def third(k):
            zz = order[k]

            def arrive():
                diag_top(zz).wait_recv()
                diag_low(zz).wait_recv()

            in_plane(k, arrive)
            if k > 0:

                @pl.when((zz < z) & (z - zz <= 1))
                def _():
                    diag_up(zz).wait_recv()

                @pl.when((zz > z) & (zz - z <= 2))
                def _():
                    diag_down(zz).wait_recv()

            if k < 3:

                @pl.when((zz == z) & (z < 3))
                def _():
                    diag_up(zz).start()

                @pl.when((zz >= z) & (zz - z <= 1) & (z > 0))
                def _():
                    diag_down(zz).start()

            to_sib(xyn, zz, 9).start()

        own_tok = pltpu.make_async_copy(tok_ref, ptok_ref, hls.at[0])
        own_seg = pltpu.make_async_copy(seg_ref, pseg_ref, hls.at[1])


        @pl.when(s == 0)
        def _():
            own_tok.start()
            own_seg.start()

        launch(0)
        launch(1)
        second(0)
        launch(2)
        launch(3)
        third(0)
        second(1)
        third(1)
        second(2)

        @pl.when(s < 7)
        def _():
            for cp in halo_copies((d, s + 1)):
                cp.start()

        second(3)
        rest(1)
        rest(2)
        rest(3)
        third(2)
        third(3)

        local.wait()
        other = 1 - c

        def sib_place(dd, zz):
            return out_ref.at[dd * 8 + zz * 2 + other]

        for k in range(4):
            zz = order[k]
            own = k == 0
            for kind, dd in ((6, d), (7, xn), (8, yn), (9, xyn)):
                remote(sib_place(dd, zz), sib_place(dd, zz), kind, zz, (d, sib)).wait_recv()
                to_sib(dd, zz, kind, own and kind == 6).wait_send()
            to_x(zz, own).wait_send()
            to_y(zz, own).wait_send()

            def halves_sent():
                on_y(zz).wait_send()
                on_x(zz).wait_send()

            in_plane(k, halves_sent)
            if k < 3:

                @pl.when((zz == z) & (z < 3))
                def _():
                    diag_up(zz).wait_send()

                @pl.when((zz >= z) & (zz - z <= 1) & (z > 0))
                def _():
                    diag_down(zz).wait_send()

            @pl.when((zz <= z) & (z < 3))
            def _():
                up(zz, own).wait_send()

            @pl.when((zz >= z) & (z > 0))
            def _():
                down(zz, own).wait_send()

        @pl.when(s < 7)
        def _():
            for cp in halo_copies((d, s + 1)):
                cp.wait_send()

        @pl.when(s > 0)
        def _():
            for cp in halo_copies((d, s - 1)):
                cp.wait_recv()

        @pl.when(s == 0)
        def _():
            own_tok.wait()
            own_seg.wait()

    return pl.pallas_call(
        kernel,
        out_shape=[
            jax.ShapeDtypeStruct((32, rows, BLK), BF16),
            jax.ShapeDtypeStruct(tokens.shape, BF16),
            jax.ShapeDtypeStruct(seg_rows.shape, jnp.int32),
        ],
        in_specs=[ANY, ANY, ANY],
        out_specs=[ANY, ANY, ANY],
        scratch_shapes=[
            pltpu.SemaphoreType.DMA,
            pltpu.SemaphoreType.DMA((12, 4)),
            pltpu.SemaphoreType.DMA((12, 4)),
            pltpu.SemaphoreType.DMA((2,)),
            pltpu.SemaphoreType.DMA((2,)),
            pltpu.SemaphoreType.DMA((2,)),
        ],
        compiler_params=params(collective_id=0, has_side_effects=True),
        name="gather_weights",
    )(payload, tokens, seg_rows)


OWNED = 24 * BLK
HALF = OWNED // 2
SMALL_ROWS = SMALL // BLK
EXTRA_ROWS = SMALL_ROWS + 8


def add_rows(dst, terms, rows, step=256):
    def body(i, carry):
        at = pl.ds(pl.multiple_of(i * step, step), step)
        if len(terms) == 2 and dst.dtype == BF16:
            dst[at] = terms[0][at] + terms[1][at]
        else:
            total = terms[0][at].astype(F32)
            for term in terms[1:]:
                total = total + term[at].astype(F32)
            dst[at] = total.astype(dst.dtype)
        return carry

    lax.fori_loop(0, rows // step, body, 0)


SCHEDULE = [
    "F0a", "F1a", "F0b", "F1b", "E0", "F2a", "S0a", "S0b", "D1a", "F2b",
    "S1a", "S1b", "F3a", "E1", "F3b", "D1b", "D2a", "D2b", "S2a", "D3a",
    "S2b", "T0a", "T0b", "E2", "D3b", "T1a", "T1b", "E3", "T2a", "T2b",
    "E4", "S3a", "S3b", "T3a", "T3b",
]


def sum_gradients(grads, extra):
    def kernel(g_ref, e_ref, out_ref, eout_ref, own, crecv, s1a, s1b, s2, zup, zdn, gup, gdn, epart, erecv, ls, ss, rs, es, er):
        d = lax.axis_index("dp")
        s = lax.axis_index("seq")
        z = s // 2
        c = s % 2
        xn = d + 1 - 2 * (d % 2)
        yn = d + 2 - 4 * (d // 2)
        xyn = 3 - d
        sib = z * 2 + 1 - c
        zpair = s + 2 - 4 * (z % 2)
        zfar = s + 4 - 8 * (z // 2)
        barrier = pltpu.get_barrier_semaphore()

        def greet(dev):
            pl.semaphore_signal(barrier, inc=1, device_id=dev, device_id_type=MESH)

        greet((d, sib))
        greet((xn, s))
        greet((yn, s))
        greet((d, zfar))

        @pl.when(z > 0)
        def _():
            greet((d, s - 2))

        @pl.when(z < 3)
        def _():
            greet((d, s + 2))

        order = [3 * (1 - z // 2), (2 + 3 * z) % 5, 1 + z % 2, z]

        ends = (z == 0) | (z == 3)
        inner = (z == 1) | (z == 2)

        def in_plane(k, act):
            if k == 3:
                act()
            elif k == 0:
                pl.when(ends)(act)

        def remote(src, dst, ssem, rsem, dev):
            return pltpu.make_async_remote_copy(
                src_ref=src, dst_ref=dst, send_sem=ssem, recv_sem=rsem, device_id=dev, device_id_type=MESH
            )

        def part(h):
            size = OWNED // 2
            half = size // 2
            rows = pl.ds(h * size, size)
            top = pl.ds(h * size, half)
            low = pl.ds(h * size + half, half)
            here = pl.ds(h * half, half)

            def owner_rows(dd, zz, cc):
                return g_ref.at[pl.ds(pl.multiple_of((dd * 8 + zz * 2 + cc) * OWNED + h * size, size), size)]

            def load(k, dd):
                zz = order[k]
                return pltpu.make_async_copy(owner_rows(dd, zz, c), own.at[zz, dd, rows], ls.at[zz * 2 + h, dd])

            def hop(src, dst, kind, zz, dev):
                return remote(src, dst, ss.at[zz * 2 + h, kind], rs.at[zz * 2 + h, kind], dev)

            def core(zz, dd):
                return hop(owner_rows(dd, zz, 1 - c), crecv.at[zz, dd, rows], dd, zz, (d, sib))

            def y_own(zz):
                return hop(own.at[zz, yn, top], s1a.at[zz, 0, here], 4, zz, (yn, s))

            def y_cross(zz):
                return hop(own.at[zz, xyn, top], s1a.at[zz, 1, here], 5, zz, (yn, s))

            def x_own(zz):
                return hop(own.at[zz, xn, low], s1b.at[zz, 0, here], 6, zz, (xn, s))

            def x_cross(zz):
                return hop(own.at[zz, xyn, low], s1b.at[zz, 1, here], 7, zz, (xn, s))

            def x_last(zz):
                return hop(own.at[zz, xn, top], s2.at[zz, top], 8, zz, (xn, s))

            def y_last(zz):
                return hop(own.at[zz, yn, low], s2.at[zz, low], 9, zz, (yn, s))

            def z_up(zz):
                return hop(own.at[zz, d, rows], zup.at[zz, rows], 10, zz, (d, s + 2))

            def z_dn(zz):
                return hop(own.at[zz, d, rows], zdn.at[zz, rows], 11, zz, (d, s - 2))

            def g_up(zz):
                return hop(own.at[zz, xyn, rows], gup.at[zz, rows], 12, zz, (d, s + 2))

            def g_dn(zz):
                return hop(own.at[zz, xyn, rows], gdn.at[zz, rows], 13, zz, (d, s - 2))

            def cross(zz):
                y_cross(zz).start()
                x_cross(zz).start()

            def along(zz, act):
                @pl.when(zz > z)
                def _():
                    act(g_up(zz))

                @pl.when(zz < z)
                def _():
                    act(g_dn(zz))

            def outward(k, act):
                if k == 0:
                    pl.when(inner)(lambda: along(order[k], act))
                elif k < 3:
                    along(order[k], act)

            def issue(k):
                for dd in (xyn, yn, xn, d):
                    core(order[k], dd).start()

            def first(k):
                zz = order[k]

                def one(dd, start):
                    load(k, dd).wait()
                    core(zz, dd).wait_recv()
                    mine = own.at[zz, dd, rows]
                    add_rows(mine, [mine, crecv.at[zz, dd, rows]], size)
                    for cp in start:
                        cp.start()

                one(xyn, [])
                if k == 0:
                    pl.when(ends)(lambda: cross(zz))
                    outward(0, lambda cp: cp.start())
                elif k < 3:
                    pl.when(ends)(lambda: along(zz, lambda cp: cp.start()))
                one(yn, [y_own(zz)])
                one(xn, [x_own(zz)])
                one(d, [])

            def diagonal(k):
                zz = order[k]
                mine = own.at[zz, xyn, rows]

                def take(cp, came):
                    cp.wait_recv()
                    add_rows(mine, [mine, came.at[zz, rows]], size)

                if k < 3:

                    @pl.when(inner)
                    def _():
                        pl.when(zz > z)(lambda: take(g_up(zz), gup))
                        pl.when(zz < z)(lambda: take(g_dn(zz), gdn))
                        along(zz, lambda cp: cp.start())
                else:
                    pl.when(z > 0)(lambda: take(g_up(zz), gup))
                    pl.when(z < 3)(lambda: take(g_dn(zz), gdn))
                    cross(zz)

            def second(k):
                zz = order[k]
                a = own.at[zz, xn, top]
                b = own.at[zz, yn, low]

                def crossed():
                    y_cross(zz).wait_recv()
                    add_rows(a, [a, s1a.at[zz, 1, here]], half)

                def crossed_low():
                    x_cross(zz).wait_recv()
                    add_rows(b, [b, s1b.at[zz, 1, here]], half)

                in_plane(k, crossed)
                x_last(zz).start()
                in_plane(k, crossed_low)
                y_last(zz).start()

            def third(k):
                zz = order[k]
                for cp in (y_own(zz), x_own(zz), x_last(zz), y_last(zz)):
                    cp.wait_recv()

                def total(to_top, to_low, *came):
                    add_rows(
                        to_top, [own.at[zz, d, top], s1a.at[zz, 0, here], s2.at[zz, top]] + [x.at[zz, top] for x in came], half
                    )
                    add_rows(
                        to_low, [own.at[zz, d, low], s1b.at[zz, 0, here], s2.at[zz, low]] + [x.at[zz, low] for x in came], half
                    )

                if k < 3:
                    mine = (own.at[zz, d, top], own.at[zz, d, low])

                    @pl.when((zz > z) & (z > 0))
                    def _():
                        z_up(zz).wait_recv()
                        total(*mine, zup)

                    @pl.when((zz < z) & (z < 3))
                    def _():
                        z_dn(zz).wait_recv()
                        total(*mine, zdn)

                    @pl.when(((zz > z) & (z == 0)) | ((zz < z) & (z == 3)))
                    def _():
                        total(*mine)

                    pl.when(zz > z)(lambda: z_up(zz).start())
                    pl.when(zz < z)(lambda: z_dn(zz).start())
                else:
                    result = (out_ref.at[top], out_ref.at[low])
                    pl.when(z > 0)(lambda: z_up(zz).wait_recv())
                    pl.when(z < 3)(lambda: z_dn(zz).wait_recv())
                    pl.when(inner)(lambda: total(*result, zup, zdn))
                    pl.when(z == 0)(lambda: total(*result, zdn))
                    pl.when(z == 3)(lambda: total(*result, zup))

            def sent(k):
                zz = order[k]
                for dd in range(4):
                    core(zz, dd).wait_send()
                for cp in (y_own(zz), x_own(zz), x_last(zz), y_last(zz)):
                    cp.wait_send()

                def crosses_sent():
                    y_cross(zz).wait_send()
                    x_cross(zz).wait_send()

                in_plane(k, crosses_sent)
                outward(k, lambda cp: cp.wait_send())
                if k < 3:
                    pl.when(zz > z)(lambda: z_up(zz).wait_send())
                    pl.when(zz < z)(lambda: z_dn(zz).wait_send())

            return dict(load=load, issue=issue, F=first, D=diagonal, S=second, T=third, sent=sent)

        parts = {"a": part(0), "b": part(1)}
        schedule = list(SCHEDULE)
        firsts = [step for step in schedule if step[0] == "F"]
        for step in firsts:
            for dd in (xyn, yn, xn, d):
                parts[step[2]]["load"](int(step[1]), dd).start()

        pl.semaphore_wait(barrier, 4 + (z + 2) // 3 + (5 - z) // 3)

        def issue_next():
            if firsts:
                step = firsts.pop(0)
                parts[step[2]]["issue"](int(step[1]))

        def extra_step(i, dev):
            return remote(epart.at[i], erecv.at[i], es.at[i], er.at[i], dev)

        extra_devs = [(d, sib), (xn, s), (yn, s), (d, zpair), (d, zfar)]

        def extra_add(i):
            extra_step(i, extra_devs[i]).wait_recv()
            a = epart[i]
            b = erecv[i]
            row = lax.broadcasted_iota(jnp.int32, a.shape, 0)
            total = jnp.where(row < SMALL_ROWS, a + b, jnp.maximum(a, b))
            if i < 4:
                epart[i + 1] = total
                extra_step(i + 1, extra_devs[i + 1]).start()
            else:
                eout_ref[...] = total

        issue_next()
        epart[0] = e_ref[...]
        extra_step(0, extra_devs[0]).start()
        for step in schedule:
            if step[0] == "E":
                extra_add(int(step[1]))
            else:
                if step[0] == "F":
                    issue_next()
                parts[step[2]][step[0]](int(step[1]))

        for i in range(5):
            extra_step(i, extra_devs[i]).wait_send()
        for k in range(4):
            for h in "ab":
                parts[h]["sent"](k)

    return pl.pallas_call(
        kernel,
        out_shape=[
            jax.ShapeDtypeStruct((OWNED, BLK), F32),
            jax.ShapeDtypeStruct((EXTRA_ROWS, BLK), F32),
        ],
        in_specs=[ANY, VMEM],
        out_specs=[VMEM, VMEM],
        scratch_shapes=[
            pltpu.VMEM((4, 4, OWNED, BLK), BF16),
            pltpu.VMEM((4, 4, OWNED, BLK), BF16),
            pltpu.VMEM((4, 2, HALF, BLK), BF16),
            pltpu.VMEM((4, 2, HALF, BLK), BF16),
            pltpu.VMEM((4, OWNED, BLK), BF16),
            pltpu.VMEM((4, OWNED, BLK), BF16),
            pltpu.VMEM((4, OWNED, BLK), BF16),
            pltpu.VMEM((4, OWNED, BLK), BF16),
            pltpu.VMEM((4, OWNED, BLK), BF16),
            pltpu.VMEM((5, EXTRA_ROWS, BLK), F32),
            pltpu.VMEM((5, EXTRA_ROWS, BLK), F32),
            pltpu.SemaphoreType.DMA((8, 4)),
            pltpu.SemaphoreType.DMA((8, 14)),
            pltpu.SemaphoreType.DMA((8, 14)),
            pltpu.SemaphoreType.DMA((5,)),
            pltpu.SemaphoreType.DMA((5,)),
        ],
        compiler_params=params(collective_id=1, has_side_effects=True),
        name="sum_gradients",
    )(grads, extra)


ROWB = 256


PAIRS = HEADS // 2


def rope(p, cos_t, fwd_t, back_t):
    return p * cos_t + pltpu.roll(p, BLK - ROT // 2, 1) * fwd_t + pltpu.roll(p, ROT // 2, 1) * back_t


def by_pair(value):
    return [value[:, j * BLK : (j + 1) * BLK] for j in range(PAIRS)]


def side_by_side(ref, at=slice(None)):
    return jnp.concatenate([ref[j, at, :] for j in range(PAIRS)], axis=1)


def spread_tables(cos8, sin8):
    none = jnp.zeros_like(cos8)
    rest = (HEAD - ROT) // none.shape[0]
    cos_t = [cos8, cos8] + [none + 1.0] * rest
    fwd_t = [-sin8, none] + [none] * rest
    back_t = [none, sin8] + [none] * rest
    return [jnp.concatenate(t * 2, axis=0).T for t in (cos_t, fwd_t, back_t)]


PROWS = 512


def project(w_rows, w_all, prev_tokens, tokens, cotangent, smalls, tables):
    rows = tokens.shape[0]
    cos8, sin8 = tables
    steps = rows // PROWS

    def kernel(
        w_rows_ref, w_ref, prev_ref, tok_ref, g_ref, small_ref, cos_ref, sin_ref,
        q_ref, k_ref, v_ref, do_ref, m_ref, wqkv, wo, sems,
    ):
        i = pl.program_id(0)

        def third_copy(third):
            def body(t):
                r, cc = t // 8, t % 8
                src = w_ref.at[pl.ds(pl.multiple_of(w_rows_ref[r * 24 + third * 8 + cc], 16), BLK)]
                dst = wqkv.at[pl.ds(pl.multiple_of(r * BLK, BLK), BLK), pl.ds(pl.multiple_of(third * D + cc * BLK, BLK), BLK)]
                pltpu.make_async_copy(src, dst, sems.at[third]).start()

            tile_loop(0, 64, body)

        def third_wait(third):
            part = wqkv.at[:, pl.ds(third * D, D)]
            pltpu.make_async_copy(part, part, sems.at[third]).wait()

        @pl.when(i == 0)
        def _():
            third_copy(1)
            third_copy(2)
            third_copy(0)

            def body(t):
                r, cc = t // 8, t % 8
                src = w_ref.at[pl.ds(pl.multiple_of(w_rows_ref[OUT_BASE + t], 16), BLK)]
                dst = wo.at[pl.ds(pl.multiple_of(r * BLK, BLK), BLK), pl.ds(pl.multiple_of(cc * BLK, BLK), BLK)]
                pltpu.make_async_copy(src, dst, sems.at[3]).start()

            tile_loop(0, 64, body)
            third_wait(1)
            third_wait(2)

        @pl.when(i == steps)
        def _():
            third_wait(0)
            pltpu.make_async_copy(wo, wo, sems.at[3]).wait()

        n = PROWS // ROWB

        def put(ref, at, pieces):
            for j in range(PAIRS):
                ref[j, at, :] = pieces[j].astype(BF16)

        def run(own):
            x_ref = tok_ref if own else prev_ref
            ins, tabs, raw = {}, {}, {}

            def prepare(c):
                at = slice(c * ROWB, (c + 1) * ROWB)
                normed, _ = norm_rows(x_ref[at, :].astype(F32))
                ins[c] = (normed * small_ref[G1, :] + small_ref[C1, :]).astype(BF16)
                if own:
                    m_ref[at, :] = (normed * small_ref[G2, :] + small_ref[C2, :]).astype(BF16)
                yield
                tabs[c] = spread_tables(cos_ref[:, at], sin_ref[:, at])
                yield

            def multiply(c):
                at = slice(c * ROWB, (c + 1) * ROWB)
                raw[c] = [dot(ins[c], wqkv[:, D : 2 * D])]
                yield
                put(v_ref, at, by_pair(dot(ins[c], wqkv[:, 2 * D :]) + small_ref[B_V, :]))
                yield
                if own:
                    raw[c].append(dot(ins[c], wqkv[:, :D]) + small_ref[B_Q, :])
                    yield
                    put(do_ref, at, by_pair(dot(g_ref[at, :], wo[...], NT)))
                    yield

            def turn(c):
                at = slice(c * ROWB, (c + 1) * ROWB)
                put(k_ref, at, [rope(p, *tabs[c]) for p in by_pair(raw[c][0])])
                yield
                if own:
                    put(q_ref, at, [rope(p, *tabs[c]) for p in by_pair(raw[c][1])])
                    yield

            for c in range(n + 2):
                parts = []
                if 0 <= c - 1 < n:
                    parts.append(multiply(c - 1))
                if c < n:
                    parts.append(prepare(c))
                if 0 <= c - 2 < n:
                    parts.append(turn(c - 2))
                interleave(*parts)

        @pl.when(i < steps)
        def _():
            run(False)

        @pl.when(i >= steps)
        def _():
            run(True)

    before = pl.BlockSpec((PROWS, D), lambda i, *_: (jnp.minimum(i, steps - 1), 0))
    block = pl.BlockSpec((PROWS, D), lambda i, *_: (jnp.maximum(i - steps, 0), 0))
    here = pl.BlockSpec((PAIRS, PROWS, BLK), lambda i, *_: (0, i, 0))
    own = pl.BlockSpec((PAIRS, PROWS, BLK), lambda i, *_: (0, jnp.maximum(i - steps, 0), 0))
    table = pl.BlockSpec((ROT // 2, PROWS), lambda i, *_: (0, i))
    return pl.pallas_call(
        kernel,
        grid_spec=pltpu.PrefetchScalarGridSpec(
            num_scalar_prefetch=1,
            grid=(2 * steps,),
            in_specs=[
                ANY, before, block, block,
                pl.BlockSpec((16, D), lambda i, *_: (0, 0)), table, table,
            ],
            out_specs=[own, here, here, own, block],
            scratch_shapes=[
                pltpu.VMEM((D, 3 * D), BF16),
                pltpu.VMEM((D, D), BF16),
                pltpu.SemaphoreType.DMA((4,)),
            ],
        ),
        out_shape=[
            jax.ShapeDtypeStruct((PAIRS, rows, BLK), BF16),
            jax.ShapeDtypeStruct((PAIRS, 2 * rows, BLK), BF16),
            jax.ShapeDtypeStruct((PAIRS, 2 * rows, BLK), BF16),
            jax.ShapeDtypeStruct((PAIRS, rows, BLK), BF16),
            jax.ShapeDtypeStruct((rows, D), BF16),
        ],
        compiler_params=params(dimension_semantics=("arbitrary",)),
        name="project",
    )(w_rows, w_all, prev_tokens, tokens, cotangent, smalls, cos8, sin8)


QB = 256
SPAN = WINDOW + QB


CHUNK = 256
SAFE_SCORE = 60.0


def attend(q, k, v, d_out, prev_seg, seg, cos8, sin8):
    rows = q.shape[1]
    blocks = rows // QB
    scale = HEAD ** (-0.5)
    half = ROT // 2
    n = SPAN // CHUNK

    def heads_apart(x):
        row = lax.broadcasted_iota(jnp.int32, x.shape, 0)
        zero = jnp.zeros_like(x)
        return jnp.concatenate([jnp.where(row < HEAD, x, zero), jnp.where(row < HEAD, zero, x)], axis=1)

    def stacked(x):
        lane = lax.broadcasted_iota(jnp.int32, x.shape, 1)
        zero = jnp.zeros_like(x)
        return jnp.concatenate([jnp.where(lane < HEAD, x, zero), jnp.where(lane < HEAD, zero, x)], axis=0)

    def fold(x, op):
        return op(x.reshape(x.shape[0] // 8, 8, x.shape[1]), axis=0)

    def two(x):
        return jnp.concatenate([x, x], axis=1)

    def kernel(
        q_ref, k_ref, v_ref, do_ref, pseg_ref, seg_ref, cos_ref, sin_ref,
        o_ref, dq_ref, dk_ref, dv_ref, halo_ref, peak_ref, bias, kt, vt, el_ref, ds_ref, dks, dvs, base, key_seg,
    ):
        p = pl.program_id(0)

        @pl.when(p == 0)
        def _():
            gap = (
                WINDOW
                + lax.broadcasted_iota(jnp.int32, (SPAN, QB), 1)
                - lax.broadcasted_iota(jnp.int32, (SPAN, QB), 0)
            )
            before = jnp.where(lax.axis_index("seq") == 0, -1, pseg_ref[...]).astype(F32)
            for part, numbers in enumerate((before, seg_ref[...].astype(F32))):
                column = jnp.broadcast_to(numbers[:1, :], (BLK, rows)).T
                key_seg[part * rows : (part + 1) * rows, :] = column
            for i in range(blocks):
                query_seg = seg_ref[:1, i * QB : (i + 1) * QB].astype(F32)
                same = key_seg[i * QB : i * QB + SPAN, :1] == query_seg
                bias[i] = jnp.where((gap >= 0) & (gap < WINDOW) & same, 0.0, MASKED)

        kt[...] = k_ref[...].T
        vt[...] = v_ref[...].T
        k_float = kt[...].astype(F32)
        q_float = q_ref[...].astype(F32) * scale
        reach = jnp.max(jnp.sum(k_float * k_float, axis=0)) * jnp.max(jnp.sum(q_float * q_float, axis=1))
        safe = reach < SAFE_SCORE * SAFE_SCORE

        def keys_at(ref, i, c):
            return ref[i * QB + c * CHUNK : i * QB + (c + 1) * CHUNK, :]

        def prepare(i):
            q_all = (q_ref[i * QB : (i + 1) * QB, :].astype(F32) * scale).astype(BF16)
            return q_all, heads_apart(q_all.T)

        def scores(i, c, q_apart):
            return dot(keys_at(k_ref, i, c), q_apart) + two(bias[i, c * CHUNK : (c + 1) * CHUNK])

        def row_tops(i):
            q_apart = prepare(i)[1]
            for c in range(n):
                t = fold(scores(i, c, q_apart), jnp.max)
                most = t if c == 0 else jnp.maximum(most, t)
            base[i] = jnp.max(most, axis=0, keepdims=True)

        def forward(i, q_apart, found):
            low = base[i]
            top8 = sum8 = None
            for c in range(n):
                st = scores(i, c, q_apart)
                e = jnp.exp(st - low)
                el_ref[i % 2, c * CHUNK : (c + 1) * CHUNK] = e.astype(BF16)
                t, u = fold(st, jnp.max), fold(e, jnp.sum)
                top8, sum8 = (t, u) if c == 0 else (jnp.maximum(top8, t), sum8 + u)
                yield
            found.append(jnp.max(top8, axis=0, keepdims=True))
            found.append(1.0 / jnp.sum(sum8, axis=0, keepdims=True))

        def per_head(x):
            return jnp.concatenate(
                [jnp.broadcast_to(x[:, :QB], (HEAD, QB)), jnp.broadcast_to(x[:, QB:], (HEAD, QB))], axis=0
            )

        def both(t, x_ref, i):
            span = slice(i * QB, i * QB + SPAN)
            return jnp.concatenate(
                [dot(t[:HEAD, span], x_ref[i % 2, :, :QB]), dot(t[HEAD:, span], x_ref[i % 2, :, QB:])], axis=0
            )

        def output(i, inv):
            raw = both(vt, el_ref, i)
            inv2 = per_head(inv)
            o_ref[i * QB : (i + 1) * QB, :] = (raw * inv2).T.astype(BF16)
            do_s = (do_ref[i * QB : (i + 1) * QB, :].astype(F32).T * inv2).astype(BF16)
            m = do_s.astype(F32) * raw
            mean = jnp.concatenate(
                [jnp.sum(m[:HEAD], axis=0, keepdims=True), jnp.sum(m[HEAD:], axis=0, keepdims=True)], axis=1
            )
            return do_s, mean * inv

        def score_grads(i, do_s, mean):
            do_apart = heads_apart(do_s)
            for c in range(n):
                w = slice(c * CHUNK, (c + 1) * CHUNK)
                dpt = dot(keys_at(v_ref, i, c), do_apart)
                ds_ref[i % 2, w] = (el_ref[i % 2, w].astype(F32) * (dpt - mean)).astype(BF16)

        def input_grads(i, q_all, do_s):
            do_rows = stacked(do_s.T)
            q_rows = stacked(q_all)
            for c in range(n):
                w = slice(c * CHUNK, (c + 1) * CHUNK)
                at = slice(i * QB + c * CHUNK, i * QB + (c + 1) * CHUNK)
                v_part = dot(el_ref[i % 2, w], do_rows)
                k_part = dot(ds_ref[i % 2, w], q_rows)
                if i == 0 or c == n - 1:
                    dvs[at, :] = v_part
                    dks[at, :] = k_part
                else:
                    dvs[at, :] += v_part
                    dks[at, :] += k_part
                yield
            dq = both(kt, ds_ref, i) * scale
            cos_t, sin_t = cos_ref[:, i * QB : (i + 1) * QB], sin_ref[:, i * QB : (i + 1) * QB]
            turned = []
            for h in range(2):
                f, g = dq[h * HEAD : h * HEAD + half], dq[h * HEAD + half : h * HEAD + ROT]
                turned += [f * cos_t + g * sin_t, g * cos_t - f * sin_t, dq[h * HEAD + ROT : (h + 1) * HEAD]]
            dq_ref[i * QB : (i + 1) * QB, :] = jnp.concatenate(turned, axis=0).T.astype(BF16)
            yield

        def run():
            top = held = None
            for i in range(blocks + 1):
                parts, found = [], []
                if held is not None:
                    parts.append(input_grads(i - 1, *held))
                if i < blocks:
                    q_all, q_apart = prepare(i)
                    parts.append(forward(i, q_apart, found))
                interleave(*parts)
                if i < blocks:
                    t, inv = found
                    top = t if top is None else jnp.maximum(top, t)
                    do_s, mean = output(i, inv)
                    score_grads(i, do_s, mean)
                    held = (q_all, do_s)
            peak_ref[...] = jnp.broadcast_to(top, peak_ref.shape)
            halo_ref[0] = dks[:rows, :].astype(BF16)
            halo_ref[1] = dvs[:rows, :].astype(BF16)
            dk_ref[...] = dks[rows:, :].astype(BF16)
            dv_ref[...] = dvs[rows:, :].astype(BF16)

        base[...] = jnp.zeros_like(base)

        @pl.when(jnp.logical_not(safe))
        def _():
            for i in range(blocks):
                row_tops(i)

        run()

    block = pl.BlockSpec((None, rows, BLK), lambda p: (p, 0, 0))
    keys = pl.BlockSpec((None, 2 * rows, BLK), lambda p: (p, 0, 0))
    whole = lambda *shape: pl.BlockSpec(shape, lambda p: (0, 0))
    own_rot = pl.BlockSpec((half, rows), lambda p: (0, 1))
    return pl.pallas_call(
        kernel,
        grid=(PAIRS,),
        in_specs=[
            block, keys, keys, block, whole(8, rows), whole(8, rows), own_rot, own_rot,
        ],
        out_specs=[
            block, block, block, block,
            pl.BlockSpec((2, None, rows, BLK), lambda p: (0, p, 0, 0)),
            pl.BlockSpec((8, 2 * QB), lambda p: (p, 0)),
        ],
        out_shape=[
            jax.ShapeDtypeStruct((PAIRS, rows, BLK), BF16),
            jax.ShapeDtypeStruct((PAIRS, rows, BLK), BF16),
            jax.ShapeDtypeStruct((PAIRS, rows, BLK), BF16),
            jax.ShapeDtypeStruct((PAIRS, rows, BLK), BF16),
            jax.ShapeDtypeStruct((2, PAIRS, rows, BLK), BF16),
            jax.ShapeDtypeStruct((8 * PAIRS, 2 * QB), F32),
        ],
        scratch_shapes=[
            pltpu.VMEM((blocks, SPAN, QB), F32),
            pltpu.VMEM((BLK, 2 * rows), BF16),
            pltpu.VMEM((BLK, 2 * rows), BF16),
            pltpu.VMEM((2, SPAN, 2 * QB), BF16),
            pltpu.VMEM((2, SPAN, 2 * QB), BF16),
            pltpu.VMEM((2 * rows, BLK), F32),
            pltpu.VMEM((2 * rows, BLK), F32),
            pltpu.VMEM((blocks, 1, 2 * QB), F32),
            pltpu.VMEM((2 * rows, BLK), F32),
        ],
        compiler_params=params(dimension_semantics=("arbitrary",)),
        cost_estimate=pl.CostEstimate(flops=40 << 30, bytes_accessed=32 << 20, transcendentals=20 << 20),
        name="attend",
    )(q, k, v, d_out, prev_seg, seg, cos8, sin8)


FB = 512


def gelu_parts(v):
    a = jnp.abs(v)
    t = 1.0 / (1.0 + a * (0.3275911 * 0.7071067811865476))
    poly = t * (
        0.5 * 0.254829592
        + t * (0.5 * -0.284496736 + t * (0.5 * 1.421413741 + t * (0.5 * -1.453152027 + t * (0.5 * 1.061405429))))
    )
    e = jnp.exp(v * v * -0.5)
    tail = poly * e
    cdf = jnp.where(v >= 0, 1.0 - tail, tail)
    return v * cdf, cdf + v * e * 0.3989422804014327


def feed_forward(w_rows, g_rows, w_all, m, cotangent, b_up):
    rows = m.shape[0]
    steps = FF // FB

    def kernel(
        w_rows_ref, g_rows_ref, w_ref, m_ref, g_ref, b_ref, low_ref, dml_ref, db_ref, gr_ref,
        mt, wup, wdn, hs, dus, gup, gdn, u_ref, h_ref, out_ref, dm_ref, wsem, gsem,
    ):
        f = pl.program_id(0)
        slot = f % 2
        per = FB // BLK

        def up_at(buf, t):
            return buf.at[pl.ds(pl.multiple_of((t // per) * BLK, BLK), BLK), pl.ds(pl.multiple_of((t % per) * BLK, BLK), BLK)]

        def up_tile(ff, t):
            return UP_BASE + (t // per) * (FF // BLK) + ff * per + t % per

        def down_at(buf, t):
            return buf.at[pl.ds(pl.multiple_of((t // 8) * BLK, BLK), BLK), pl.ds(pl.multiple_of((t % 8) * BLK, BLK), BLK)]

        def down_tile(ff, t):
            return DOWN_BASE + ff * per * 8 + t

        def fetch_one(ff, sl, t):
            src = w_ref.at[pl.ds(pl.multiple_of(w_rows_ref[up_tile(ff, t)], 16), BLK)]
            pltpu.make_async_copy(src, up_at(wup.at[sl], t), wsem.at[0, sl]).start()
            src = w_ref.at[pl.ds(pl.multiple_of(w_rows_ref[down_tile(ff, t)], 16), BLK)]
            pltpu.make_async_copy(src, down_at(wdn.at[sl], t), wsem.at[1, sl]).start()

        def store_one(ff, sl, t):
            dst = gr_ref.at[pl.ds(pl.multiple_of(g_rows_ref[up_tile(ff, t)], 16), BLK)]
            pltpu.make_async_copy(up_at(gup.at[sl], t), dst, gsem.at[0, sl]).start()
            dst = gr_ref.at[pl.ds(pl.multiple_of(g_rows_ref[down_tile(ff, t)], 16), BLK)]
            pltpu.make_async_copy(down_at(gdn.at[sl], t), dst, gsem.at[1, sl]).start()

        def whole_wait(buf, sem):
            pltpu.make_async_copy(buf, buf, sem).wait()

        count = 8 * per

        @pl.when(f == 0)
        def _():
            tile_loop(0, count, lambda t: fetch_one(0, 0, t))
            mt[...] = m_ref[...].T
            out_ref[...] = jnp.zeros_like(out_ref)
            dm_ref[...] = jnp.zeros_like(dm_ref)

        whole_wait(wup.at[slot], wsem.at[0, slot])
        whole_wait(wdn.at[slot], wsem.at[1, slot])

        @pl.when(f >= 2)
        def _():
            whole_wait(gup.at[slot], gsem.at[0, slot])
            whole_wait(gdn.at[slot], gsem.at[1, slot])

        n = rows // ROWB

        def stage1(c):
            at = slice(c * ROWB, (c + 1) * ROWB)
            for k in range(FB // 256):
                cols = slice(k * 256, (k + 1) * 256)
                u_ref[c % 2, :, cols] = dot(m_ref[at, :], wup[slot, :, cols]) + b_ref[:, cols]
                yield
                h_ref[c % 2, :, cols] = dot(g_ref[at, :], wdn[slot, cols, :], NT)
                yield

        db = [None]

        def stage2(c):
            step = ROWB // 8
            for k in range(8):
                at = slice(k * step, (k + 1) * step)
                to = slice(c * ROWB + k * step, c * ROWB + (k + 1) * step)
                hidden, slope = gelu_parts(u_ref[c % 2, at, :])
                hs[to, :] = hidden.astype(BF16)
                du = (h_ref[c % 2, at, :] * slope).astype(BF16)
                dus[to, :] = du
                t = jnp.sum(du.astype(F32).reshape(step // 8, 8, FB), axis=0)
                db[0] = t if db[0] is None else db[0] + t
                yield

        def stage3(c):
            at = slice(c * ROWB, (c + 1) * ROWB)
            for k in range(D // 256):
                cols = slice(k * 256, (k + 1) * 256)
                out_ref[at, cols] += dot(hs[at, :], wdn[slot, :, cols])
                yield
                dm_ref[at, cols] += dot(dus[at, :], wup[slot, cols, :], NT)
                yield

        nxt = jnp.minimum(f + 1, steps - 1)
        for t in range(count):
            fetch_one(nxt, 1 - slot, t)

        for c in range(n + 2):
            gens = []
            if c < n:
                gens.append(stage1(c))
            if 0 <= c - 1 < n:
                gens.append(stage2(c - 1))
            if 0 <= c - 2 < n:
                gens.append(stage3(c - 2))
            interleave(*gens)
        db_ref[...] = jnp.sum(db[0], axis=0, keepdims=True)
        gdn[slot] = dot(hs[...], g_ref[...], TN).astype(BF16)
        gup[slot] = dot(mt[...], dus[...]).astype(BF16)
        for t in range(count):
            store_one(f, slot, t)


        @pl.when(f == steps - 1)
        def _():
            low_ref[...] = out_ref[...].astype(BF16)
            dml_ref[...] = dm_ref[...].astype(BF16)
            whole_wait(wup.at[1 - slot], wsem.at[0, 1 - slot])
            whole_wait(wdn.at[1 - slot], wsem.at[1, 1 - slot])
            for sl in range(2):
                whole_wait(gup.at[sl], gsem.at[0, sl])
                whole_wait(gdn.at[sl], gsem.at[1, sl])

    full = pl.BlockSpec((rows, D), lambda f, *_: (0, 0))
    bias = pl.BlockSpec((1, FB), lambda f, *_: (0, f))
    return pl.pallas_call(
        kernel,
        grid_spec=pltpu.PrefetchScalarGridSpec(
            num_scalar_prefetch=2,
            grid=(steps,),
            in_specs=[ANY, full, full, bias],
            out_specs=[full, full, bias, ANY],
            scratch_shapes=[
                pltpu.VMEM((D, rows), BF16),
                pltpu.VMEM((2, D, FB), BF16),
                pltpu.VMEM((2, FB, D), BF16),
                pltpu.VMEM((rows, FB), BF16),
                pltpu.VMEM((rows, FB), BF16),
                pltpu.VMEM((2, D, FB), BF16),
                pltpu.VMEM((2, FB, D), BF16),
                pltpu.VMEM((2, ROWB, FB), F32),
                pltpu.VMEM((2, ROWB, FB), F32),
                pltpu.VMEM((rows, D), F32),
                pltpu.VMEM((rows, D), F32),
                pltpu.SemaphoreType.DMA((2, 2)),
                pltpu.SemaphoreType.DMA((2, 2)),
            ],
        ),
        out_shape=[
            jax.ShapeDtypeStruct((rows, D), BF16),
            jax.ShapeDtypeStruct((rows, D), BF16),
            jax.ShapeDtypeStruct((1, FF), F32),
            jax.ShapeDtypeStruct((TILES * BLK, BLK), BF16),
        ],
        compiler_params=params(dimension_semantics=("arbitrary",)),
        cost_estimate=pl.CostEstimate(flops=52 << 30, bytes_accessed=48 << 20, transcendentals=8 << 20),
        name="feed_forward",
    )(w_rows, g_rows, w_all, m, cotangent, b_up)


def finish(
    w_rows, g_rows, w_all, tokens, cotangent, smalls, attn_out, mlp_out, dm, dq, dk, dv, halo, tables, grads
):
    rows = tokens.shape[0]
    steps = rows // ROWB
    q_cols = 3 * D // FB
    o_cols = D // FB
    per = FB // BLK
    last = steps + q_cols + o_cols
    cos8, sin8 = tables

    def kernel(
        w_rows_ref, g_rows_ref, w_ref, tok_ref, g_ref, small_ref, o_ref, mlp_ref, dm_ref, dq_ref, dk_ref, dv_ref,
        halo_ref, cos_ref, sin_ref, _,
        out_ref, dx_ref, sum_ref, gr_ref, wqkv, wo, at, dp, stage, sems, gsem,
    ):
        i = pl.program_id(0)

        def fetch(first, count, width, dst, sem):
            def body(t):
                src = w_ref.at[pl.ds(pl.multiple_of(w_rows_ref[first + t], 16), BLK)]
                r, c = t // width, t % width
                to = dst.at[pl.ds(pl.multiple_of(r * BLK, BLK), BLK), pl.ds(pl.multiple_of(c * BLK, BLK), BLK)]
                pltpu.make_async_copy(src, to, sem).start()

            tile_loop(0, count, body)

        @pl.when(i == 0)
        def _():
            fetch(OUT_BASE, OUT_TILES, D // BLK, wo, sems.at[0])
            fetch(0, QKV_TILES, 3 * D // BLK, wqkv, sems.at[1])
            sum_ref[...] = jnp.zeros_like(sum_ref)
            pltpu.make_async_copy(wo, wo, sems.at[0]).wait()

        @pl.when(i < steps)
        def _():
            here = pl.ds(pl.multiple_of(i * ROWB, ROWB), ROWB)
            x = tok_ref[...].astype(F32)
            grad = g_ref[here, :].astype(F32)
            normed, inv = norm_rows(x)
            g1, g2 = small_ref[G1, :], small_ref[G2, :]
            attn = dot(side_by_side(o_ref, here), wo[...]) + small_ref[B_O, :]
            out_ref[...] = (x + attn + (mlp_ref[...].astype(F32) + small_ref[B_DOWN, :])).astype(BF16)
            back = spread_tables(cos_ref[...], -sin_ref[...])
            for j in range(PAIRS):
                cols = j * BLK
                dk_all = dk_ref[j].astype(F32) + halo_ref[0, j].astype(F32)
                dv_all = dv_ref[j].astype(F32) + halo_ref[1, j].astype(F32)
                dp[here, cols : cols + BLK] = dq_ref[j]
                dp[here, D + cols : D + cols + BLK] = rope(dk_all, *back).astype(BF16)
                dp[here, 2 * D + cols : 2 * D + cols + BLK] = dv_all.astype(BF16)

            @pl.when(i == 0)
            def _():
                pltpu.make_async_copy(wqkv, wqkv, sems.at[1]).wait()

            da = dot(dp[here, :], wqkv[...], NT)
            at[:, here] = (normed * g1 + small_ref[C1, :]).astype(BF16).T
            dmv = dm_ref[...].astype(F32)
            dn = da * g1 + dmv * g2
            mean_dn = jnp.mean(dn, axis=-1, keepdims=True)
            mean_dnn = jnp.mean(dn * normed, axis=-1, keepdims=True)
            dx_ref[...] = grad + inv * (dn - mean_dn - normed * mean_dnn)

            def add(row, value):
                sum_ref[row : row + 1, :] += jnp.sum(value, axis=0, keepdims=True)

            add(0, dp[here, :D].astype(F32))
            add(1, dp[here, 2 * D :].astype(F32))
            add(2, grad)
            add(3, da * normed)
            add(4, da)
            add(5, dmv * normed)
            add(6, dmv)

        slot = i % 2

        def drain(sl):
            pltpu.make_async_copy(stage.at[sl], stage.at[sl], gsem.at[sl]).wait()

        def send(first, width, c):
            for t in range(8 * per):
                tile = first + (t // per) * width + c * per + t % per
                dst = gr_ref.at[pl.ds(pl.multiple_of(g_rows_ref[tile], 16), BLK)]
                r, k = t // per * BLK, t % per * BLK
                pltpu.make_async_copy(stage.at[slot, r : r + BLK, k : k + BLK], dst, gsem.at[slot]).start()

        @pl.when(i >= steps + 2)
        def _():
            drain(slot)

        @pl.when((i >= steps) & (i < steps + q_cols))
        def _():
            c = i - steps
            stage[slot] = dot(at[...], dp[:, pl.ds(pl.multiple_of(c * FB, FB), FB)]).astype(BF16)
            send(0, 3 * D // BLK, c)

        @pl.when(i >= steps + q_cols)
        def _():
            c = i - steps - q_cols
            stage[slot] = dot(side_by_side(o_ref), g_ref[:, pl.ds(pl.multiple_of(c * FB, FB), FB)], TN).astype(BF16)
            send(OUT_BASE, D // BLK, c)

        @pl.when(i == last - 1)
        def _():
            drain(0)
            drain(1)

    here = lambda i, *_: (jnp.minimum(i, steps - 1), 0)
    whole = lambda *shape: pl.BlockSpec(shape, lambda i, *_: (0, 0))
    block = pl.BlockSpec((ROWB, D), here)
    pairs = pl.BlockSpec((PAIRS, ROWB, BLK), lambda i, *_: (0, jnp.minimum(i, steps - 1), 0))
    table = pl.BlockSpec((ROT // 2, ROWB), lambda i, *_: (0, steps + jnp.minimum(i, steps - 1)))
    return pl.pallas_call(
        kernel,
        grid_spec=pltpu.PrefetchScalarGridSpec(
            num_scalar_prefetch=2,
            grid=(last,),
            in_specs=[
                ANY, block, whole(rows, D), whole(16, D), pl.BlockSpec((PAIRS, rows, BLK), lambda i, *_: (0, 0, 0)),
                block, block, pairs, pairs, pairs,
                pl.BlockSpec((2, PAIRS, ROWB, BLK), lambda i, *_: (0, 0, jnp.minimum(i, steps - 1), 0)),
                table, table, ANY,
            ],
            out_specs=[block, block, whole(8, D), ANY],
            scratch_shapes=[
                pltpu.VMEM((D, 3 * D), BF16),
                pltpu.VMEM((D, D), BF16),
                pltpu.VMEM((D, rows), BF16),
                pltpu.VMEM((rows, 3 * D), BF16),
                pltpu.VMEM((2, D, FB), BF16),
                pltpu.SemaphoreType.DMA((2,)),
                pltpu.SemaphoreType.DMA((2,)),
            ],
        ),
        out_shape=[
            jax.ShapeDtypeStruct((rows, D), BF16),
            jax.ShapeDtypeStruct((rows, D), F32),
            jax.ShapeDtypeStruct((8, D), F32),
            jax.ShapeDtypeStruct(grads.shape, BF16),
        ],
        input_output_aliases={15: 3},
        compiler_params=params(dimension_semantics=("arbitrary",)),
        name="finish",
    )(w_rows, g_rows, w_all, tokens, cotangent, smalls, attn_out, mlp_out, dm, dq, dk, dv, halo, cos8, sin8, grads)


def halves(x):
    high = x.astype(BF16)
    return high, (x - high.astype(F32)).astype(BF16)


def dot3(a, b, dims=NN):
    return dot(a[0], b[0], dims) + (dot(a[0], b[1], dims) + dot(a[1], b[0], dims))


def update_tiles(grads, tiles, left, right, first, second, scale):
    count = tiles.shape[0]
    group = max(g for g in (1, 2, 3, 4, 6, 8) if count % g == 0)

    def kernel(g_ref, w_ref, l_ref, r_ref, m_ref, v_ref, s_ref, w_out, low_out, m_out, v_out):
        turned = []
        for t in range(group):
            l, r = halves(l_ref[t]), halves(r_ref[t])
            turned.append(dot3(halves(dot3(l, halves(g_ref[t]), TN)), r))
        for t in range(group):
            l, r = halves(l_ref[t]), halves(r_ref[t])
            m_new = BETA * m_ref[t] + (1.0 - BETA) * turned[t]
            v_new = BETA * v_ref[t] + (1.0 - BETA) * turned[t] * turned[t]
            ratio = m_new / (jnp.sqrt(v_new) + ADAM_EPS)
            back = dot3(halves(dot3(l, halves(ratio))), r, NT)
            w_new = (w_ref[t] - LEARN * back) * s_ref[t]
            w_out[t] = w_new
            low_out[t] = w_new.astype(BF16)
            m_out[t] = m_new
            v_out[t] = v_new

    block = pl.BlockSpec((group, BLK, BLK), lambda i: (i, 0, 0))
    row = pl.BlockSpec((group, 1, BLK), lambda i: (i, 0, 0))
    like = lambda t: jax.ShapeDtypeStruct(tiles.shape, t)
    return pl.pallas_call(
        kernel,
        grid=(count // group,),
        in_specs=[block] * 6 + [row],
        out_specs=[block] * 4,
        out_shape=[like(F32), like(BF16), like(F32), like(F32)],
        compiler_params=params(dimension_semantics=("arbitrary",)),
        name="update_tiles",
    )(grads, tiles, left, right, first, second, scale)


def column_scales(tile_ids, factors):
    columns = (tile_ids % (3 * D // BLK))[:, None] * BLK + jnp.arange(BLK, dtype=jnp.int32)[None, :]
    head_index = columns % D // HEAD
    root_factor = jnp.sqrt(factors)
    picked = jnp.sum(
        jnp.where(head_index[..., None] == jnp.arange(HEADS, dtype=jnp.int32), root_factor, 0.0),
        axis=-1,
    )
    clipped = (tile_ids[:, None] < QKV_TILES) & (columns < 2 * D)
    return jnp.where(clipped, picked, 1.0)


def small_update(grads, params_, first_moment, second_moment):
    first_new = BETA * first_moment + (1.0 - BETA) * grads
    second_new = BETA * second_moment + (1.0 - BETA) * grads * grads
    updated = params_ - SMALL_LEARN * first_new / (jnp.sqrt(second_new) + ADAM_EPS)
    return (updated, first_new, second_new)


def passed_along(value, axis, steps):
    count = lax.axis_size(axis)
    leading, last = (max(0, -steps), min(count, count - steps))
    return lax.ppermute(value, axis, [(source, source + steps) for source in range(leading, last)])


def on_device(
    ring,
    tokens,
    segments,
    cotangent,
    tile_of_slot,
    tiles,
    left_bases,
    right_bases,
    first_moments,
    second_moments,
    small_params,
    small_first,
    small_second,
    threshold,
):
    rows = tokens.shape[0]
    slot_count = tiles.shape[0]
    small_count = small_params.shape[0]
    axes = ("dp", "seq")
    seq_index = lax.axis_index("seq")
    owner_index = lax.axis_index(axes)
    first_place = seq_index * rows
    seg_rows = jnp.broadcast_to(segments.reshape(1, rows), (8, rows))

    numbers = jnp.arange(TILES, dtype=jnp.int32)
    slot_of_tile = jnp.sum(
        jnp.where(tile_of_slot[None, :] == numbers[:, None], numbers[None, :], 0), axis=1
    ).astype(jnp.int32)
    g_rows = slot_of_tile * BLK

    if ring:
        features = small_count // 12
        kinds = jnp.tile(small_params.reshape(features, 12).T, (1, BLK // features))
        place = jnp.arange(BLK, dtype=jnp.int32) // features == owner_index % (BLK // features)
        small_block = jnp.concatenate([jnp.where(place, kinds, 0.0), jnp.zeros((4, BLK), F32)], axis=0)
        payload = jnp.concatenate(
            [tiles.astype(BF16).reshape(slot_count * BLK, BLK), small_block.astype(BF16)], axis=0
        )
        gathered, prev_tokens, prev_seg = gather_weights(payload, tokens, seg_rows)
        stride = payload.shape[0]
        w_all = gathered.reshape(-1, BLK)
        w_rows = slot_of_tile // slot_count * stride + slot_of_tile % slot_count * BLK
        tail = slot_count * BLK
        group = BLK // features
        by_kind = jnp.sum(gathered[:, tail:, :].astype(F32).reshape(D // BLK, group, 16, BLK), axis=1)
        by_kind = by_kind.transpose(1, 0, 2).reshape(16, D)
    else:
        w_all = lax.all_gather(tiles.astype(BF16), axes, axis=0, tiled=True).reshape(-1, BLK)
        w_rows = g_rows
        small_all = lax.all_gather(small_params.astype(BF16), axes, axis=0, tiled=True)
        by_kind = jnp.pad(small_all.astype(F32).reshape(D, 12).T, ((0, 4), (0, 0)))
        prev_tokens, prev_seg = passed_along((tokens, seg_rows), "seq", 1)

    b_up = by_kind[3:7].T.reshape(1, FF)

    half = ROT // 2
    exponent = jnp.arange(half, dtype=F32) * (2.0 / ROT)
    frequency = jnp.power(ROPE_BASE, -exponent)
    places = first_place - rows + jnp.arange(2 * rows, dtype=jnp.int32)
    angle = places.astype(F32)[None, :] * frequency[:, None]
    cos8, sin8 = jnp.cos(angle), jnp.sin(angle)
    tables = (cos8, sin8)

    q, k, v, d_out, m = project(w_rows, w_all, prev_tokens, tokens, cotangent, by_kind, tables)
    attn_out, dq, dk, dv, halo, peaks = attend(q, k, v, d_out, prev_seg, seg_rows, cos8, sin8)
    halo = passed_along(halo, "seq", -1)
    mlp_out, dm, db_up, grads = feed_forward(w_rows, g_rows, w_all, m, cotangent, b_up)
    block_output, input_grad, sums, grads = finish(
        w_rows, g_rows, w_all, tokens, cotangent, by_kind, attn_out, mlp_out, dm, dq, dk, dv, halo, tables, grads
    )

    small_terms = jnp.concatenate(
        [
            sums[:3].T,
            db_up.reshape(D, FF // D),
            sums[2:7].T,
        ],
        axis=1,
    ).reshape(SMALL)
    head_peak = jnp.max(peaks.reshape(PAIRS, 8, 2, QB)[:, 0], axis=-1).reshape(HEADS)
    if ring:
        peak_rows = jnp.zeros((8, BLK), F32).at[:, :HEADS].set(head_peak[None, :])
        extra = jnp.concatenate([small_terms.reshape(SMALL_ROWS, BLK), peak_rows], axis=0)
        tile_grads, extra = sum_gradients(grads, extra)
        tile_grads = tile_grads.reshape(slot_count, BLK, BLK)
        small_grads = lax.dynamic_slice_in_dim(
            extra[:SMALL_ROWS].reshape(SMALL), owner_index * small_count, small_count, 0
        )
        head_peak = extra[SMALL_ROWS, :HEADS]
    else:
        tile_grads = lax.psum_scatter(
            grads.astype(F32).reshape(TILES, BLK, BLK), axes, scatter_dimension=0, tiled=True
        )
        small_grads = lax.psum_scatter(small_terms, axes, scatter_dimension=0, tiled=True)
        head_peak = lax.pmax(head_peak, axes)

    local_ids = lax.dynamic_slice_in_dim(tile_of_slot, owner_index * slot_count, slot_count, 0)
    limit = threshold[0]
    factors = limit / jnp.maximum(head_peak, limit)
    scale = column_scales(local_ids, factors).reshape(slot_count, 1, BLK)
    new_tiles, new_low, new_first, new_second = update_tiles(
        tile_grads, tiles, left_bases, right_bases, first_moments, second_moments, scale
    )
    new_small, new_small_first, new_small_second = small_update(
        small_grads, small_params, small_first, small_second
    )
    return (
        block_output,
        input_grad,
        tile_grads,
        small_grads,
        new_tiles,
        new_low,
        new_first,
        new_second,
        new_small,
        new_small.astype(BF16),
        new_small_first,
        new_small_second,
        factors,
    )


def solution(mesh):
    split = P(("dp", "seq"))
    in_specs = (split, P("dp", "seq"), split, P()) + (split,) * 8 + (P(),)
    out_specs = (split,) * 12 + (P(),)
    ring = (mesh.shape["dp"], mesh.shape["seq"]) == (4, 8)
    return jax.shard_map(
        functools.partial(on_device, ring), mesh=mesh, in_specs=in_specs, out_specs=out_specs, check_vma=False
    )
```

```python
import functools

import jax
import jax.numpy as jnp
from jax import lax
from jax.experimental import pallas as pl
from jax.experimental.pallas import tpu as pltpu
from jax.sharding import PartitionSpec as P

D = 1024
FF = 4096
HEADS = 16
HEAD = 64
ROT = 16
BLK = 128
WINDOW = 1024
TILES = 768
SMALL = 12288
QKV_TILES = D // BLK * (3 * D // BLK)
OUT_TILES = D // BLK * (D // BLK)
UP_TILES = D // BLK * (FF // BLK)
OUT_BASE = QKV_TILES
UP_BASE = QKV_TILES + OUT_TILES
DOWN_BASE = UP_BASE + UP_TILES

B_Q, B_V, B_O = slice(0, 1), slice(1, 2), slice(2, 3)
B_DOWN, G1, C1, G2, C2 = slice(7, 8), slice(8, 9), slice(9, 10), slice(10, 11), slice(11, 12)

NORM_EPS = 1e-05
ADAM_EPS = 1e-08
BETA = 0.5
LEARN = 0.03
SMALL_LEARN = 0.2
ROPE_BASE = 10000.0
MASKED = -1e30
HIGH = lax.Precision.HIGHEST

F32 = jnp.float32
BF16 = jnp.bfloat16
MESH = pl.DeviceIdType.MESH
ANY = pl.BlockSpec(memory_space=pl.ANY)
VMEM = pl.BlockSpec(memory_space=pltpu.VMEM)
VMEM_LIMIT = 58 << 20

NN = (((1,), (0,)), ((), ()))
NT = (((1,), (1,)), ((), ()))
TN = (((0,), (0,)), ((), ()))


def dot(a, b, dims=NN, precision=None):
    return lax.dot_general(a, b, dims, precision=precision, preferred_element_type=F32)


def interleave(*parts):
    live = list(parts)
    while live:
        for part in list(live):
            try:
                next(part)
            except StopIteration:
                live.remove(part)


def params(**kw):
    return pltpu.CompilerParams(vmem_limit_bytes=VMEM_LIMIT, **kw)


def norm_rows(x):
    centered = x - jnp.mean(x, axis=-1, keepdims=True)
    inv = lax.rsqrt(jnp.mean(centered * centered, axis=-1, keepdims=True) + NORM_EPS)
    return centered * inv, inv


def tile_loop(first, count, body):
    def step(t, carry):
        body(t)
        return carry

    lax.fori_loop(first, first + count, step, 0)


ROWS_PER_TILE = BLK
HALF_ROWS = 1536


def gather_weights(payload, tokens, seg_rows):
    rows = payload.shape[0]
    top = pl.ds(0, HALF_ROWS)
    low = pl.ds(HALF_ROWS, rows - HALF_ROWS)

    def kernel(x_ref, tok_ref, seg_ref, out_ref, ptok_ref, pseg_ref, lsem, ss, rs, hss, hrs, hls):
        d = lax.axis_index("dp")
        s = lax.axis_index("seq")
        z = s // 2
        c = s % 2
        xn = d + 1 - 2 * (d % 2)
        yn = d + 2 - 4 * (d // 2)
        xyn = 3 - d
        sib = z * 2 + 1 - c
        halo = s - 1 + 2 * c
        halo_ok = ((c == 0) & (z > 0)) | ((c == 1) & (z < 3))

        barrier = pltpu.get_barrier_semaphore()

        def greet(dev):
            pl.semaphore_signal(barrier, inc=1, device_id=dev, device_id_type=MESH)

        greet((d, sib))
        greet((xn, s))
        greet((yn, s))

        @pl.when(z > 0)
        def _():
            greet((d, s - 2))

        @pl.when(z < 3)
        def _():
            greet((d, s + 2))

        @pl.when(halo_ok)
        def _():
            greet((d, halo))

        below, above = (z + 2) // 3, (5 - z) // 3
        pl.semaphore_wait(barrier, 3 + below + above + (1 - c) * below + c * above)

        def place(dd, zz):
            return out_ref.at[dd * 8 + zz * 2 + c]

        def remote(src, dst, kind, zz, dev):
            return pltpu.make_async_remote_copy(
                src_ref=src,
                dst_ref=dst,
                send_sem=ss.at[kind, zz],
                recv_sem=rs.at[kind, zz],
                device_id=dev,
                device_id_type=MESH,
            )

        def block_of(zz, own):
            return x_ref if own else place(d, zz)

        def up(zz, own):
            return remote(block_of(zz, own), place(d, zz), 0, zz, (d, s + 2))

        def down(zz, own):
            return remote(block_of(zz, own), place(d, zz), 1, zz, (d, s - 2))

        def to_x(zz, own):
            return remote(block_of(zz, own), place(d, zz), 2, zz, (xn, s))

        def to_y(zz, own):
            return remote(block_of(zz, own), place(d, zz), 3, zz, (yn, s))

        def on_y(zz):
            return remote(place(xn, zz).at[top], place(xn, zz).at[top], 4, zz, (yn, s))

        def on_x(zz):
            return remote(place(yn, zz).at[low], place(yn, zz).at[low], 5, zz, (xn, s))

        def to_sib(dd, zz, kind, own=False):
            src = x_ref if own else place(dd, zz)
            return remote(src, place(dd, zz), kind, zz, (d, sib))

        def from_x(zz):
            return remote(x_ref, place(xn, zz), 2, zz, (xn, s))

        def from_y(zz):
            return remote(x_ref, place(yn, zz), 3, zz, (yn, s))

        def diag_up(zz):
            return remote(place(xyn, zz), place(xyn, zz), 10, zz, (d, s + 2))

        def diag_down(zz):
            return remote(place(xyn, zz), place(xyn, zz), 11, zz, (d, s - 2))

        def diag_top(zz):
            return remote(x_ref.at[top], place(xyn, zz).at[top], 4, zz, (yn, s))

        def diag_low(zz):
            return remote(x_ref.at[low], place(xyn, zz).at[low], 5, zz, (xn, s))

        order = [z, 1 + z % 2, (2 + 3 * z) % 5, 3 * (1 - z // 2)]
        local = pltpu.make_async_copy(x_ref, place(d, z), lsem)
        local.start()

        def halo_copies(dev):
            tok = pltpu.make_async_remote_copy(
                src_ref=tok_ref,
                dst_ref=ptok_ref,
                send_sem=hss.at[0],
                recv_sem=hrs.at[0],
                device_id=dev,
                device_id_type=MESH,
            )
            seg = pltpu.make_async_remote_copy(
                src_ref=seg_ref,
                dst_ref=pseg_ref,
                send_sem=hss.at[1],
                recv_sem=hrs.at[1],
                device_id=dev,
                device_id_type=MESH,
            )
            return tok, seg

        def in_plane(k, body):
            if k == 0:
                body()
            else:
                pl.when((z - order[k] >= 2) | (order[k] - z >= 3))(body)

        def on_line(k, body):
            pl.when((z - order[k] < 2) & (order[k] - z < 3))(body)

        def launch(k):
            zz = order[k]
            own = k == 0
            if own:

                @pl.when(z < 3)
                def _():
                    up(zz, True).start()

                @pl.when(z > 0)
                def _():
                    down(zz, True).start()
            else:

                @pl.when(zz < z)
                def _():
                    up(zz, False).wait_recv()

                @pl.when((zz < z) & (z < 3))
                def _():
                    up(zz, False).start()

                @pl.when(zz > z)
                def _():
                    down(zz, False).wait_recv()

                @pl.when((zz > z) & (z > 0))
                def _():
                    down(zz, False).start()

            to_x(zz, own).start()
            to_y(zz, own).start()
            to_sib(d, zz, 6, own).start()

        def second(k):
            zz = order[k]

            def pass_on():
                from_x(zz).wait_recv()
                on_y(zz).start()
                to_sib(xn, zz, 7).start()
                from_y(zz).wait_recv()
                on_x(zz).start()
                to_sib(yn, zz, 8).start()

            in_plane(k, pass_on)

        def rest(k):
            zz = order[k]

            def share():
                from_x(zz).wait_recv()
                to_sib(xn, zz, 7).start()
                from_y(zz).wait_recv()
                to_sib(yn, zz, 8).start()

            on_line(k, share)

        def third(k):
            zz = order[k]

            def arrive():
                diag_top(zz).wait_recv()
                diag_low(zz).wait_recv()

            in_plane(k, arrive)
            if k > 0:

                @pl.when((zz < z) & (z - zz <= 1))
                def _():
                    diag_up(zz).wait_recv()

                @pl.when((zz > z) & (zz - z <= 2))
                def _():
                    diag_down(zz).wait_recv()

            if k < 3:

                @pl.when((zz == z) & (z < 3))
                def _():
                    diag_up(zz).start()

                @pl.when((zz >= z) & (zz - z <= 1) & (z > 0))
                def _():
                    diag_down(zz).start()

            to_sib(xyn, zz, 9).start()

        own_tok = pltpu.make_async_copy(tok_ref, ptok_ref, hls.at[0])
        own_seg = pltpu.make_async_copy(seg_ref, pseg_ref, hls.at[1])


        @pl.when(s == 0)
        def _():
            own_tok.start()
            own_seg.start()

        launch(0)
        launch(1)
        second(0)
        launch(2)
        launch(3)
        third(0)
        second(1)
        third(1)
        second(2)

        @pl.when(s < 7)
        def _():
            for cp in halo_copies((d, s + 1)):
                cp.start()

        second(3)
        rest(1)
        rest(2)
        rest(3)
        third(2)
        third(3)

        local.wait()
        other = 1 - c

        def sib_place(dd, zz):
            return out_ref.at[dd * 8 + zz * 2 + other]

        for k in range(4):
            zz = order[k]
            own = k == 0
            for kind, dd in ((6, d), (7, xn), (8, yn), (9, xyn)):
                remote(sib_place(dd, zz), sib_place(dd, zz), kind, zz, (d, sib)).wait_recv()
                to_sib(dd, zz, kind, own and kind == 6).wait_send()
            to_x(zz, own).wait_send()
            to_y(zz, own).wait_send()

            def halves_sent():
                on_y(zz).wait_send()
                on_x(zz).wait_send()

            in_plane(k, halves_sent)
            if k < 3:

                @pl.when((zz == z) & (z < 3))
                def _():
                    diag_up(zz).wait_send()

                @pl.when((zz >= z) & (zz - z <= 1) & (z > 0))
                def _():
                    diag_down(zz).wait_send()

            @pl.when((zz <= z) & (z < 3))
            def _():
                up(zz, own).wait_send()

            @pl.when((zz >= z) & (z > 0))
            def _():
                down(zz, own).wait_send()

        @pl.when(s < 7)
        def _():
            for cp in halo_copies((d, s + 1)):
                cp.wait_send()

        @pl.when(s > 0)
        def _():
            for cp in halo_copies((d, s - 1)):
                cp.wait_recv()

        @pl.when(s == 0)
        def _():
            own_tok.wait()
            own_seg.wait()

    return pl.pallas_call(
        kernel,
        out_shape=[
            jax.ShapeDtypeStruct((32, rows, BLK), BF16),
            jax.ShapeDtypeStruct(tokens.shape, BF16),
            jax.ShapeDtypeStruct(seg_rows.shape, jnp.int32),
        ],
        in_specs=[ANY, ANY, ANY],
        out_specs=[ANY, ANY, ANY],
        scratch_shapes=[
            pltpu.SemaphoreType.DMA,
            pltpu.SemaphoreType.DMA((12, 4)),
            pltpu.SemaphoreType.DMA((12, 4)),
            pltpu.SemaphoreType.DMA((2,)),
            pltpu.SemaphoreType.DMA((2,)),
            pltpu.SemaphoreType.DMA((2,)),
        ],
        compiler_params=params(collective_id=0, has_side_effects=True),
        name="gather_weights",
    )(payload, tokens, seg_rows)


OWNED = 24 * BLK
HALF = OWNED // 2
SMALL_ROWS = SMALL // BLK
EXTRA_ROWS = SMALL_ROWS + 8


def add_rows(dst, terms, rows, step=256):
    def body(i, carry):
        at = pl.ds(pl.multiple_of(i * step, step), step)
        if len(terms) == 2 and dst.dtype == BF16:
            dst[at] = terms[0][at] + terms[1][at]
        else:
            total = terms[0][at].astype(F32)
            for term in terms[1:]:
                total = total + term[at].astype(F32)
            dst[at] = total.astype(dst.dtype)
        return carry

    lax.fori_loop(0, rows // step, body, 0)


SCHEDULE = [
    "F0a", "F1a", "F0b", "F1b", "E0", "F2a", "S0a", "S0b", "D1a", "F2b",
    "S1a", "S1b", "F3a", "E1", "F3b", "D1b", "D2a", "D2b", "S2a", "D3a",
    "S2b", "T0a", "T0b", "E2", "D3b", "T1a", "T1b", "E3", "T2a", "T2b",
    "E4", "S3a", "S3b", "T3a", "T3b",
]


def sum_gradients(grads, extra):
    def kernel(g_ref, e_ref, out_ref, eout_ref, own, crecv, s1a, s1b, s2, zup, zdn, gup, gdn, epart, erecv, ls, ss, rs, es, er):
        d = lax.axis_index("dp")
        s = lax.axis_index("seq")
        z = s // 2
        c = s % 2
        xn = d + 1 - 2 * (d % 2)
        yn = d + 2 - 4 * (d // 2)
        xyn = 3 - d
        sib = z * 2 + 1 - c
        zpair = s + 2 - 4 * (z % 2)
        zfar = s + 4 - 8 * (z // 2)
        barrier = pltpu.get_barrier_semaphore()

        def greet(dev):
            pl.semaphore_signal(barrier, inc=1, device_id=dev, device_id_type=MESH)

        greet((d, sib))
        greet((xn, s))
        greet((yn, s))
        greet((d, zfar))

        @pl.when(z > 0)
        def _():
            greet((d, s - 2))

        @pl.when(z < 3)
        def _():
            greet((d, s + 2))

        order = [3 * (1 - z // 2), (2 + 3 * z) % 5, 1 + z % 2, z]

        ends = (z == 0) | (z == 3)
        inner = (z == 1) | (z == 2)

        def in_plane(k, act):
            if k == 3:
                act()
            elif k == 0:
                pl.when(ends)(act)

        def remote(src, dst, ssem, rsem, dev):
            return pltpu.make_async_remote_copy(
                src_ref=src, dst_ref=dst, send_sem=ssem, recv_sem=rsem, device_id=dev, device_id_type=MESH
            )

        def part(h):
            size = OWNED // 2
            half = size // 2
            rows = pl.ds(h * size, size)
            top = pl.ds(h * size, half)
            low = pl.ds(h * size + half, half)
            here = pl.ds(h * half, half)

            def owner_rows(dd, zz, cc):
                return g_ref.at[pl.ds(pl.multiple_of((dd * 8 + zz * 2 + cc) * OWNED + h * size, size), size)]

            def load(k, dd):
                zz = order[k]
                return pltpu.make_async_copy(owner_rows(dd, zz, c), own.at[zz, dd, rows], ls.at[zz * 2 + h, dd])

            def hop(src, dst, kind, zz, dev):
                return remote(src, dst, ss.at[zz * 2 + h, kind], rs.at[zz * 2 + h, kind], dev)

            def core(zz, dd):
                return hop(owner_rows(dd, zz, 1 - c), crecv.at[zz, dd, rows], dd, zz, (d, sib))

            def y_own(zz):
                return hop(own.at[zz, yn, top], s1a.at[zz, 0, here], 4, zz, (yn, s))

            def y_cross(zz):
                return hop(own.at[zz, xyn, top], s1a.at[zz, 1, here], 5, zz, (yn, s))

            def x_own(zz):
                return hop(own.at[zz, xn, low], s1b.at[zz, 0, here], 6, zz, (xn, s))

            def x_cross(zz):
                return hop(own.at[zz, xyn, low], s1b.at[zz, 1, here], 7, zz, (xn, s))

            def x_last(zz):
                return hop(own.at[zz, xn, top], s2.at[zz, top], 8, zz, (xn, s))

            def y_last(zz):
                return hop(own.at[zz, yn, low], s2.at[zz, low], 9, zz, (yn, s))

            def z_up(zz):
                return hop(own.at[zz, d, rows], zup.at[zz, rows], 10, zz, (d, s + 2))

            def z_dn(zz):
                return hop(own.at[zz, d, rows], zdn.at[zz, rows], 11, zz, (d, s - 2))

            def g_up(zz):
                return hop(own.at[zz, xyn, rows], gup.at[zz, rows], 12, zz, (d, s + 2))

            def g_dn(zz):
                return hop(own.at[zz, xyn, rows], gdn.at[zz, rows], 13, zz, (d, s - 2))

            def cross(zz):
                y_cross(zz).start()
                x_cross(zz).start()

            def along(zz, act):
                @pl.when(zz > z)
                def _():
                    act(g_up(zz))

                @pl.when(zz < z)
                def _():
                    act(g_dn(zz))

            def outward(k, act):
                if k == 0:
                    pl.when(inner)(lambda: along(order[k], act))
                elif k < 3:
                    along(order[k], act)

            def issue(k):
                for dd in (xyn, yn, xn, d):
                    core(order[k], dd).start()

            def first(k):
                zz = order[k]

                def one(dd, start):
                    load(k, dd).wait()
                    core(zz, dd).wait_recv()
                    mine = own.at[zz, dd, rows]
                    add_rows(mine, [mine, crecv.at[zz, dd, rows]], size)
                    for cp in start:
                        cp.start()

                one(xyn, [])
                if k == 0:
                    pl.when(ends)(lambda: cross(zz))
                    outward(0, lambda cp: cp.start())
                elif k < 3:
                    pl.when(ends)(lambda: along(zz, lambda cp: cp.start()))
                one(yn, [y_own(zz)])
                one(xn, [x_own(zz)])
                one(d, [])

            def diagonal(k):
                zz = order[k]
                mine = own.at[zz, xyn, rows]

                def take(cp, came):
                    cp.wait_recv()
                    add_rows(mine, [mine, came.at[zz, rows]], size)

                if k < 3:

                    @pl.when(inner)
                    def _():
                        pl.when(zz > z)(lambda: take(g_up(zz), gup))
                        pl.when(zz < z)(lambda: take(g_dn(zz), gdn))
                        along(zz, lambda cp: cp.start())
                else:
                    pl.when(z > 0)(lambda: take(g_up(zz), gup))
                    pl.when(z < 3)(lambda: take(g_dn(zz), gdn))
                    cross(zz)

            def second(k):
                zz = order[k]
                a = own.at[zz, xn, top]
                b = own.at[zz, yn, low]

                def crossed():
                    y_cross(zz).wait_recv()
                    add_rows(a, [a, s1a.at[zz, 1, here]], half)

                def crossed_low():
                    x_cross(zz).wait_recv()
                    add_rows(b, [b, s1b.at[zz, 1, here]], half)

                in_plane(k, crossed)
                x_last(zz).start()
                in_plane(k, crossed_low)
                y_last(zz).start()

            def third(k):
                zz = order[k]
                for cp in (y_own(zz), x_own(zz), x_last(zz), y_last(zz)):
                    cp.wait_recv()

                def total(to_top, to_low, *came):
                    add_rows(
                        to_top, [own.at[zz, d, top], s1a.at[zz, 0, here], s2.at[zz, top]] + [x.at[zz, top] for x in came], half
                    )
                    add_rows(
                        to_low, [own.at[zz, d, low], s1b.at[zz, 0, here], s2.at[zz, low]] + [x.at[zz, low] for x in came], half
                    )

                if k < 3:
                    mine = (own.at[zz, d, top], own.at[zz, d, low])

                    @pl.when((zz > z) & (z > 0))
                    def _():
                        z_up(zz).wait_recv()
                        total(*mine, zup)

                    @pl.when((zz < z) & (z < 3))
                    def _():
                        z_dn(zz).wait_recv()
                        total(*mine, zdn)

                    @pl.when(((zz > z) & (z == 0)) | ((zz < z) & (z == 3)))
                    def _():
                        total(*mine)

                    pl.when(zz > z)(lambda: z_up(zz).start())
                    pl.when(zz < z)(lambda: z_dn(zz).start())
                else:
                    result = (out_ref.at[top], out_ref.at[low])
                    pl.when(z > 0)(lambda: z_up(zz).wait_recv())
                    pl.when(z < 3)(lambda: z_dn(zz).wait_recv())
                    pl.when(inner)(lambda: total(*result, zup, zdn))
                    pl.when(z == 0)(lambda: total(*result, zdn))
                    pl.when(z == 3)(lambda: total(*result, zup))

            def sent(k):
                zz = order[k]
                for dd in range(4):
                    core(zz, dd).wait_send()
                for cp in (y_own(zz), x_own(zz), x_last(zz), y_last(zz)):
                    cp.wait_send()

                def crosses_sent():
                    y_cross(zz).wait_send()
                    x_cross(zz).wait_send()

                in_plane(k, crosses_sent)
                outward(k, lambda cp: cp.wait_send())
                if k < 3:
                    pl.when(zz > z)(lambda: z_up(zz).wait_send())
                    pl.when(zz < z)(lambda: z_dn(zz).wait_send())

            return dict(load=load, issue=issue, F=first, D=diagonal, S=second, T=third, sent=sent)

        parts = {"a": part(0), "b": part(1)}
        schedule = list(SCHEDULE)
        firsts = [step for step in schedule if step[0] == "F"]
        for step in firsts:
            for dd in (xyn, yn, xn, d):
                parts[step[2]]["load"](int(step[1]), dd).start()

        pl.semaphore_wait(barrier, 4 + (z + 2) // 3 + (5 - z) // 3)

        def issue_next():
            if firsts:
                step = firsts.pop(0)
                parts[step[2]]["issue"](int(step[1]))

        def extra_step(i, dev):
            return remote(epart.at[i], erecv.at[i], es.at[i], er.at[i], dev)

        extra_devs = [(d, sib), (xn, s), (yn, s), (d, zpair), (d, zfar)]

        def extra_add(i):
            extra_step(i, extra_devs[i]).wait_recv()
            a = epart[i]
            b = erecv[i]
            row = lax.broadcasted_iota(jnp.int32, a.shape, 0)
            total = jnp.where(row < SMALL_ROWS, a + b, jnp.maximum(a, b))
            if i < 4:
                epart[i + 1] = total
                extra_step(i + 1, extra_devs[i + 1]).start()
            else:
                eout_ref[...] = total

        issue_next()
        epart[0] = e_ref[...]
        extra_step(0, extra_devs[0]).start()
        for step in schedule:
            if step[0] == "E":
                extra_add(int(step[1]))
            else:
                if step[0] == "F":
                    issue_next()
                parts[step[2]][step[0]](int(step[1]))

        for i in range(5):
            extra_step(i, extra_devs[i]).wait_send()
        for k in range(4):
            for h in "ab":
                parts[h]["sent"](k)

    return pl.pallas_call(
        kernel,
        out_shape=[
            jax.ShapeDtypeStruct((OWNED, BLK), F32),
            jax.ShapeDtypeStruct((EXTRA_ROWS, BLK), F32),
        ],
        in_specs=[ANY, VMEM],
        out_specs=[VMEM, VMEM],
        scratch_shapes=[
            pltpu.VMEM((4, 4, OWNED, BLK), BF16),
            pltpu.VMEM((4, 4, OWNED, BLK), BF16),
            pltpu.VMEM((4, 2, HALF, BLK), BF16),
            pltpu.VMEM((4, 2, HALF, BLK), BF16),
            pltpu.VMEM((4, OWNED, BLK), BF16),
            pltpu.VMEM((4, OWNED, BLK), BF16),
            pltpu.VMEM((4, OWNED, BLK), BF16),
            pltpu.VMEM((4, OWNED, BLK), BF16),
            pltpu.VMEM((4, OWNED, BLK), BF16),
            pltpu.VMEM((5, EXTRA_ROWS, BLK), F32),
            pltpu.VMEM((5, EXTRA_ROWS, BLK), F32),
            pltpu.SemaphoreType.DMA((8, 4)),
            pltpu.SemaphoreType.DMA((8, 14)),
            pltpu.SemaphoreType.DMA((8, 14)),
            pltpu.SemaphoreType.DMA((5,)),
            pltpu.SemaphoreType.DMA((5,)),
        ],
        compiler_params=params(collective_id=1, has_side_effects=True),
        name="sum_gradients",
    )(grads, extra)


ROWB = 256


PAIRS = HEADS // 2


def rope(p, cos_t, fwd_t, back_t):
    return p * cos_t + pltpu.roll(p, BLK - ROT // 2, 1) * fwd_t + pltpu.roll(p, ROT // 2, 1) * back_t


def by_pair(value):
    return [value[:, j * BLK : (j + 1) * BLK] for j in range(PAIRS)]


def side_by_side(ref, at=slice(None)):
    return jnp.concatenate([ref[j, at, :] for j in range(PAIRS)], axis=1)


def spread_tables(cos8, sin8):
    none = jnp.zeros_like(cos8)
    rest = (HEAD - ROT) // none.shape[0]
    cos_t = [cos8, cos8] + [none + 1.0] * rest
    fwd_t = [-sin8, none] + [none] * rest
    back_t = [none, sin8] + [none] * rest
    return [jnp.concatenate(t * 2, axis=0).T for t in (cos_t, fwd_t, back_t)]


PROWS = 512


def project(w_rows, w_all, prev_tokens, tokens, cotangent, smalls, tables):
    rows = tokens.shape[0]
    cos8, sin8 = tables
    steps = rows // PROWS

    def kernel(
        w_rows_ref, w_ref, prev_ref, tok_ref, g_ref, small_ref, cos_ref, sin_ref,
        q_ref, k_ref, v_ref, do_ref, m_ref, wqkv, wo, sems,
    ):
        i = pl.program_id(0)

        def third_copy(third):
            def body(t):
                r, cc = t // 8, t % 8
                src = w_ref.at[pl.ds(pl.multiple_of(w_rows_ref[r * 24 + third * 8 + cc], 16), BLK)]
                dst = wqkv.at[pl.ds(pl.multiple_of(r * BLK, BLK), BLK), pl.ds(pl.multiple_of(third * D + cc * BLK, BLK), BLK)]
                pltpu.make_async_copy(src, dst, sems.at[third]).start()

            tile_loop(0, 64, body)

        def third_wait(third):
            part = wqkv.at[:, pl.ds(third * D, D)]
            pltpu.make_async_copy(part, part, sems.at[third]).wait()

        @pl.when(i == 0)
        def _():
            third_copy(1)
            third_copy(2)
            third_copy(0)

            def body(t):
                r, cc = t // 8, t % 8
                src = w_ref.at[pl.ds(pl.multiple_of(w_rows_ref[OUT_BASE + t], 16), BLK)]
                dst = wo.at[pl.ds(pl.multiple_of(r * BLK, BLK), BLK), pl.ds(pl.multiple_of(cc * BLK, BLK), BLK)]
                pltpu.make_async_copy(src, dst, sems.at[3]).start()

            tile_loop(0, 64, body)
            third_wait(1)
            third_wait(2)

        @pl.when(i == steps)
        def _():
            third_wait(0)
            pltpu.make_async_copy(wo, wo, sems.at[3]).wait()

        n = PROWS // ROWB

        def put(ref, at, pieces):
            for j in range(PAIRS):
                ref[j, at, :] = pieces[j].astype(BF16)

        def run(own):
            x_ref = tok_ref if own else prev_ref
            ins, tabs, raw = {}, {}, {}

            def prepare(c):
                at = slice(c * ROWB, (c + 1) * ROWB)
                normed, _ = norm_rows(x_ref[at, :].astype(F32))
                ins[c] = (normed * small_ref[G1, :] + small_ref[C1, :]).astype(BF16)
                if own:
                    m_ref[at, :] = (normed * small_ref[G2, :] + small_ref[C2, :]).astype(BF16)
                yield
                tabs[c] = spread_tables(cos_ref[:, at], sin_ref[:, at])
                yield

            def multiply(c):
                at = slice(c * ROWB, (c + 1) * ROWB)
                raw[c] = [dot(ins[c], wqkv[:, D : 2 * D])]
                yield
                put(v_ref, at, by_pair(dot(ins[c], wqkv[:, 2 * D :]) + small_ref[B_V, :]))
                yield
                if own:
                    raw[c].append(dot(ins[c], wqkv[:, :D]) + small_ref[B_Q, :])
                    yield
                    put(do_ref, at, by_pair(dot(g_ref[at, :], wo[...], NT)))
                    yield

            def turn(c):
                at = slice(c * ROWB, (c + 1) * ROWB)
                put(k_ref, at, [rope(p, *tabs[c]) for p in by_pair(raw[c][0])])
                yield
                if own:
                    put(q_ref, at, [rope(p, *tabs[c]) for p in by_pair(raw[c][1])])
                    yield

            for c in range(n + 2):
                parts = []
                if 0 <= c - 1 < n:
                    parts.append(multiply(c - 1))
                if c < n:
                    parts.append(prepare(c))
                if 0 <= c - 2 < n:
                    parts.append(turn(c - 2))
                interleave(*parts)

        @pl.when(i < steps)
        def _():
            run(False)

        @pl.when(i >= steps)
        def _():
            run(True)

    before = pl.BlockSpec((PROWS, D), lambda i, *_: (jnp.minimum(i, steps - 1), 0))
    block = pl.BlockSpec((PROWS, D), lambda i, *_: (jnp.maximum(i - steps, 0), 0))
    here = pl.BlockSpec((PAIRS, PROWS, BLK), lambda i, *_: (0, i, 0))
    own = pl.BlockSpec((PAIRS, PROWS, BLK), lambda i, *_: (0, jnp.maximum(i - steps, 0), 0))
    table = pl.BlockSpec((ROT // 2, PROWS), lambda i, *_: (0, i))
    return pl.pallas_call(
        kernel,
        grid_spec=pltpu.PrefetchScalarGridSpec(
            num_scalar_prefetch=1,
            grid=(2 * steps,),
            in_specs=[
                ANY, before, block, block,
                pl.BlockSpec((16, D), lambda i, *_: (0, 0)), table, table,
            ],
            out_specs=[own, here, here, own, block],
            scratch_shapes=[
                pltpu.VMEM((D, 3 * D), BF16),
                pltpu.VMEM((D, D), BF16),
                pltpu.SemaphoreType.DMA((4,)),
            ],
        ),
        out_shape=[
            jax.ShapeDtypeStruct((PAIRS, rows, BLK), BF16),
            jax.ShapeDtypeStruct((PAIRS, 2 * rows, BLK), BF16),
            jax.ShapeDtypeStruct((PAIRS, 2 * rows, BLK), BF16),
            jax.ShapeDtypeStruct((PAIRS, rows, BLK), BF16),
            jax.ShapeDtypeStruct((rows, D), BF16),
        ],
        compiler_params=params(dimension_semantics=("arbitrary",)),
        name="project",
    )(w_rows, w_all, prev_tokens, tokens, cotangent, smalls, cos8, sin8)


QB = 256
SPAN = WINDOW + QB


CHUNK = 256
SAFE_SCORE = 60.0


def attend(q, k, v, d_out, prev_seg, seg, cos8, sin8):
    rows = q.shape[1]
    blocks = rows // QB
    scale = HEAD ** (-0.5)
    half = ROT // 2
    n = SPAN // CHUNK

    def heads_apart(x):
        row = lax.broadcasted_iota(jnp.int32, x.shape, 0)
        zero = jnp.zeros_like(x)
        return jnp.concatenate([jnp.where(row < HEAD, x, zero), jnp.where(row < HEAD, zero, x)], axis=1)

    def stacked(x):
        lane = lax.broadcasted_iota(jnp.int32, x.shape, 1)
        zero = jnp.zeros_like(x)
        return jnp.concatenate([jnp.where(lane < HEAD, x, zero), jnp.where(lane < HEAD, zero, x)], axis=0)

    def fold(x, op):
        return op(x.reshape(x.shape[0] // 8, 8, x.shape[1]), axis=0)

    def two(x):
        return jnp.concatenate([x, x], axis=1)

    def kernel(
        q_ref, k_ref, v_ref, do_ref, pseg_ref, seg_ref, cos_ref, sin_ref,
        o_ref, dq_ref, dk_ref, dv_ref, halo_ref, peak_ref, bias, kt, vt, el_ref, ds_ref, dks, dvs, key_seg,
    ):
        p = pl.program_id(0)

        @pl.when(p == 0)
        def _():
            gap = (
                WINDOW
                + lax.broadcasted_iota(jnp.int32, (SPAN, QB), 1)
                - lax.broadcasted_iota(jnp.int32, (SPAN, QB), 0)
            )
            before = jnp.where(lax.axis_index("seq") == 0, -1, pseg_ref[...]).astype(F32)
            for part, numbers in enumerate((before, seg_ref[...].astype(F32))):
                column = jnp.broadcast_to(numbers[:1, :], (BLK, rows)).T
                key_seg[part * rows : (part + 1) * rows, :] = column
            for i in range(blocks):
                query_seg = seg_ref[:1, i * QB : (i + 1) * QB].astype(F32)
                same = key_seg[i * QB : i * QB + SPAN, :1] == query_seg
                bias[i] = jnp.where((gap >= 0) & (gap < WINDOW) & same, 0.0, MASKED)

        kt[...] = k_ref[...].T
        vt[...] = v_ref[...].T
        k_float = kt[...].astype(F32)
        q_float = q_ref[...].astype(F32) * scale
        reach = jnp.max(jnp.sum(k_float * k_float, axis=0)) * jnp.max(jnp.sum(q_float * q_float, axis=1))
        safe = reach < SAFE_SCORE * SAFE_SCORE

        def rows_from(i, offset, count):
            first = i * QB + offset
            return pl.ds(first if isinstance(i, int) else pl.multiple_of(first, QB), count)

        def keys_at(ref, i, c):
            return ref[rows_from(i, c * CHUNK, CHUNK), :]

        def prepare(i):
            q_all = (q_ref[rows_from(i, 0, QB), :].astype(F32) * scale).astype(BF16)
            return q_all, heads_apart(q_all.T)

        def scores(i, c, q_apart):
            return dot(keys_at(k_ref, i, c), q_apart) + two(bias[i, c * CHUNK : (c + 1) * CHUNK])

        def row_tops(i, q_apart):
            for c in range(n):
                t = fold(scores(i, c, q_apart), jnp.max)
                most = t if c == 0 else jnp.maximum(most, t)
            return jnp.max(most, axis=0, keepdims=True)

        def forward(i, q_apart, found, low=None):
            top8 = sum8 = None
            for c in range(n):
                st = scores(i, c, q_apart)
                e = jnp.exp(st if low is None else st - low)
                el_ref[i % 2, c * CHUNK : (c + 1) * CHUNK] = e.astype(BF16)
                t, u = fold(st, jnp.max), fold(e, jnp.sum)
                top8, sum8 = (t, u) if c == 0 else (jnp.maximum(top8, t), sum8 + u)
                yield
            found.append(jnp.max(top8, axis=0, keepdims=True))
            found.append(1.0 / jnp.sum(sum8, axis=0, keepdims=True))

        def per_head(x):
            return jnp.concatenate(
                [jnp.broadcast_to(x[:, :QB], (HEAD, QB)), jnp.broadcast_to(x[:, QB:], (HEAD, QB))], axis=0
            )

        def both(t, x_ref, i):
            span = rows_from(i, 0, SPAN)
            return jnp.concatenate(
                [dot(t[:HEAD, span], x_ref[i % 2, :, :QB]), dot(t[HEAD:, span], x_ref[i % 2, :, QB:])], axis=0
            )

        def output(i, inv):
            raw = both(vt, el_ref, i)
            inv2 = per_head(inv)
            o_ref[rows_from(i, 0, QB), :] = (raw * inv2).T.astype(BF16)
            do_s = (do_ref[rows_from(i, 0, QB), :].astype(F32).T * inv2).astype(BF16)
            m = do_s.astype(F32) * raw
            mean = jnp.concatenate(
                [jnp.sum(m[:HEAD], axis=0, keepdims=True), jnp.sum(m[HEAD:], axis=0, keepdims=True)], axis=1
            )
            return do_s, mean * inv

        def score_grads(i, do_s, mean):
            do_apart = heads_apart(do_s)
            for c in range(n):
                w = slice(c * CHUNK, (c + 1) * CHUNK)
                dpt = dot(keys_at(v_ref, i, c), do_apart)
                ds_ref[i % 2, w] = (el_ref[i % 2, w].astype(F32) * (dpt - mean)).astype(BF16)

        def input_grads(i, q_all, do_s):
            do_rows = stacked(do_s.T)
            q_rows = stacked(q_all)
            for c in range(n):
                w = slice(c * CHUNK, (c + 1) * CHUNK)
                at = rows_from(i, c * CHUNK, CHUNK)
                v_part = dot(el_ref[i % 2, w], do_rows)
                k_part = dot(ds_ref[i % 2, w], q_rows)
                if c == n - 1 or (isinstance(i, int) and i == 0):
                    dvs[at, :] = v_part
                    dks[at, :] = k_part
                else:
                    dvs[at, :] += v_part
                    dks[at, :] += k_part
                yield
            dq = both(kt, ds_ref, i) * scale
            cos_t, sin_t = cos_ref[:, rows_from(i, 0, QB)], sin_ref[:, rows_from(i, 0, QB)]
            turned = []
            for h in range(2):
                f, g = dq[h * HEAD : h * HEAD + half], dq[h * HEAD + half : h * HEAD + ROT]
                turned += [f * cos_t + g * sin_t, g * cos_t - f * sin_t, dq[h * HEAD + ROT : (h + 1) * HEAD]]
            dq_ref[rows_from(i, 0, QB), :] = jnp.concatenate(turned, axis=0).T.astype(BF16)
            yield

        def run():
            top = held = None
            for i in range(blocks + 1):
                parts, found = [], []
                if held is not None:
                    parts.append(input_grads(i - 1, *held))
                if i < blocks:
                    q_all, q_apart = prepare(i)
                    parts.append(forward(i, q_apart, found))
                interleave(*parts)
                if i < blocks:
                    t, inv = found
                    top = t if top is None else jnp.maximum(top, t)
                    do_s, mean = output(i, inv)
                    score_grads(i, do_s, mean)
                    held = (q_all, do_s)
            peak_ref[...] = jnp.broadcast_to(top, peak_ref.shape)

        def run_shifted():
            dks[:WINDOW, :] = jnp.zeros((WINDOW, BLK), F32)
            dvs[:WINDOW, :] = jnp.zeros((WINDOW, BLK), F32)
            peak_ref[...] = jnp.full(peak_ref.shape, MASKED, F32)

            def body(i, carry):
                q_all, q_apart = prepare(i)
                found = []
                interleave(forward(i, q_apart, found, row_tops(i, q_apart)))
                do_s, mean = output(i, found[1])
                score_grads(i, do_s, mean)
                interleave(input_grads(i, q_all, do_s))
                peak_ref[...] = jnp.maximum(peak_ref[...], found[0])
                return carry

            lax.fori_loop(0, blocks, body, 0)

        pl.when(safe)(run)
        pl.when(jnp.logical_not(safe))(run_shifted)
        halo_ref[0] = dks[:rows, :].astype(BF16)
        halo_ref[1] = dvs[:rows, :].astype(BF16)
        dk_ref[...] = dks[rows:, :].astype(BF16)
        dv_ref[...] = dvs[rows:, :].astype(BF16)

    block = pl.BlockSpec((None, rows, BLK), lambda p: (p, 0, 0))
    keys = pl.BlockSpec((None, 2 * rows, BLK), lambda p: (p, 0, 0))
    whole = lambda *shape: pl.BlockSpec(shape, lambda p: (0, 0))
    own_rot = pl.BlockSpec((half, rows), lambda p: (0, 1))
    return pl.pallas_call(
        kernel,
        grid=(PAIRS,),
        in_specs=[
            block, keys, keys, block, whole(8, rows), whole(8, rows), own_rot, own_rot,
        ],
        out_specs=[
            block, block, block, block,
            pl.BlockSpec((2, None, rows, BLK), lambda p: (0, p, 0, 0)),
            pl.BlockSpec((8, 2 * QB), lambda p: (p, 0)),
        ],
        out_shape=[
            jax.ShapeDtypeStruct((PAIRS, rows, BLK), BF16),
            jax.ShapeDtypeStruct((PAIRS, rows, BLK), BF16),
            jax.ShapeDtypeStruct((PAIRS, rows, BLK), BF16),
            jax.ShapeDtypeStruct((PAIRS, rows, BLK), BF16),
            jax.ShapeDtypeStruct((2, PAIRS, rows, BLK), BF16),
            jax.ShapeDtypeStruct((8 * PAIRS, 2 * QB), F32),
        ],
        scratch_shapes=[
            pltpu.VMEM((blocks, SPAN, QB), F32),
            pltpu.VMEM((BLK, 2 * rows), BF16),
            pltpu.VMEM((BLK, 2 * rows), BF16),
            pltpu.VMEM((2, SPAN, 2 * QB), BF16),
            pltpu.VMEM((2, SPAN, 2 * QB), BF16),
            pltpu.VMEM((2 * rows, BLK), F32),
            pltpu.VMEM((2 * rows, BLK), F32),
            pltpu.VMEM((2 * rows, BLK), F32),
        ],
        compiler_params=params(dimension_semantics=("arbitrary",)),
        cost_estimate=pl.CostEstimate(flops=40 << 30, bytes_accessed=32 << 20, transcendentals=20 << 20),
        name="attend",
    )(q, k, v, d_out, prev_seg, seg, cos8, sin8)


FB = 512


def gelu_parts(v):
    a = jnp.abs(v)
    t = 1.0 / (1.0 + a * (0.3275911 * 0.7071067811865476))
    poly = t * (
        0.5 * 0.254829592
        + t * (0.5 * -0.284496736 + t * (0.5 * 1.421413741 + t * (0.5 * -1.453152027 + t * (0.5 * 1.061405429))))
    )
    e = jnp.exp(v * v * -0.5)
    tail = poly * e
    cdf = jnp.where(v >= 0, 1.0 - tail, tail)
    return v * cdf, cdf + v * e * 0.3989422804014327


def feed_forward(w_rows, g_rows, w_all, m, cotangent, b_up):
    rows = m.shape[0]
    steps = FF // FB

    def kernel(
        w_rows_ref, g_rows_ref, w_ref, m_ref, g_ref, b_ref, low_ref, dml_ref, db_ref, gr_ref,
        mt, wup, wdn, hs, dus, gup, gdn, u_ref, h_ref, out_ref, dm_ref, wsem, gsem,
    ):
        f = pl.program_id(0)
        slot = f % 2
        per = FB // BLK

        def up_at(buf, t):
            return buf.at[pl.ds(pl.multiple_of((t // per) * BLK, BLK), BLK), pl.ds(pl.multiple_of((t % per) * BLK, BLK), BLK)]

        def up_tile(ff, t):
            return UP_BASE + (t // per) * (FF // BLK) + ff * per + t % per

        def down_at(buf, t):
            return buf.at[pl.ds(pl.multiple_of((t // 8) * BLK, BLK), BLK), pl.ds(pl.multiple_of((t % 8) * BLK, BLK), BLK)]

        def down_tile(ff, t):
            return DOWN_BASE + ff * per * 8 + t

        def fetch_one(ff, sl, t):
            src = w_ref.at[pl.ds(pl.multiple_of(w_rows_ref[up_tile(ff, t)], 16), BLK)]
            pltpu.make_async_copy(src, up_at(wup.at[sl], t), wsem.at[0, sl]).start()
            src = w_ref.at[pl.ds(pl.multiple_of(w_rows_ref[down_tile(ff, t)], 16), BLK)]
            pltpu.make_async_copy(src, down_at(wdn.at[sl], t), wsem.at[1, sl]).start()

        def store_one(ff, sl, t):
            dst = gr_ref.at[pl.ds(pl.multiple_of(g_rows_ref[up_tile(ff, t)], 16), BLK)]
            pltpu.make_async_copy(up_at(gup.at[sl], t), dst, gsem.at[0, sl]).start()
            dst = gr_ref.at[pl.ds(pl.multiple_of(g_rows_ref[down_tile(ff, t)], 16), BLK)]
            pltpu.make_async_copy(down_at(gdn.at[sl], t), dst, gsem.at[1, sl]).start()

        def whole_wait(buf, sem):
            pltpu.make_async_copy(buf, buf, sem).wait()

        count = 8 * per

        @pl.when(f == 0)
        def _():
            tile_loop(0, count, lambda t: fetch_one(0, 0, t))
            mt[...] = m_ref[...].T
            out_ref[...] = jnp.zeros_like(out_ref)
            dm_ref[...] = jnp.zeros_like(dm_ref)

        whole_wait(wup.at[slot], wsem.at[0, slot])
        whole_wait(wdn.at[slot], wsem.at[1, slot])

        @pl.when(f >= 2)
        def _():
            whole_wait(gup.at[slot], gsem.at[0, slot])
            whole_wait(gdn.at[slot], gsem.at[1, slot])

        n = rows // ROWB

        def stage1(c):
            at = slice(c * ROWB, (c + 1) * ROWB)
            for k in range(FB // 256):
                cols = slice(k * 256, (k + 1) * 256)
                u_ref[c % 2, :, cols] = dot(m_ref[at, :], wup[slot, :, cols]) + b_ref[:, cols]
                yield
                h_ref[c % 2, :, cols] = dot(g_ref[at, :], wdn[slot, cols, :], NT)
                yield

        db = [None]

        def stage2(c):
            step = ROWB // 8
            for k in range(8):
                at = slice(k * step, (k + 1) * step)
                to = slice(c * ROWB + k * step, c * ROWB + (k + 1) * step)
                hidden, slope = gelu_parts(u_ref[c % 2, at, :])
                hs[to, :] = hidden.astype(BF16)
                du = (h_ref[c % 2, at, :] * slope).astype(BF16)
                dus[to, :] = du
                t = jnp.sum(du.astype(F32).reshape(step // 8, 8, FB), axis=0)
                db[0] = t if db[0] is None else db[0] + t
                yield

        def stage3(c):
            at = slice(c * ROWB, (c + 1) * ROWB)
            for k in range(D // 256):
                cols = slice(k * 256, (k + 1) * 256)
                out_ref[at, cols] += dot(hs[at, :], wdn[slot, :, cols])
                yield
                dm_ref[at, cols] += dot(dus[at, :], wup[slot, cols, :], NT)
                yield

        nxt = jnp.minimum(f + 1, steps - 1)
        for t in range(count):
            fetch_one(nxt, 1 - slot, t)

        for c in range(n + 2):
            gens = []
            if c < n:
                gens.append(stage1(c))
            if 0 <= c - 1 < n:
                gens.append(stage2(c - 1))
            if 0 <= c - 2 < n:
                gens.append(stage3(c - 2))
            interleave(*gens)
        db_ref[...] = jnp.sum(db[0], axis=0, keepdims=True)
        gdn[slot] = dot(hs[...], g_ref[...], TN).astype(BF16)
        gup[slot] = dot(mt[...], dus[...]).astype(BF16)
        for t in range(count):
            store_one(f, slot, t)


        @pl.when(f == steps - 1)
        def _():
            low_ref[...] = out_ref[...].astype(BF16)
            dml_ref[...] = dm_ref[...].astype(BF16)
            whole_wait(wup.at[1 - slot], wsem.at[0, 1 - slot])
            whole_wait(wdn.at[1 - slot], wsem.at[1, 1 - slot])
            for sl in range(2):
                whole_wait(gup.at[sl], gsem.at[0, sl])
                whole_wait(gdn.at[sl], gsem.at[1, sl])

    full = pl.BlockSpec((rows, D), lambda f, *_: (0, 0))
    bias = pl.BlockSpec((1, FB), lambda f, *_: (0, f))
    return pl.pallas_call(
        kernel,
        grid_spec=pltpu.PrefetchScalarGridSpec(
            num_scalar_prefetch=2,
            grid=(steps,),
            in_specs=[ANY, full, full, bias],
            out_specs=[full, full, bias, ANY],
            scratch_shapes=[
                pltpu.VMEM((D, rows), BF16),
                pltpu.VMEM((2, D, FB), BF16),
                pltpu.VMEM((2, FB, D), BF16),
                pltpu.VMEM((rows, FB), BF16),
                pltpu.VMEM((rows, FB), BF16),
                pltpu.VMEM((2, D, FB), BF16),
                pltpu.VMEM((2, FB, D), BF16),
                pltpu.VMEM((2, ROWB, FB), F32),
                pltpu.VMEM((2, ROWB, FB), F32),
                pltpu.VMEM((rows, D), F32),
                pltpu.VMEM((rows, D), F32),
                pltpu.SemaphoreType.DMA((2, 2)),
                pltpu.SemaphoreType.DMA((2, 2)),
            ],
        ),
        out_shape=[
            jax.ShapeDtypeStruct((rows, D), BF16),
            jax.ShapeDtypeStruct((rows, D), BF16),
            jax.ShapeDtypeStruct((1, FF), F32),
            jax.ShapeDtypeStruct((TILES * BLK, BLK), BF16),
        ],
        compiler_params=params(dimension_semantics=("arbitrary",)),
        cost_estimate=pl.CostEstimate(flops=52 << 30, bytes_accessed=48 << 20, transcendentals=8 << 20),
        name="feed_forward",
    )(w_rows, g_rows, w_all, m, cotangent, b_up)


def finish(
    w_rows, g_rows, w_all, tokens, cotangent, smalls, attn_out, mlp_out, dm, dq, dk, dv, halo, tables, grads
):
    rows = tokens.shape[0]
    steps = rows // ROWB
    q_cols = 3 * D // FB
    o_cols = D // FB
    per = FB // BLK
    last = steps + q_cols + o_cols
    cos8, sin8 = tables

    def kernel(
        w_rows_ref, g_rows_ref, w_ref, tok_ref, g_ref, small_ref, o_ref, mlp_ref, dm_ref, dq_ref, dk_ref, dv_ref,
        halo_ref, cos_ref, sin_ref, _,
        out_ref, dx_ref, sum_ref, gr_ref, wqkv, wo, at, dp, das, stage, sems, gsem,
    ):
        i = pl.program_id(0)

        def fetch(first, count, width, dst, sem):
            def body(t):
                src = w_ref.at[pl.ds(pl.multiple_of(w_rows_ref[first + t], 16), BLK)]
                r, c = t // width, t % width
                to = dst.at[pl.ds(pl.multiple_of(r * BLK, BLK), BLK), pl.ds(pl.multiple_of(c * BLK, BLK), BLK)]
                pltpu.make_async_copy(src, to, sem).start()

            tile_loop(0, count, body)

        @pl.when(i == 0)
        def _():
            fetch(0, QKV_TILES, 3 * D // BLK, wqkv, sems.at[1])
            fetch(OUT_BASE, OUT_TILES, D // BLK, wo, sems.at[0])
            sum_ref[...] = jnp.zeros_like(sum_ref)
            pltpu.make_async_copy(wqkv, wqkv, sems.at[1]).wait()

        @pl.when(i == 1)
        def _():
            pltpu.make_async_copy(wo, wo, sems.at[0]).wait()

        def at_block(j):
            return pl.ds(pl.multiple_of(j * ROWB, ROWB), ROWB)

        def add(row, value):
            sum_ref[row : row + 1, :] += jnp.sum(value, axis=0, keepdims=True)

        def front():
            here = at_block(i)
            back_turn = spread_tables(cos_ref[...], -sin_ref[...])
            for j in range(PAIRS):
                cols = j * BLK
                dk_all = dk_ref[j].astype(F32) + halo_ref[0, j].astype(F32)
                dv_all = dv_ref[j].astype(F32) + halo_ref[1, j].astype(F32)
                dp[here, cols : cols + BLK] = dq_ref[j]
                dp[here, D + cols : D + cols + BLK] = rope(dk_all, *back_turn).astype(BF16)
                dp[here, 2 * D + cols : 2 * D + cols + BLK] = dv_all.astype(BF16)
            das[i % 2] = dot(dp[here, :], wqkv[...], NT)

        def back():
            here = at_block(i - 1)
            x = tok_ref[...].astype(F32)
            grad = g_ref[here, :].astype(F32)
            normed, inv = norm_rows(x)
            g1, g2 = small_ref[G1, :], small_ref[G2, :]
            attn = dot(side_by_side(o_ref, here), wo[...]) + small_ref[B_O, :]
            out_ref[...] = (x + attn + (mlp_ref[...].astype(F32) + small_ref[B_DOWN, :])).astype(BF16)
            da = das[(i - 1) % 2]
            at[:, here] = (normed * g1 + small_ref[C1, :]).astype(BF16).T
            dmv = dm_ref[...].astype(F32)
            dn = da * g1 + dmv * g2
            mean_dn = jnp.mean(dn, axis=-1, keepdims=True)
            mean_dnn = jnp.mean(dn * normed, axis=-1, keepdims=True)
            dx_ref[...] = grad + inv * (dn - mean_dn - normed * mean_dnn)
            add(0, dp[here, :D].astype(F32))
            add(1, dp[here, 2 * D :].astype(F32))
            add(2, grad)
            add(3, da * normed)
            add(4, da)
            add(5, dmv * normed)
            add(6, dmv)

        @pl.when(i == 0)
        def _():
            front()

        @pl.when((i > 0) & (i < steps))
        def _():
            back()
            front()

        slot = i % 2

        def drain(sl):
            pltpu.make_async_copy(stage.at[sl], stage.at[sl], gsem.at[sl]).wait()

        def send(first, width, c):
            for t in range(8 * per):
                tile = first + (t // per) * width + c * per + t % per
                dst = gr_ref.at[pl.ds(pl.multiple_of(g_rows_ref[tile], 16), BLK)]
                r, k = t // per * BLK, t % per * BLK
                pltpu.make_async_copy(stage.at[slot, r : r + BLK, k : k + BLK], dst, gsem.at[slot]).start()

        @pl.when(i >= steps + 2)
        def _():
            drain(slot)

        def out_columns(c):
            stage[slot] = dot(side_by_side(o_ref), g_ref[:, c * FB : (c + 1) * FB], TN).astype(BF16)
            send(OUT_BASE, D // BLK, c)

        @pl.when(i == steps)
        def _():
            out_columns(0)
            back()

        @pl.when((i > steps) & (i <= steps + q_cols))
        def _():
            c = i - steps - 1
            stage[slot] = dot(at[...], dp[:, pl.ds(pl.multiple_of(c * FB, FB), FB)]).astype(BF16)
            send(0, 3 * D // BLK, c)

        for c in range(1, o_cols):

            @pl.when(i == steps + q_cols + c)
            def _():
                out_columns(c)

        @pl.when(i == last - 1)
        def _():
            drain(0)
            drain(1)

    ahead = lambda i: jnp.minimum(i, steps - 1)
    behind = lambda i: jnp.clip(i - 1, 0, steps - 1)
    whole = lambda *shape: pl.BlockSpec(shape, lambda i, *_: (0, 0))
    block = pl.BlockSpec((ROWB, D), lambda i, *_: (behind(i), 0))
    pairs = pl.BlockSpec((PAIRS, ROWB, BLK), lambda i, *_: (0, ahead(i), 0))
    table = pl.BlockSpec((ROT // 2, ROWB), lambda i, *_: (0, steps + ahead(i)))
    return pl.pallas_call(
        kernel,
        grid_spec=pltpu.PrefetchScalarGridSpec(
            num_scalar_prefetch=2,
            grid=(last,),
            in_specs=[
                ANY, block, whole(rows, D), whole(16, D), pl.BlockSpec((PAIRS, rows, BLK), lambda i, *_: (0, 0, 0)),
                block, block, pairs, pairs, pairs,
                pl.BlockSpec((2, PAIRS, ROWB, BLK), lambda i, *_: (0, 0, ahead(i), 0)),
                table, table, ANY,
            ],
            out_specs=[block, block, whole(8, D), ANY],
            scratch_shapes=[
                pltpu.VMEM((D, 3 * D), BF16),
                pltpu.VMEM((D, D), BF16),
                pltpu.VMEM((D, rows), BF16),
                pltpu.VMEM((rows, 3 * D), BF16),
                pltpu.VMEM((2, ROWB, D), F32),
                pltpu.VMEM((2, D, FB), BF16),
                pltpu.SemaphoreType.DMA((2,)),
                pltpu.SemaphoreType.DMA((2,)),
            ],
        ),
        out_shape=[
            jax.ShapeDtypeStruct((rows, D), BF16),
            jax.ShapeDtypeStruct((rows, D), F32),
            jax.ShapeDtypeStruct((8, D), F32),
            jax.ShapeDtypeStruct(grads.shape, BF16),
        ],
        input_output_aliases={15: 3},
        compiler_params=params(dimension_semantics=("arbitrary",)),
        name="finish",
    )(w_rows, g_rows, w_all, tokens, cotangent, smalls, attn_out, mlp_out, dm, dq, dk, dv, halo, cos8, sin8, grads)


def halves(x):
    high = x.astype(BF16)
    return high, (x - high.astype(F32)).astype(BF16)


def dot3(a, b, dims=NN):
    return dot(a[0], b[0], dims) + (dot(a[0], b[1], dims) + dot(a[1], b[0], dims))


def update_tiles(ids, roots, grads, tiles, left, right, first, second):
    count = tiles.shape[0]
    group = max(g for g in (1, 2, 3, 4, 6, 8) if count % g == 0)

    def kernel(ids_ref, roots_ref, g_ref, w_ref, l_ref, r_ref, m_ref, v_ref, w_out, low_out, m_out, v_out):
        lane = lax.broadcasted_iota(jnp.int32, (1, BLK), 1)

        def column_scale(t):
            number = ids_ref[pl.program_id(0) * group + t]
            column = number % (3 * D // BLK)
            head = column % PAIRS * 2
            clipped = (number < QKV_TILES) & (column < 2 * PAIRS)
            picked = jnp.where(lane < HEAD, roots_ref[head], roots_ref[head + 1])
            return jnp.where(clipped, picked, 1.0)

        turned = []
        for t in range(group):
            l, r = halves(l_ref[t]), halves(r_ref[t])
            turned.append(dot3(halves(dot3(l, halves(g_ref[t]), TN)), r))
        for t in range(group):
            l, r = halves(l_ref[t]), halves(r_ref[t])
            m_new = BETA * m_ref[t] + (1.0 - BETA) * turned[t]
            v_new = BETA * v_ref[t] + (1.0 - BETA) * turned[t] * turned[t]
            ratio = m_new / (jnp.sqrt(v_new) + ADAM_EPS)
            back = dot3(halves(dot3(l, halves(ratio))), r, NT)
            w_new = (w_ref[t] - LEARN * back) * column_scale(t)
            w_out[t] = w_new
            low_out[t] = w_new.astype(BF16)
            m_out[t] = m_new
            v_out[t] = v_new

    block = pl.BlockSpec((group, BLK, BLK), lambda i, *_: (i, 0, 0))
    like = lambda t: jax.ShapeDtypeStruct(tiles.shape, t)
    return pl.pallas_call(
        kernel,
        grid_spec=pltpu.PrefetchScalarGridSpec(
            num_scalar_prefetch=2,
            grid=(count // group,),
            in_specs=[block] * 6,
            out_specs=[block] * 4,
        ),
        out_shape=[like(F32), like(BF16), like(F32), like(F32)],
        compiler_params=params(dimension_semantics=("arbitrary",)),
        name="update_tiles",
    )(ids, roots, grads, tiles, left, right, first, second)


def small_update(grads, params_, first_moment, second_moment):
    first_new = BETA * first_moment + (1.0 - BETA) * grads
    second_new = BETA * second_moment + (1.0 - BETA) * grads * grads
    updated = params_ - SMALL_LEARN * first_new / (jnp.sqrt(second_new) + ADAM_EPS)
    return (updated, first_new, second_new)


def passed_along(value, axis, steps):
    count = lax.axis_size(axis)
    leading, last = (max(0, -steps), min(count, count - steps))
    return lax.ppermute(value, axis, [(source, source + steps) for source in range(leading, last)])


def on_device(
    ring,
    tokens,
    segments,
    cotangent,
    tile_of_slot,
    tiles,
    left_bases,
    right_bases,
    first_moments,
    second_moments,
    small_params,
    small_first,
    small_second,
    threshold,
):
    rows = tokens.shape[0]
    slot_count = tiles.shape[0]
    small_count = small_params.shape[0]
    axes = ("dp", "seq")
    seq_index = lax.axis_index("seq")
    owner_index = lax.axis_index(axes)
    first_place = seq_index * rows
    seg_rows = jnp.broadcast_to(segments.reshape(1, rows), (8, rows))

    numbers = jnp.arange(TILES, dtype=jnp.int32)
    slot_of_tile = jnp.sum(
        jnp.where(tile_of_slot[None, :] == numbers[:, None], numbers[None, :], 0), axis=1
    ).astype(jnp.int32)
    g_rows = slot_of_tile * BLK

    if ring:
        features = small_count // 12
        kinds = jnp.tile(small_params.reshape(features, 12).T, (1, BLK // features))
        place = jnp.arange(BLK, dtype=jnp.int32) // features == owner_index % (BLK // features)
        small_block = jnp.concatenate([jnp.where(place, kinds, 0.0), jnp.zeros((4, BLK), F32)], axis=0)
        payload = jnp.concatenate(
            [tiles.astype(BF16).reshape(slot_count * BLK, BLK), small_block.astype(BF16)], axis=0
        )
        gathered, prev_tokens, prev_seg = gather_weights(payload, tokens, seg_rows)
        stride = payload.shape[0]
        w_all = gathered.reshape(-1, BLK)
        w_rows = slot_of_tile // slot_count * stride + slot_of_tile % slot_count * BLK
        tail = slot_count * BLK
        group = BLK // features
        by_kind = jnp.sum(gathered[:, tail:, :].astype(F32).reshape(D // BLK, group, 16, BLK), axis=1)
        by_kind = by_kind.transpose(1, 0, 2).reshape(16, D)
    else:
        w_all = lax.all_gather(tiles.astype(BF16), axes, axis=0, tiled=True).reshape(-1, BLK)
        w_rows = g_rows
        small_all = lax.all_gather(small_params.astype(BF16), axes, axis=0, tiled=True)
        by_kind = jnp.pad(small_all.astype(F32).reshape(D, 12).T, ((0, 4), (0, 0)))
        prev_tokens, prev_seg = passed_along((tokens, seg_rows), "seq", 1)

    b_up = by_kind[3:7].T.reshape(1, FF)

    half = ROT // 2
    exponent = jnp.arange(half, dtype=F32) * (2.0 / ROT)
    frequency = jnp.power(ROPE_BASE, -exponent)
    places = first_place - rows + jnp.arange(2 * rows, dtype=jnp.int32)
    angle = places.astype(F32)[None, :] * frequency[:, None]
    cos8, sin8 = jnp.cos(angle), jnp.sin(angle)
    tables = (cos8, sin8)

    q, k, v, d_out, m = project(w_rows, w_all, prev_tokens, tokens, cotangent, by_kind, tables)
    attn_out, dq, dk, dv, halo, peaks = attend(q, k, v, d_out, prev_seg, seg_rows, cos8, sin8)
    halo = passed_along(halo, "seq", -1)
    mlp_out, dm, db_up, grads = feed_forward(w_rows, g_rows, w_all, m, cotangent, b_up)
    block_output, input_grad, sums, grads = finish(
        w_rows, g_rows, w_all, tokens, cotangent, by_kind, attn_out, mlp_out, dm, dq, dk, dv, halo, tables, grads
    )

    small_terms = jnp.concatenate(
        [
            sums[:3].T,
            db_up.reshape(D, FF // D),
            sums[2:7].T,
        ],
        axis=1,
    ).reshape(SMALL)
    head_peak = jnp.max(peaks.reshape(PAIRS, 8, 2, QB)[:, 0], axis=-1).reshape(HEADS)
    if ring:
        peak_rows = jnp.zeros((8, BLK), F32).at[:, :HEADS].set(head_peak[None, :])
        extra = jnp.concatenate([small_terms.reshape(SMALL_ROWS, BLK), peak_rows], axis=0)
        tile_grads, extra = sum_gradients(grads, extra)
        tile_grads = tile_grads.reshape(slot_count, BLK, BLK)
        small_grads = lax.dynamic_slice_in_dim(
            extra[:SMALL_ROWS].reshape(SMALL), owner_index * small_count, small_count, 0
        )
        head_peak = extra[SMALL_ROWS, :HEADS]
    else:
        tile_grads = lax.psum_scatter(
            grads.astype(F32).reshape(TILES, BLK, BLK), axes, scatter_dimension=0, tiled=True
        )
        small_grads = lax.psum_scatter(small_terms, axes, scatter_dimension=0, tiled=True)
        head_peak = lax.pmax(head_peak, axes)

    local_ids = lax.dynamic_slice_in_dim(tile_of_slot, owner_index * slot_count, slot_count, 0)
    limit = threshold[0]
    factors = limit / jnp.maximum(head_peak, limit)
    new_tiles, new_low, new_first, new_second = update_tiles(
        local_ids, jnp.sqrt(factors), tile_grads, tiles, left_bases, right_bases, first_moments, second_moments
    )
    new_small, new_small_first, new_small_second = small_update(
        small_grads, small_params, small_first, small_second
    )
    return (
        block_output,
        input_grad,
        tile_grads,
        small_grads,
        new_tiles,
        new_low,
        new_first,
        new_second,
        new_small,
        new_small.astype(BF16),
        new_small_first,
        new_small_second,
        factors,
    )


def solution(mesh):
    split = P(("dp", "seq"))
    in_specs = (split, P("dp", "seq"), split, P()) + (split,) * 8 + (P(),)
    out_specs = (split,) * 12 + (P(),)
    ring = (mesh.shape["dp"], mesh.shape["seq"]) == (4, 8)
    return jax.shard_map(
        functools.partial(on_device, ring), mesh=mesh, in_specs=in_specs, out_specs=out_specs, check_vma=False
    )
```

```python
import functools

import jax
import jax.numpy as jnp
from jax import lax
from jax.experimental import pallas as pl
from jax.experimental.pallas import tpu as pltpu
from jax.sharding import PartitionSpec as P

D = 1024
FF = 4096
HEADS = 16
HEAD = 64
ROT = 16
BLK = 128
WINDOW = 1024
TILES = 768
SMALL = 12288
QKV_TILES = D // BLK * (3 * D // BLK)
OUT_TILES = D // BLK * (D // BLK)
UP_TILES = D // BLK * (FF // BLK)
OUT_BASE = QKV_TILES
UP_BASE = QKV_TILES + OUT_TILES
DOWN_BASE = UP_BASE + UP_TILES

B_Q, B_V, B_O = slice(0, 1), slice(1, 2), slice(2, 3)
B_DOWN, G1, C1, G2, C2 = slice(7, 8), slice(8, 9), slice(9, 10), slice(10, 11), slice(11, 12)

NORM_EPS = 1e-05
ADAM_EPS = 1e-08
BETA = 0.5
LEARN = 0.03
SMALL_LEARN = 0.2
ROPE_BASE = 10000.0
MASKED = -1e30
HIGH = lax.Precision.HIGHEST

F32 = jnp.float32
BF16 = jnp.bfloat16
MESH = pl.DeviceIdType.MESH
ANY = pl.BlockSpec(memory_space=pl.ANY)
VMEM = pl.BlockSpec(memory_space=pltpu.VMEM)
VMEM_LIMIT = 58 << 20

NN = (((1,), (0,)), ((), ()))
NT = (((1,), (1,)), ((), ()))
TN = (((0,), (0,)), ((), ()))


def dot(a, b, dims=NN, precision=None):
    return lax.dot_general(a, b, dims, precision=precision, preferred_element_type=F32)


def interleave(*parts):
    live = list(parts)
    while live:
        for part in list(live):
            try:
                next(part)
            except StopIteration:
                live.remove(part)


def params(**kw):
    return pltpu.CompilerParams(vmem_limit_bytes=VMEM_LIMIT, **kw)


def norm_rows(x):
    centered = x - jnp.mean(x, axis=-1, keepdims=True)
    inv = lax.rsqrt(jnp.mean(centered * centered, axis=-1, keepdims=True) + NORM_EPS)
    return centered * inv, inv


def tile_loop(first, count, body):
    def step(t, carry):
        body(t)
        return carry

    lax.fori_loop(first, first + count, step, 0)


ROWS_PER_TILE = BLK
HALF_ROWS = 1536


def gather_weights(payload, tokens, seg_rows):
    rows = payload.shape[0]
    top = pl.ds(0, HALF_ROWS)
    low = pl.ds(HALF_ROWS, rows - HALF_ROWS)

    def kernel(x_ref, tok_ref, seg_ref, out_ref, ptok_ref, pseg_ref, lsem, ss, rs, hss, hrs, hls):
        d = lax.axis_index("dp")
        s = lax.axis_index("seq")
        z = s // 2
        c = s % 2
        xn = d + 1 - 2 * (d % 2)
        yn = d + 2 - 4 * (d // 2)
        xyn = 3 - d
        sib = z * 2 + 1 - c
        halo = s - 1 + 2 * c
        halo_ok = ((c == 0) & (z > 0)) | ((c == 1) & (z < 3))

        barrier = pltpu.get_barrier_semaphore()

        def greet(dev):
            pl.semaphore_signal(barrier, inc=1, device_id=dev, device_id_type=MESH)

        greet((d, sib))
        greet((xn, s))
        greet((yn, s))

        @pl.when(z > 0)
        def _():
            greet((d, s - 2))

        @pl.when(z < 3)
        def _():
            greet((d, s + 2))

        @pl.when(halo_ok)
        def _():
            greet((d, halo))

        below, above = (z + 2) // 3, (5 - z) // 3
        pl.semaphore_wait(barrier, 3 + below + above + (1 - c) * below + c * above)

        def place(dd, zz):
            return out_ref.at[dd * 8 + zz * 2 + c]

        def remote(src, dst, kind, zz, dev):
            return pltpu.make_async_remote_copy(
                src_ref=src,
                dst_ref=dst,
                send_sem=ss.at[kind, zz],
                recv_sem=rs.at[kind, zz],
                device_id=dev,
                device_id_type=MESH,
            )

        def block_of(zz, own):
            return x_ref if own else place(d, zz)

        def up(zz, own):
            return remote(block_of(zz, own), place(d, zz), 0, zz, (d, s + 2))

        def down(zz, own):
            return remote(block_of(zz, own), place(d, zz), 1, zz, (d, s - 2))

        def to_x(zz, own):
            return remote(block_of(zz, own), place(d, zz), 2, zz, (xn, s))

        def to_y(zz, own):
            return remote(block_of(zz, own), place(d, zz), 3, zz, (yn, s))

        def on_y(zz):
            return remote(place(xn, zz).at[top], place(xn, zz).at[top], 4, zz, (yn, s))

        def on_x(zz):
            return remote(place(yn, zz).at[low], place(yn, zz).at[low], 5, zz, (xn, s))

        def to_sib(dd, zz, kind, own=False):
            src = x_ref if own else place(dd, zz)
            return remote(src, place(dd, zz), kind, zz, (d, sib))

        def from_x(zz):
            return remote(x_ref, place(xn, zz), 2, zz, (xn, s))

        def from_y(zz):
            return remote(x_ref, place(yn, zz), 3, zz, (yn, s))

        def diag_up(zz):
            return remote(place(xyn, zz), place(xyn, zz), 10, zz, (d, s + 2))

        def diag_down(zz):
            return remote(place(xyn, zz), place(xyn, zz), 11, zz, (d, s - 2))

        def diag_top(zz):
            return remote(x_ref.at[top], place(xyn, zz).at[top], 4, zz, (yn, s))

        def diag_low(zz):
            return remote(x_ref.at[low], place(xyn, zz).at[low], 5, zz, (xn, s))

        order = [z, 1 + z % 2, (2 + 3 * z) % 5, 3 * (1 - z // 2)]
        local = pltpu.make_async_copy(x_ref, place(d, z), lsem)
        local.start()

        def halo_copies(dev):
            tok = pltpu.make_async_remote_copy(
                src_ref=tok_ref,
                dst_ref=ptok_ref,
                send_sem=hss.at[0],
                recv_sem=hrs.at[0],
                device_id=dev,
                device_id_type=MESH,
            )
            seg = pltpu.make_async_remote_copy(
                src_ref=seg_ref,
                dst_ref=pseg_ref,
                send_sem=hss.at[1],
                recv_sem=hrs.at[1],
                device_id=dev,
                device_id_type=MESH,
            )
            return tok, seg

        def in_plane(k, body):
            if k == 0:
                body()
            else:
                pl.when((z - order[k] >= 2) | (order[k] - z >= 3))(body)

        def on_line(k, body):
            pl.when((z - order[k] < 2) & (order[k] - z < 3))(body)

        def launch(k):
            zz = order[k]
            own = k == 0
            if own:

                @pl.when(z < 3)
                def _():
                    up(zz, True).start()

                @pl.when(z > 0)
                def _():
                    down(zz, True).start()
            else:

                @pl.when(zz < z)
                def _():
                    up(zz, False).wait_recv()

                @pl.when((zz < z) & (z < 3))
                def _():
                    up(zz, False).start()

                @pl.when(zz > z)
                def _():
                    down(zz, False).wait_recv()

                @pl.when((zz > z) & (z > 0))
                def _():
                    down(zz, False).start()

            to_x(zz, own).start()
            to_y(zz, own).start()
            to_sib(d, zz, 6, own).start()

        def second(k):
            zz = order[k]

            def pass_on():
                from_x(zz).wait_recv()
                on_y(zz).start()
                to_sib(xn, zz, 7).start()
                from_y(zz).wait_recv()
                on_x(zz).start()
                to_sib(yn, zz, 8).start()

            in_plane(k, pass_on)

        def rest(k):
            zz = order[k]

            def share():
                from_x(zz).wait_recv()
                to_sib(xn, zz, 7).start()
                from_y(zz).wait_recv()
                to_sib(yn, zz, 8).start()

            on_line(k, share)

        def third(k):
            zz = order[k]

            def arrive():
                diag_top(zz).wait_recv()
                diag_low(zz).wait_recv()

            in_plane(k, arrive)
            if k > 0:

                @pl.when((zz < z) & (z - zz <= 1))
                def _():
                    diag_up(zz).wait_recv()

                @pl.when((zz > z) & (zz - z <= 2))
                def _():
                    diag_down(zz).wait_recv()

            if k < 3:

                @pl.when((zz == z) & (z < 3))
                def _():
                    diag_up(zz).start()

                @pl.when((zz >= z) & (zz - z <= 1) & (z > 0))
                def _():
                    diag_down(zz).start()

            to_sib(xyn, zz, 9).start()

        own_tok = pltpu.make_async_copy(tok_ref, ptok_ref, hls.at[0])
        own_seg = pltpu.make_async_copy(seg_ref, pseg_ref, hls.at[1])


        @pl.when(s == 0)
        def _():
            own_tok.start()
            own_seg.start()

        launch(0)
        launch(1)
        second(0)
        launch(2)
        launch(3)
        third(0)
        second(1)
        third(1)
        second(2)

        @pl.when(s < 7)
        def _():
            for cp in halo_copies((d, s + 1)):
                cp.start()

        second(3)
        rest(1)
        rest(2)
        rest(3)
        third(2)
        third(3)

        local.wait()
        other = 1 - c

        def sib_place(dd, zz):
            return out_ref.at[dd * 8 + zz * 2 + other]

        for k in range(4):
            zz = order[k]
            own = k == 0
            for kind, dd in ((6, d), (7, xn), (8, yn), (9, xyn)):
                remote(sib_place(dd, zz), sib_place(dd, zz), kind, zz, (d, sib)).wait_recv()
                to_sib(dd, zz, kind, own and kind == 6).wait_send()
            to_x(zz, own).wait_send()
            to_y(zz, own).wait_send()

            def halves_sent():
                on_y(zz).wait_send()
                on_x(zz).wait_send()

            in_plane(k, halves_sent)
            if k < 3:

                @pl.when((zz == z) & (z < 3))
                def _():
                    diag_up(zz).wait_send()

                @pl.when((zz >= z) & (zz - z <= 1) & (z > 0))
                def _():
                    diag_down(zz).wait_send()

            @pl.when((zz <= z) & (z < 3))
            def _():
                up(zz, own).wait_send()

            @pl.when((zz >= z) & (z > 0))
            def _():
                down(zz, own).wait_send()

        @pl.when(s < 7)
        def _():
            for cp in halo_copies((d, s + 1)):
                cp.wait_send()

        @pl.when(s > 0)
        def _():
            for cp in halo_copies((d, s - 1)):
                cp.wait_recv()

        @pl.when(s == 0)
        def _():
            own_tok.wait()
            own_seg.wait()

    return pl.pallas_call(
        kernel,
        out_shape=[
            jax.ShapeDtypeStruct((32, rows, BLK), BF16),
            jax.ShapeDtypeStruct(tokens.shape, BF16),
            jax.ShapeDtypeStruct(seg_rows.shape, jnp.int32),
        ],
        in_specs=[ANY, ANY, ANY],
        out_specs=[ANY, ANY, ANY],
        scratch_shapes=[
            pltpu.SemaphoreType.DMA,
            pltpu.SemaphoreType.DMA((12, 4)),
            pltpu.SemaphoreType.DMA((12, 4)),
            pltpu.SemaphoreType.DMA((2,)),
            pltpu.SemaphoreType.DMA((2,)),
            pltpu.SemaphoreType.DMA((2,)),
        ],
        compiler_params=params(collective_id=0, has_side_effects=True),
        name="gather_weights",
    )(payload, tokens, seg_rows)


OWNED = 24 * BLK
HALF = OWNED // 2
SMALL_ROWS = SMALL // BLK
EXTRA_ROWS = SMALL_ROWS + 8


def add_rows(dst, terms, rows, step=256):
    def body(i, carry):
        at = pl.ds(pl.multiple_of(i * step, step), step)
        if len(terms) == 2 and dst.dtype == BF16:
            dst[at] = terms[0][at] + terms[1][at]
        else:
            total = terms[0][at].astype(F32)
            for term in terms[1:]:
                total = total + term[at].astype(F32)
            dst[at] = total.astype(dst.dtype)
        return carry

    lax.fori_loop(0, rows // step, body, 0)


SCHEDULE = [
    "F0a", "F1a", "F0b", "F1b", "E0", "F2a", "S0a", "S0b", "D1a", "F2b",
    "S1a", "S1b", "F3a", "E1", "F3b", "D1b", "D2a", "D2b", "S2a", "D3a",
    "S2b", "T0a", "T0b", "E2", "D3b", "T1a", "T1b", "E3", "T2a", "T2b",
    "E4", "S3a", "S3b", "T3a", "T3b",
]


def sum_gradients(grads, extra):
    def kernel(g_ref, e_ref, out_ref, eout_ref, own, crecv, s1a, s1b, s2, zup, zdn, gup, gdn, epart, erecv, ls, ss, rs, es, er):
        d = lax.axis_index("dp")
        s = lax.axis_index("seq")
        z = s // 2
        c = s % 2
        xn = d + 1 - 2 * (d % 2)
        yn = d + 2 - 4 * (d // 2)
        xyn = 3 - d
        sib = z * 2 + 1 - c
        zpair = s + 2 - 4 * (z % 2)
        zfar = s + 4 - 8 * (z // 2)
        barrier = pltpu.get_barrier_semaphore()

        def greet(dev):
            pl.semaphore_signal(barrier, inc=1, device_id=dev, device_id_type=MESH)

        greet((d, sib))
        greet((xn, s))
        greet((yn, s))
        greet((d, zfar))

        @pl.when(z > 0)
        def _():
            greet((d, s - 2))

        @pl.when(z < 3)
        def _():
            greet((d, s + 2))

        order = [3 * (1 - z // 2), (2 + 3 * z) % 5, 1 + z % 2, z]

        ends = (z == 0) | (z == 3)
        inner = (z == 1) | (z == 2)

        def in_plane(k, act):
            if k == 3:
                act()
            elif k == 0:
                pl.when(ends)(act)

        def remote(src, dst, ssem, rsem, dev):
            return pltpu.make_async_remote_copy(
                src_ref=src, dst_ref=dst, send_sem=ssem, recv_sem=rsem, device_id=dev, device_id_type=MESH
            )

        def part(h):
            size = OWNED // 2
            half = size // 2
            rows = pl.ds(h * size, size)
            top = pl.ds(h * size, half)
            low = pl.ds(h * size + half, half)
            here = pl.ds(h * half, half)

            def owner_rows(dd, zz, cc):
                return g_ref.at[pl.ds(pl.multiple_of((dd * 8 + zz * 2 + cc) * OWNED + h * size, size), size)]

            def load(k, dd):
                zz = order[k]
                return pltpu.make_async_copy(owner_rows(dd, zz, c), own.at[zz, dd, rows], ls.at[zz * 2 + h, dd])

            def hop(src, dst, kind, zz, dev):
                return remote(src, dst, ss.at[zz * 2 + h, kind], rs.at[zz * 2 + h, kind], dev)

            def core(zz, dd):
                return hop(owner_rows(dd, zz, 1 - c), crecv.at[zz, dd, rows], dd, zz, (d, sib))

            def y_own(zz):
                return hop(own.at[zz, yn, top], s1a.at[zz, 0, here], 4, zz, (yn, s))

            def y_cross(zz):
                return hop(own.at[zz, xyn, top], s1a.at[zz, 1, here], 5, zz, (yn, s))

            def x_own(zz):
                return hop(own.at[zz, xn, low], s1b.at[zz, 0, here], 6, zz, (xn, s))

            def x_cross(zz):
                return hop(own.at[zz, xyn, low], s1b.at[zz, 1, here], 7, zz, (xn, s))

            def x_last(zz):
                return hop(own.at[zz, xn, top], s2.at[zz, top], 8, zz, (xn, s))

            def y_last(zz):
                return hop(own.at[zz, yn, low], s2.at[zz, low], 9, zz, (yn, s))

            def z_up(zz):
                return hop(own.at[zz, d, rows], zup.at[zz, rows], 10, zz, (d, s + 2))

            def z_dn(zz):
                return hop(own.at[zz, d, rows], zdn.at[zz, rows], 11, zz, (d, s - 2))

            def g_up(zz):
                return hop(own.at[zz, xyn, rows], gup.at[zz, rows], 12, zz, (d, s + 2))

            def g_dn(zz):
                return hop(own.at[zz, xyn, rows], gdn.at[zz, rows], 13, zz, (d, s - 2))

            def cross(zz):
                y_cross(zz).start()
                x_cross(zz).start()

            def along(zz, act):
                @pl.when(zz > z)
                def _():
                    act(g_up(zz))

                @pl.when(zz < z)
                def _():
                    act(g_dn(zz))

            def outward(k, act):
                if k == 0:
                    pl.when(inner)(lambda: along(order[k], act))
                elif k < 3:
                    along(order[k], act)

            def issue(k):
                for dd in (xyn, yn, xn, d):
                    core(order[k], dd).start()

            def first(k):
                zz = order[k]

                def one(dd, start):
                    load(k, dd).wait()
                    core(zz, dd).wait_recv()
                    mine = own.at[zz, dd, rows]
                    add_rows(mine, [mine, crecv.at[zz, dd, rows]], size)
                    for cp in start:
                        cp.start()

                one(xyn, [])
                if k == 0:
                    pl.when(ends)(lambda: cross(zz))
                    outward(0, lambda cp: cp.start())
                elif k < 3:
                    pl.when(ends)(lambda: along(zz, lambda cp: cp.start()))
                one(yn, [y_own(zz)])
                one(xn, [x_own(zz)])
                one(d, [])

            def diagonal(k):
                zz = order[k]
                mine = own.at[zz, xyn, rows]

                def take(cp, came):
                    cp.wait_recv()
                    add_rows(mine, [mine, came.at[zz, rows]], size)

                if k < 3:

                    @pl.when(inner)
                    def _():
                        pl.when(zz > z)(lambda: take(g_up(zz), gup))
                        pl.when(zz < z)(lambda: take(g_dn(zz), gdn))
                        along(zz, lambda cp: cp.start())
                else:
                    pl.when(z > 0)(lambda: take(g_up(zz), gup))
                    pl.when(z < 3)(lambda: take(g_dn(zz), gdn))
                    cross(zz)

            def second(k):
                zz = order[k]
                a = own.at[zz, xn, top]
                b = own.at[zz, yn, low]

                def crossed():
                    y_cross(zz).wait_recv()
                    add_rows(a, [a, s1a.at[zz, 1, here]], half)

                def crossed_low():
                    x_cross(zz).wait_recv()
                    add_rows(b, [b, s1b.at[zz, 1, here]], half)

                in_plane(k, crossed)
                x_last(zz).start()
                in_plane(k, crossed_low)
                y_last(zz).start()

            def third(k):
                zz = order[k]
                for cp in (y_own(zz), x_own(zz), x_last(zz), y_last(zz)):
                    cp.wait_recv()

                def total(to_top, to_low, *came):
                    add_rows(
                        to_top, [own.at[zz, d, top], s1a.at[zz, 0, here], s2.at[zz, top]] + [x.at[zz, top] for x in came], half
                    )
                    add_rows(
                        to_low, [own.at[zz, d, low], s1b.at[zz, 0, here], s2.at[zz, low]] + [x.at[zz, low] for x in came], half
                    )

                if k < 3:
                    mine = (own.at[zz, d, top], own.at[zz, d, low])

                    @pl.when((zz > z) & (z > 0))
                    def _():
                        z_up(zz).wait_recv()
                        total(*mine, zup)

                    @pl.when((zz < z) & (z < 3))
                    def _():
                        z_dn(zz).wait_recv()
                        total(*mine, zdn)

                    @pl.when(((zz > z) & (z == 0)) | ((zz < z) & (z == 3)))
                    def _():
                        total(*mine)

                    pl.when(zz > z)(lambda: z_up(zz).start())
                    pl.when(zz < z)(lambda: z_dn(zz).start())
                else:
                    result = (out_ref.at[top], out_ref.at[low])
                    pl.when(z > 0)(lambda: z_up(zz).wait_recv())
                    pl.when(z < 3)(lambda: z_dn(zz).wait_recv())
                    pl.when(inner)(lambda: total(*result, zup, zdn))
                    pl.when(z == 0)(lambda: total(*result, zdn))
                    pl.when(z == 3)(lambda: total(*result, zup))

            def sent(k):
                zz = order[k]
                for dd in range(4):
                    core(zz, dd).wait_send()
                for cp in (y_own(zz), x_own(zz), x_last(zz), y_last(zz)):
                    cp.wait_send()

                def crosses_sent():
                    y_cross(zz).wait_send()
                    x_cross(zz).wait_send()

                in_plane(k, crosses_sent)
                outward(k, lambda cp: cp.wait_send())
                if k < 3:
                    pl.when(zz > z)(lambda: z_up(zz).wait_send())
                    pl.when(zz < z)(lambda: z_dn(zz).wait_send())

            return dict(load=load, issue=issue, F=first, D=diagonal, S=second, T=third, sent=sent)

        parts = {"a": part(0), "b": part(1)}
        schedule = list(SCHEDULE)
        firsts = [step for step in schedule if step[0] == "F"]
        for step in firsts:
            for dd in (xyn, yn, xn, d):
                parts[step[2]]["load"](int(step[1]), dd).start()

        pl.semaphore_wait(barrier, 4 + (z + 2) // 3 + (5 - z) // 3)

        def issue_next():
            if firsts:
                step = firsts.pop(0)
                parts[step[2]]["issue"](int(step[1]))

        def extra_step(i, dev):
            return remote(epart.at[i], erecv.at[i], es.at[i], er.at[i], dev)

        extra_devs = [(d, sib), (xn, s), (yn, s), (d, zpair), (d, zfar)]

        def extra_add(i):
            extra_step(i, extra_devs[i]).wait_recv()
            a = epart[i]
            b = erecv[i]
            row = lax.broadcasted_iota(jnp.int32, a.shape, 0)
            total = jnp.where(row < SMALL_ROWS, a + b, jnp.maximum(a, b))
            if i < 4:
                epart[i + 1] = total
                extra_step(i + 1, extra_devs[i + 1]).start()
            else:
                eout_ref[...] = total

        issue_next()
        epart[0] = e_ref[...]
        extra_step(0, extra_devs[0]).start()
        for step in schedule:
            if step[0] == "E":
                extra_add(int(step[1]))
            else:
                if step[0] == "F":
                    issue_next()
                parts[step[2]][step[0]](int(step[1]))

        for i in range(5):
            extra_step(i, extra_devs[i]).wait_send()
        for k in range(4):
            for h in "ab":
                parts[h]["sent"](k)

    return pl.pallas_call(
        kernel,
        out_shape=[
            jax.ShapeDtypeStruct((OWNED, BLK), F32),
            jax.ShapeDtypeStruct((EXTRA_ROWS, BLK), F32),
        ],
        in_specs=[ANY, VMEM],
        out_specs=[VMEM, VMEM],
        scratch_shapes=[
            pltpu.VMEM((4, 4, OWNED, BLK), BF16),
            pltpu.VMEM((4, 4, OWNED, BLK), BF16),
            pltpu.VMEM((4, 2, HALF, BLK), BF16),
            pltpu.VMEM((4, 2, HALF, BLK), BF16),
            pltpu.VMEM((4, OWNED, BLK), BF16),
            pltpu.VMEM((4, OWNED, BLK), BF16),
            pltpu.VMEM((4, OWNED, BLK), BF16),
            pltpu.VMEM((4, OWNED, BLK), BF16),
            pltpu.VMEM((4, OWNED, BLK), BF16),
            pltpu.VMEM((5, EXTRA_ROWS, BLK), F32),
            pltpu.VMEM((5, EXTRA_ROWS, BLK), F32),
            pltpu.SemaphoreType.DMA((8, 4)),
            pltpu.SemaphoreType.DMA((8, 14)),
            pltpu.SemaphoreType.DMA((8, 14)),
            pltpu.SemaphoreType.DMA((5,)),
            pltpu.SemaphoreType.DMA((5,)),
        ],
        compiler_params=params(collective_id=1, has_side_effects=True),
        name="sum_gradients",
    )(grads, extra)


ROWB = 256


PAIRS = HEADS // 2


def rope(p, cos_t, fwd_t, back_t):
    return p * cos_t + pltpu.roll(p, BLK - ROT // 2, 1) * fwd_t + pltpu.roll(p, ROT // 2, 1) * back_t


def by_pair(value):
    return [value[:, j * BLK : (j + 1) * BLK] for j in range(PAIRS)]


def side_by_side(ref, at=slice(None)):
    return jnp.concatenate([ref[j, at, :] for j in range(PAIRS)], axis=1)


def spread_tables(cos8, sin8):
    none = jnp.zeros_like(cos8)
    rest = (HEAD - ROT) // none.shape[0]
    cos_t = [cos8, cos8] + [none + 1.0] * rest
    fwd_t = [-sin8, none] + [none] * rest
    back_t = [none, sin8] + [none] * rest
    return [jnp.concatenate(t * 2, axis=0).T for t in (cos_t, fwd_t, back_t)]


PROWS = 512


def project(w_rows, w_all, prev_tokens, tokens, cotangent, smalls, tables):
    rows = tokens.shape[0]
    cos8, sin8 = tables
    steps = rows // PROWS

    def kernel(
        w_rows_ref, w_ref, prev_ref, tok_ref, g_ref, small_ref, cos_ref, sin_ref,
        q_ref, k_ref, v_ref, do_ref, m_ref, wqkv, wo, sems,
    ):
        i = pl.program_id(0)

        def third_copy(third):
            def body(t):
                r, cc = t // 8, t % 8
                src = w_ref.at[pl.ds(pl.multiple_of(w_rows_ref[r * 24 + third * 8 + cc], 16), BLK)]
                dst = wqkv.at[pl.ds(pl.multiple_of(r * BLK, BLK), BLK), pl.ds(pl.multiple_of(third * D + cc * BLK, BLK), BLK)]
                pltpu.make_async_copy(src, dst, sems.at[third]).start()

            tile_loop(0, 64, body)

        def third_wait(third):
            part = wqkv.at[:, pl.ds(third * D, D)]
            pltpu.make_async_copy(part, part, sems.at[third]).wait()

        @pl.when(i == 0)
        def _():
            third_copy(1)
            third_copy(2)
            third_copy(0)

            def body(t):
                r, cc = t // 8, t % 8
                src = w_ref.at[pl.ds(pl.multiple_of(w_rows_ref[OUT_BASE + t], 16), BLK)]
                dst = wo.at[pl.ds(pl.multiple_of(r * BLK, BLK), BLK), pl.ds(pl.multiple_of(cc * BLK, BLK), BLK)]
                pltpu.make_async_copy(src, dst, sems.at[3]).start()

            tile_loop(0, 64, body)
            third_wait(1)
            third_wait(2)

        @pl.when(i == steps)
        def _():
            third_wait(0)
            pltpu.make_async_copy(wo, wo, sems.at[3]).wait()

        n = PROWS // ROWB

        def put(ref, at, pieces):
            for j in range(PAIRS):
                ref[j, at, :] = pieces[j].astype(BF16)

        def run(own):
            x_ref = tok_ref if own else prev_ref
            ins, tabs, raw = {}, {}, {}

            def prepare(c):
                at = slice(c * ROWB, (c + 1) * ROWB)
                normed, _ = norm_rows(x_ref[at, :].astype(F32))
                ins[c] = (normed * small_ref[G1, :] + small_ref[C1, :]).astype(BF16)
                if own:
                    m_ref[at, :] = (normed * small_ref[G2, :] + small_ref[C2, :]).astype(BF16)
                yield
                tabs[c] = spread_tables(cos_ref[:, at], sin_ref[:, at])
                yield

            def multiply(c):
                at = slice(c * ROWB, (c + 1) * ROWB)
                raw[c] = [dot(ins[c], wqkv[:, D : 2 * D])]
                yield
                put(v_ref, at, by_pair(dot(ins[c], wqkv[:, 2 * D :]) + small_ref[B_V, :]))
                yield
                if own:
                    raw[c].append(dot(ins[c], wqkv[:, :D]) + small_ref[B_Q, :])
                    yield
                    put(do_ref, at, by_pair(dot(g_ref[at, :], wo[...], NT)))
                    yield

            def turn(c):
                at = slice(c * ROWB, (c + 1) * ROWB)
                put(k_ref, at, [rope(p, *tabs[c]) for p in by_pair(raw[c][0])])
                yield
                if own:
                    put(q_ref, at, [rope(p, *tabs[c]) for p in by_pair(raw[c][1])])
                    yield

            for c in range(n + 2):
                parts = []
                if 0 <= c - 1 < n:
                    parts.append(multiply(c - 1))
                if c < n:
                    parts.append(prepare(c))
                if 0 <= c - 2 < n:
                    parts.append(turn(c - 2))
                interleave(*parts)

        @pl.when(i < steps)
        def _():
            run(False)

        @pl.when(i >= steps)
        def _():
            run(True)

    before = pl.BlockSpec((PROWS, D), lambda i, *_: (jnp.minimum(i, steps - 1), 0))
    block = pl.BlockSpec((PROWS, D), lambda i, *_: (jnp.maximum(i - steps, 0), 0))
    here = pl.BlockSpec((PAIRS, PROWS, BLK), lambda i, *_: (0, i, 0))
    own = pl.BlockSpec((PAIRS, PROWS, BLK), lambda i, *_: (0, jnp.maximum(i - steps, 0), 0))
    table = pl.BlockSpec((ROT // 2, PROWS), lambda i, *_: (0, i))
    return pl.pallas_call(
        kernel,
        grid_spec=pltpu.PrefetchScalarGridSpec(
            num_scalar_prefetch=1,
            grid=(2 * steps,),
            in_specs=[
                ANY, before, block, block,
                pl.BlockSpec((16, D), lambda i, *_: (0, 0)), table, table,
            ],
            out_specs=[own, here, here, own, block],
            scratch_shapes=[
                pltpu.VMEM((D, 3 * D), BF16),
                pltpu.VMEM((D, D), BF16),
                pltpu.SemaphoreType.DMA((4,)),
            ],
        ),
        out_shape=[
            jax.ShapeDtypeStruct((PAIRS, rows, BLK), BF16),
            jax.ShapeDtypeStruct((PAIRS, 2 * rows, BLK), BF16),
            jax.ShapeDtypeStruct((PAIRS, 2 * rows, BLK), BF16),
            jax.ShapeDtypeStruct((PAIRS, rows, BLK), BF16),
            jax.ShapeDtypeStruct((rows, D), BF16),
        ],
        compiler_params=params(dimension_semantics=("arbitrary",)),
        name="project",
    )(w_rows, w_all, prev_tokens, tokens, cotangent, smalls, cos8, sin8)


QB = 256
SPAN = WINDOW + QB


CHUNK = 256
SAFE_SCORE = 60.0


def attend(q, k, v, d_out, prev_seg, seg, cos8, sin8):
    rows = q.shape[1]
    blocks = rows // QB
    scale = HEAD ** (-0.5)
    half = ROT // 2
    n = SPAN // CHUNK

    def heads_apart(x):
        row = lax.broadcasted_iota(jnp.int32, x.shape, 0)
        zero = jnp.zeros_like(x)
        return jnp.concatenate([jnp.where(row < HEAD, x, zero), jnp.where(row < HEAD, zero, x)], axis=1)

    def stacked(x):
        lane = lax.broadcasted_iota(jnp.int32, x.shape, 1)
        zero = jnp.zeros_like(x)
        return jnp.concatenate([jnp.where(lane < HEAD, x, zero), jnp.where(lane < HEAD, zero, x)], axis=0)

    def fold(x, op):
        return op(x.reshape(x.shape[0] // 8, 8, x.shape[1]), axis=0)

    def two(x):
        return jnp.concatenate([x, x], axis=1)

    def kernel(
        q_ref, k_ref, v_ref, do_ref, pseg_ref, seg_ref, cos_ref, sin_ref,
        o_ref, dq_ref, dk_ref, dv_ref, halo_ref, peak_ref, bias, kt, vt, el_ref, ds_ref, dks, dvs, key_seg, tops,
    ):
        p = pl.program_id(0)

        @pl.when(p == 0)
        def _():
            gap = (
                WINDOW
                + lax.broadcasted_iota(jnp.int32, (SPAN, QB), 1)
                - lax.broadcasted_iota(jnp.int32, (SPAN, QB), 0)
            )
            before = jnp.where(lax.axis_index("seq") == 0, -1, pseg_ref[...]).astype(F32)
            for part, numbers in enumerate((before, seg_ref[...].astype(F32))):
                column = jnp.broadcast_to(numbers[:1, :], (BLK, rows)).T
                key_seg[part * rows : (part + 1) * rows, :] = column
            for i in range(blocks):
                query_seg = seg_ref[:1, i * QB : (i + 1) * QB].astype(F32)
                same = key_seg[i * QB : i * QB + SPAN, :1] == query_seg
                bias[i] = jnp.where((gap >= 0) & (gap < WINDOW) & same, 0.0, MASKED)

        kt[...] = k_ref[...].T
        vt[...] = v_ref[...].T
        k_float = kt[...].astype(F32)
        q_float = q_ref[...].astype(F32) * scale
        reach = jnp.max(jnp.sum(k_float * k_float, axis=0)) * jnp.max(jnp.sum(q_float * q_float, axis=1))
        safe = reach < SAFE_SCORE * SAFE_SCORE

        def rows_from(i, offset, count):
            first = i * QB + offset
            return pl.ds(first if isinstance(i, int) else pl.multiple_of(first, QB), count)

        def keys_at(ref, i, c):
            return ref[rows_from(i, c * CHUNK, CHUNK), :]

        def prepare(i):
            q_all = (q_ref[rows_from(i, 0, QB), :].astype(F32) * scale).astype(BF16)
            return q_all, heads_apart(q_all.T)

        def scores(i, c, q_apart):
            return dot(keys_at(k_ref, i, c), q_apart) + two(bias[i, c * CHUNK : (c + 1) * CHUNK])

        def row_tops(i, q_apart):
            for c in range(n):
                t = fold(scores(i, c, q_apart), jnp.max)
                most = t if c == 0 else jnp.maximum(most, t)
            return jnp.max(most, axis=0, keepdims=True)

        def forward(i, q_apart, found, low=None):
            top8 = sum8 = None
            for c in range(n):
                st = scores(i, c, q_apart)
                e = jnp.exp(st if low is None else st - low)
                el_ref[i % 2, c * CHUNK : (c + 1) * CHUNK] = e.astype(BF16)
                t, u = fold(st, jnp.max), fold(e, jnp.sum)
                top8, sum8 = (t, u) if c == 0 else (jnp.maximum(top8, t), sum8 + u)
                yield
            found.append(jnp.max(top8, axis=0, keepdims=True))
            found.append(1.0 / jnp.sum(sum8, axis=0, keepdims=True))

        def per_head(x):
            return jnp.concatenate(
                [jnp.broadcast_to(x[:, :QB], (HEAD, QB)), jnp.broadcast_to(x[:, QB:], (HEAD, QB))], axis=0
            )

        def both(t, x_ref, i):
            span = rows_from(i, 0, SPAN)
            return jnp.concatenate(
                [dot(t[:HEAD, span], x_ref[i % 2, :, :QB]), dot(t[HEAD:, span], x_ref[i % 2, :, QB:])], axis=0
            )

        def output(i, inv):
            raw = both(vt, el_ref, i)
            inv2 = per_head(inv)
            o_ref[rows_from(i, 0, QB), :] = (raw * inv2).T.astype(BF16)
            do_s = (do_ref[rows_from(i, 0, QB), :].astype(F32).T * inv2).astype(BF16)
            m = do_s.astype(F32) * raw
            mean = jnp.concatenate(
                [jnp.sum(m[:HEAD], axis=0, keepdims=True), jnp.sum(m[HEAD:], axis=0, keepdims=True)], axis=1
            )
            return do_s, mean * inv

        def score_grads(i, do_s, mean):
            do_apart = heads_apart(do_s)
            for c in range(n):
                w = slice(c * CHUNK, (c + 1) * CHUNK)
                dpt = dot(keys_at(v_ref, i, c), do_apart)
                ds_ref[i % 2, w] = (el_ref[i % 2, w].astype(F32) * (dpt - mean)).astype(BF16)

        def input_grads(i, q_all, do_s):
            do_rows = stacked(do_s.T)
            q_rows = stacked(q_all)
            for c in range(n):
                w = slice(c * CHUNK, (c + 1) * CHUNK)
                at = rows_from(i, c * CHUNK, CHUNK)
                v_part = dot(el_ref[i % 2, w], do_rows)
                k_part = dot(ds_ref[i % 2, w], q_rows)
                if c == n - 1 or (isinstance(i, int) and i == 0):
                    dvs[at, :] = v_part
                    dks[at, :] = k_part
                else:
                    dvs[at, :] += v_part
                    dks[at, :] += k_part
                yield
            dq = both(kt, ds_ref, i) * scale
            cos_t, sin_t = cos_ref[:, rows_from(i, 0, QB)], sin_ref[:, rows_from(i, 0, QB)]
            turned = []
            for h in range(2):
                f, g = dq[h * HEAD : h * HEAD + half], dq[h * HEAD + half : h * HEAD + ROT]
                turned += [f * cos_t + g * sin_t, g * cos_t - f * sin_t, dq[h * HEAD + ROT : (h + 1) * HEAD]]
            dq_ref[rows_from(i, 0, QB), :] = jnp.concatenate(turned, axis=0).T.astype(BF16)
            yield

        def run():
            top = held = None
            for i in range(blocks + 1):
                parts, found = [], []
                if held is not None:
                    parts.append(input_grads(i - 1, *held))
                if i < blocks:
                    q_all, q_apart = prepare(i)
                    parts.append(forward(i, q_apart, found))
                interleave(*parts)
                if i < blocks:
                    t, inv = found
                    top = t if top is None else jnp.maximum(top, t)
                    do_s, mean = output(i, inv)
                    score_grads(i, do_s, mean)
                    held = (q_all, do_s)
            tops[...] = jnp.broadcast_to(top, tops.shape)

        def run_shifted():
            dks[:WINDOW, :] = jnp.zeros((WINDOW, BLK), F32)
            dvs[:WINDOW, :] = jnp.zeros((WINDOW, BLK), F32)
            tops[...] = jnp.full(tops.shape, MASKED, F32)

            def body(i, carry):
                q_all, q_apart = prepare(i)
                found = []
                interleave(forward(i, q_apart, found, row_tops(i, q_apart)))
                do_s, mean = output(i, found[1])
                score_grads(i, do_s, mean)
                interleave(input_grads(i, q_all, do_s))
                tops[...] = jnp.maximum(tops[...], found[0])
                return carry

            lax.fori_loop(0, blocks, body, 0)

        pl.when(safe)(run)
        pl.when(jnp.logical_not(safe))(run_shifted)
        head_tops = [jnp.max(tops[0:1, h * QB : (h + 1) * QB], axis=1, keepdims=True) for h in range(2)]
        lane = lax.broadcasted_iota(jnp.int32, peak_ref.shape, 1)
        peak_ref[...] = jnp.where(lane == 0, head_tops[0], head_tops[1])
        halo_ref[0] = dks[:rows, :].astype(BF16)
        halo_ref[1] = dvs[:rows, :].astype(BF16)
        dk_ref[...] = dks[rows:, :].astype(BF16)
        dv_ref[...] = dvs[rows:, :].astype(BF16)

    block = pl.BlockSpec((None, rows, BLK), lambda p: (p, 0, 0))
    keys = pl.BlockSpec((None, 2 * rows, BLK), lambda p: (p, 0, 0))
    whole = lambda *shape: pl.BlockSpec(shape, lambda p: (0, 0))
    own_rot = pl.BlockSpec((half, rows), lambda p: (0, 1))
    return pl.pallas_call(
        kernel,
        grid=(PAIRS,),
        in_specs=[
            block, keys, keys, block, whole(8, rows), whole(8, rows), own_rot, own_rot,
        ],
        out_specs=[
            block, block, block, block,
            pl.BlockSpec((2, None, rows, BLK), lambda p: (0, p, 0, 0)),
            pl.BlockSpec((8, BLK), lambda p: (p, 0)),
        ],
        out_shape=[
            jax.ShapeDtypeStruct((PAIRS, rows, BLK), BF16),
            jax.ShapeDtypeStruct((PAIRS, rows, BLK), BF16),
            jax.ShapeDtypeStruct((PAIRS, rows, BLK), BF16),
            jax.ShapeDtypeStruct((PAIRS, rows, BLK), BF16),
            jax.ShapeDtypeStruct((2, PAIRS, rows, BLK), BF16),
            jax.ShapeDtypeStruct((8 * PAIRS, BLK), F32),
        ],
        scratch_shapes=[
            pltpu.VMEM((blocks, SPAN, QB), F32),
            pltpu.VMEM((BLK, 2 * rows), BF16),
            pltpu.VMEM((BLK, 2 * rows), BF16),
            pltpu.VMEM((2, SPAN, 2 * QB), BF16),
            pltpu.VMEM((2, SPAN, 2 * QB), BF16),
            pltpu.VMEM((2 * rows, BLK), F32),
            pltpu.VMEM((2 * rows, BLK), F32),
            pltpu.VMEM((2 * rows, BLK), F32),
            pltpu.VMEM((8, 2 * QB), F32),
        ],
        compiler_params=params(dimension_semantics=("arbitrary",)),
        cost_estimate=pl.CostEstimate(flops=40 << 30, bytes_accessed=32 << 20, transcendentals=20 << 20),
        name="attend",
    )(q, k, v, d_out, prev_seg, seg, cos8, sin8)


FB = 512


def gelu_parts(v):
    a = jnp.abs(v)
    t = 1.0 / (1.0 + a * (0.3275911 * 0.7071067811865476))
    poly = t * (
        0.5 * 0.254829592
        + t * (0.5 * -0.284496736 + t * (0.5 * 1.421413741 + t * (0.5 * -1.453152027 + t * (0.5 * 1.061405429))))
    )
    e = jnp.exp(v * v * -0.5)
    tail = poly * e
    cdf = jnp.where(v >= 0, 1.0 - tail, tail)
    return v * cdf, cdf + v * e * 0.3989422804014327


def feed_forward(w_rows, g_rows, w_all, m, cotangent, b_up):
    rows = m.shape[0]
    steps = FF // FB

    def kernel(
        w_rows_ref, g_rows_ref, w_ref, m_ref, g_ref, b_ref, low_ref, dml_ref, db_ref, gr_ref,
        mt, wup, wdn, hs, dus, gup, gdn, u_ref, h_ref, out_ref, dm_ref, wsem, gsem,
    ):
        f = pl.program_id(0)
        slot = f % 2
        per = FB // BLK

        def up_at(buf, t):
            return buf.at[pl.ds(pl.multiple_of((t // per) * BLK, BLK), BLK), pl.ds(pl.multiple_of((t % per) * BLK, BLK), BLK)]

        def up_tile(ff, t):
            return UP_BASE + (t // per) * (FF // BLK) + ff * per + t % per

        def down_at(buf, t):
            return buf.at[pl.ds(pl.multiple_of((t // 8) * BLK, BLK), BLK), pl.ds(pl.multiple_of((t % 8) * BLK, BLK), BLK)]

        def down_tile(ff, t):
            return DOWN_BASE + ff * per * 8 + t

        def fetch_one(ff, sl, t):
            src = w_ref.at[pl.ds(pl.multiple_of(w_rows_ref[up_tile(ff, t)], 16), BLK)]
            pltpu.make_async_copy(src, up_at(wup.at[sl], t), wsem.at[0, sl]).start()
            src = w_ref.at[pl.ds(pl.multiple_of(w_rows_ref[down_tile(ff, t)], 16), BLK)]
            pltpu.make_async_copy(src, down_at(wdn.at[sl], t), wsem.at[1, sl]).start()

        def store_one(ff, sl, t):
            dst = gr_ref.at[pl.ds(pl.multiple_of(g_rows_ref[up_tile(ff, t)], 16), BLK)]
            pltpu.make_async_copy(up_at(gup.at[sl], t), dst, gsem.at[0, sl]).start()
            dst = gr_ref.at[pl.ds(pl.multiple_of(g_rows_ref[down_tile(ff, t)], 16), BLK)]
            pltpu.make_async_copy(down_at(gdn.at[sl], t), dst, gsem.at[1, sl]).start()

        def whole_wait(buf, sem):
            pltpu.make_async_copy(buf, buf, sem).wait()

        count = 8 * per

        @pl.when(f == 0)
        def _():
            tile_loop(0, count, lambda t: fetch_one(0, 0, t))
            mt[...] = m_ref[...].T
            out_ref[...] = jnp.zeros_like(out_ref)
            dm_ref[...] = jnp.zeros_like(dm_ref)

        whole_wait(wup.at[slot], wsem.at[0, slot])
        whole_wait(wdn.at[slot], wsem.at[1, slot])

        @pl.when(f >= 2)
        def _():
            whole_wait(gup.at[slot], gsem.at[0, slot])
            whole_wait(gdn.at[slot], gsem.at[1, slot])

        n = rows // ROWB

        def stage1(c):
            at = slice(c * ROWB, (c + 1) * ROWB)
            for k in range(FB // 256):
                cols = slice(k * 256, (k + 1) * 256)
                u_ref[c % 2, :, cols] = dot(m_ref[at, :], wup[slot, :, cols]) + b_ref[:, cols]
                yield
                h_ref[c % 2, :, cols] = dot(g_ref[at, :], wdn[slot, cols, :], NT)
                yield

        db = [None]

        def stage2(c):
            step = ROWB // 8
            for k in range(8):
                at = slice(k * step, (k + 1) * step)
                to = slice(c * ROWB + k * step, c * ROWB + (k + 1) * step)
                hidden, slope = gelu_parts(u_ref[c % 2, at, :])
                hs[to, :] = hidden.astype(BF16)
                du = (h_ref[c % 2, at, :] * slope).astype(BF16)
                dus[to, :] = du
                t = jnp.sum(du.astype(F32).reshape(step // 8, 8, FB), axis=0)
                db[0] = t if db[0] is None else db[0] + t
                yield

        def stage3(c):
            at = slice(c * ROWB, (c + 1) * ROWB)
            for k in range(D // 256):
                cols = slice(k * 256, (k + 1) * 256)
                out_ref[at, cols] += dot(hs[at, :], wdn[slot, :, cols])
                yield
                dm_ref[at, cols] += dot(dus[at, :], wup[slot, cols, :], NT)
                yield

        nxt = jnp.minimum(f + 1, steps - 1)
        for t in range(count):
            fetch_one(nxt, 1 - slot, t)

        for c in range(n + 2):
            gens = []
            if c < n:
                gens.append(stage1(c))
            if 0 <= c - 1 < n:
                gens.append(stage2(c - 1))
            if 0 <= c - 2 < n:
                gens.append(stage3(c - 2))
            interleave(*gens)
        db_ref[...] = jnp.sum(db[0], axis=0, keepdims=True)
        gdn[slot] = dot(hs[...], g_ref[...], TN).astype(BF16)
        gup[slot] = dot(mt[...], dus[...]).astype(BF16)
        for t in range(count):
            store_one(f, slot, t)


        @pl.when(f == steps - 1)
        def _():
            low_ref[...] = out_ref[...].astype(BF16)
            dml_ref[...] = dm_ref[...].astype(BF16)
            whole_wait(wup.at[1 - slot], wsem.at[0, 1 - slot])
            whole_wait(wdn.at[1 - slot], wsem.at[1, 1 - slot])
            for sl in range(2):
                whole_wait(gup.at[sl], gsem.at[0, sl])
                whole_wait(gdn.at[sl], gsem.at[1, sl])

    full = pl.BlockSpec((rows, D), lambda f, *_: (0, 0))
    bias = pl.BlockSpec((1, FB), lambda f, *_: (0, f))
    return pl.pallas_call(
        kernel,
        grid_spec=pltpu.PrefetchScalarGridSpec(
            num_scalar_prefetch=2,
            grid=(steps,),
            in_specs=[ANY, full, full, bias],
            out_specs=[full, full, bias, ANY],
            scratch_shapes=[
                pltpu.VMEM((D, rows), BF16),
                pltpu.VMEM((2, D, FB), BF16),
                pltpu.VMEM((2, FB, D), BF16),
                pltpu.VMEM((rows, FB), BF16),
                pltpu.VMEM((rows, FB), BF16),
                pltpu.VMEM((2, D, FB), BF16),
                pltpu.VMEM((2, FB, D), BF16),
                pltpu.VMEM((2, ROWB, FB), F32),
                pltpu.VMEM((2, ROWB, FB), F32),
                pltpu.VMEM((rows, D), F32),
                pltpu.VMEM((rows, D), F32),
                pltpu.SemaphoreType.DMA((2, 2)),
                pltpu.SemaphoreType.DMA((2, 2)),
            ],
        ),
        out_shape=[
            jax.ShapeDtypeStruct((rows, D), BF16),
            jax.ShapeDtypeStruct((rows, D), BF16),
            jax.ShapeDtypeStruct((1, FF), F32),
            jax.ShapeDtypeStruct((TILES * BLK, BLK), BF16),
        ],
        compiler_params=params(dimension_semantics=("arbitrary",)),
        cost_estimate=pl.CostEstimate(flops=52 << 30, bytes_accessed=48 << 20, transcendentals=8 << 20),
        name="feed_forward",
    )(w_rows, g_rows, w_all, m, cotangent, b_up)


def finish(
    w_rows, g_rows, w_all, tokens, cotangent, smalls, attn_out, mlp_out, dm, dq, dk, dv, halo, tables, grads
):
    rows = tokens.shape[0]
    steps = rows // ROWB
    q_cols = 3 * D // FB
    o_cols = D // FB
    per = FB // BLK
    last = steps + q_cols + o_cols
    cos8, sin8 = tables

    def kernel(
        w_rows_ref, g_rows_ref, w_ref, tok_ref, g_ref, small_ref, o_ref, mlp_ref, dm_ref, dq_ref, dk_ref, dv_ref,
        halo_ref, cos_ref, sin_ref, _,
        out_ref, dx_ref, sum_ref, gr_ref, wqkv, wo, at, dp, das, stage, sems, gsem,
    ):
        i = pl.program_id(0)

        def fetch(first, count, width, dst, sem):
            def body(t):
                src = w_ref.at[pl.ds(pl.multiple_of(w_rows_ref[first + t], 16), BLK)]
                r, c = t // width, t % width
                to = dst.at[pl.ds(pl.multiple_of(r * BLK, BLK), BLK), pl.ds(pl.multiple_of(c * BLK, BLK), BLK)]
                pltpu.make_async_copy(src, to, sem).start()

            tile_loop(0, count, body)

        @pl.when(i == 0)
        def _():
            fetch(0, QKV_TILES, 3 * D // BLK, wqkv, sems.at[1])
            fetch(OUT_BASE, OUT_TILES, D // BLK, wo, sems.at[0])
            sum_ref[...] = jnp.zeros_like(sum_ref)
            pltpu.make_async_copy(wqkv, wqkv, sems.at[1]).wait()

        @pl.when(i == 1)
        def _():
            pltpu.make_async_copy(wo, wo, sems.at[0]).wait()

        def at_block(j):
            return pl.ds(pl.multiple_of(j * ROWB, ROWB), ROWB)

        def add(row, value):
            sum_ref[row : row + 1, :] += jnp.sum(value, axis=0, keepdims=True)

        def front():
            here = at_block(i)
            back_turn = spread_tables(cos_ref[...], -sin_ref[...])
            for j in range(PAIRS):
                cols = j * BLK
                dk_all = dk_ref[j].astype(F32) + halo_ref[0, j].astype(F32)
                dv_all = dv_ref[j].astype(F32) + halo_ref[1, j].astype(F32)
                dp[here, cols : cols + BLK] = dq_ref[j]
                dp[here, D + cols : D + cols + BLK] = rope(dk_all, *back_turn).astype(BF16)
                dp[here, 2 * D + cols : 2 * D + cols + BLK] = dv_all.astype(BF16)
            das[i % 2] = dot(dp[here, :], wqkv[...], NT)

        def back():
            here = at_block(i - 1)
            x = tok_ref[...].astype(F32)
            grad = g_ref[here, :].astype(F32)
            normed, inv = norm_rows(x)
            g1, g2 = small_ref[G1, :], small_ref[G2, :]
            attn = dot(side_by_side(o_ref, here), wo[...]) + small_ref[B_O, :]
            out_ref[...] = (x + attn + (mlp_ref[...].astype(F32) + small_ref[B_DOWN, :])).astype(BF16)
            da = das[(i - 1) % 2]
            at[:, here] = (normed * g1 + small_ref[C1, :]).astype(BF16).T
            dmv = dm_ref[...].astype(F32)
            dn = da * g1 + dmv * g2
            mean_dn = jnp.mean(dn, axis=-1, keepdims=True)
            mean_dnn = jnp.mean(dn * normed, axis=-1, keepdims=True)
            dx_ref[...] = grad + inv * (dn - mean_dn - normed * mean_dnn)
            add(0, dp[here, :D].astype(F32))
            add(1, dp[here, 2 * D :].astype(F32))
            add(2, grad)
            add(3, da * normed)
            add(4, da)
            add(5, dmv * normed)
            add(6, dmv)

        @pl.when(i == 0)
        def _():
            front()

        @pl.when((i > 0) & (i < steps))
        def _():
            back()
            front()

        slot = i % 2

        def drain(sl):
            pltpu.make_async_copy(stage.at[sl], stage.at[sl], gsem.at[sl]).wait()

        def send(first, width, c):
            for t in range(8 * per):
                tile = first + (t // per) * width + c * per + t % per
                dst = gr_ref.at[pl.ds(pl.multiple_of(g_rows_ref[tile], 16), BLK)]
                r, k = t // per * BLK, t % per * BLK
                pltpu.make_async_copy(stage.at[slot, r : r + BLK, k : k + BLK], dst, gsem.at[slot]).start()

        @pl.when(i >= steps + 2)
        def _():
            drain(slot)

        def out_columns(c):
            stage[slot] = dot(side_by_side(o_ref), g_ref[:, c * FB : (c + 1) * FB], TN).astype(BF16)
            send(OUT_BASE, D // BLK, c)

        @pl.when(i == steps)
        def _():
            out_columns(0)
            back()

        @pl.when((i > steps) & (i <= steps + q_cols))
        def _():
            c = i - steps - 1
            stage[slot] = dot(at[...], dp[:, pl.ds(pl.multiple_of(c * FB, FB), FB)]).astype(BF16)
            send(0, 3 * D // BLK, c)

        for c in range(1, o_cols):

            @pl.when(i == steps + q_cols + c)
            def _():
                out_columns(c)

        @pl.when(i == last - 1)
        def _():
            drain(0)
            drain(1)

    ahead = lambda i: jnp.minimum(i, steps - 1)
    behind = lambda i: jnp.clip(i - 1, 0, steps - 1)
    whole = lambda *shape: pl.BlockSpec(shape, lambda i, *_: (0, 0))
    block = pl.BlockSpec((ROWB, D), lambda i, *_: (behind(i), 0))
    pairs = pl.BlockSpec((PAIRS, ROWB, BLK), lambda i, *_: (0, ahead(i), 0))
    table = pl.BlockSpec((ROT // 2, ROWB), lambda i, *_: (0, steps + ahead(i)))
    return pl.pallas_call(
        kernel,
        grid_spec=pltpu.PrefetchScalarGridSpec(
            num_scalar_prefetch=2,
            grid=(last,),
            in_specs=[
                ANY, block, whole(rows, D), whole(16, D), pl.BlockSpec((PAIRS, rows, BLK), lambda i, *_: (0, 0, 0)),
                block, block, pairs, pairs, pairs,
                pl.BlockSpec((2, PAIRS, ROWB, BLK), lambda i, *_: (0, 0, ahead(i), 0)),
                table, table, ANY,
            ],
            out_specs=[block, block, whole(8, D), ANY],
            scratch_shapes=[
                pltpu.VMEM((D, 3 * D), BF16),
                pltpu.VMEM((D, D), BF16),
                pltpu.VMEM((D, rows), BF16),
                pltpu.VMEM((rows, 3 * D), BF16),
                pltpu.VMEM((2, ROWB, D), F32),
                pltpu.VMEM((2, D, FB), BF16),
                pltpu.SemaphoreType.DMA((2,)),
                pltpu.SemaphoreType.DMA((2,)),
            ],
        ),
        out_shape=[
            jax.ShapeDtypeStruct((rows, D), BF16),
            jax.ShapeDtypeStruct((rows, D), F32),
            jax.ShapeDtypeStruct((8, D), F32),
            jax.ShapeDtypeStruct(grads.shape, BF16),
        ],
        input_output_aliases={15: 3},
        compiler_params=params(dimension_semantics=("arbitrary",)),
        name="finish",
    )(w_rows, g_rows, w_all, tokens, cotangent, smalls, attn_out, mlp_out, dm, dq, dk, dv, halo, cos8, sin8, grads)


def halves(x):
    high = x.astype(BF16)
    return high, (x - high.astype(F32)).astype(BF16)


def dot3(a, b, dims=NN):
    return dot(a[0], b[0], dims) + (dot(a[0], b[1], dims) + dot(a[1], b[0], dims))


def update_tiles(ids, roots, grads, tiles, left, right, first, second):
    count = tiles.shape[0]
    group = max(g for g in (1, 2, 3, 4, 6, 8) if count % g == 0)

    first_slot = lambda: (lax.axis_index("dp") * lax.axis_size("seq") + lax.axis_index("seq")) * count

    def kernel(ids_ref, roots_ref, g_ref, w_ref, l_ref, r_ref, m_ref, v_ref, w_out, low_out, m_out, v_out):
        lane = lax.broadcasted_iota(jnp.int32, (1, BLK), 1)

        def column_scale(t):
            number = ids_ref[first_slot() + pl.program_id(0) * group + t]
            column = number % (3 * D // BLK)
            head = column % PAIRS * 2
            clipped = (number < QKV_TILES) & (column < 2 * PAIRS)
            picked = jnp.where(lane < HEAD, roots_ref[head], roots_ref[head + 1])
            return jnp.where(clipped, picked, 1.0)

        turned = []
        for t in range(group):
            l, r = halves(l_ref[t]), halves(r_ref[t])
            turned.append(dot3(halves(dot3(l, halves(g_ref[t]), TN)), r))
        for t in range(group):
            l, r = halves(l_ref[t]), halves(r_ref[t])
            m_new = BETA * m_ref[t] + (1.0 - BETA) * turned[t]
            v_new = BETA * v_ref[t] + (1.0 - BETA) * turned[t] * turned[t]
            ratio = m_new / (jnp.sqrt(v_new) + ADAM_EPS)
            back = dot3(halves(dot3(l, halves(ratio))), r, NT)
            w_new = (w_ref[t] - LEARN * back) * column_scale(t)
            w_out[t] = w_new
            low_out[t] = w_new.astype(BF16)
            m_out[t] = m_new
            v_out[t] = v_new

    block = pl.BlockSpec((group, BLK, BLK), lambda i, *_: (i, 0, 0))
    like = lambda t: jax.ShapeDtypeStruct(tiles.shape, t)
    return pl.pallas_call(
        kernel,
        grid_spec=pltpu.PrefetchScalarGridSpec(
            num_scalar_prefetch=2,
            grid=(count // group,),
            in_specs=[block] * 6,
            out_specs=[block] * 4,
        ),
        out_shape=[like(F32), like(BF16), like(F32), like(F32)],
        compiler_params=params(dimension_semantics=("arbitrary",)),
        name="update_tiles",
    )(ids, roots, grads, tiles, left, right, first, second)


def small_update(grads, params_, first_moment, second_moment):
    first_new = BETA * first_moment + (1.0 - BETA) * grads
    second_new = BETA * second_moment + (1.0 - BETA) * grads * grads
    updated = params_ - SMALL_LEARN * first_new / (jnp.sqrt(second_new) + ADAM_EPS)
    return (updated, first_new, second_new)


def passed_along(value, axis, steps):
    count = lax.axis_size(axis)
    leading, last = (max(0, -steps), min(count, count - steps))
    return lax.ppermute(value, axis, [(source, source + steps) for source in range(leading, last)])


def on_device(
    ring,
    tokens,
    segments,
    cotangent,
    tile_of_slot,
    tiles,
    left_bases,
    right_bases,
    first_moments,
    second_moments,
    small_params,
    small_first,
    small_second,
    threshold,
):
    rows = tokens.shape[0]
    slot_count = tiles.shape[0]
    small_count = small_params.shape[0]
    axes = ("dp", "seq")
    seq_index = lax.axis_index("seq")
    owner_index = lax.axis_index(axes)
    first_place = seq_index * rows
    seg_rows = jnp.broadcast_to(segments.reshape(1, rows), (8, rows))

    numbers = jnp.arange(TILES, dtype=jnp.int32)
    slot_of_tile = jnp.sum(
        jnp.where(tile_of_slot[None, :] == numbers[:, None], numbers[None, :], 0), axis=1
    ).astype(jnp.int32)
    g_rows = slot_of_tile * BLK

    if ring:
        features = small_count // 12
        kinds = jnp.tile(small_params.reshape(features, 12).T, (1, BLK // features))
        place = jnp.arange(BLK, dtype=jnp.int32) // features == owner_index % (BLK // features)
        small_block = jnp.concatenate([jnp.where(place, kinds, 0.0), jnp.zeros((4, BLK), F32)], axis=0)
        payload = jnp.concatenate(
            [tiles.astype(BF16).reshape(slot_count * BLK, BLK), small_block.astype(BF16)], axis=0
        )
        gathered, prev_tokens, prev_seg = gather_weights(payload, tokens, seg_rows)
        stride = payload.shape[0]
        w_all = gathered.reshape(-1, BLK)
        w_rows = slot_of_tile // slot_count * stride + slot_of_tile % slot_count * BLK
        tail = slot_count * BLK
        group = BLK // features
        by_kind = jnp.sum(gathered[:, tail:, :].astype(F32).reshape(D // BLK, group, 16, BLK), axis=1)
        by_kind = by_kind.transpose(1, 0, 2).reshape(16, D)
    else:
        w_all = lax.all_gather(tiles.astype(BF16), axes, axis=0, tiled=True).reshape(-1, BLK)
        w_rows = g_rows
        small_all = lax.all_gather(small_params.astype(BF16), axes, axis=0, tiled=True)
        by_kind = jnp.pad(small_all.astype(F32).reshape(D, 12).T, ((0, 4), (0, 0)))
        prev_tokens, prev_seg = passed_along((tokens, seg_rows), "seq", 1)

    b_up = by_kind[3:7].T.reshape(1, FF)

    half = ROT // 2
    exponent = jnp.arange(half, dtype=F32) * (2.0 / ROT)
    frequency = jnp.power(ROPE_BASE, -exponent)
    places = first_place - rows + jnp.arange(2 * rows, dtype=jnp.int32)
    angle = places.astype(F32)[None, :] * frequency[:, None]
    cos8, sin8 = jnp.cos(angle), jnp.sin(angle)
    tables = (cos8, sin8)

    q, k, v, d_out, m = project(w_rows, w_all, prev_tokens, tokens, cotangent, by_kind, tables)
    attn_out, dq, dk, dv, halo, peaks = attend(q, k, v, d_out, prev_seg, seg_rows, cos8, sin8)
    halo = passed_along(halo, "seq", -1)
    mlp_out, dm, db_up, grads = feed_forward(w_rows, g_rows, w_all, m, cotangent, b_up)
    block_output, input_grad, sums, grads = finish(
        w_rows, g_rows, w_all, tokens, cotangent, by_kind, attn_out, mlp_out, dm, dq, dk, dv, halo, tables, grads
    )

    small_terms = jnp.concatenate(
        [
            sums[:3].T,
            db_up.reshape(D, FF // D),
            sums[2:7].T,
        ],
        axis=1,
    ).reshape(SMALL)
    head_peak = peaks.reshape(PAIRS, 8, BLK)[:, 0, :2].reshape(HEADS)
    if ring:
        peak_rows = jnp.zeros((8, BLK), F32).at[:, :HEADS].set(head_peak[None, :])
        extra = jnp.concatenate([small_terms.reshape(SMALL_ROWS, BLK), peak_rows], axis=0)
        tile_grads, extra = sum_gradients(grads, extra)
        tile_grads = tile_grads.reshape(slot_count, BLK, BLK)
        small_grads = lax.dynamic_slice_in_dim(
            extra[:SMALL_ROWS].reshape(SMALL), owner_index * small_count, small_count, 0
        )
        head_peak = extra[SMALL_ROWS, :HEADS]
    else:
        tile_grads = lax.psum_scatter(
            grads.astype(F32).reshape(TILES, BLK, BLK), axes, scatter_dimension=0, tiled=True
        )
        small_grads = lax.psum_scatter(small_terms, axes, scatter_dimension=0, tiled=True)
        head_peak = lax.pmax(head_peak, axes)

    limit = threshold[0]
    factors = limit / jnp.maximum(head_peak, limit)
    new_tiles, new_low, new_first, new_second = update_tiles(
        tile_of_slot, jnp.sqrt(factors), tile_grads, tiles, left_bases, right_bases, first_moments, second_moments
    )
    new_small, new_small_first, new_small_second = small_update(
        small_grads, small_params, small_first, small_second
    )
    return (
        block_output,
        input_grad,
        tile_grads,
        small_grads,
        new_tiles,
        new_low,
        new_first,
        new_second,
        new_small,
        new_small.astype(BF16),
        new_small_first,
        new_small_second,
        factors,
    )


def solution(mesh):
    split = P(("dp", "seq"))
    in_specs = (split, P("dp", "seq"), split, P()) + (split,) * 8 + (P(),)
    out_specs = (split,) * 12 + (P(),)
    ring = (mesh.shape["dp"], mesh.shape["seq"]) == (4, 8)
    return jax.shard_map(
        functools.partial(on_device, ring), mesh=mesh, in_specs=in_specs, out_specs=out_specs, check_vma=False
    )
```

```python
import functools

import jax
import jax.numpy as jnp
from jax import lax
from jax.experimental import pallas as pl
from jax.experimental.pallas import tpu as pltpu
from jax.sharding import PartitionSpec as P

D = 1024
FF = 4096
HEADS = 16
HEAD = 64
ROT = 16
BLK = 128
WINDOW = 1024
TILES = 768
SMALL = 12288
QKV_TILES = D // BLK * (3 * D // BLK)
OUT_TILES = D // BLK * (D // BLK)
UP_TILES = D // BLK * (FF // BLK)
OUT_BASE = QKV_TILES
UP_BASE = QKV_TILES + OUT_TILES
DOWN_BASE = UP_BASE + UP_TILES

B_Q, B_V, B_O = slice(0, 1), slice(1, 2), slice(2, 3)
B_DOWN, G1, C1, G2, C2 = slice(7, 8), slice(8, 9), slice(9, 10), slice(10, 11), slice(11, 12)

NORM_EPS = 1e-05
ADAM_EPS = 1e-08
BETA = 0.5
LEARN = 0.03
SMALL_LEARN = 0.2
ROPE_BASE = 10000.0
MASKED = -1e30
HIGH = lax.Precision.HIGHEST

F32 = jnp.float32
BF16 = jnp.bfloat16
MESH = pl.DeviceIdType.MESH
ANY = pl.BlockSpec(memory_space=pl.ANY)
VMEM = pl.BlockSpec(memory_space=pltpu.VMEM)
VMEM_LIMIT = 58 << 20

NN = (((1,), (0,)), ((), ()))
NT = (((1,), (1,)), ((), ()))
TN = (((0,), (0,)), ((), ()))


def dot(a, b, dims=NN, precision=None):
    return lax.dot_general(a, b, dims, precision=precision, preferred_element_type=F32)


def interleave(*parts):
    live = list(parts)
    while live:
        for part in list(live):
            try:
                next(part)
            except StopIteration:
                live.remove(part)


def params(**kw):
    return pltpu.CompilerParams(vmem_limit_bytes=VMEM_LIMIT, **kw)


def norm_rows(x):
    centered = x - jnp.mean(x, axis=-1, keepdims=True)
    inv = lax.rsqrt(jnp.mean(centered * centered, axis=-1, keepdims=True) + NORM_EPS)
    return centered * inv, inv


def tile_loop(first, count, body):
    def step(t, carry):
        body(t)
        return carry

    lax.fori_loop(first, first + count, step, 0)


ROWS_PER_TILE = BLK
HALF_ROWS = 1536


def gather_weights(payload, tokens, seg_rows):
    rows = payload.shape[0]
    top = pl.ds(0, HALF_ROWS)
    low = pl.ds(HALF_ROWS, rows - HALF_ROWS)

    def kernel(x_ref, tok_ref, seg_ref, out_ref, ptok_ref, pseg_ref, lsem, ss, rs, hss, hrs, hls):
        d = lax.axis_index("dp")
        s = lax.axis_index("seq")
        z = s // 2
        c = s % 2
        xn = d + 1 - 2 * (d % 2)
        yn = d + 2 - 4 * (d // 2)
        xyn = 3 - d
        sib = z * 2 + 1 - c
        halo = s - 1 + 2 * c
        halo_ok = ((c == 0) & (z > 0)) | ((c == 1) & (z < 3))

        barrier = pltpu.get_barrier_semaphore()

        def greet(dev):
            pl.semaphore_signal(barrier, inc=1, device_id=dev, device_id_type=MESH)

        greet((d, sib))
        greet((xn, s))
        greet((yn, s))

        @pl.when(z > 0)
        def _():
            greet((d, s - 2))

        @pl.when(z < 3)
        def _():
            greet((d, s + 2))

        @pl.when(halo_ok)
        def _():
            greet((d, halo))

        below, above = (z + 2) // 3, (5 - z) // 3
        pl.semaphore_wait(barrier, 3 + below + above + (1 - c) * below + c * above)

        def place(dd, zz):
            return out_ref.at[dd * 8 + zz * 2 + c]

        def remote(src, dst, kind, zz, dev):
            return pltpu.make_async_remote_copy(
                src_ref=src,
                dst_ref=dst,
                send_sem=ss.at[kind, zz],
                recv_sem=rs.at[kind, zz],
                device_id=dev,
                device_id_type=MESH,
            )

        def block_of(zz, own):
            return x_ref if own else place(d, zz)

        def up(zz, own):
            return remote(block_of(zz, own), place(d, zz), 0, zz, (d, s + 2))

        def down(zz, own):
            return remote(block_of(zz, own), place(d, zz), 1, zz, (d, s - 2))

        def to_x(zz, own):
            return remote(block_of(zz, own), place(d, zz), 2, zz, (xn, s))

        def to_y(zz, own):
            return remote(block_of(zz, own), place(d, zz), 3, zz, (yn, s))

        def on_y(zz):
            return remote(place(xn, zz).at[top], place(xn, zz).at[top], 4, zz, (yn, s))

        def on_x(zz):
            return remote(place(yn, zz).at[low], place(yn, zz).at[low], 5, zz, (xn, s))

        def to_sib(dd, zz, kind, own=False):
            src = x_ref if own else place(dd, zz)
            return remote(src, place(dd, zz), kind, zz, (d, sib))

        def from_x(zz):
            return remote(x_ref, place(xn, zz), 2, zz, (xn, s))

        def from_y(zz):
            return remote(x_ref, place(yn, zz), 3, zz, (yn, s))

        def diag_up(zz):
            return remote(place(xyn, zz), place(xyn, zz), 10, zz, (d, s + 2))

        def diag_down(zz):
            return remote(place(xyn, zz), place(xyn, zz), 11, zz, (d, s - 2))

        def diag_top(zz):
            return remote(x_ref.at[top], place(xyn, zz).at[top], 4, zz, (yn, s))

        def diag_low(zz):
            return remote(x_ref.at[low], place(xyn, zz).at[low], 5, zz, (xn, s))

        order = [z, 1 + z % 2, (2 + 3 * z) % 5, 3 * (1 - z // 2)]
        local = pltpu.make_async_copy(x_ref, place(d, z), lsem)
        local.start()

        def halo_copies(dev):
            tok = pltpu.make_async_remote_copy(
                src_ref=tok_ref,
                dst_ref=ptok_ref,
                send_sem=hss.at[0],
                recv_sem=hrs.at[0],
                device_id=dev,
                device_id_type=MESH,
            )
            seg = pltpu.make_async_remote_copy(
                src_ref=seg_ref,
                dst_ref=pseg_ref,
                send_sem=hss.at[1],
                recv_sem=hrs.at[1],
                device_id=dev,
                device_id_type=MESH,
            )
            return tok, seg

        def in_plane(k, body):
            if k == 0:
                body()
            else:
                pl.when((z - order[k] >= 2) | (order[k] - z >= 3))(body)

        def on_line(k, body):
            pl.when((z - order[k] < 2) & (order[k] - z < 3))(body)

        def launch(k):
            zz = order[k]
            own = k == 0
            if own:

                @pl.when(z < 3)
                def _():
                    up(zz, True).start()

                @pl.when(z > 0)
                def _():
                    down(zz, True).start()
            else:

                @pl.when(zz < z)
                def _():
                    up(zz, False).wait_recv()

                @pl.when((zz < z) & (z < 3))
                def _():
                    up(zz, False).start()

                @pl.when(zz > z)
                def _():
                    down(zz, False).wait_recv()

                @pl.when((zz > z) & (z > 0))
                def _():
                    down(zz, False).start()

            to_x(zz, own).start()
            to_y(zz, own).start()
            to_sib(d, zz, 6, own).start()

        def second(k):
            zz = order[k]

            def pass_on():
                from_x(zz).wait_recv()
                on_y(zz).start()
                to_sib(xn, zz, 7).start()
                from_y(zz).wait_recv()
                on_x(zz).start()
                to_sib(yn, zz, 8).start()

            in_plane(k, pass_on)

        def rest(k):
            zz = order[k]

            def share():
                from_x(zz).wait_recv()
                to_sib(xn, zz, 7).start()
                from_y(zz).wait_recv()
                to_sib(yn, zz, 8).start()

            on_line(k, share)

        def third(k):
            zz = order[k]

            def arrive():
                diag_top(zz).wait_recv()
                diag_low(zz).wait_recv()

            in_plane(k, arrive)
            if k > 0:

                @pl.when((zz < z) & (z - zz <= 1))
                def _():
                    diag_up(zz).wait_recv()

                @pl.when((zz > z) & (zz - z <= 2))
                def _():
                    diag_down(zz).wait_recv()

            if k < 3:

                @pl.when((zz == z) & (z < 3))
                def _():
                    diag_up(zz).start()

                @pl.when((zz >= z) & (zz - z <= 1) & (z > 0))
                def _():
                    diag_down(zz).start()

            to_sib(xyn, zz, 9).start()

        own_tok = pltpu.make_async_copy(tok_ref, ptok_ref, hls.at[0])
        own_seg = pltpu.make_async_copy(seg_ref, pseg_ref, hls.at[1])


        @pl.when(s == 0)
        def _():
            own_tok.start()
            own_seg.start()

        launch(0)
        launch(1)
        second(0)
        launch(2)
        launch(3)
        third(0)
        second(1)
        third(1)
        second(2)

        @pl.when(s < 7)
        def _():
            for cp in halo_copies((d, s + 1)):
                cp.start()

        second(3)
        rest(1)
        rest(2)
        rest(3)
        third(2)
        third(3)

        local.wait()
        other = 1 - c

        def sib_place(dd, zz):
            return out_ref.at[dd * 8 + zz * 2 + other]

        for k in range(4):
            zz = order[k]
            own = k == 0
            for kind, dd in ((6, d), (7, xn), (8, yn), (9, xyn)):
                remote(sib_place(dd, zz), sib_place(dd, zz), kind, zz, (d, sib)).wait_recv()
                to_sib(dd, zz, kind, own and kind == 6).wait_send()
            to_x(zz, own).wait_send()
            to_y(zz, own).wait_send()

            def halves_sent():
                on_y(zz).wait_send()
                on_x(zz).wait_send()

            in_plane(k, halves_sent)
            if k < 3:

                @pl.when((zz == z) & (z < 3))
                def _():
                    diag_up(zz).wait_send()

                @pl.when((zz >= z) & (zz - z <= 1) & (z > 0))
                def _():
                    diag_down(zz).wait_send()

            @pl.when((zz <= z) & (z < 3))
            def _():
                up(zz, own).wait_send()

            @pl.when((zz >= z) & (z > 0))
            def _():
                down(zz, own).wait_send()

        @pl.when(s < 7)
        def _():
            for cp in halo_copies((d, s + 1)):
                cp.wait_send()

        @pl.when(s > 0)
        def _():
            for cp in halo_copies((d, s - 1)):
                cp.wait_recv()

        @pl.when(s == 0)
        def _():
            own_tok.wait()
            own_seg.wait()

    return pl.pallas_call(
        kernel,
        out_shape=[
            jax.ShapeDtypeStruct((32, rows, BLK), BF16),
            jax.ShapeDtypeStruct(tokens.shape, BF16),
            jax.ShapeDtypeStruct(seg_rows.shape, jnp.int32),
        ],
        in_specs=[ANY, ANY, ANY],
        out_specs=[ANY, ANY, ANY],
        scratch_shapes=[
            pltpu.SemaphoreType.DMA,
            pltpu.SemaphoreType.DMA((12, 4)),
            pltpu.SemaphoreType.DMA((12, 4)),
            pltpu.SemaphoreType.DMA((2,)),
            pltpu.SemaphoreType.DMA((2,)),
            pltpu.SemaphoreType.DMA((2,)),
        ],
        compiler_params=params(collective_id=0, has_side_effects=True),
        name="gather_weights",
    )(payload, tokens, seg_rows)


OWNED = 24 * BLK
HALF = OWNED // 2
SMALL_ROWS = SMALL // BLK
EXTRA_ROWS = SMALL_ROWS + 8


def add_rows(dst, terms, rows, step=256):
    def body(i, carry):
        at = pl.ds(pl.multiple_of(i * step, step), step)
        if len(terms) == 2 and dst.dtype == BF16:
            dst[at] = terms[0][at] + terms[1][at]
        else:
            total = terms[0][at].astype(F32)
            for term in terms[1:]:
                total = total + term[at].astype(F32)
            dst[at] = total.astype(dst.dtype)
        return carry

    lax.fori_loop(0, rows // step, body, 0)


SCHEDULE = [
    "F0a", "F1a", "F0b", "F1b", "E0", "F2a", "S0a", "S0b", "D1a", "F2b",
    "S1a", "S1b", "F3a", "E1", "F3b", "D1b", "D2a", "D2b", "S2a", "D3a",
    "S2b", "T0a", "T0b", "E2", "D3b", "T1a", "T1b", "E3", "T2a", "T2b",
    "E4", "S3a", "S3b", "T3a", "T3b",
]


def sum_gradients(grads, extra):
    def kernel(g_ref, e_ref, out_ref, eout_ref, own, crecv, s1a, s1b, s2, zup, zdn, gup, gdn, epart, erecv, ls, ss, rs, es, er):
        d = lax.axis_index("dp")
        s = lax.axis_index("seq")
        z = s // 2
        c = s % 2
        xn = d + 1 - 2 * (d % 2)
        yn = d + 2 - 4 * (d // 2)
        xyn = 3 - d
        sib = z * 2 + 1 - c
        zpair = s + 2 - 4 * (z % 2)
        zfar = s + 4 - 8 * (z // 2)
        barrier = pltpu.get_barrier_semaphore()

        def greet(dev):
            pl.semaphore_signal(barrier, inc=1, device_id=dev, device_id_type=MESH)

        greet((d, sib))
        greet((xn, s))
        greet((yn, s))
        greet((d, zfar))

        @pl.when(z > 0)
        def _():
            greet((d, s - 2))

        @pl.when(z < 3)
        def _():
            greet((d, s + 2))

        order = [3 * (1 - z // 2), (2 + 3 * z) % 5, 1 + z % 2, z]

        ends = (z == 0) | (z == 3)
        inner = (z == 1) | (z == 2)

        def in_plane(k, act):
            if k == 3:
                act()
            elif k == 0:
                pl.when(ends)(act)

        def remote(src, dst, ssem, rsem, dev):
            return pltpu.make_async_remote_copy(
                src_ref=src, dst_ref=dst, send_sem=ssem, recv_sem=rsem, device_id=dev, device_id_type=MESH
            )

        def part(h):
            size = OWNED // 2
            half = size // 2
            rows = pl.ds(h * size, size)
            top = pl.ds(h * size, half)
            low = pl.ds(h * size + half, half)
            here = pl.ds(h * half, half)

            def owner_rows(dd, zz, cc):
                return g_ref.at[pl.ds(pl.multiple_of((dd * 8 + zz * 2 + cc) * OWNED + h * size, size), size)]

            def load(k, dd):
                zz = order[k]
                return pltpu.make_async_copy(owner_rows(dd, zz, c), own.at[zz, dd, rows], ls.at[zz * 2 + h, dd])

            def hop(src, dst, kind, zz, dev):
                return remote(src, dst, ss.at[zz * 2 + h, kind], rs.at[zz * 2 + h, kind], dev)

            def core(zz, dd):
                return hop(owner_rows(dd, zz, 1 - c), crecv.at[zz, dd, rows], dd, zz, (d, sib))

            def y_own(zz):
                return hop(own.at[zz, yn, top], s1a.at[zz, 0, here], 4, zz, (yn, s))

            def y_cross(zz):
                return hop(own.at[zz, xyn, top], s1a.at[zz, 1, here], 5, zz, (yn, s))

            def x_own(zz):
                return hop(own.at[zz, xn, low], s1b.at[zz, 0, here], 6, zz, (xn, s))

            def x_cross(zz):
                return hop(own.at[zz, xyn, low], s1b.at[zz, 1, here], 7, zz, (xn, s))

            def x_last(zz):
                return hop(own.at[zz, xn, top], s2.at[zz, top], 8, zz, (xn, s))

            def y_last(zz):
                return hop(own.at[zz, yn, low], s2.at[zz, low], 9, zz, (yn, s))

            def z_up(zz):
                return hop(own.at[zz, d, rows], zup.at[zz, rows], 10, zz, (d, s + 2))

            def z_dn(zz):
                return hop(own.at[zz, d, rows], zdn.at[zz, rows], 11, zz, (d, s - 2))

            def g_up(zz):
                return hop(own.at[zz, xyn, rows], gup.at[zz, rows], 12, zz, (d, s + 2))

            def g_dn(zz):
                return hop(own.at[zz, xyn, rows], gdn.at[zz, rows], 13, zz, (d, s - 2))

            def cross(zz):
                y_cross(zz).start()
                x_cross(zz).start()

            def along(zz, act):
                @pl.when(zz > z)
                def _():
                    act(g_up(zz))

                @pl.when(zz < z)
                def _():
                    act(g_dn(zz))

            def outward(k, act):
                if k == 0:
                    pl.when(inner)(lambda: along(order[k], act))
                elif k < 3:
                    along(order[k], act)

            def issue(k):
                for dd in (xyn, yn, xn, d):
                    core(order[k], dd).start()

            def first(k):
                zz = order[k]

                def one(dd, start):
                    load(k, dd).wait()
                    core(zz, dd).wait_recv()
                    mine = own.at[zz, dd, rows]
                    add_rows(mine, [mine, crecv.at[zz, dd, rows]], size)
                    for cp in start:
                        cp.start()

                one(xyn, [])
                if k == 0:
                    pl.when(ends)(lambda: cross(zz))
                    outward(0, lambda cp: cp.start())
                elif k < 3:
                    pl.when(ends)(lambda: along(zz, lambda cp: cp.start()))
                one(yn, [y_own(zz)])
                one(xn, [x_own(zz)])
                one(d, [])

            def diagonal(k):
                zz = order[k]
                mine = own.at[zz, xyn, rows]

                def take(cp, came):
                    cp.wait_recv()
                    add_rows(mine, [mine, came.at[zz, rows]], size)

                if k < 3:

                    @pl.when(inner)
                    def _():
                        pl.when(zz > z)(lambda: take(g_up(zz), gup))
                        pl.when(zz < z)(lambda: take(g_dn(zz), gdn))
                        along(zz, lambda cp: cp.start())
                else:
                    pl.when(z > 0)(lambda: take(g_up(zz), gup))
                    pl.when(z < 3)(lambda: take(g_dn(zz), gdn))
                    cross(zz)

            def second(k):
                zz = order[k]
                a = own.at[zz, xn, top]
                b = own.at[zz, yn, low]

                def crossed():
                    y_cross(zz).wait_recv()
                    add_rows(a, [a, s1a.at[zz, 1, here]], half)

                def crossed_low():
                    x_cross(zz).wait_recv()
                    add_rows(b, [b, s1b.at[zz, 1, here]], half)

                in_plane(k, crossed)
                x_last(zz).start()
                in_plane(k, crossed_low)
                y_last(zz).start()

            def third(k):
                zz = order[k]
                for cp in (y_own(zz), x_own(zz), x_last(zz), y_last(zz)):
                    cp.wait_recv()

                def total(to_top, to_low, *came):
                    add_rows(
                        to_top, [own.at[zz, d, top], s1a.at[zz, 0, here], s2.at[zz, top]] + [x.at[zz, top] for x in came], half
                    )
                    add_rows(
                        to_low, [own.at[zz, d, low], s1b.at[zz, 0, here], s2.at[zz, low]] + [x.at[zz, low] for x in came], half
                    )

                if k < 3:
                    mine = (own.at[zz, d, top], own.at[zz, d, low])

                    @pl.when((zz > z) & (z > 0))
                    def _():
                        z_up(zz).wait_recv()
                        total(*mine, zup)

                    @pl.when((zz < z) & (z < 3))
                    def _():
                        z_dn(zz).wait_recv()
                        total(*mine, zdn)

                    @pl.when(((zz > z) & (z == 0)) | ((zz < z) & (z == 3)))
                    def _():
                        total(*mine)

                    pl.when(zz > z)(lambda: z_up(zz).start())
                    pl.when(zz < z)(lambda: z_dn(zz).start())
                else:
                    result = (out_ref.at[top], out_ref.at[low])
                    pl.when(z > 0)(lambda: z_up(zz).wait_recv())
                    pl.when(z < 3)(lambda: z_dn(zz).wait_recv())
                    pl.when(inner)(lambda: total(*result, zup, zdn))
                    pl.when(z == 0)(lambda: total(*result, zdn))
                    pl.when(z == 3)(lambda: total(*result, zup))

            def sent(k):
                zz = order[k]
                for dd in range(4):
                    core(zz, dd).wait_send()
                for cp in (y_own(zz), x_own(zz), x_last(zz), y_last(zz)):
                    cp.wait_send()

                def crosses_sent():
                    y_cross(zz).wait_send()
                    x_cross(zz).wait_send()

                in_plane(k, crosses_sent)
                outward(k, lambda cp: cp.wait_send())
                if k < 3:
                    pl.when(zz > z)(lambda: z_up(zz).wait_send())
                    pl.when(zz < z)(lambda: z_dn(zz).wait_send())

            return dict(load=load, issue=issue, F=first, D=diagonal, S=second, T=third, sent=sent)

        parts = {"a": part(0), "b": part(1)}
        schedule = list(SCHEDULE)
        firsts = [step for step in schedule if step[0] == "F"]
        for step in firsts:
            for dd in (xyn, yn, xn, d):
                parts[step[2]]["load"](int(step[1]), dd).start()

        pl.semaphore_wait(barrier, 4 + (z + 2) // 3 + (5 - z) // 3)

        def issue_next():
            if firsts:
                step = firsts.pop(0)
                parts[step[2]]["issue"](int(step[1]))

        def extra_step(i, dev):
            return remote(epart.at[i], erecv.at[i], es.at[i], er.at[i], dev)

        extra_devs = [(d, sib), (xn, s), (yn, s), (d, zpair), (d, zfar)]

        def extra_add(i):
            extra_step(i, extra_devs[i]).wait_recv()
            a = epart[i]
            b = erecv[i]
            row = lax.broadcasted_iota(jnp.int32, a.shape, 0)
            total = jnp.where(row < SMALL_ROWS, a + b, jnp.maximum(a, b))
            if i < 4:
                epart[i + 1] = total
                extra_step(i + 1, extra_devs[i + 1]).start()
            else:
                eout_ref[...] = total

        issue_next()
        epart[0] = e_ref[...]
        extra_step(0, extra_devs[0]).start()
        for step in schedule:
            if step[0] == "E":
                extra_add(int(step[1]))
            else:
                if step[0] == "F":
                    issue_next()
                parts[step[2]][step[0]](int(step[1]))

        for i in range(5):
            extra_step(i, extra_devs[i]).wait_send()
        for k in range(4):
            for h in "ab":
                parts[h]["sent"](k)

    return pl.pallas_call(
        kernel,
        out_shape=[
            jax.ShapeDtypeStruct((OWNED, BLK), F32),
            jax.ShapeDtypeStruct((EXTRA_ROWS, BLK), F32),
        ],
        in_specs=[ANY, VMEM],
        out_specs=[VMEM, VMEM],
        scratch_shapes=[
            pltpu.VMEM((4, 4, OWNED, BLK), BF16),
            pltpu.VMEM((4, 4, OWNED, BLK), BF16),
            pltpu.VMEM((4, 2, HALF, BLK), BF16),
            pltpu.VMEM((4, 2, HALF, BLK), BF16),
            pltpu.VMEM((4, OWNED, BLK), BF16),
            pltpu.VMEM((4, OWNED, BLK), BF16),
            pltpu.VMEM((4, OWNED, BLK), BF16),
            pltpu.VMEM((4, OWNED, BLK), BF16),
            pltpu.VMEM((4, OWNED, BLK), BF16),
            pltpu.VMEM((5, EXTRA_ROWS, BLK), F32),
            pltpu.VMEM((5, EXTRA_ROWS, BLK), F32),
            pltpu.SemaphoreType.DMA((8, 4)),
            pltpu.SemaphoreType.DMA((8, 14)),
            pltpu.SemaphoreType.DMA((8, 14)),
            pltpu.SemaphoreType.DMA((5,)),
            pltpu.SemaphoreType.DMA((5,)),
        ],
        compiler_params=params(collective_id=1, has_side_effects=True),
        name="sum_gradients",
    )(grads, extra)


ROWB = 256


PAIRS = HEADS // 2


def rope(p, cos_t, fwd_t, back_t):
    return p * cos_t + pltpu.roll(p, BLK - ROT // 2, 1) * fwd_t + pltpu.roll(p, ROT // 2, 1) * back_t


def by_pair(value):
    return [value[:, j * BLK : (j + 1) * BLK] for j in range(PAIRS)]


def side_by_side(ref, at=slice(None)):
    return jnp.concatenate([ref[j, at, :] for j in range(PAIRS)], axis=1)


def spread_tables(cos8, sin8):
    none = jnp.zeros_like(cos8)
    rest = (HEAD - ROT) // none.shape[0]
    cos_t = [cos8, cos8] + [none + 1.0] * rest
    fwd_t = [-sin8, none] + [none] * rest
    back_t = [none, sin8] + [none] * rest
    return [jnp.concatenate(t * 2, axis=0).T for t in (cos_t, fwd_t, back_t)]


PROWS = 512


def project(w_rows, w_all, prev_tokens, tokens, cotangent, smalls, tables):
    rows = tokens.shape[0]
    cos8, sin8 = tables
    steps = rows // PROWS

    def kernel(
        w_rows_ref, w_ref, prev_ref, tok_ref, g_ref, small_ref, cos_ref, sin_ref,
        q_ref, k_ref, v_ref, do_ref, m_ref, wqkv, wo, sems,
    ):
        i = pl.program_id(0)

        def third_copy(third):
            def body(t):
                r, cc = t // 8, t % 8
                src = w_ref.at[pl.ds(pl.multiple_of(w_rows_ref[r * 24 + third * 8 + cc], 16), BLK)]
                dst = wqkv.at[pl.ds(pl.multiple_of(r * BLK, BLK), BLK), pl.ds(pl.multiple_of(third * D + cc * BLK, BLK), BLK)]
                pltpu.make_async_copy(src, dst, sems.at[third]).start()

            tile_loop(0, 64, body)

        def third_wait(third):
            part = wqkv.at[:, pl.ds(third * D, D)]
            pltpu.make_async_copy(part, part, sems.at[third]).wait()

        @pl.when(i == 0)
        def _():
            third_copy(1)
            third_copy(2)
            third_copy(0)

            def body(t):
                r, cc = t // 8, t % 8
                src = w_ref.at[pl.ds(pl.multiple_of(w_rows_ref[OUT_BASE + t], 16), BLK)]
                dst = wo.at[pl.ds(pl.multiple_of(r * BLK, BLK), BLK), pl.ds(pl.multiple_of(cc * BLK, BLK), BLK)]
                pltpu.make_async_copy(src, dst, sems.at[3]).start()

            tile_loop(0, 64, body)
            third_wait(1)
            third_wait(2)

        @pl.when(i == steps)
        def _():
            third_wait(0)
            pltpu.make_async_copy(wo, wo, sems.at[3]).wait()

        n = PROWS // ROWB

        def put(ref, at, pieces):
            for j in range(PAIRS):
                ref[j, at, :] = pieces[j].astype(BF16)

        def run(own):
            x_ref = tok_ref if own else prev_ref
            ins, tabs, raw = {}, {}, {}

            def prepare(c):
                at = slice(c * ROWB, (c + 1) * ROWB)
                normed, _ = norm_rows(x_ref[at, :].astype(F32))
                ins[c] = (normed * small_ref[G1, :] + small_ref[C1, :]).astype(BF16)
                if own:
                    m_ref[at, :] = (normed * small_ref[G2, :] + small_ref[C2, :]).astype(BF16)
                yield
                tabs[c] = spread_tables(cos_ref[:, at], sin_ref[:, at])
                yield

            def multiply(c):
                at = slice(c * ROWB, (c + 1) * ROWB)
                raw[c] = [dot(ins[c], wqkv[:, D : 2 * D])]
                yield
                put(v_ref, at, by_pair(dot(ins[c], wqkv[:, 2 * D :]) + small_ref[B_V, :]))
                yield
                if own:
                    raw[c].append(dot(ins[c], wqkv[:, :D]) + small_ref[B_Q, :])
                    yield
                    put(do_ref, at, by_pair(dot(g_ref[at, :], wo[...], NT)))
                    yield

            def turn(c):
                at = slice(c * ROWB, (c + 1) * ROWB)
                put(k_ref, at, [rope(p, *tabs[c]) for p in by_pair(raw[c][0])])
                yield
                if own:
                    put(q_ref, at, [rope(p, *tabs[c]) for p in by_pair(raw[c][1])])
                    yield

            for c in range(n + 2):
                parts = []
                if 0 <= c - 1 < n:
                    parts.append(multiply(c - 1))
                if c < n:
                    parts.append(prepare(c))
                if 0 <= c - 2 < n:
                    parts.append(turn(c - 2))
                interleave(*parts)

        @pl.when(i < steps)
        def _():
            run(False)

        @pl.when(i >= steps)
        def _():
            run(True)

    before = pl.BlockSpec((PROWS, D), lambda i, *_: (jnp.minimum(i, steps - 1), 0))
    block = pl.BlockSpec((PROWS, D), lambda i, *_: (jnp.maximum(i - steps, 0), 0))
    here = pl.BlockSpec((PAIRS, PROWS, BLK), lambda i, *_: (0, i, 0))
    own = pl.BlockSpec((PAIRS, PROWS, BLK), lambda i, *_: (0, jnp.maximum(i - steps, 0), 0))
    table = pl.BlockSpec((ROT // 2, PROWS), lambda i, *_: (0, i))
    return pl.pallas_call(
        kernel,
        grid_spec=pltpu.PrefetchScalarGridSpec(
            num_scalar_prefetch=1,
            grid=(2 * steps,),
            in_specs=[
                ANY, before, block, block,
                pl.BlockSpec((16, D), lambda i, *_: (0, 0)), table, table,
            ],
            out_specs=[own, here, here, own, block],
            scratch_shapes=[
                pltpu.VMEM((D, 3 * D), BF16),
                pltpu.VMEM((D, D), BF16),
                pltpu.SemaphoreType.DMA((4,)),
            ],
        ),
        out_shape=[
            jax.ShapeDtypeStruct((PAIRS, rows, BLK), BF16),
            jax.ShapeDtypeStruct((PAIRS, 2 * rows, BLK), BF16),
            jax.ShapeDtypeStruct((PAIRS, 2 * rows, BLK), BF16),
            jax.ShapeDtypeStruct((PAIRS, rows, BLK), BF16),
            jax.ShapeDtypeStruct((rows, D), BF16),
        ],
        compiler_params=params(dimension_semantics=("arbitrary",)),
        name="project",
    )(w_rows, w_all, prev_tokens, tokens, cotangent, smalls, cos8, sin8)


QB = 256
SPAN = WINDOW + QB


CHUNK = 256
SAFE_SCORE = 60.0


def attend(q, k, v, d_out, prev_seg, seg, cos8, sin8):
    rows = q.shape[1]
    blocks = rows // QB
    scale = HEAD ** (-0.5)
    half = ROT // 2
    n = SPAN // CHUNK

    def heads_apart(x):
        row = lax.broadcasted_iota(jnp.int32, x.shape, 0)
        zero = jnp.zeros_like(x)
        return jnp.concatenate([jnp.where(row < HEAD, x, zero), jnp.where(row < HEAD, zero, x)], axis=1)

    def stacked(x):
        lane = lax.broadcasted_iota(jnp.int32, x.shape, 1)
        zero = jnp.zeros_like(x)
        return jnp.concatenate([jnp.where(lane < HEAD, x, zero), jnp.where(lane < HEAD, zero, x)], axis=0)

    def fold(x, op):
        return op(x.reshape(x.shape[0] // 8, 8, x.shape[1]), axis=0)

    def two(x):
        return jnp.concatenate([x, x], axis=1)

    def kernel(
        q_ref, k_ref, v_ref, do_ref, pseg_ref, seg_ref, cos_ref, sin_ref,
        o_ref, dq_ref, dk_ref, dv_ref, halo_ref, peak_ref, bias, kt, vt, el_ref, ds_ref, dks, dvs, key_seg, tops,
    ):
        p = pl.program_id(0)

        @pl.when(p == 0)
        def _():
            gap = (
                WINDOW
                + lax.broadcasted_iota(jnp.int32, (SPAN, QB), 1)
                - lax.broadcasted_iota(jnp.int32, (SPAN, QB), 0)
            )
            before = jnp.where(lax.axis_index("seq") == 0, -1, pseg_ref[...]).astype(F32)
            for part, numbers in enumerate((before, seg_ref[...].astype(F32))):
                column = jnp.broadcast_to(numbers[:1, :], (BLK, rows)).T
                key_seg[part * rows : (part + 1) * rows, :] = column
            for i in range(blocks):
                query_seg = seg_ref[:1, i * QB : (i + 1) * QB].astype(F32)
                same = key_seg[i * QB : i * QB + SPAN, :1] == query_seg
                bias[i] = jnp.where((gap >= 0) & (gap < WINDOW) & same, 0.0, MASKED)

        kt[...] = k_ref[...].T
        vt[...] = v_ref[...].T
        k_float = kt[...].astype(F32)
        q_float = q_ref[...].astype(F32) * scale
        reach = jnp.max(jnp.sum(k_float * k_float, axis=0)) * jnp.max(jnp.sum(q_float * q_float, axis=1))
        safe = reach < SAFE_SCORE * SAFE_SCORE

        def rows_from(i, offset, count):
            first = i * QB + offset
            return pl.ds(first if isinstance(i, int) else pl.multiple_of(first, QB), count)

        def keys_at(ref, i, c):
            return ref[rows_from(i, c * CHUNK, CHUNK), :]

        def prepare(i):
            q_all = (q_ref[rows_from(i, 0, QB), :].astype(F32) * scale).astype(BF16)
            return q_all, heads_apart(q_all.T)

        def scores(i, c, q_apart):
            return dot(keys_at(k_ref, i, c), q_apart) + two(bias[i, c * CHUNK : (c + 1) * CHUNK])

        def row_tops(i, q_apart):
            for c in range(n):
                t = fold(scores(i, c, q_apart), jnp.max)
                most = t if c == 0 else jnp.maximum(most, t)
            return jnp.max(most, axis=0, keepdims=True)

        def forward(i, q_apart, found, low=None):
            top8 = sum8 = None
            for c in range(n):
                st = scores(i, c, q_apart)
                e = jnp.exp(st if low is None else st - low)
                el_ref[i % 2, c * CHUNK : (c + 1) * CHUNK] = e.astype(BF16)
                t, u = fold(st, jnp.max), fold(e, jnp.sum)
                top8, sum8 = (t, u) if c == 0 else (jnp.maximum(top8, t), sum8 + u)
                yield
            found.append(jnp.max(top8, axis=0, keepdims=True))
            found.append(1.0 / jnp.sum(sum8, axis=0, keepdims=True))

        def per_head(x):
            return jnp.concatenate(
                [jnp.broadcast_to(x[:, :QB], (HEAD, QB)), jnp.broadcast_to(x[:, QB:], (HEAD, QB))], axis=0
            )

        def both(t, x_ref, i):
            span = rows_from(i, 0, SPAN)
            return jnp.concatenate(
                [dot(t[:HEAD, span], x_ref[i % 2, :, :QB]), dot(t[HEAD:, span], x_ref[i % 2, :, QB:])], axis=0
            )

        def output(i, inv):
            raw = both(vt, el_ref, i)
            inv2 = per_head(inv)
            o_ref[rows_from(i, 0, QB), :] = (raw * inv2).T.astype(BF16)
            do_s = (do_ref[rows_from(i, 0, QB), :].astype(F32).T * inv2).astype(BF16)
            m = do_s.astype(F32) * raw
            mean = jnp.concatenate(
                [jnp.sum(m[:HEAD], axis=0, keepdims=True), jnp.sum(m[HEAD:], axis=0, keepdims=True)], axis=1
            )
            return do_s, mean * inv

        def score_grads(i, do_s, mean):
            do_apart = heads_apart(do_s)
            for c in range(n):
                w = slice(c * CHUNK, (c + 1) * CHUNK)
                dpt = dot(keys_at(v_ref, i, c), do_apart)
                ds_ref[i % 2, w] = (el_ref[i % 2, w].astype(F32) * (dpt - mean)).astype(BF16)

        def input_grads(i, q_all, do_s):
            do_rows = stacked(do_s.T)
            q_rows = stacked(q_all)
            for c in range(n):
                w = slice(c * CHUNK, (c + 1) * CHUNK)
                at = rows_from(i, c * CHUNK, CHUNK)
                v_part = dot(el_ref[i % 2, w], do_rows)
                k_part = dot(ds_ref[i % 2, w], q_rows)
                if c == n - 1 or (isinstance(i, int) and i == 0):
                    dvs[at, :] = v_part
                    dks[at, :] = k_part
                else:
                    dvs[at, :] += v_part
                    dks[at, :] += k_part
                yield
            dq = both(kt, ds_ref, i) * scale
            cos_t, sin_t = cos_ref[:, rows_from(i, 0, QB)], sin_ref[:, rows_from(i, 0, QB)]
            turned = []
            for h in range(2):
                f, g = dq[h * HEAD : h * HEAD + half], dq[h * HEAD + half : h * HEAD + ROT]
                turned += [f * cos_t + g * sin_t, g * cos_t - f * sin_t, dq[h * HEAD + ROT : (h + 1) * HEAD]]
            dq_ref[rows_from(i, 0, QB), :] = jnp.concatenate(turned, axis=0).T.astype(BF16)
            yield

        def run():
            top = held = None
            for i in range(blocks + 1):
                parts, found = [], []
                if held is not None:
                    parts.append(input_grads(i - 1, *held))
                if i < blocks:
                    q_all, q_apart = prepare(i)
                    parts.append(forward(i, q_apart, found))
                interleave(*parts)
                if i < blocks:
                    t, inv = found
                    top = t if top is None else jnp.maximum(top, t)
                    do_s, mean = output(i, inv)
                    score_grads(i, do_s, mean)
                    held = (q_all, do_s)
            tops[...] = jnp.broadcast_to(top, tops.shape)

        def run_shifted():
            dks[:WINDOW, :] = jnp.zeros((WINDOW, BLK), F32)
            dvs[:WINDOW, :] = jnp.zeros((WINDOW, BLK), F32)
            tops[...] = jnp.full(tops.shape, MASKED, F32)

            def body(i, carry):
                q_all, q_apart = prepare(i)
                found = []
                interleave(forward(i, q_apart, found, row_tops(i, q_apart)))
                do_s, mean = output(i, found[1])
                score_grads(i, do_s, mean)
                interleave(input_grads(i, q_all, do_s))
                tops[...] = jnp.maximum(tops[...], found[0])
                return carry

            lax.fori_loop(0, blocks, body, 0)

        pl.when(safe)(run)
        pl.when(jnp.logical_not(safe))(run_shifted)
        head_tops = [jnp.max(tops[0:1, h * QB : (h + 1) * QB], axis=1, keepdims=True) for h in range(2)]
        lane = lax.broadcasted_iota(jnp.int32, peak_ref.shape, 1)
        peak_ref[...] = jnp.where(lane == 0, head_tops[0], head_tops[1])
        halo_ref[0] = dks[:rows, :].astype(BF16)
        halo_ref[1] = dvs[:rows, :].astype(BF16)
        dk_ref[...] = dks[rows:, :].astype(BF16)
        dv_ref[...] = dvs[rows:, :].astype(BF16)

    block = pl.BlockSpec((None, rows, BLK), lambda p: (p, 0, 0))
    keys = pl.BlockSpec((None, 2 * rows, BLK), lambda p: (p, 0, 0))
    whole = lambda *shape: pl.BlockSpec(shape, lambda p: (0, 0))
    own_rot = pl.BlockSpec((half, rows), lambda p: (0, 1))
    return pl.pallas_call(
        kernel,
        grid=(PAIRS,),
        in_specs=[
            block, keys, keys, block, whole(8, rows), whole(8, rows), own_rot, own_rot,
        ],
        out_specs=[
            block, block, block, block,
            pl.BlockSpec((2, None, rows, BLK), lambda p: (0, p, 0, 0)),
            pl.BlockSpec((8, BLK), lambda p: (p, 0)),
        ],
        out_shape=[
            jax.ShapeDtypeStruct((PAIRS, rows, BLK), BF16),
            jax.ShapeDtypeStruct((PAIRS, rows, BLK), BF16),
            jax.ShapeDtypeStruct((PAIRS, rows, BLK), BF16),
            jax.ShapeDtypeStruct((PAIRS, rows, BLK), BF16),
            jax.ShapeDtypeStruct((2, PAIRS, rows, BLK), BF16),
            jax.ShapeDtypeStruct((8 * PAIRS, BLK), F32),
        ],
        scratch_shapes=[
            pltpu.VMEM((blocks, SPAN, QB), F32),
            pltpu.VMEM((BLK, 2 * rows), BF16),
            pltpu.VMEM((BLK, 2 * rows), BF16),
            pltpu.VMEM((2, SPAN, 2 * QB), BF16),
            pltpu.VMEM((2, SPAN, 2 * QB), BF16),
            pltpu.VMEM((2 * rows, BLK), F32),
            pltpu.VMEM((2 * rows, BLK), F32),
            pltpu.VMEM((2 * rows, BLK), F32),
            pltpu.VMEM((8, 2 * QB), F32),
        ],
        compiler_params=params(dimension_semantics=("arbitrary",)),
        cost_estimate=pl.CostEstimate(flops=40 << 30, bytes_accessed=32 << 20, transcendentals=20 << 20),
        name="attend",
    )(q, k, v, d_out, prev_seg, seg, cos8, sin8)


FB = 512


def gelu_parts(v):
    a = jnp.abs(v)
    t = 1.0 / (1.0 + a * (0.3275911 * 0.7071067811865476))
    poly = t * (
        0.5 * 0.254829592
        + t * (0.5 * -0.284496736 + t * (0.5 * 1.421413741 + t * (0.5 * -1.453152027 + t * (0.5 * 1.061405429))))
    )
    e = jnp.exp(v * v * -0.5)
    tail = poly * e
    cdf = jnp.where(v >= 0, 1.0 - tail, tail)
    return v * cdf, cdf + v * e * 0.3989422804014327


def feed_forward(w_rows, g_rows, w_all, m, cotangent, b_up):
    rows = m.shape[0]
    steps = FF // FB

    def kernel(
        w_rows_ref, g_rows_ref, w_ref, m_ref, g_ref, b_ref, low_ref, dml_ref, db_ref, gr_ref,
        mt, wup, wdn, hs, dus, gup, gdn, u_ref, h_ref, out_ref, dm_ref, wsem, gsem,
    ):
        f = pl.program_id(0)
        slot = f % 2
        per = FB // BLK

        def up_at(buf, t):
            return buf.at[pl.ds(pl.multiple_of((t // per) * BLK, BLK), BLK), pl.ds(pl.multiple_of((t % per) * BLK, BLK), BLK)]

        def up_tile(ff, t):
            return UP_BASE + (t // per) * (FF // BLK) + ff * per + t % per

        def down_at(buf, t):
            return buf.at[pl.ds(pl.multiple_of((t // 8) * BLK, BLK), BLK), pl.ds(pl.multiple_of((t % 8) * BLK, BLK), BLK)]

        def down_tile(ff, t):
            return DOWN_BASE + ff * per * 8 + t

        def fetch_one(ff, sl, t):
            src = w_ref.at[pl.ds(pl.multiple_of(w_rows_ref[up_tile(ff, t)], 16), BLK)]
            pltpu.make_async_copy(src, up_at(wup.at[sl], t), wsem.at[0, sl]).start()
            src = w_ref.at[pl.ds(pl.multiple_of(w_rows_ref[down_tile(ff, t)], 16), BLK)]
            pltpu.make_async_copy(src, down_at(wdn.at[sl], t), wsem.at[1, sl]).start()

        def store_one(ff, sl, t):
            dst = gr_ref.at[pl.ds(pl.multiple_of(g_rows_ref[up_tile(ff, t)], 16), BLK)]
            pltpu.make_async_copy(up_at(gup.at[sl], t), dst, gsem.at[0, sl]).start()
            dst = gr_ref.at[pl.ds(pl.multiple_of(g_rows_ref[down_tile(ff, t)], 16), BLK)]
            pltpu.make_async_copy(down_at(gdn.at[sl], t), dst, gsem.at[1, sl]).start()

        def whole_wait(buf, sem):
            pltpu.make_async_copy(buf, buf, sem).wait()

        count = 8 * per

        @pl.when(f == 0)
        def _():
            tile_loop(0, count, lambda t: fetch_one(0, 0, t))
            mt[...] = m_ref[...].T
            out_ref[...] = jnp.zeros_like(out_ref)
            dm_ref[...] = jnp.zeros_like(dm_ref)

        whole_wait(wup.at[slot], wsem.at[0, slot])
        whole_wait(wdn.at[slot], wsem.at[1, slot])

        @pl.when(f >= 2)
        def _():
            whole_wait(gup.at[slot], gsem.at[0, slot])
            whole_wait(gdn.at[slot], gsem.at[1, slot])

        n = rows // ROWB

        def stage1(c):
            at = slice(c * ROWB, (c + 1) * ROWB)
            for k in range(FB // 256):
                cols = slice(k * 256, (k + 1) * 256)
                u_ref[c % 2, :, cols] = dot(m_ref[at, :], wup[slot, :, cols]) + b_ref[:, cols]
                yield
                h_ref[c % 2, :, cols] = dot(g_ref[at, :], wdn[slot, cols, :], NT)
                yield

        db = [None]

        def stage2(c):
            step = ROWB // 16
            for k in range(16):
                at = slice(k * step, (k + 1) * step)
                to = slice(c * ROWB + k * step, c * ROWB + (k + 1) * step)
                hidden, slope = gelu_parts(u_ref[c % 2, at, :])
                hs[to, :] = hidden.astype(BF16)
                du = (h_ref[c % 2, at, :] * slope).astype(BF16)
                dus[to, :] = du
                t = jnp.sum(du.astype(F32).reshape(step // 8, 8, FB), axis=0)
                db[0] = t if db[0] is None else db[0] + t
                yield

        def stage3(c):
            at = slice(c * ROWB, (c + 1) * ROWB)
            for k in range(D // 256):
                cols = slice(k * 256, (k + 1) * 256)
                out_ref[at, cols] += dot(hs[at, :], wdn[slot, :, cols])
                yield
                dm_ref[at, cols] += dot(dus[at, :], wup[slot, cols, :], NT)
                yield

        nxt = jnp.minimum(f + 1, steps - 1)
        for t in range(count):
            fetch_one(nxt, 1 - slot, t)

        for c in range(n + 2):
            gens = []
            if c < n:
                gens.append(stage1(c))
            if 0 <= c - 1 < n:
                gens.append(stage2(c - 1))
            if 0 <= c - 2 < n:
                gens.append(stage3(c - 2))
            interleave(*gens)
        db_ref[...] = jnp.sum(db[0], axis=0, keepdims=True)
        gdn[slot] = dot(hs[...], g_ref[...], TN).astype(BF16)
        gup[slot] = dot(mt[...], dus[...]).astype(BF16)
        for t in range(count):
            store_one(f, slot, t)


        @pl.when(f == steps - 1)
        def _():
            low_ref[...] = out_ref[...].astype(BF16)
            dml_ref[...] = dm_ref[...].astype(BF16)
            whole_wait(wup.at[1 - slot], wsem.at[0, 1 - slot])
            whole_wait(wdn.at[1 - slot], wsem.at[1, 1 - slot])
            for sl in range(2):
                whole_wait(gup.at[sl], gsem.at[0, sl])
                whole_wait(gdn.at[sl], gsem.at[1, sl])

    full = pl.BlockSpec((rows, D), lambda f, *_: (0, 0))
    bias = pl.BlockSpec((1, FB), lambda f, *_: (0, f))
    return pl.pallas_call(
        kernel,
        grid_spec=pltpu.PrefetchScalarGridSpec(
            num_scalar_prefetch=2,
            grid=(steps,),
            in_specs=[ANY, full, full, bias],
            out_specs=[full, full, bias, ANY],
            scratch_shapes=[
                pltpu.VMEM((D, rows), BF16),
                pltpu.VMEM((2, D, FB), BF16),
                pltpu.VMEM((2, FB, D), BF16),
                pltpu.VMEM((rows, FB), BF16),
                pltpu.VMEM((rows, FB), BF16),
                pltpu.VMEM((2, D, FB), BF16),
                pltpu.VMEM((2, FB, D), BF16),
                pltpu.VMEM((2, ROWB, FB), F32),
                pltpu.VMEM((2, ROWB, FB), F32),
                pltpu.VMEM((rows, D), F32),
                pltpu.VMEM((rows, D), F32),
                pltpu.SemaphoreType.DMA((2, 2)),
                pltpu.SemaphoreType.DMA((2, 2)),
            ],
        ),
        out_shape=[
            jax.ShapeDtypeStruct((rows, D), BF16),
            jax.ShapeDtypeStruct((rows, D), BF16),
            jax.ShapeDtypeStruct((1, FF), F32),
            jax.ShapeDtypeStruct((TILES * BLK, BLK), BF16),
        ],
        compiler_params=params(dimension_semantics=("arbitrary",)),
        cost_estimate=pl.CostEstimate(flops=52 << 30, bytes_accessed=48 << 20, transcendentals=8 << 20),
        name="feed_forward",
    )(w_rows, g_rows, w_all, m, cotangent, b_up)


def finish(
    w_rows, g_rows, w_all, tokens, cotangent, smalls, attn_out, mlp_out, dm, dq, dk, dv, halo, tables, grads
):
    rows = tokens.shape[0]
    steps = rows // ROWB
    q_cols = 3 * D // FB
    o_cols = D // FB
    per = FB // BLK
    last = steps + q_cols + o_cols
    cos8, sin8 = tables

    def kernel(
        w_rows_ref, g_rows_ref, w_ref, tok_ref, g_ref, small_ref, o_ref, mlp_ref, dm_ref, dq_ref, dk_ref, dv_ref,
        halo_ref, cos_ref, sin_ref, _,
        out_ref, dx_ref, sum_ref, gr_ref, wqkv, wo, at, dp, das, stage, sems, gsem,
    ):
        i = pl.program_id(0)

        def fetch(first, count, width, dst, sem):
            def body(t):
                src = w_ref.at[pl.ds(pl.multiple_of(w_rows_ref[first + t], 16), BLK)]
                r, c = t // width, t % width
                to = dst.at[pl.ds(pl.multiple_of(r * BLK, BLK), BLK), pl.ds(pl.multiple_of(c * BLK, BLK), BLK)]
                pltpu.make_async_copy(src, to, sem).start()

            tile_loop(0, count, body)

        @pl.when(i == 0)
        def _():
            fetch(0, QKV_TILES, 3 * D // BLK, wqkv, sems.at[1])
            fetch(OUT_BASE, OUT_TILES, D // BLK, wo, sems.at[0])
            sum_ref[...] = jnp.zeros_like(sum_ref)
            pltpu.make_async_copy(wqkv, wqkv, sems.at[1]).wait()

        @pl.when(i == 1)
        def _():
            pltpu.make_async_copy(wo, wo, sems.at[0]).wait()

        def at_block(j):
            return pl.ds(pl.multiple_of(j * ROWB, ROWB), ROWB)

        def add(row, value):
            sum_ref[row : row + 1, :] += jnp.sum(value, axis=0, keepdims=True)

        def front():
            here = at_block(i)
            back_turn = spread_tables(cos_ref[...], -sin_ref[...])
            for j in range(PAIRS):
                cols = j * BLK
                dk_all = dk_ref[j].astype(F32) + halo_ref[0, j].astype(F32)
                dv_all = dv_ref[j].astype(F32) + halo_ref[1, j].astype(F32)
                dp[here, cols : cols + BLK] = dq_ref[j]
                dp[here, D + cols : D + cols + BLK] = rope(dk_all, *back_turn).astype(BF16)
                dp[here, 2 * D + cols : 2 * D + cols + BLK] = dv_all.astype(BF16)
            das[i % 2] = dot(dp[here, :], wqkv[...], NT)

        def back():
            here = at_block(i - 1)
            x = tok_ref[...].astype(F32)
            grad = g_ref[here, :].astype(F32)
            normed, inv = norm_rows(x)
            g1, g2 = small_ref[G1, :], small_ref[G2, :]
            attn = dot(side_by_side(o_ref, here), wo[...]) + small_ref[B_O, :]
            out_ref[...] = (x + attn + (mlp_ref[...].astype(F32) + small_ref[B_DOWN, :])).astype(BF16)
            da = das[(i - 1) % 2]
            at[:, here] = (normed * g1 + small_ref[C1, :]).astype(BF16).T
            dmv = dm_ref[...].astype(F32)
            dn = da * g1 + dmv * g2
            mean_dn = jnp.mean(dn, axis=-1, keepdims=True)
            mean_dnn = jnp.mean(dn * normed, axis=-1, keepdims=True)
            dx_ref[...] = grad + inv * (dn - mean_dn - normed * mean_dnn)
            add(0, dp[here, :D].astype(F32))
            add(1, dp[here, 2 * D :].astype(F32))
            add(2, grad)
            add(3, da * normed)
            add(4, da)
            add(5, dmv * normed)
            add(6, dmv)

        @pl.when(i == 0)
        def _():
            front()

        @pl.when((i > 0) & (i < steps))
        def _():
            back()
            front()

        slot = i % 2

        def drain(sl):
            pltpu.make_async_copy(stage.at[sl], stage.at[sl], gsem.at[sl]).wait()

        def send(first, width, c):
            for t in range(8 * per):
                tile = first + (t // per) * width + c * per + t % per
                dst = gr_ref.at[pl.ds(pl.multiple_of(g_rows_ref[tile], 16), BLK)]
                r, k = t // per * BLK, t % per * BLK
                pltpu.make_async_copy(stage.at[slot, r : r + BLK, k : k + BLK], dst, gsem.at[slot]).start()

        @pl.when(i >= steps + 2)
        def _():
            drain(slot)

        def out_columns(c):
            stage[slot] = dot(side_by_side(o_ref), g_ref[:, c * FB : (c + 1) * FB], TN).astype(BF16)
            send(OUT_BASE, D // BLK, c)

        @pl.when(i == steps)
        def _():
            out_columns(0)
            back()

        @pl.when((i > steps) & (i <= steps + q_cols))
        def _():
            c = i - steps - 1
            stage[slot] = dot(at[...], dp[:, pl.ds(pl.multiple_of(c * FB, FB), FB)]).astype(BF16)
            send(0, 3 * D // BLK, c)

        for c in range(1, o_cols):

            @pl.when(i == steps + q_cols + c)
            def _():
                out_columns(c)

        @pl.when(i == last - 1)
        def _():
            drain(0)
            drain(1)

    ahead = lambda i: jnp.minimum(i, steps - 1)
    behind = lambda i: jnp.clip(i - 1, 0, steps - 1)
    whole = lambda *shape: pl.BlockSpec(shape, lambda i, *_: (0, 0))
    block = pl.BlockSpec((ROWB, D), lambda i, *_: (behind(i), 0))
    pairs = pl.BlockSpec((PAIRS, ROWB, BLK), lambda i, *_: (0, ahead(i), 0))
    table = pl.BlockSpec((ROT // 2, ROWB), lambda i, *_: (0, steps + ahead(i)))
    return pl.pallas_call(
        kernel,
        grid_spec=pltpu.PrefetchScalarGridSpec(
            num_scalar_prefetch=2,
            grid=(last,),
            in_specs=[
                ANY, block, whole(rows, D), whole(16, D), pl.BlockSpec((PAIRS, rows, BLK), lambda i, *_: (0, 0, 0)),
                block, block, pairs, pairs, pairs,
                pl.BlockSpec((2, PAIRS, ROWB, BLK), lambda i, *_: (0, 0, ahead(i), 0)),
                table, table, ANY,
            ],
            out_specs=[block, block, whole(8, D), ANY],
            scratch_shapes=[
                pltpu.VMEM((D, 3 * D), BF16),
                pltpu.VMEM((D, D), BF16),
                pltpu.VMEM((D, rows), BF16),
                pltpu.VMEM((rows, 3 * D), BF16),
                pltpu.VMEM((2, ROWB, D), F32),
                pltpu.VMEM((2, D, FB), BF16),
                pltpu.SemaphoreType.DMA((2,)),
                pltpu.SemaphoreType.DMA((2,)),
            ],
        ),
        out_shape=[
            jax.ShapeDtypeStruct((rows, D), BF16),
            jax.ShapeDtypeStruct((rows, D), F32),
            jax.ShapeDtypeStruct((8, D), F32),
            jax.ShapeDtypeStruct(grads.shape, BF16),
        ],
        input_output_aliases={15: 3},
        compiler_params=params(dimension_semantics=("arbitrary",)),
        name="finish",
    )(w_rows, g_rows, w_all, tokens, cotangent, smalls, attn_out, mlp_out, dm, dq, dk, dv, halo, cos8, sin8, grads)


def halves(x):
    high = x.astype(BF16)
    return high, (x - high.astype(F32)).astype(BF16)


def dot3(a, b, dims=NN):
    return dot(a[0], b[0], dims) + (dot(a[0], b[1], dims) + dot(a[1], b[0], dims))


def update_tiles(ids, roots, grads, tiles, left, right, first, second):
    count = tiles.shape[0]
    group = max(g for g in (1, 2, 3, 4, 6, 8) if count % g == 0)

    first_slot = lambda: (lax.axis_index("dp") * lax.axis_size("seq") + lax.axis_index("seq")) * count

    def kernel(ids_ref, roots_ref, g_ref, w_ref, l_ref, r_ref, m_ref, v_ref, w_out, low_out, m_out, v_out):
        lane = lax.broadcasted_iota(jnp.int32, (1, BLK), 1)

        def column_scale(t):
            number = ids_ref[first_slot() + pl.program_id(0) * group + t]
            column = number % (3 * D // BLK)
            head = column % PAIRS * 2
            clipped = (number < QKV_TILES) & (column < 2 * PAIRS)
            picked = jnp.where(lane < HEAD, roots_ref[head], roots_ref[head + 1])
            return jnp.where(clipped, picked, 1.0)

        turned = []
        for t in range(group):
            l, r = halves(l_ref[t]), halves(r_ref[t])
            turned.append(dot3(halves(dot3(l, halves(g_ref[t]), TN)), r))
        for t in range(group):
            l, r = halves(l_ref[t]), halves(r_ref[t])
            m_new = BETA * m_ref[t] + (1.0 - BETA) * turned[t]
            v_new = BETA * v_ref[t] + (1.0 - BETA) * turned[t] * turned[t]
            ratio = m_new / (jnp.sqrt(v_new) + ADAM_EPS)
            back = dot3(halves(dot3(l, halves(ratio))), r, NT)
            w_new = (w_ref[t] - LEARN * back) * column_scale(t)
            w_out[t] = w_new
            low_out[t] = w_new.astype(BF16)
            m_out[t] = m_new
            v_out[t] = v_new

    block = pl.BlockSpec((group, BLK, BLK), lambda i, *_: (i, 0, 0))
    like = lambda t: jax.ShapeDtypeStruct(tiles.shape, t)
    return pl.pallas_call(
        kernel,
        grid_spec=pltpu.PrefetchScalarGridSpec(
            num_scalar_prefetch=2,
            grid=(count // group,),
            in_specs=[block] * 6,
            out_specs=[block] * 4,
        ),
        out_shape=[like(F32), like(BF16), like(F32), like(F32)],
        compiler_params=params(dimension_semantics=("arbitrary",)),
        name="update_tiles",
    )(ids, roots, grads, tiles, left, right, first, second)


def small_update(grads, params_, first_moment, second_moment):
    first_new = BETA * first_moment + (1.0 - BETA) * grads
    second_new = BETA * second_moment + (1.0 - BETA) * grads * grads
    updated = params_ - SMALL_LEARN * first_new / (jnp.sqrt(second_new) + ADAM_EPS)
    return (updated, first_new, second_new)


def passed_along(value, axis, steps):
    count = lax.axis_size(axis)
    leading, last = (max(0, -steps), min(count, count - steps))
    return lax.ppermute(value, axis, [(source, source + steps) for source in range(leading, last)])


def on_device(
    ring,
    tokens,
    segments,
    cotangent,
    tile_of_slot,
    tiles,
    left_bases,
    right_bases,
    first_moments,
    second_moments,
    small_params,
    small_first,
    small_second,
    threshold,
):
    rows = tokens.shape[0]
    slot_count = tiles.shape[0]
    small_count = small_params.shape[0]
    axes = ("dp", "seq")
    seq_index = lax.axis_index("seq")
    owner_index = lax.axis_index(axes)
    first_place = seq_index * rows
    seg_rows = jnp.broadcast_to(segments.reshape(1, rows), (8, rows))

    numbers = jnp.arange(TILES, dtype=jnp.int32)
    slot_of_tile = jnp.sum(
        jnp.where(tile_of_slot[None, :] == numbers[:, None], numbers[None, :], 0), axis=1
    ).astype(jnp.int32)
    g_rows = slot_of_tile * BLK

    if ring:
        features = small_count // 12
        kinds = jnp.tile(small_params.reshape(features, 12).T, (1, BLK // features))
        place = jnp.arange(BLK, dtype=jnp.int32) // features == owner_index % (BLK // features)
        small_block = jnp.concatenate([jnp.where(place, kinds, 0.0), jnp.zeros((4, BLK), F32)], axis=0)
        payload = jnp.concatenate(
            [tiles.astype(BF16).reshape(slot_count * BLK, BLK), small_block.astype(BF16)], axis=0
        )
        gathered, prev_tokens, prev_seg = gather_weights(payload, tokens, seg_rows)
        stride = payload.shape[0]
        w_all = gathered.reshape(-1, BLK)
        w_rows = slot_of_tile // slot_count * stride + slot_of_tile % slot_count * BLK
        tail = slot_count * BLK
        group = BLK // features
        by_kind = jnp.sum(gathered[:, tail:, :].astype(F32).reshape(D // BLK, group, 16, BLK), axis=1)
        by_kind = by_kind.transpose(1, 0, 2).reshape(16, D)
    else:
        w_all = lax.all_gather(tiles.astype(BF16), axes, axis=0, tiled=True).reshape(-1, BLK)
        w_rows = g_rows
        small_all = lax.all_gather(small_params.astype(BF16), axes, axis=0, tiled=True)
        by_kind = jnp.pad(small_all.astype(F32).reshape(D, 12).T, ((0, 4), (0, 0)))
        prev_tokens, prev_seg = passed_along((tokens, seg_rows), "seq", 1)

    b_up = by_kind[3:7].T.reshape(1, FF)

    half = ROT // 2
    exponent = jnp.arange(half, dtype=F32) * (2.0 / ROT)
    frequency = jnp.power(ROPE_BASE, -exponent)
    places = first_place - rows + jnp.arange(2 * rows, dtype=jnp.int32)
    angle = places.astype(F32)[None, :] * frequency[:, None]
    cos8, sin8 = jnp.cos(angle), jnp.sin(angle)
    tables = (cos8, sin8)

    q, k, v, d_out, m = project(w_rows, w_all, prev_tokens, tokens, cotangent, by_kind, tables)
    attn_out, dq, dk, dv, halo, peaks = attend(q, k, v, d_out, prev_seg, seg_rows, cos8, sin8)
    halo = passed_along(halo, "seq", -1)
    mlp_out, dm, db_up, grads = feed_forward(w_rows, g_rows, w_all, m, cotangent, b_up)
    block_output, input_grad, sums, grads = finish(
        w_rows, g_rows, w_all, tokens, cotangent, by_kind, attn_out, mlp_out, dm, dq, dk, dv, halo, tables, grads
    )

    small_terms = jnp.concatenate(
        [
            sums[:3].T,
            db_up.reshape(D, FF // D),
            sums[2:7].T,
        ],
        axis=1,
    ).reshape(SMALL)
    head_peak = peaks.reshape(PAIRS, 8, BLK)[:, 0, :2].reshape(HEADS)
    if ring:
        peak_rows = jnp.zeros((8, BLK), F32).at[:, :HEADS].set(head_peak[None, :])
        extra = jnp.concatenate([small_terms.reshape(SMALL_ROWS, BLK), peak_rows], axis=0)
        tile_grads, extra = sum_gradients(grads, extra)
        tile_grads = tile_grads.reshape(slot_count, BLK, BLK)
        small_grads = lax.dynamic_slice_in_dim(
            extra[:SMALL_ROWS].reshape(SMALL), owner_index * small_count, small_count, 0
        )
        head_peak = extra[SMALL_ROWS, :HEADS]
    else:
        tile_grads = lax.psum_scatter(
            grads.astype(F32).reshape(TILES, BLK, BLK), axes, scatter_dimension=0, tiled=True
        )
        small_grads = lax.psum_scatter(small_terms, axes, scatter_dimension=0, tiled=True)
        head_peak = lax.pmax(head_peak, axes)

    limit = threshold[0]
    factors = limit / jnp.maximum(head_peak, limit)
    new_tiles, new_low, new_first, new_second = update_tiles(
        tile_of_slot, jnp.sqrt(factors), tile_grads, tiles, left_bases, right_bases, first_moments, second_moments
    )
    new_small, new_small_first, new_small_second = small_update(
        small_grads, small_params, small_first, small_second
    )
    return (
        block_output,
        input_grad,
        tile_grads,
        small_grads,
        new_tiles,
        new_low,
        new_first,
        new_second,
        new_small,
        new_small.astype(BF16),
        new_small_first,
        new_small_second,
        factors,
    )


def solution(mesh):
    split = P(("dp", "seq"))
    in_specs = (split, P("dp", "seq"), split, P()) + (split,) * 8 + (P(),)
    out_specs = (split,) * 12 + (P(),)
    ring = (mesh.shape["dp"], mesh.shape["seq"]) == (4, 8)
    return jax.shard_map(
        functools.partial(on_device, ring), mesh=mesh, in_specs=in_specs, out_specs=out_specs, check_vma=False
    )
```
